32 devices in a mesh: ctx: 8 (over y, x, core), fsdp: 4 (over z).
Axes of the slice: x: 2, y: 2, z: 4, core: 2. Of those that a mesh axis runs over, the one named last changes fastest.
Arguments:
- inputs: bfloat16 [4, 1024, 2048], P('fsdp', 'ctx'), may hold values from -6 to 6
- out_grad: bfloat16 [4, 1024, 2048], P('fsdp', 'ctx'), may hold values from -6 to 6
- doc_ids: int32 [4, 1024], P('fsdp'), may hold values from 0 to 2, as said below
- block_pairs: int32 [8, 2], replicated, may hold values from 0 to 15, as said below
- qkv_weight: float32 [2048, 6144], P(('ctx', 'fsdp')), may hold values from -0.125 to 0.125
- proj_weight: float32 [2048, 2048], P(('ctx', 'fsdp')), may hold values from -1.5 to 1.5
- ffn_in_weight: float32 [2048, 11264], P(('ctx', 'fsdp')), may hold values from -0.125 to 0.125
- ffn_out_weight: float32 [5632, 2048], P(('ctx', 'fsdp')), may hold values from -0.078125 to 0.078125
- small_params: float32 [7, 2048], P(None, ('ctx', 'fsdp')), may hold values from -0.9 to 1.4, as said below
- qkv_first: float32 [2048, 6144], P(('ctx', 'fsdp')), may hold values from -40 to 40
- proj_first: float32 [2048, 2048], P(('ctx', 'fsdp')), may hold values from -4 to 4
- ffn_in_first: float32 [2048, 11264], P(('ctx', 'fsdp')), may hold values from -14 to 14
- ffn_out_first: float32 [5632, 2048], P(('ctx', 'fsdp')), may hold values from -24 to 24
- small_first: float32 [7, 2048], P(None, ('ctx', 'fsdp')), may hold values from -64 to 64
- qkv_second: float32 [2048, 6144], P(('ctx', 'fsdp')), may hold values from 217.088 to 860.16
- proj_second: float32 [2048, 2048], P(('ctx', 'fsdp')), may hold values from 1.68 to 6.72
- ffn_in_second: float32 [2048, 11264], P(('ctx', 'fsdp')), may hold values from 23.7568 to 94.208
- ffn_out_second: float32 [5632, 2048], P(('ctx', 'fsdp')), may hold values from 77.824 to 311.296
- small_second: float32 [7, 2048], P(None, ('ctx', 'fsdp')), may hold values from 614.4 to 2457.6
Outputs:
- layer_out: bfloat16 [4, 1024, 2048], P('fsdp', 'ctx')
- input_grad: bfloat16 [4, 1024, 2048], P('fsdp', 'ctx')
- qkv_weight_new: float32 [2048, 6144], P(('ctx', 'fsdp'))
- proj_weight_new: float32 [2048, 2048], P(('ctx', 'fsdp'))
- ffn_in_weight_new: float32 [2048, 11264], P(('ctx', 'fsdp'))
- ffn_out_weight_new: float32 [5632, 2048], P(('ctx', 'fsdp'))
- small_params_new: float32 [7, 2048], P(None, ('ctx', 'fsdp'))
- qkv_first_new: float32 [2048, 6144], P(('ctx', 'fsdp'))
- proj_first_new: float32 [2048, 2048], P(('ctx', 'fsdp'))
- ffn_in_first_new: float32 [2048, 11264], P(('ctx', 'fsdp'))
- ffn_out_first_new: float32 [5632, 2048], P(('ctx', 'fsdp'))
- small_first_new: float32 [7, 2048], P(None, ('ctx', 'fsdp'))
- qkv_second_new: float32 [2048, 6144], P(('ctx', 'fsdp'))
- proj_second_new: float32 [2048, 2048], P(('ctx', 'fsdp'))
- ffn_in_second_new: float32 [2048, 11264], P(('ctx', 'fsdp'))
- ffn_out_second_new: float32 [5632, 2048], P(('ctx', 'fsdp'))
- small_second_new: float32 [7, 2048], P(None, ('ctx', 'fsdp'))
- small_grads: float32 [7, 2048], P(None, ('ctx', 'fsdp'))
The draws below stay inside these ranges and needn't reach their ends.
Inputs may be any that keep to these rules, and one draw needn't show every extreme that they name: `doc_ids`: each row of ids never falls and holds all three documents; the first and the last document each hold 128 to 256 positions. `block_pairs`: every half-block of positions is named exactly once; the two numbers of a row add up to 15. `small_params`: rows 0 and 2 lie in 0.6 to 1.4; the other rows are biases.
All inputs are finite; a program needn't handle non-finite values.
Results may differ from the reference program's by a relative error of at most 0.017.
Values may be sent and summed in bfloat16 or wider, within the bound.
A program may use at most 512 MiB of HBM per device.

```python
import math
import jax
import jax.numpy as jnp
from jax import lax

D = 2048
HEADS = 32
HEAD_DIM = 64
FF = 5632
ROT = 16
TOK_DEV = 128
STEP = 10
SEQ_LEN = 1024
SEQS = 4
TOKENS = 4096


def draw_doc_ids(key, part):
    key = jax.random.fold_in(key, 23)
    first_key, last_key = jax.random.split(key)
    lowest = SEQ_LEN // 8
    highest = SEQ_LEN // 4
    first_len = jax.random.randint(first_key, (SEQS, 1), lowest, highest + 1).astype(jnp.int32)
    last_len = jax.random.randint(last_key, (SEQS, 1), lowest, highest + 1).astype(jnp.int32)
    places = jnp.arange(SEQ_LEN, dtype=jnp.int32)[None, :]
    return (places >= first_len).astype(jnp.int32) + (places >= SEQ_LEN - last_len).astype(jnp.int32)


def draw_block_pairs(key, part):
    key = jax.random.fold_in(key, 11)
    order_key, flip_key = jax.random.split(key)
    slots = SEQ_LEN // TOK_DEV
    order = jax.random.permutation(order_key, slots).astype(jnp.int32)
    flipped = jax.random.randint(flip_key, (slots,), 0, 2).astype(jnp.int32)
    mirror = 2 * slots - 1 - order
    first_half = jnp.where(flipped == 1, mirror, order)
    second_half = jnp.where(flipped == 1, order, mirror)
    return jnp.stack([first_half, second_half], axis=1).astype(jnp.int32)


def draw_small_params(key, part):
    key = jax.random.fold_in(key, 37)
    gain_key, shift_key, bias_key = jax.random.split(key, 3)
    gains = jax.random.uniform(gain_key, (2, D), jnp.float32, 0.6, 1.4)
    shifts = 0.3 * jnp.clip(jax.random.normal(shift_key, (2, D), jnp.float32), -3.0, 3.0)
    biases = 0.03 * jnp.clip(jax.random.normal(bias_key, (3, D), jnp.float32), -3.0, 3.0)
    return jnp.concatenate([gains[0:1], shifts[0:1], gains[1:2], shifts[1:2], biases], axis=0)


def levels(stream_key, shape, shards, low, top_value):
    gain, own = 1.0, jax.random.fold_in(stream_key, 6)
    for axis_at, parts in shards:
        steps = jnp.exp(jax.random.uniform(jax.random.fold_in(own, axis_at), (parts,), jnp.float32, low / len(shards), top_value / len(shards)))
        gain = gain * jnp.repeat(steps, shape[axis_at] // parts).reshape([-1 if axis == axis_at else 1 for axis in range(len(shape))])
    return gain


def normal_values(rng, shape, width, most, cuts=(), held_as=jnp.bfloat16):
    values = jax.random.normal(rng, shape, jnp.float32) * width
    if len(cuts) > 0:
        values = levels(rng, shape, cuts, -0.22, 0.18) * values
    return jnp.clip(values, min=-most, max=most).astype(held_as)


def setup_inputs(seed: int = 0) -> dict:
    seeds = jax.random.split(jax.random.key(seed), 20)
    inputs = normal_values(seeds[0], (SEQS, SEQ_LEN, D), 1.0, 6.0, ((0, 4), (1, 8)))
    out_grad = normal_values(seeds[1], (SEQS, SEQ_LEN, D), 1.0, 6.0, ((0, 4), (1, 8)))
    doc_ids = draw_doc_ids(jax.random.fold_in(seeds[19], 71), 0)
    block_pairs = draw_block_pairs(jax.random.fold_in(seeds[19], 71), 0)
    qkv_weight = normal_values(seeds[4], (D, 3 * D), D ** -0.5, 0.125, ((0, 32),), jnp.float32)
    proj_weight = normal_values(seeds[5], (D, D), (max(8 * D // SEQ_LEN, 1)) ** -0.5, 1.5, ((0, 32),), jnp.float32)
    ffn_in_weight = normal_values(seeds[6], (D, 2 * FF), D ** -0.5, 0.125, ((0, 32),), jnp.float32)
    ffn_out_weight = normal_values(seeds[7], (FF, D), FF ** -0.5, 0.078125, ((0, 32),), jnp.float32)
    small_params = draw_small_params(jax.random.fold_in(seeds[19], 71), 0)
    qkv_first = normal_values(seeds[9], (D, 3 * D), (0.11 * TOKENS ** 0.5), 40.0, ((0, 32),), jnp.float32)
    proj_first = normal_values(seeds[10], (D, D), (0.31 * SEQS ** 0.5), 4.0, ((0, 32),), jnp.float32)
    ffn_in_first = normal_values(seeds[11], (D, 2 * FF), (0.037 * TOKENS ** 0.5), 14.0, ((0, 32),), jnp.float32)
    ffn_out_first = normal_values(seeds[12], (FF, D), (0.067 * TOKENS ** 0.5), 24.0, ((0, 32),), jnp.float32)
    small_first = normal_values(seeds[13], (7, D), (0.19 * TOKENS ** 0.5), 64.0, ((1, 32),), jnp.float32)
    qkv_second = jnp.clip(jnp.exp(math.log(860.16) - 1.3768156 * jax.random.uniform(seeds[14], (D, 3 * D), jnp.float32) ** levels(seeds[14], (D, 3 * D), ((0, 32),), -0.2, 0.2)), 217.088, 860.16)
    proj_second = jnp.clip(jnp.exp(math.log(6.72) - 1.3862944 * jax.random.uniform(seeds[15], (D, D), jnp.float32) ** levels(seeds[15], (D, D), ((0, 32),), -0.2, 0.2)), 1.68, 6.72)
    ffn_in_second = jnp.clip(jnp.exp(math.log(94.208) - 1.3776363 * jax.random.uniform(seeds[16], (D, 2 * FF), jnp.float32) ** levels(seeds[16], (D, 2 * FF), ((0, 32),), -0.2, 0.2)), 23.7568, 94.208)
    ffn_out_second = jnp.clip(jnp.exp(math.log(311.296) - 1.3862944 * jax.random.uniform(seeds[17], (FF, D), jnp.float32) ** levels(seeds[17], (FF, D), ((0, 32),), -0.2, 0.2)), 77.824, 311.296)
    small_second = jnp.clip(jnp.exp(math.log(2457.6) - 1.3862944 * jax.random.uniform(seeds[18], (7, D), jnp.float32) ** levels(seeds[18], (7, D), ((1, 32),), -0.2, 0.2)), 614.4, 2457.6)
    return dict(inputs=inputs, out_grad=out_grad, doc_ids=doc_ids, block_pairs=block_pairs, qkv_weight=qkv_weight, proj_weight=proj_weight, ffn_in_weight=ffn_in_weight, ffn_out_weight=ffn_out_weight, small_params=small_params, qkv_first=qkv_first, proj_first=proj_first, ffn_in_first=ffn_in_first, ffn_out_first=ffn_out_first, small_first=small_first, qkv_second=qkv_second, proj_second=proj_second, ffn_in_second=ffn_in_second, ffn_out_second=ffn_out_second, small_second=small_second)


@jax.custom_vjp
def low(v):
    return lax.optimization_barrier(v.astype(jnp.bfloat16)).astype(jnp.float32)

@jax.custom_vjp
def low_back(v):
    return v

def low_keep(v):
    return (low(v), None)

def low_pass(kept, grad):
    return (grad,)

def back_keep(v):
    return (v, None)

def back_low(kept, grad):
    return (low(grad),)
low.defvjp(low_keep, low_pass)
low_back.defvjp(back_keep, back_low)
norm_eps = 1e-05
beta_first = 0.9
beta_second = 0.95
adam_eps = 1e-08
matrix_decay = 0.1
small_rate = 0.5

def norm_rows(values, gain_row, shift_row):
    center_mean = lax.optimization_barrier(jnp.mean(values, axis=-1, keepdims=True))
    centered = values - center_mean
    inv_std = lax.rsqrt(lax.optimization_barrier(jnp.mean(centered * centered, axis=-1, keepdims=True)) + norm_eps)
    return centered * inv_std * gain_row + shift_row

def rotary_tables(positions):
    half_rot = ROT // 2
    inverse = 10000.0 ** (-2.0 * jnp.arange(half_rot, dtype=jnp.float32) / ROT)
    angles = positions.astype(jnp.float32)[:, None] * inverse[None, :]
    angles = jnp.concatenate([angles, angles], axis=1)
    return (jnp.cos(angles), jnp.sin(angles))

def rotate(values, cosine_table, sine_table):
    half_rot = ROT // 2
    rotated = values[..., :ROT]
    turned = jnp.concatenate([-rotated[..., half_rot:], rotated[..., :half_rot]], axis=-1)
    rotated = rotated * cosine_table[:, None, :] + turned * sine_table[:, None, :]
    return jnp.concatenate([rotated, values[..., ROT:]], axis=-1)

def matmul_hi(left_mat, right_mat):
    return jnp.dot(left_mat, right_mat, precision=lax.Precision.HIGHEST, preferred_element_type=jnp.float32)

def adam_update(weight, first_moment, second_moment, gradient, step_rate, decay_factor):
    new_first = beta_first * first_moment + (1.0 - beta_first) * gradient
    new_second = beta_second * second_moment + (1.0 - beta_second) * gradient * gradient
    correct_first = 1.0 - beta_first ** STEP
    correct_second = 1.0 - beta_second ** STEP
    update = new_first / correct_first / (jnp.sqrt(new_second / correct_second) + adam_eps)
    return (weight - step_rate * (update + decay_factor * weight), new_first, new_second)

def layer_forward(data_in, qkv_weight, proj_weight, ffn_in_weight, ffn_out_weight, small_params, positions, doc_ids):
    qkv_low = low(qkv_weight)
    proj_low = low(proj_weight)
    ffn_in_low = low(ffn_in_weight)
    ffn_out_low = low(ffn_out_weight)
    cosine_table, sine_table = rotary_tables(positions)
    score_scale = HEAD_DIM ** (-0.5)
    block_rows = math.gcd(512, SEQ_LEN)
    block_count = SEQ_LEN // block_rows

    def one_row(row_args):
        residual, doc_row = row_args
        row_docs = jnp.take(doc_row, positions)
        attn_in = low(norm_rows(residual, small_params[0], small_params[1]))
        joined_qkv = low_back(matmul_hi(attn_in, qkv_low) + small_params[4:7].reshape(3 * D))
        shaped = joined_qkv.reshape(SEQ_LEN, 3, HEADS, HEAD_DIM)
        queries = low(rotate(shaped[:, 0], cosine_table, sine_table))
        key_rows = low(rotate(shaped[:, 1], cosine_table, sine_table))
        values = low(shaped[:, 2])

        def attend(block_args):
            query_blk, query_pos, query_doc = block_args
            scores = low_back(jnp.einsum('qhd,khd->hqk', query_blk, key_rows, precision=lax.Precision.HIGHEST) * score_scale)
            allowed = (positions[None, :] <= query_pos[:, None]) & (row_docs[None, :] == query_doc[:, None])
            weights = jnp.where(allowed[None], jnp.exp(scores), 0.0)
            totals = lax.optimization_barrier(jnp.sum(weights, axis=2))
            weighted = low_back(jnp.einsum('hqk,khd->qhd', low(weights), values, precision=lax.Precision.HIGHEST))
            return weighted / totals.T[:, :, None]
        mixed_rows = lax.map(jax.checkpoint(attend), (queries.reshape(block_count, block_rows, HEADS, HEAD_DIM), positions.reshape(block_count, block_rows), row_docs.reshape(block_count, block_rows)))
        mixed_low = low(mixed_rows.reshape(SEQ_LEN, D))
        hidden_state = residual + low_back(matmul_hi(mixed_low, proj_low))
        mlp_in = low(norm_rows(hidden_state, small_params[2], small_params[3]))
        gate_up = low_back(matmul_hi(mlp_in, ffn_in_low))
        inner_low = low(jax.nn.silu(gate_up[:, :FF]) * gate_up[:, FF:])
        return hidden_state + low_back(matmul_hi(inner_low, ffn_out_low))
    return lax.map(one_row, (data_in, doc_ids))

def reference(inputs, out_grad, doc_ids, block_pairs, qkv_weight, proj_weight, ffn_in_weight, ffn_out_weight, small_params, qkv_first, proj_first, ffn_in_first, ffn_out_first, small_first, qkv_second, proj_second, ffn_in_second, ffn_out_second, small_second):
    half_rows = TOK_DEV // 2
    offsets = jnp.arange(half_rows, dtype=jnp.int32)
    positions = (block_pairs.astype(jnp.int32)[:, :, None] * half_rows + offsets[None, None, :]).reshape(SEQ_LEN).astype(jnp.int32)

    def wrapped(data_in, weight_qkv, weight_proj, weight_in, weight_out, weight_small):
        return layer_forward(data_in, weight_qkv, weight_proj, weight_in, weight_out, weight_small, positions, doc_ids)
    result, pullback = jax.vjp(wrapped, inputs.astype(jnp.float32), qkv_weight, proj_weight, ffn_in_weight, ffn_out_weight, small_params)
    grad_data, grad_qkv, grad_proj, grad_in, grad_out, grad_small = pullback(out_grad.astype(jnp.float32))
    proj_fan = max(8 * D // SEQ_LEN, 1)
    qkv_new = adam_update(qkv_weight, qkv_first, qkv_second, grad_qkv, 2.0 / math.sqrt(D), matrix_decay)
    proj_new = adam_update(proj_weight, proj_first, proj_second, grad_proj, 2.0 / math.sqrt(proj_fan), matrix_decay)
    in_new = adam_update(ffn_in_weight, ffn_in_first, ffn_in_second, grad_in, 2.0 / math.sqrt(D), matrix_decay)
    out_new = adam_update(ffn_out_weight, ffn_out_first, ffn_out_second, grad_out, 2.0 / math.sqrt(FF), matrix_decay)
    small_new = adam_update(small_params, small_first, small_second, grad_small, small_rate, 0.0)
    return (result.astype(jnp.bfloat16), grad_data.astype(jnp.bfloat16), qkv_new[0], proj_new[0], in_new[0], out_new[0], small_new[0], qkv_new[1], proj_new[1], in_new[1], out_new[1], small_new[1], qkv_new[2], proj_new[2], in_new[2], out_new[2], small_new[2], grad_small)
```

```python
import functools
import math

import jax
import jax.numpy as jnp
from jax import lax
from jax.experimental import pallas as pl
from jax.experimental.pallas import tpu as pltpu
from jax.sharding import Mesh, PartitionSpec as P

D = 2048
HEADS = 32
HEAD_DIM = 64
FF = 5632
ROT = 16
STEP = 10


norm_eps = 1e-05
beta_first = 0.9
beta_second = 0.95
adam_eps = 1e-08
matrix_decay = 0.1
small_rate = 0.5


def norm_rows(values, gain_row, shift_row):
    center_mean = jnp.mean(values, axis=-1, keepdims=True)
    centered = values - center_mean
    inv_std = lax.rsqrt(jnp.mean(centered * centered, axis=-1, keepdims=True) + norm_eps)
    normed = centered * inv_std
    return (normed * gain_row + shift_row, normed, inv_std)


def norm_back(grad_rows, normed, inv_std, gain_row):
    scaled = grad_rows * gain_row
    return inv_std * (
        scaled
        - jnp.mean(scaled, axis=-1, keepdims=True)
        - normed * jnp.mean(scaled * normed, axis=-1, keepdims=True)
    )


def cross_dot(left_mat, right_mat):
    return lax.dot_general(
        left_mat, right_mat, (((0,), (0,)), ((), ())), preferred_element_type=jnp.float32
    )


def back_dot(left_mat, weight):
    return lax.dot_general(
        left_mat, weight, (((1,), (1,)), ((), ())), preferred_element_type=jnp.float32
    )


def adam_update(weight, first_moment, second_moment, gradient, step_rate, decay_factor):
    new_first = beta_first * first_moment + (1.0 - beta_first) * gradient
    new_second = beta_second * second_moment + (1.0 - beta_second) * gradient * gradient
    correct_first = 1.0 - beta_first**STEP
    correct_second = 1.0 - beta_second**STEP
    update = new_first / correct_first / (jnp.sqrt(new_second / correct_second) + adam_eps)
    return (weight - step_rate * (update + decay_factor * weight), new_first, new_second)


ROW = ("cu", "cl")
FFN_GROUP = ("cl", "fsdp")
EVERY = ("cu", "cl", "fsdp")
SCALE = HEAD_DIM**-0.5


def rotary_tables(positions, heads):
    half_rot = ROT // 2
    inverse = 10000.0 ** (-2.0 * jnp.arange(half_rot, dtype=jnp.float32) / ROT)
    angles = positions.astype(jnp.float32)[:, None] * inverse[None, :]
    cosine, sine = jnp.cos(angles), jnp.sin(angles)
    rows = positions.shape[0]
    rest = HEAD_DIM - ROT
    ones, zeros = jnp.ones((rows, rest), jnp.float32), jnp.zeros((rows, rest), jnp.float32)
    none = jnp.zeros_like(sine)
    keep = jnp.concatenate([cosine, cosine, ones], axis=1)
    lower = jnp.concatenate([-sine, none, zeros], axis=1)
    upper = jnp.concatenate([none, sine, zeros], axis=1)
    return tuple(jnp.tile(t, (1, heads)) for t in (keep, lower, upper))


def turn(values, tables, sign):
    keep, lower, upper = tables
    half_rot = ROT // 2
    return values * keep + sign * (
        jnp.roll(values, -half_rot, axis=1) * lower + jnp.roll(values, half_rot, axis=1) * upper
    )


def dot_t(left, right):
    return lax.dot_general(left, right, (((1,), (1,)), ((), ())), preferred_element_type=jnp.float32)


def attend_kernel(heads, q_ref, k_ref, v_ref, pq_ref, dq_ref, pk_ref, dk_ref, mixed_ref, low_ref, tot_ref):
    allowed = (pk_ref[...] <= pq_ref[...]) & (dk_ref[...] == dq_ref[...])
    for head in range(heads):
        cols = slice(head * HEAD_DIM, (head + 1) * HEAD_DIM)
        scores = dot_t(q_ref[:, cols], k_ref[:, cols]) * SCALE
        weights = jnp.where(allowed, jnp.exp(scores), 0.0)
        total = jnp.sum(weights, axis=1, keepdims=True)
        weighted = jnp.dot(weights.astype(jnp.bfloat16), v_ref[:, cols], preferred_element_type=jnp.float32)
        mixed = weighted / total
        mixed_ref[:, cols] = mixed
        low_ref[:, cols] = mixed.astype(jnp.bfloat16)
        tot_ref[:, head : head + 1] = total


def attend(queries, keys, values, marks, heads):
    pos_col, doc_col, pos_row, doc_row = marks
    rows, width = queries.shape
    block = min(256, rows)
    by_query = pl.BlockSpec((block, width), lambda i: (i, 0))
    whole = pl.BlockSpec((rows, width), lambda i: (0, 0))
    col = pl.BlockSpec((block, 1), lambda i: (i, 0))
    row = pl.BlockSpec((1, rows), lambda i: (0, 0))
    return pl.pallas_call(
        functools.partial(attend_kernel, heads),
        grid=(rows // block,),
        in_specs=[by_query, whole, whole, col, col, row, row],
        out_specs=[by_query, by_query, pl.BlockSpec((block, heads), lambda i: (i, 0))],
        out_shape=[
            jax.ShapeDtypeStruct((rows, width), jnp.float32),
            jax.ShapeDtypeStruct((rows, width), jnp.bfloat16),
            jax.ShapeDtypeStruct((rows, heads), jnp.float32),
        ],
        compiler_params=pltpu.CompilerParams(vmem_limit_bytes=48 << 20),
    )(queries, keys, values, pos_col, doc_col, pos_row, doc_row)


def attend_back_kernel(
    heads, q_ref, k_ref, v_ref, gm_ref, mixed_ref, tot_ref, pq_ref, dq_ref, pk_ref, dk_ref, gq_ref, gk_ref, gv_ref
):
    @pl.when(pl.program_id(0) == 0)
    def _():
        gk_ref[...] = jnp.zeros_like(gk_ref)
        gv_ref[...] = jnp.zeros_like(gv_ref)

    allowed = (pk_ref[...] <= pq_ref[...]) & (dk_ref[...] == dq_ref[...])
    for head in range(heads):
        cols = slice(head * HEAD_DIM, (head + 1) * HEAD_DIM)
        q, k, v = q_ref[:, cols], k_ref[:, cols], v_ref[:, cols]
        inverse = 1.0 / tot_ref[:, head : head + 1]
        grad_mixed = gm_ref[:, cols]
        grad_weighted = (grad_mixed * inverse).astype(jnp.bfloat16)
        grad_total = -jnp.sum(grad_mixed * mixed_ref[:, cols], axis=1, keepdims=True) * inverse
        weights = jnp.where(allowed, jnp.exp(dot_t(q, k) * SCALE), 0.0)
        grad_scores = (weights * (dot_t(grad_weighted, v) + grad_total)).astype(jnp.bfloat16)
        gq_ref[:, cols] = jnp.dot(grad_scores, k, preferred_element_type=jnp.float32) * SCALE
        gk_ref[:, cols] += cross_dot(grad_scores, q) * SCALE
        gv_ref[:, cols] += cross_dot(weights.astype(jnp.bfloat16), grad_weighted)


def attend_back(queries, keys, values, grad_mixed, mixed, totals, marks, heads):
    pos_col, doc_col, pos_row, doc_row = marks
    rows, width = queries.shape
    block = min(256, rows)
    by_query = pl.BlockSpec((block, width), lambda i: (i, 0))
    whole = pl.BlockSpec((rows, width), lambda i: (0, 0))
    col = pl.BlockSpec((block, 1), lambda i: (i, 0))
    row = pl.BlockSpec((1, rows), lambda i: (0, 0))
    full = jax.ShapeDtypeStruct((rows, width), jnp.float32)
    return pl.pallas_call(
        functools.partial(attend_back_kernel, heads),
        grid=(rows // block,),
        in_specs=[
            by_query, whole, whole, by_query, by_query,
            pl.BlockSpec((block, heads), lambda i: (i, 0)), col, col, row, row,
        ],
        out_specs=[by_query, whole, whole],
        out_shape=[full, full, full],
        compiler_params=pltpu.CompilerParams(vmem_limit_bytes=56 << 20),
    )(queries, keys, values, grad_mixed, mixed, totals, pos_col, doc_col, pos_row, doc_row)


def body(
    inputs, out_grad, doc_ids, block_pairs, qkv_weight, proj_weight, ffn_in_weight, ffn_out_weight, small_params,
    qkv_first, proj_first, ffn_in_first, ffn_out_first, small_first,
    qkv_second, proj_second, ffn_in_second, ffn_out_second, small_second,
):
    bf16 = jnp.bfloat16
    tok_rows = inputs.shape[1]
    half_rows = tok_rows // 2
    cu, cl, zs = lax.axis_size("cu"), lax.axis_size("cl"), lax.axis_size("fsdp")
    ctx_count = cu * cl
    group = cl * zs
    seq_len = tok_rows * ctx_count
    my_index = lax.axis_index(ROW)
    heads = HEADS // ctx_count
    width = heads * HEAD_DIM
    slab = qkv_weight.shape[0]
    units = ffn_out_weight.shape[0]
    hidden = units * cu
    offsets = jnp.arange(half_rows, dtype=jnp.int32)
    all_pos = (block_pairs[:, :, None] * half_rows + offsets[None, None, :]).reshape(seq_len)
    key_docs = jnp.take(doc_ids[0], all_pos)
    marks = (all_pos[:, None], key_docs[:, None], all_pos[None, :], key_docs[None, :])
    tables = rotary_tables(all_pos, heads)

    qkv_cast = qkv_weight.astype(bf16).reshape(slab, 3, ctx_count, width)
    qkv_cut = lax.all_to_all(qkv_cast, ROW, split_axis=2, concat_axis=0, tiled=True).reshape(
        ctx_count, 1, slab, 3 * width
    )
    qkv_low = lax.all_gather(qkv_cut, "fsdp", axis=1, tiled=True).reshape(D, 3 * width)
    params = lax.all_gather(small_params, EVERY, axis=1, tiled=True)
    row_in = lax.all_gather(inputs[0], ROW, axis=0, tiled=True)
    proj_low = lax.all_gather(proj_weight.astype(bf16), "fsdp", axis=0, tiled=True)
    in_cast = (
        ffn_in_weight.astype(bf16).reshape(slab, 2, cu, group, units).transpose(3, 0, 1, 2, 4)
        .reshape(group * slab, 2 * hidden)
    )
    in_cut = lax.all_to_all(in_cast, FFN_GROUP, split_axis=0, concat_axis=0, tiled=True)
    in_low = lax.all_gather(in_cut, "cu", axis=0, tiled=True)
    out_low = lax.all_gather(ffn_out_weight.astype(bf16), "cu", axis=0, tiled=True)
    grad_all = lax.all_gather(out_grad[0], FFN_GROUP, axis=0, tiled=True)

    normed_in, _, _ = norm_rows(row_in.astype(jnp.float32), params[0], params[1])
    attn_in = normed_in.astype(bf16)
    bias = lax.dynamic_slice_in_dim(params[4:7], my_index * width, width, 1).reshape(3 * width)
    joined = jnp.dot(attn_in, qkv_low, preferred_element_type=jnp.float32) + bias
    queries = turn(joined[:, :width], tables, 1.0).astype(bf16)
    keys = turn(joined[:, width : 2 * width], tables, 1.0).astype(bf16)
    values = joined[:, 2 * width :].astype(bf16)
    mixed, mixed_low, totals = attend(queries, keys, values, marks, heads)
    branch = jnp.dot(mixed_low, proj_low, preferred_element_type=jnp.float32).astype(bf16)
    branch_own = lax.psum_scatter(branch, ROW, scatter_dimension=0, tiled=True)
    residual = inputs[0].astype(jnp.float32)
    hidden_state = residual + branch_own.astype(jnp.float32)
    normed_mid, hat_mid, inv_mid = norm_rows(hidden_state, params[2], params[3])

    mlp_in = lax.all_gather(normed_mid.astype(bf16), FFN_GROUP, axis=0, tiled=True)
    gate_up = jnp.dot(mlp_in, in_low, preferred_element_type=jnp.float32)
    gate_part, up_part = gate_up[:, :hidden], gate_up[:, hidden:]
    sigmoid_gate = jax.nn.sigmoid(gate_part)
    silu_gate = gate_part * sigmoid_gate
    inner_low = (silu_gate * up_part).astype(bf16)
    grad_inner = back_dot(grad_all, out_low)
    grad_up = grad_inner * silu_gate
    grad_gate = grad_inner * up_part * (sigmoid_gate * (1.0 + gate_part * (1.0 - sigmoid_gate)))
    grad_gate_up = jnp.concatenate([grad_gate, grad_up], axis=1).astype(bf16)
    grad_mid_part = back_dot(grad_gate_up, in_low).astype(bf16)
    grad_mid = lax.psum_scatter(grad_mid_part, FFN_GROUP, scatter_dimension=0, tiled=True).astype(jnp.float32)
    out_part = jnp.dot(inner_low, out_low, preferred_element_type=jnp.float32).astype(bf16)
    out_own = lax.psum_scatter(out_part, FFN_GROUP, scatter_dimension=0, tiled=True)
    layer_out = (hidden_state + out_own.astype(jnp.float32)).astype(bf16)[None]
    grad_ffn_out = cross_dot(inner_low, grad_all).astype(bf16)
    grad_ffn_in = cross_dot(mlp_in, grad_gate_up).astype(bf16)
    ffn_out_grad = lax.psum_scatter(grad_ffn_out, "cu", scatter_dimension=0, tiled=True)
    in_grad_cut = lax.psum_scatter(grad_ffn_in, "cu", scatter_dimension=0, tiled=True)
    in_grad = lax.all_to_all(in_grad_cut, FFN_GROUP, split_axis=0, concat_axis=0, tiled=True)
    ffn_in_grad = in_grad.reshape(group, slab, 2, cu, units).transpose(1, 2, 3, 0, 4).reshape(slab, 2 * FF)

    gain_mid = jnp.sum(grad_mid * hat_mid, axis=0)
    shift_mid = jnp.sum(grad_mid, axis=0)
    grad_hidden = out_grad[0].astype(jnp.float32) + norm_back(grad_mid, hat_mid, inv_mid, params[2])
    grad_branch = lax.all_gather(grad_hidden.astype(bf16), ROW, axis=0, tiled=True)
    grad_proj = cross_dot(mixed_low, grad_branch).astype(bf16)
    proj_grad = lax.psum_scatter(grad_proj, "fsdp", scatter_dimension=0, tiled=True)
    grad_mixed = back_dot(grad_branch, proj_low)
    grad_queries, grad_keys, grad_values = attend_back(
        queries, keys, values, grad_mixed, mixed, totals, marks, heads
    )
    grad_joined = jnp.concatenate(
        [turn(grad_queries, tables, -1.0), turn(grad_keys, tables, -1.0), grad_values], axis=1
    ).astype(bf16)
    grad_norm_part = back_dot(grad_joined, qkv_low).astype(bf16)
    grad_norm = lax.psum_scatter(grad_norm_part, ROW, scatter_dimension=0, tiled=True).astype(jnp.float32)
    grad_qkv = cross_dot(attn_in, grad_joined).astype(bf16).reshape(ctx_count, zs, slab, 3 * width)
    qkv_grad_cut = lax.psum_scatter(grad_qkv, "fsdp", scatter_dimension=1, tiled=True)
    qkv_grad = lax.all_to_all(
        qkv_grad_cut.reshape(ctx_count * slab, 3, 1, width), ROW, split_axis=0, concat_axis=2, tiled=True
    ).reshape(slab, 3 * D)
    _, hat_in, inv_in = norm_rows(residual, params[0], params[1])
    gain_in = jnp.sum(grad_norm * hat_in, axis=0)
    shift_in = jnp.sum(grad_norm, axis=0)
    grad_input = grad_hidden + norm_back(grad_norm, hat_in, inv_in, params[0])
    input_grad = grad_input.astype(bf16)[None]
    bias_own = jnp.sum(grad_joined.astype(jnp.float32), axis=0).reshape(3, width)
    grad_bias = lax.dynamic_update_slice(jnp.zeros((3, D), jnp.float32), bias_own, (0, my_index * width))
    small_terms = jnp.concatenate(
        [gain_in[None], shift_in[None], gain_mid[None], shift_mid[None], grad_bias], axis=0
    )
    small_grad = lax.psum_scatter(small_terms, EVERY, scatter_dimension=1, tiled=True)

    proj_fan = max(8 * D // seq_len, 1)
    f32 = jnp.float32
    qkv_new = adam_update(
        qkv_weight, qkv_first, qkv_second, qkv_grad.astype(f32), 2.0 / math.sqrt(D), matrix_decay
    )
    proj_new = adam_update(
        proj_weight, proj_first, proj_second, proj_grad.astype(f32), 2.0 / math.sqrt(proj_fan), matrix_decay
    )
    in_new = adam_update(
        ffn_in_weight, ffn_in_first, ffn_in_second, ffn_in_grad.astype(f32), 2.0 / math.sqrt(D), matrix_decay
    )
    out_new = adam_update(
        ffn_out_weight, ffn_out_first, ffn_out_second, ffn_out_grad.astype(f32), 2.0 / math.sqrt(FF), matrix_decay
    )
    small_new = adam_update(small_params, small_first, small_second, small_grad, small_rate, 0.0)
    news = (qkv_new, proj_new, in_new, out_new, small_new)
    return (layer_out, input_grad, *(n[0] for n in news), *(n[1] for n in news), *(n[2] for n in news), small_grad)


def solution(mesh):
    ctx_count, fsdp_count = mesh.devices.shape
    fine = Mesh(mesh.devices.reshape(ctx_count // 2, 2, fsdp_count), ("cu", "cl", "fsdp"))
    tokens = P("fsdp", ROW, None)
    matrix = P(EVERY, None)
    small = P(None, EVERY)
    five = (matrix, matrix, matrix, matrix, small)
    in_specs = (tokens, tokens, P("fsdp", None), P(), *five, *five, *five)
    out_specs = (tokens, tokens, *five, *five, *five, small)
    return jax.shard_map(body, mesh=fine, in_specs=in_specs, out_specs=out_specs, check_vma=False)
```

```python
import functools
import math

import jax
import jax.numpy as jnp
from jax import lax
from jax.experimental import pallas as pl
from jax.experimental.pallas import tpu as pltpu
from jax.sharding import Mesh, PartitionSpec as P

D = 2048
HEADS = 32
HEAD_DIM = 64
FF = 5632
ROT = 16
STEP = 10


norm_eps = 1e-05
beta_first = 0.9
beta_second = 0.95
adam_eps = 1e-08
matrix_decay = 0.1
small_rate = 0.5


def norm_rows(values, gain_row, shift_row):
    center_mean = jnp.mean(values, axis=-1, keepdims=True)
    centered = values - center_mean
    inv_std = lax.rsqrt(jnp.mean(centered * centered, axis=-1, keepdims=True) + norm_eps)
    normed = centered * inv_std
    return (normed * gain_row + shift_row, normed, inv_std)


def norm_back(grad_rows, normed, inv_std, gain_row):
    scaled = grad_rows * gain_row
    return inv_std * (
        scaled
        - jnp.mean(scaled, axis=-1, keepdims=True)
        - normed * jnp.mean(scaled * normed, axis=-1, keepdims=True)
    )


def cross_dot(left_mat, right_mat):
    return lax.dot_general(
        left_mat, right_mat, (((0,), (0,)), ((), ())), preferred_element_type=jnp.float32
    )


def back_dot(left_mat, weight):
    return lax.dot_general(
        left_mat, weight, (((1,), (1,)), ((), ())), preferred_element_type=jnp.float32
    )


def adam_update(weight, first_moment, second_moment, gradient, step_rate, decay_factor):
    new_first = beta_first * first_moment + (1.0 - beta_first) * gradient
    new_second = beta_second * second_moment + (1.0 - beta_second) * gradient * gradient
    correct_first = 1.0 - beta_first**STEP
    correct_second = 1.0 - beta_second**STEP
    update = new_first / correct_first / (jnp.sqrt(new_second / correct_second) + adam_eps)
    return (weight - step_rate * (update + decay_factor * weight), new_first, new_second)


ROW = ("cu", "cl")
FFN_GROUP = ("cl", "fsdp")
EVERY = ("cu", "cl", "fsdp")
SCALE = HEAD_DIM**-0.5


def rotary_tables(positions, heads):
    half_rot = ROT // 2
    inverse = 10000.0 ** (-2.0 * jnp.arange(half_rot, dtype=jnp.float32) / ROT)
    angles = positions.astype(jnp.float32)[:, None] * inverse[None, :]
    cosine, sine = jnp.cos(angles), jnp.sin(angles)
    rows = positions.shape[0]
    rest = HEAD_DIM - ROT
    ones, zeros = jnp.ones((rows, rest), jnp.float32), jnp.zeros((rows, rest), jnp.float32)
    none = jnp.zeros_like(sine)
    keep = jnp.concatenate([cosine, cosine, ones], axis=1)
    lower = jnp.concatenate([-sine, none, zeros], axis=1)
    upper = jnp.concatenate([none, sine, zeros], axis=1)
    return tuple(jnp.tile(t, (1, heads)) for t in (keep, lower, upper))


def turn(values, tables, sign):
    keep, lower, upper = tables
    half_rot = ROT // 2
    return values * keep + sign * (
        jnp.roll(values, -half_rot, axis=1) * lower + jnp.roll(values, half_rot, axis=1) * upper
    )


def dot_t(left, right):
    return lax.dot_general(left, right, (((1,), (1,)), ((), ())), preferred_element_type=jnp.float32)


def attend_kernel(heads, q_ref, k_ref, v_ref, pq_ref, dq_ref, pk_ref, dk_ref, mixed_ref, low_ref, tot_ref):
    allowed = (pk_ref[...] <= pq_ref[...]) & (dk_ref[...] == dq_ref[...])
    for head in range(heads):
        cols = slice(head * HEAD_DIM, (head + 1) * HEAD_DIM)
        scores = dot_t(q_ref[:, cols], k_ref[:, cols]) * SCALE
        weights = jnp.where(allowed, jnp.exp(scores), 0.0)
        total = jnp.sum(weights, axis=1, keepdims=True)
        weighted = jnp.dot(weights.astype(jnp.bfloat16), v_ref[:, cols], preferred_element_type=jnp.float32)
        mixed = weighted / total
        mixed_ref[:, cols] = mixed
        low_ref[:, cols] = mixed.astype(jnp.bfloat16)
        tot_ref[:, head : head + 1] = total


def attend(queries, keys, values, marks, heads):
    pos_col, doc_col, pos_row, doc_row = marks
    rows, width = queries.shape
    block = min(256, rows)
    by_query = pl.BlockSpec((block, width), lambda i: (i, 0))
    whole = pl.BlockSpec((rows, width), lambda i: (0, 0))
    col = pl.BlockSpec((block, 1), lambda i: (i, 0))
    row = pl.BlockSpec((1, rows), lambda i: (0, 0))
    return pl.pallas_call(
        functools.partial(attend_kernel, heads),
        grid=(rows // block,),
        in_specs=[by_query, whole, whole, col, col, row, row],
        out_specs=[by_query, by_query, pl.BlockSpec((block, heads), lambda i: (i, 0))],
        out_shape=[
            jax.ShapeDtypeStruct((rows, width), jnp.float32),
            jax.ShapeDtypeStruct((rows, width), jnp.bfloat16),
            jax.ShapeDtypeStruct((rows, heads), jnp.float32),
        ],
        compiler_params=pltpu.CompilerParams(vmem_limit_bytes=48 << 20),
    )(queries, keys, values, pos_col, doc_col, pos_row, doc_row)


def attend_back_kernel(
    heads, q_ref, k_ref, v_ref, gm_ref, mixed_ref, tot_ref, pq_ref, dq_ref, pk_ref, dk_ref, gq_ref, gk_ref, gv_ref
):
    @pl.when(pl.program_id(0) == 0)
    def _():
        gk_ref[...] = jnp.zeros_like(gk_ref)
        gv_ref[...] = jnp.zeros_like(gv_ref)

    allowed = (pk_ref[...] <= pq_ref[...]) & (dk_ref[...] == dq_ref[...])
    for head in range(heads):
        cols = slice(head * HEAD_DIM, (head + 1) * HEAD_DIM)
        q, k, v = q_ref[:, cols], k_ref[:, cols], v_ref[:, cols]
        inverse = 1.0 / tot_ref[:, head : head + 1]
        grad_mixed = gm_ref[:, cols]
        grad_weighted = (grad_mixed * inverse).astype(jnp.bfloat16)
        grad_total = -jnp.sum(grad_mixed * mixed_ref[:, cols], axis=1, keepdims=True) * inverse
        weights = jnp.where(allowed, jnp.exp(dot_t(q, k) * SCALE), 0.0)
        grad_scores = (weights * (dot_t(grad_weighted, v) + grad_total)).astype(jnp.bfloat16)
        gq_ref[:, cols] = jnp.dot(grad_scores, k, preferred_element_type=jnp.float32) * SCALE
        gk_ref[:, cols] += cross_dot(grad_scores, q) * SCALE
        gv_ref[:, cols] += cross_dot(weights.astype(jnp.bfloat16), grad_weighted)


def attend_back(queries, keys, values, grad_mixed, mixed, totals, marks, heads):
    pos_col, doc_col, pos_row, doc_row = marks
    rows, width = queries.shape
    block = min(256, rows)
    by_query = pl.BlockSpec((block, width), lambda i: (i, 0))
    whole = pl.BlockSpec((rows, width), lambda i: (0, 0))
    col = pl.BlockSpec((block, 1), lambda i: (i, 0))
    row = pl.BlockSpec((1, rows), lambda i: (0, 0))
    full = jax.ShapeDtypeStruct((rows, width), jnp.float32)
    return pl.pallas_call(
        functools.partial(attend_back_kernel, heads),
        grid=(rows // block,),
        in_specs=[
            by_query, whole, whole, by_query, by_query,
            pl.BlockSpec((block, heads), lambda i: (i, 0)), col, col, row, row,
        ],
        out_specs=[by_query, whole, whole],
        out_shape=[full, full, full],
        compiler_params=pltpu.CompilerParams(vmem_limit_bytes=56 << 20),
    )(queries, keys, values, grad_mixed, mixed, totals, pos_col, doc_col, pos_row, doc_row)


MESH = pl.DeviceIdType.MESH
ANY = pl.BlockSpec(memory_space=pl.ANY)
VMEM = pl.BlockSpec(memory_space=pltpu.VMEM)
DMA = pltpu.SemaphoreType.DMA
BF16, F32 = jnp.bfloat16, jnp.float32


class Transfer:
    def __init__(self, src, dst, send, recv, device):
        self.parts = (src, dst, send, recv, device)

    def copy(self):
        src, dst, send, recv, device = self.parts
        return pltpu.make_async_remote_copy(
            src_ref=src, dst_ref=dst, send_sem=send, recv_sem=recv, device_id=device, device_id_type=MESH
        )

    def start(self):
        self.copy().start()

    def wait_recv(self):
        self.copy().wait_recv()

    def wait_send(self):
        self.copy().wait_send()

    def wait(self):
        self.copy().wait()


rcopy = Transfer


def flip(index, mask):
    bit = 1
    while bit <= mask:
        if mask & bit:
            index = index + bit * (1 - 2 * lax.rem(index // bit, 2))
        bit *= 2
    return index


def place():
    return lax.axis_index("cu"), lax.axis_index("cl"), lax.axis_index("fsdp")


def sizes():
    return lax.axis_size("cu"), lax.axis_size("cl"), lax.axis_size("fsdp")


def greet(row, line):
    u, c, z = place()
    cu, cl, zs = sizes()
    n, me = cu * cl, u * cl + c
    barrier = pltpu.get_barrier_semaphore()

    def signal_row(m, carry):
        other = lax.rem(me + m, n)
        pl.semaphore_signal(barrier, inc=1, device_id=(other // cl, lax.rem(other, cl), z), device_id_type=MESH)
        return carry

    def signal_line(m, carry):
        pl.semaphore_signal(barrier, inc=1, device_id=(u, c, lax.rem(z + m, zs)), device_id_type=MESH)
        return carry

    if row:
        lax.fori_loop(1, n, signal_row, 0)
    if line:
        lax.fori_loop(1, zs, signal_line, 0)
    pl.semaphore_wait(barrier, row * (n - 1) + line * (zs - 1))


def head_kernel(
    x, small, qkv, row, par, wq, own, x_send, x_recv, s_send, s_recv, p_send, p_recv, q_send, q_recv,
    a_send, a_recv, up_send, up_recv, dn_send, dn_recv,
):
    u, c, z = place()
    cu, cl, zs = sizes()
    n, me = cu * cl, u * cl + c
    sibling = (u, 1 - c, z)
    mine = [
        pltpu.make_async_copy(qkv.at[me], wq.at[me, z], own.at[0]),
        pltpu.make_async_copy(x, row.at[u, c], own.at[1]),
        pltpu.make_async_copy(small, par.at[me, z], own.at[2]),
    ]
    for copy in mine:
        copy.start()
    greet(True, True)

    def exchange(m):
        other, source = lax.rem(me + m, n), lax.rem(me - m + n, n)
        out = rcopy(
            qkv.at[other], wq.at[me, z], a_send.at[m], a_recv.at[m], (other // cl, lax.rem(other, cl), z)
        )
        into = rcopy(qkv.at[other], wq.at[source, z], a_send.at[m], a_recv.at[m], sibling)
        return out, into

    def params_line(m):
        other, source = lax.rem(z + m, zs), lax.rem(z - m + zs, zs)
        return (
            rcopy(small, par.at[me, z], p_send.at[m], p_recv.at[m], (u, c, other)),
            rcopy(small, par.at[me, source], p_send.at[m], p_recv.at[m], sibling),
        )

    def params_row(m):
        other, source = lax.rem(me + m, n), lax.rem(me - m + n, n)
        return (
            rcopy(par.at[me], par.at[me], q_send.at[m], q_recv.at[m], (other // cl, lax.rem(other, cl), z)),
            rcopy(par.at[me], par.at[source], q_send.at[m], q_recv.at[m], sibling),
        )

    def x_far(i):
        out = rcopy(x, row.at[u, c], x_send.at[i], x_recv.at[i], (flip(u, i), c, z))
        into = rcopy(x, row.at[flip(u, i), c], x_send.at[i], x_recv.at[i], sibling)
        return out, into

    def x_near(i):
        part = row.at[flip(u, i), c]
        out = rcopy(part, part, s_send.at[i], s_recv.at[i], sibling)
        into = rcopy(part, row.at[flip(u, i), 1 - c], s_send.at[i], s_recv.at[i], sibling)
        return out, into

    def loop(low, high, step):
        def run(m, carry):
            step(m)
            return carry

        lax.fori_loop(low, high, run, 0)

    loop(1, n, lambda m: exchange(m)[0].start())
    loop(1, zs, lambda m: params_line(m)[0].start())
    for copy in mine:
        copy.wait()
    for i in range(1, cu):
        x_far(i)[0].start()
    x_near(0)[0].start()

    def chain(step, m):
        piece = lax.rem(me - m + n, n)
        above, below = wq.at[piece, lax.rem(z + step, zs)], wq.at[piece, lax.rem(z - step + zs, zs)]
        return (
            rcopy(below, below, up_send.at[step, m], up_recv.at[step, m], (u, c, lax.rem(z + 1, zs))),
            rcopy(above, above, dn_send.at[step, m], dn_recv.at[step, m], (u, c, lax.rem(z - 1 + zs, zs))),
        )

    def arrival(step, m):
        piece = lax.rem(me - m + n, n)
        above, below = wq.at[piece, lax.rem(z + step + 1, zs)], wq.at[piece, lax.rem(z - step - 1 + zs, zs)]
        return (
            rcopy(below, below, up_send.at[step, m], up_recv.at[step, m], sibling),
            rcopy(above, above, dn_send.at[step, m], dn_recv.at[step, m], sibling),
        )

    def first(m):
        @pl.when(m > 0)
        def _():
            exchange(m)[1].wait_recv()

        @pl.when(z + 1 < zs)
        def _():
            chain(0, m)[0].start()

        @pl.when(z > 0)
        def _():
            chain(0, m)[1].start()

    loop(0, n, first)
    for m in range(1, zs):
        params_line(m)[1].wait_recv()
    loop(1, n, lambda m: params_row(m)[0].start())
    for i in range(1, cu):
        x_far(i)[1].wait_recv()
        x_near(i)[0].start()
    for step in range(1, zs):

        def later(m, step=step):
            @pl.when(z >= step)
            def _():
                arrival(step - 1, m)[0].wait_recv()

            @pl.when((z >= step) & (z + 1 < zs))
            def _():
                chain(step, m)[0].start()

            @pl.when(z + step < zs)
            def _():
                arrival(step - 1, m)[1].wait_recv()

            @pl.when((z + step < zs) & (z > 0))
            def _():
                chain(step, m)[1].start()

        loop(0, n, later)
    loop(1, n, lambda m: params_row(m)[1].wait_recv())
    for i in range(cu):
        x_near(i)[1].wait_recv()
    loop(1, n, lambda m: exchange(m)[0].wait_send())
    loop(1, zs, lambda m: params_line(m)[0].wait_send())
    loop(1, n, lambda m: params_row(m)[0].wait_send())
    for i in range(cu):
        x_near(i)[0].wait_send()
        if i:
            x_far(i)[0].wait_send()
    for step in range(zs - 1):

        def sent(m, step=step):
            @pl.when((z >= step) & (z + 1 < zs))
            def _():
                chain(step, m)[0].wait_send()

            @pl.when((z + step < zs) & (z > 0))
            def _():
                chain(step, m)[1].wait_send()

        loop(0, n, sent)


def gather_head(x, small, qkv_cut):
    cu, cl, zs = sizes()
    n = cu * cl
    return pl.pallas_call(
        head_kernel,
        in_specs=[ANY, ANY, ANY],
        out_specs=[ANY, ANY, ANY],
        out_shape=[
            jax.ShapeDtypeStruct((cu, cl, *x.shape), x.dtype),
            jax.ShapeDtypeStruct((n, zs, *small.shape), small.dtype),
            jax.ShapeDtypeStruct((n, zs, *qkv_cut.shape[1:]), qkv_cut.dtype),
        ],
        scratch_shapes=[
            DMA((3,)), DMA((cu,)), DMA((cu,)), DMA((cu,)), DMA((cu,)), DMA((zs,)), DMA((zs,)), DMA((n,)), DMA((n,)),
            DMA((n,)), DMA((n,)), DMA((zs, n)), DMA((zs, n)), DMA((zs, n)), DMA((zs, n)),
        ],
        cost_estimate=pl.CostEstimate(flops=0, bytes_accessed=200 << 20, transcendentals=0),
        compiler_params=pltpu.CompilerParams(collective_id=0, has_side_effects=True),
    )(x, small, qkv_cut)


ITEMS = 4


def loop(low, high, step):
    def run(m, carry):
        step(m)
        return carry

    lax.fori_loop(low, high, run, 0)


def bits_of(count):
    return [1 << b for b in range(count.bit_length() - 1)]


def combos(bits):
    masks = [0]
    for b in bits:
        masks = masks + [m | b for m in masks]
    return masks


def order_of(item, count):
    return bits_of(count) if item < ITEMS // 2 else bits_of(count)[::-1]


def add_low(left, right):
    return (left.astype(F32) + right.astype(F32)).astype(BF16)


class RowReduce:
    def __init__(self, parts, held, beside, came, load, sib_s, sib_r, out_s, out_r):
        self.parts, self.held, self.beside, self.came = parts, held, beside, came
        self.load, self.sib_s, self.sib_r, self.out_s, self.out_r = load, sib_s, sib_r, out_s, out_r
        self.u, self.c, self.z = place()
        self.count = sizes()[0]
        self.phases = self.count.bit_length() - 1

    def sib(self, mask):
        return Transfer(
            self.parts.at[flip(self.u, mask), 1 - self.c], self.beside.at[mask], self.sib_s.at[mask],
            self.sib_r.at[mask], (self.u, 1 - self.c, self.z),
        )

    def loading(self, mask):
        return pltpu.make_async_copy(
            self.parts.at[flip(self.u, mask), self.c], self.held.at[mask], self.load.at[mask]
        )

    def start(self):
        for mask in reversed(range(self.count)):
            self.sib(mask).start()
            self.loading(mask).start()

    def merge(self):
        for mask in reversed(range(self.count)):
            self.loading(mask).wait()
            self.sib(mask).wait_recv()
            self.held[mask] = add_low(self.held[mask], self.beside[mask])

    def steps(self, item, phase):
        order = order_of(item, self.count)
        slot = self.count - (self.count >> phase)
        for k, rest in enumerate(combos(order[phase + 1 :])):
            yield slot + k, rest, Transfer(
                self.held.at[order[phase] | rest, item], self.came.at[slot + k, item], self.out_s.at[slot + k, item],
                self.out_r.at[slot + k, item], (flip(self.u, order[phase]), self.c, self.z),
            )

    def send(self, item, phase):
        for _, _, transfer in self.steps(item, phase):
            transfer.start()

    def add(self, item, phase):
        for slot, rest, transfer in self.steps(item, phase):
            transfer.wait_recv()
            self.held[rest, item] = add_low(self.held[rest, item], self.came[slot, item])

    def total(self, item):
        ((slot, _, transfer),) = self.steps(item, self.phases - 1)
        transfer.wait_recv()
        return self.held[0, item].astype(F32) + self.came[slot, item].astype(F32)

    def drain(self):
        for mask in range(self.count):
            self.sib(mask).wait_send()
        for item in range(ITEMS):
            for phase in range(self.phases):
                for _, _, transfer in self.steps(item, phase):
                    transfer.wait_send()

    @staticmethod
    def scratch(count, rows, width):
        block = (count, ITEMS, rows // ITEMS, width)
        return [
            pltpu.VMEM(block, BF16), pltpu.VMEM(block, BF16), pltpu.VMEM(block, BF16), DMA((count,)), DMA((count,)),
            DMA((count,)), DMA((count, ITEMS)), DMA((count, ITEMS)),
        ]


class RowGather:
    def __init__(self, own, full, keep, out_s, out_r, sib_s, sib_r):
        self.own, self.full, self.keep = own, full, keep
        self.out_s, self.out_r, self.sib_s, self.sib_r = out_s, out_r, sib_s, sib_r
        self.u, self.c, self.z = place()
        self.count = sizes()[0]
        self.phases = self.count.bit_length() - 1

    def kept(self, item):
        return pltpu.make_async_copy(self.own.at[item], self.full.at[self.u, self.c, item], self.keep.at[item])

    def source(self, mask, item):
        return self.own.at[item] if mask == 0 else self.full.at[flip(self.u, mask), self.c, item]

    def sib(self, mask, item):
        return Transfer(
            self.source(mask, item), self.full.at[flip(self.u, mask), self.c, item], self.sib_s.at[mask, item],
            self.sib_r.at[mask, item], (self.u, 1 - self.c, self.z),
        )

    def steps(self, item, phase):
        order = order_of(item, self.count)
        for k, mask in enumerate(combos(order[:phase])):
            slot = (1 << phase) - 1 + k
            yield mask | order[phase], Transfer(
                self.source(mask, item), self.full.at[flip(self.u, mask), self.c, item], self.out_s.at[slot, item],
                self.out_r.at[slot, item], (flip(self.u, order[phase]), self.c, self.z),
            )

    def start(self, item):
        self.send(item, 0)
        self.sib(0, item).start()
        self.kept(item).start()

    def send(self, item, phase):
        for _, transfer in self.steps(item, phase):
            transfer.start()

    def pass_on(self, item, phase):
        for mask, transfer in self.steps(item, phase):
            transfer.wait_recv()
            self.sib(mask, item).start()

    def drain(self):
        for item in range(ITEMS):
            self.kept(item).wait()
            for mask in range(self.count):
                self.sib(mask, item).wait()
            for phase in range(self.phases):
                for _, transfer in self.steps(item, phase):
                    transfer.wait_send()

    @staticmethod
    def scratch(count):
        return [DMA((ITEMS,)), *[DMA((count, ITEMS))] * 4]


class LineGather:
    def __init__(self, own, full, keep, up_s, up_r, dn_s, dn_r, sib_s, sib_r):
        self.own, self.full, self.keep = own, full, keep
        self.up_s, self.up_r, self.dn_s, self.dn_r, self.sib_s, self.sib_r = up_s, up_r, dn_s, dn_r, sib_s, sib_r
        self.u, self.c, self.z = place()
        self.count = sizes()[2]

    def kept(self, item):
        return pltpu.make_async_copy(self.own.at[item], self.full.at[self.c, self.z, item], self.keep.at[item])

    def up(self, item, step):
        origin = lax.rem(self.z - step + self.count, self.count)
        block = self.full.at[self.c, origin, item]
        source = self.own.at[item] if step == 0 else block
        to = lax.rem(self.z + 1, self.count)
        return Transfer(source, block, self.up_s.at[step, item], self.up_r.at[step, item], (self.u, self.c, to))

    def down(self, item, step):
        block = self.full.at[self.c, lax.rem(self.z + step, self.count), item]
        source = self.own.at[item] if step == 0 else block
        to = lax.rem(self.z - 1 + self.count, self.count)
        return Transfer(source, block, self.dn_s.at[step, item], self.dn_r.at[step, item], (self.u, self.c, to))

    def sib(self, item, origin, own=False):
        block = self.full.at[self.c, origin, item]
        return Transfer(
            self.own.at[item] if own else block, block, self.sib_s.at[origin, item], self.sib_r.at[origin, item],
            (self.u, 1 - self.c, self.z),
        )

    def start(self, item):
        @pl.when(self.z + 1 < self.count)
        def _():
            self.up(item, 0).start()

        @pl.when(self.z > 0)
        def _():
            self.down(item, 0).start()

        self.sib(item, self.z, True).start()
        self.kept(item).start()

    def forward(self, item, step):
        z, count = self.z, self.count

        @pl.when(z >= step)
        def _():
            self.up(item, step - 1).wait_recv()
            if step < count - 1:

                @pl.when(z + 1 < count)
                def _():
                    self.up(item, step).start()

            self.sib(item, z - step).start()

        @pl.when(z + step < count)
        def _():
            self.down(item, step - 1).wait_recv()
            if step < count - 1:

                @pl.when(z > 0)
                def _():
                    self.down(item, step).start()

            self.sib(item, z + step).start()

    def drain(self):
        z, count = self.z, self.count
        for item in range(ITEMS):
            self.kept(item).wait()
            for origin in range(count):
                self.sib(item, origin).wait()
            for step in range(count - 1):

                @pl.when((z >= step) & (z + 1 < count))
                def _(item=item, step=step):
                    self.up(item, step).wait_send()

                @pl.when((z + step < count) & (z > 0))
                def _(item=item, step=step):
                    self.down(item, step).wait_send()

    @staticmethod
    def scratch(count):
        return [DMA((ITEMS,)), *[DMA((count, ITEMS))] * 6]


class LineReduce:
    def __init__(self, held, from_below, from_above, pieces, up_s, up_r, dn_s, dn_r):
        self.held, self.from_below, self.from_above, self.pieces = held, from_below, from_above, pieces
        self.up_s, self.up_r, self.dn_s, self.dn_r = up_s, up_r, dn_s, dn_r
        self.u, self.c, self.z = place()
        self.count = sizes()[2]

    def up(self, to, piece):
        return Transfer(
            self.held.at[to, piece], self.from_below.at[to, piece], self.up_s.at[to, piece], self.up_r.at[to, piece],
            (self.u, self.c, lax.rem(self.z + 1, self.count)),
        )

    def down(self, to, piece):
        return Transfer(
            self.held.at[to, piece], self.from_above.at[to, piece], self.dn_s.at[to, piece], self.dn_r.at[to, piece],
            (self.u, self.c, lax.rem(self.z - 1 + self.count, self.count)),
        )

    def step(self, t):
        z, count = self.z, self.count
        far_up, far_down = count - 1 - t, t

        def upward(piece):
            @pl.when(z > 0)
            def _():
                self.up(far_up, piece).wait_recv()
                self.held[far_up, piece] = add_low(self.held[far_up, piece], self.from_below[far_up, piece])

            self.up(far_up, piece).start()

        def downward(piece):
            @pl.when(z < count - 1)
            def _():
                self.down(far_down, piece).wait_recv()
                self.held[far_down, piece] = add_low(self.held[far_down, piece], self.from_above[far_down, piece])

            self.down(far_down, piece).start()

        lag = min(3, self.pieces // 2)
        late_up = lag * ((2 * z) // count)

        def one(i):
            piece_up, piece_down = i - late_up, i - (lag - late_up)

            @pl.when((z < far_up) & (piece_up >= 0) & (piece_up < self.pieces))
            def _():
                upward(piece_up)

            @pl.when((z > far_down) & (piece_down >= 0) & (piece_down < self.pieces))
            def _():
                downward(piece_down)

        loop(0, self.pieces + lag, one)

    def total(self, piece, into):
        z, count = self.z, self.count
        into[...] = self.held[z, piece].astype(F32)

        @pl.when(z > 0)
        def _():
            self.up(z, piece).wait_recv()
            into[...] += self.from_below[z, piece].astype(F32)

        @pl.when(z < count - 1)
        def _():
            self.down(z, piece).wait_recv()
            into[...] += self.from_above[z, piece].astype(F32)

    def drain(self):
        z, count = self.z, self.count
        for t in range(count - 1):
            far_up, far_down = count - 1 - t, t

            def one(piece, far_up=far_up, far_down=far_down):
                @pl.when(z < far_up)
                def _():
                    self.up(far_up, piece).wait_send()

                @pl.when(z > far_down)
                def _():
                    self.down(far_down, piece).wait_send()

            loop(0, self.pieces, one)

    @staticmethod
    def scratch(count, pieces, block):
        shape = (count, pieces, *block)
        return [*[pltpu.VMEM(shape, BF16)] * 3, *[DMA((count, pieces))] * 4]


def mid_forward_kernel(branch, x, params, hidden, mlp, low, *scratch):
    reduce = RowReduce(branch, *scratch[:8])
    gather = LineGather(low, mlp, *scratch[8:])
    greet(True, True)
    reduce.start()
    reduce.merge()
    for item in range(ITEMS):
        reduce.send(item, 0)
    for phase in range(1, reduce.phases):
        for item in range(ITEMS):
            reduce.add(item, phase - 1)
            reduce.send(item, phase)
    for item in range(ITEMS):
        state = x[item].astype(F32) + reduce.total(item)
        hidden[item] = state
        low[item] = norm_rows(state, params[0:1], params[1:2])[0].astype(BF16)
        gather.start(item)
    for step in range(1, gather.count):
        for item in range(ITEMS):
            gather.forward(item, step)
    gather.drain()
    reduce.drain()


def mid_forward(branch, x, params):
    cu, cl, zs = sizes()
    rows, width = x.shape
    block = (ITEMS, rows // ITEMS, width)
    hidden, mlp, _ = pl.pallas_call(
        mid_forward_kernel,
        in_specs=[ANY, VMEM, VMEM],
        out_specs=[VMEM, ANY, VMEM],
        out_shape=[
            jax.ShapeDtypeStruct(block, F32),
            jax.ShapeDtypeStruct((cl, zs, *block), BF16),
            jax.ShapeDtypeStruct(block, BF16),
        ],
        scratch_shapes=[*RowReduce.scratch(cu, rows, width), *LineGather.scratch(zs)],
        cost_estimate=pl.CostEstimate(flops=0, bytes_accessed=200 << 20, transcendentals=0),
        compiler_params=pltpu.CompilerParams(collective_id=1, has_side_effects=True, vmem_limit_bytes=56 << 20),
    )(branch.reshape(cu, cl, *block), x.reshape(block), params)
    return hidden.reshape(rows, width), mlp.reshape(cl * zs * rows, width)


def mid_backward_kernel(parts, hidden, out_grad, params, grad_hidden, full, sums, low, held, below, above, up_s, up_r,
                        dn_s, dn_r, beside, total, load, sib_s, sib_r, *scratch):
    u, c, z = place()
    zs = sizes()[2]
    reduce = LineReduce(held, below, above, ITEMS, up_s, up_r, dn_s, dn_r)
    gather = RowGather(low, full, *scratch)
    greet(True, True)

    def sib(to):
        return Transfer(parts.at[1 - c, to], beside.at[to], sib_s.at[to], sib_r.at[to], (u, 1 - c, z))

    def loading(to):
        return pltpu.make_async_copy(parts.at[c, to], held.at[to], load.at[to])

    order = sorted(range(zs), key=lambda to: -abs(2 * to - zs + 1))
    for to in order:
        sib(to).start()
        loading(to).start()
    for to in order:
        loading(to).wait()
        sib(to).wait_recv()
        held[to] = add_low(held[to], beside[to])
    for t in range(zs - 1):
        reduce.step(t)
    sums[...] = jnp.zeros_like(sums)
    for item in range(ITEMS):
        reduce.total(item, total)
        _, hat, inverse = norm_rows(hidden[item], params[0:1], params[1:2])
        grad = total[...]
        sums[0:1] += jnp.sum(grad * hat, axis=0, keepdims=True)
        sums[1:2] += jnp.sum(grad, axis=0, keepdims=True)
        grad = out_grad[item].astype(F32) + norm_back(grad, hat, inverse, params[0:1])
        grad_hidden[item] = grad
        low[item] = grad.astype(BF16)
        gather.start(item)
    for phase in range(gather.phases):
        for item in range(ITEMS):
            gather.pass_on(item, phase)
            if phase + 1 < gather.phases:
                gather.send(item, phase + 1)
    gather.drain()
    reduce.drain()
    for to in range(zs):
        sib(to).wait_send()


def mid_backward(parts, hidden, out_grad, params):
    cu, cl, zs = sizes()
    rows, width = out_grad.shape
    block = (ITEMS, rows // ITEMS, width)
    grad_hidden, full, sums, _ = pl.pallas_call(
        mid_backward_kernel,
        in_specs=[ANY, VMEM, VMEM, VMEM],
        out_specs=[VMEM, ANY, VMEM, VMEM],
        out_shape=[
            jax.ShapeDtypeStruct(block, F32),
            jax.ShapeDtypeStruct((cu, cl, *block), BF16),
            jax.ShapeDtypeStruct((2, width), F32),
            jax.ShapeDtypeStruct(block, BF16),
        ],
        scratch_shapes=[
            *LineReduce.scratch(zs, ITEMS, block[1:]), pltpu.VMEM((zs, *block), BF16), pltpu.VMEM(block[1:], F32),
            DMA((zs,)), DMA((zs,)), DMA((zs,)), *RowGather.scratch(cu),
        ],
        cost_estimate=pl.CostEstimate(flops=0, bytes_accessed=200 << 20, transcendentals=0),
        compiler_params=pltpu.CompilerParams(collective_id=2, has_side_effects=True, vmem_limit_bytes=56 << 20),
    )(parts.reshape(cl, zs, *block), hidden.reshape(block), out_grad.reshape(block), params)
    return grad_hidden.reshape(rows, width), full.reshape(cu * cl * rows, width), sums


def tail_kernel(parts, x, grad_hidden, params, terms, grads, input_grad, small, cut, pile, line_in, row_in, total,
                row_total, line_s, line_r, row_s, row_r, a_send, a_recv, own, held_load, low, *scratch):
    u, c, z = place()
    cu, cl, zs = sizes()
    n, me = cu * cl, u * cl + c
    reduce = RowReduce(parts, *scratch[:8])
    held = scratch[8]
    line = LineReduce(*scratch[8:11], n, *scratch[11:])
    load = pltpu.make_async_copy(grads, held, held_load.at[0])
    load.start()
    greet(True, True)
    reduce.start()
    load.wait()
    line.step(0)
    reduce.merge()
    for item in range(ITEMS):
        reduce.send(item, 0)
    for t in range(1, zs - 1):
        line.step(t)
    for phase in range(1, reduce.phases):
        for item in range(ITEMS):
            reduce.add(item, phase - 1)
            reduce.send(item, phase)
    pile[...] = terms[...]
    for item in range(ITEMS):
        grad = reduce.total(item)
        _, hat, inverse = norm_rows(x[item].astype(F32), params[0:1], params[1:2])
        pile[0:1] += jnp.sum(grad * hat, axis=0, keepdims=True)
        pile[1:2] += jnp.sum(grad, axis=0, keepdims=True)
        grad = grad_hidden[item] + norm_back(grad, hat, inverse, params[0:1])
        input_grad[item] = grad.astype(BF16)

    def along_line(m):
        return Transfer(pile, line_in.at[m], line_s.at[m], line_r.at[m], (u, c, lax.rem(z + m, zs)))

    def along_row(m):
        other = lax.rem(me + m, n)
        return Transfer(
            total, row_in.at[m], row_s.at[m], row_r.at[m], (other // cl, lax.rem(other, cl), z)
        )

    def exchange(m):
        other = lax.rem(me + m, n)
        return Transfer(
            low.at[other], cut.at[me], a_send.at[m], a_recv.at[m], (other // cl, lax.rem(other, cl), z)
        )

    def landed(m):
        source = lax.rem(me - m + n, n)
        return Transfer(
            low.at[source], cut.at[source], a_send.at[m], a_recv.at[m], (u, 1 - c, z)
        )

    loop(1, zs, lambda m: along_line(m).start())

    def finish(m):
        piece = lax.rem(me + m, n)
        line.total(piece, row_total)
        low[piece] = row_total[...].astype(BF16)

        @pl.when(m > 0)
        def _():
            exchange(m).start()

    loop(0, n, finish)
    mine = pltpu.make_async_copy(low.at[me], cut.at[me], own.at[0])
    mine.start()
    total[...] = pile[...]
    for m in range(1, zs):
        along_line(m).wait_recv()
        total[...] += line_in[m]
    loop(1, n, lambda m: along_row(m).start())
    small[...] = total[...]

    def collect(m):
        along_row(m).wait_recv()
        small[...] += row_in[m]

    loop(1, n, collect)
    loop(1, n, lambda m: landed(m).wait_recv())
    mine.wait()
    loop(1, n, lambda m: exchange(m).wait_send())
    loop(1, n, lambda m: along_row(m).wait_send())
    loop(1, zs, lambda m: along_line(m).wait_send())
    reduce.drain()
    line.drain()


def tail(parts, x, grad_hidden, params, terms, grads):
    cu, cl, zs = sizes()
    n = cu * cl
    rows, width = x.shape
    block = (ITEMS, rows // ITEMS, width)
    piece = grads.shape[2:]
    input_grad, small, cut = pl.pallas_call(
        tail_kernel,
        in_specs=[ANY, VMEM, VMEM, VMEM, VMEM, ANY],
        out_specs=[VMEM, VMEM, ANY],
        out_shape=[
            jax.ShapeDtypeStruct(block, BF16),
            jax.ShapeDtypeStruct((8, width), F32),
            jax.ShapeDtypeStruct((n, *piece), BF16),
        ],
        scratch_shapes=[
            pltpu.VMEM((8, width), F32), pltpu.VMEM((zs, 8, width), F32), pltpu.VMEM((n, 8, width), F32),
            pltpu.VMEM((8, width), F32), pltpu.VMEM(piece, F32), DMA((zs,)), DMA((zs,)), DMA((n,)), DMA((n,)),
            DMA((n,)), DMA((n,)), DMA((1,)), DMA((1,)), pltpu.VMEM((n, *piece), BF16),
            *RowReduce.scratch(cu, rows, width), *LineReduce.scratch(zs, n, piece),
        ],
        cost_estimate=pl.CostEstimate(flops=0, bytes_accessed=200 << 20, transcendentals=0),
        compiler_params=pltpu.CompilerParams(collective_id=3, has_side_effects=True, vmem_limit_bytes=60 << 20),
    )(parts.reshape(cu, cl, *block), x.reshape(block), grad_hidden.reshape(block), params, terms, grads)
    return input_grad.reshape(rows, width), small, cut


def body(
    inputs, out_grad, doc_ids, block_pairs, qkv_weight, proj_weight, ffn_in_weight, ffn_out_weight, small_params,
    qkv_first, proj_first, ffn_in_first, ffn_out_first, small_first,
    qkv_second, proj_second, ffn_in_second, ffn_out_second, small_second,
):
    bf16 = jnp.bfloat16
    tok_rows = inputs.shape[1]
    half_rows = tok_rows // 2
    cu, cl, zs = lax.axis_size("cu"), lax.axis_size("cl"), lax.axis_size("fsdp")
    ctx_count = cu * cl
    group = cl * zs
    seq_len = tok_rows * ctx_count
    my_index = lax.axis_index(ROW)
    heads = HEADS // ctx_count
    width = heads * HEAD_DIM
    slab = qkv_weight.shape[0]
    units = ffn_out_weight.shape[0]
    hidden = units * cu
    offsets = jnp.arange(half_rows, dtype=jnp.int32)
    all_pos = (block_pairs[:, :, None] * half_rows + offsets[None, None, :]).reshape(seq_len)
    key_docs = jnp.take(doc_ids[0], all_pos)
    marks = (all_pos[:, None], key_docs[:, None], all_pos[None, :], key_docs[None, :])
    tables = rotary_tables(all_pos, heads)

    qkv_cut = qkv_weight.astype(bf16).reshape(slab, 3, ctx_count, width).transpose(2, 0, 1, 3)
    small_pad = jnp.pad(small_params, ((0, 1), (0, -slab % 128)))
    row_in, params, qkv_low = gather_head(inputs[0], small_pad, qkv_cut.reshape(ctx_count, slab, 3 * width))
    row_in = row_in.reshape(seq_len, D)
    params = params[:, :, :7, :slab].transpose(2, 0, 1, 3).reshape(7, D)
    qkv_low = qkv_low.reshape(D, 3 * width)
    proj_low = lax.all_gather(proj_weight.astype(bf16), "fsdp", axis=0, tiled=True)
    in_cast = (
        ffn_in_weight.astype(bf16).reshape(slab, 2, cu, group, units).transpose(3, 0, 1, 2, 4)
        .reshape(group * slab, 2 * hidden)
    )
    in_cut = lax.all_to_all(in_cast, FFN_GROUP, split_axis=0, concat_axis=0, tiled=True)
    in_low = lax.all_gather(in_cut, "cu", axis=0, tiled=True)
    out_low = lax.all_gather(ffn_out_weight.astype(bf16), "cu", axis=0, tiled=True)
    grad_all = lax.all_gather(out_grad[0], FFN_GROUP, axis=0, tiled=True)

    normed_in, _, _ = norm_rows(row_in.astype(jnp.float32), params[0], params[1])
    attn_in = normed_in.astype(bf16)
    bias = lax.dynamic_slice_in_dim(params[4:7], my_index * width, width, 1).reshape(3 * width)
    joined = jnp.dot(attn_in, qkv_low, preferred_element_type=jnp.float32) + bias
    queries = turn(joined[:, :width], tables, 1.0).astype(bf16)
    keys = turn(joined[:, width : 2 * width], tables, 1.0).astype(bf16)
    values = joined[:, 2 * width :].astype(bf16)
    mixed, mixed_low, totals = attend(queries, keys, values, marks, heads)
    branch = jnp.dot(mixed_low, proj_low, preferred_element_type=jnp.float32).astype(bf16)
    hidden_state, mlp_in = mid_forward(branch, inputs[0], params[2:4])

    gate_up = jnp.dot(mlp_in, in_low, preferred_element_type=jnp.float32)
    gate_part, up_part = gate_up[:, :hidden], gate_up[:, hidden:]
    sigmoid_gate = jax.nn.sigmoid(gate_part)
    silu_gate = gate_part * sigmoid_gate
    inner_low = (silu_gate * up_part).astype(bf16)
    grad_inner = back_dot(grad_all, out_low)
    grad_up = grad_inner * silu_gate
    grad_gate = grad_inner * up_part * (sigmoid_gate * (1.0 + gate_part * (1.0 - sigmoid_gate)))
    grad_gate_up = jnp.concatenate([grad_gate, grad_up], axis=1).astype(bf16)
    grad_mid_part = back_dot(grad_gate_up, in_low).astype(bf16)
    out_part = jnp.dot(inner_low, out_low, preferred_element_type=jnp.float32).astype(bf16)
    out_own = lax.psum_scatter(out_part, FFN_GROUP, scatter_dimension=0, tiled=True)
    layer_out = (hidden_state + out_own.astype(jnp.float32)).astype(bf16)[None]
    grad_ffn_out = cross_dot(inner_low, grad_all).astype(bf16)
    grad_ffn_in = cross_dot(mlp_in, grad_gate_up).astype(bf16)
    ffn_out_grad = lax.psum_scatter(grad_ffn_out, "cu", scatter_dimension=0, tiled=True)
    in_grad_cut = lax.psum_scatter(grad_ffn_in, "cu", scatter_dimension=0, tiled=True)
    in_grad = lax.all_to_all(in_grad_cut, FFN_GROUP, split_axis=0, concat_axis=0, tiled=True)
    ffn_in_grad = in_grad.reshape(group, slab, 2, cu, units).transpose(1, 2, 3, 0, 4).reshape(slab, 2 * FF)

    grad_hidden, grad_branch, mid_sums = mid_backward(grad_mid_part, hidden_state, out_grad[0], params[2:4])
    grad_proj = cross_dot(mixed_low, grad_branch).astype(bf16)
    proj_grad = lax.psum_scatter(grad_proj, "fsdp", scatter_dimension=0, tiled=True)
    grad_mixed = back_dot(grad_branch, proj_low)
    grad_queries, grad_keys, grad_values = attend_back(
        queries, keys, values, grad_mixed, mixed, totals, marks, heads
    )
    grad_joined = jnp.concatenate(
        [turn(grad_queries, tables, -1.0), turn(grad_keys, tables, -1.0), grad_values], axis=1
    ).astype(bf16)
    grad_norm_part = back_dot(grad_joined, qkv_low).astype(bf16)
    grad_qkv = (
        cross_dot(attn_in, grad_joined).astype(bf16).reshape(ctx_count, zs, slab, 3 * width).transpose(1, 0, 2, 3)
    )
    bias_own = jnp.sum(grad_joined.astype(jnp.float32), axis=0).reshape(3, width)
    grad_bias = lax.dynamic_update_slice(jnp.zeros((3, D), jnp.float32), bias_own, (0, my_index * width))
    zero_rows = jnp.zeros((2, D), jnp.float32)
    terms = jnp.concatenate([zero_rows, mid_sums, grad_bias, zero_rows[:1]], axis=0)
    input_grad, small_sum, qkv_grad_cut = tail(
        grad_norm_part, inputs[0], grad_hidden, params[0:2], terms, grad_qkv
    )
    input_grad = input_grad[None]
    qkv_grad = qkv_grad_cut.reshape(ctx_count, slab, 3, width).transpose(1, 2, 0, 3).reshape(slab, 3 * D)
    my_slab = (my_index * zs + lax.axis_index("fsdp")) * slab
    small_grad = lax.dynamic_slice_in_dim(small_sum, my_slab, slab, 1)[:7]

    proj_fan = max(8 * D // seq_len, 1)
    f32 = jnp.float32
    qkv_new = adam_update(
        qkv_weight, qkv_first, qkv_second, qkv_grad.astype(f32), 2.0 / math.sqrt(D), matrix_decay
    )
    proj_new = adam_update(
        proj_weight, proj_first, proj_second, proj_grad.astype(f32), 2.0 / math.sqrt(proj_fan), matrix_decay
    )
    in_new = adam_update(
        ffn_in_weight, ffn_in_first, ffn_in_second, ffn_in_grad.astype(f32), 2.0 / math.sqrt(D), matrix_decay
    )
    out_new = adam_update(
        ffn_out_weight, ffn_out_first, ffn_out_second, ffn_out_grad.astype(f32), 2.0 / math.sqrt(FF), matrix_decay
    )
    small_new = adam_update(small_params, small_first, small_second, small_grad, small_rate, 0.0)
    news = (qkv_new, proj_new, in_new, out_new, small_new)
    return (layer_out, input_grad, *(n[0] for n in news), *(n[1] for n in news), *(n[2] for n in news), small_grad)


def solution(mesh):
    ctx_count, fsdp_count = mesh.devices.shape
    fine = Mesh(mesh.devices.reshape(ctx_count // 2, 2, fsdp_count), ("cu", "cl", "fsdp"))
    tokens = P("fsdp", ROW, None)
    matrix = P(EVERY, None)
    small = P(None, EVERY)
    five = (matrix, matrix, matrix, matrix, small)
    in_specs = (tokens, tokens, P("fsdp", None), P(), *five, *five, *five)
    out_specs = (tokens, tokens, *five, *five, *five, small)
    return jax.shard_map(body, mesh=fine, in_specs=in_specs, out_specs=out_specs, check_vma=False)
```

```python
import functools
import math

import jax
import jax.numpy as jnp
from jax import lax
from jax.experimental import pallas as pl
from jax.experimental.pallas import tpu as pltpu
from jax.sharding import Mesh, PartitionSpec as P

D = 2048
HEADS = 32
HEAD_DIM = 64
FF = 5632
ROT = 16
STEP = 10


norm_eps = 1e-05
beta_first = 0.9
beta_second = 0.95
adam_eps = 1e-08
matrix_decay = 0.1
small_rate = 0.5


def norm_rows(values, gain_row, shift_row):
    center_mean = jnp.mean(values, axis=-1, keepdims=True)
    centered = values - center_mean
    inv_std = lax.rsqrt(jnp.mean(centered * centered, axis=-1, keepdims=True) + norm_eps)
    normed = centered * inv_std
    return (normed * gain_row + shift_row, normed, inv_std)


def norm_back(grad_rows, normed, inv_std, gain_row):
    scaled = grad_rows * gain_row
    return inv_std * (
        scaled
        - jnp.mean(scaled, axis=-1, keepdims=True)
        - normed * jnp.mean(scaled * normed, axis=-1, keepdims=True)
    )


def cross_dot(left_mat, right_mat):
    return lax.dot_general(
        left_mat, right_mat, (((0,), (0,)), ((), ())), preferred_element_type=jnp.float32
    )


def back_dot(left_mat, weight):
    return lax.dot_general(
        left_mat, weight, (((1,), (1,)), ((), ())), preferred_element_type=jnp.float32
    )


def adam_update(weight, first_moment, second_moment, gradient, step_rate, decay_factor):
    new_first = beta_first * first_moment + (1.0 - beta_first) * gradient
    new_second = beta_second * second_moment + (1.0 - beta_second) * gradient * gradient
    correct_first = 1.0 - beta_first**STEP
    correct_second = 1.0 - beta_second**STEP
    update = new_first / correct_first / (jnp.sqrt(new_second / correct_second) + adam_eps)
    return (weight - step_rate * (update + decay_factor * weight), new_first, new_second)


ROW = ("cu", "cl")
FFN_GROUP = ("cl", "fsdp")
EVERY = ("cu", "cl", "fsdp")
SCALE = HEAD_DIM**-0.5


LANES = 128


def rotary_tables(positions):
    half_rot = ROT // 2
    lane = jnp.arange(LANES) % HEAD_DIM
    inverse = 10000.0 ** (-2.0 * (lane % half_rot).astype(jnp.float32) / ROT)
    angles = positions.astype(jnp.float32)[:, None] * jnp.where(lane < ROT, inverse, 0.0)[None, :]
    sine = jnp.sin(angles)
    lower = jnp.where(lane < half_rot, -sine, 0.0)
    upper = jnp.where(lane < half_rot, 0.0, sine)
    return jnp.concatenate([jnp.cos(angles), lower, upper], axis=1)


def turn(values, table, sign):
    keep, lower, upper = (table[:, i * LANES : (i + 1) * LANES] for i in range(3))
    half_rot = ROT // 2
    shifted = pltpu.roll(values, LANES - half_rot, 1) * lower + pltpu.roll(values, half_rot, 1) * upper
    return values * keep + sign * shifted


def dot_t(left, right):
    return lax.dot_general(left, right, (((1,), (1,)), ((), ())), preferred_element_type=jnp.float32)


def row_block(rows):
    return min(256, rows)


def project_kernel(x_ref, params_ref, w_ref, bias_ref, table_ref, normed_ref, qkv_ref):
    normed = norm_rows(x_ref[...].astype(jnp.float32), params_ref[0:1], params_ref[1:2])[0].astype(jnp.bfloat16)
    normed_ref[...] = normed
    joined = jnp.dot(normed, w_ref[...], preferred_element_type=jnp.float32) + bias_ref[...]
    turned = 2 * (joined.shape[1] // 3)
    for start in range(0, turned, LANES):
        cols = slice(start, start + LANES)
        qkv_ref[:, cols] = turn(joined[:, cols], table_ref[...], 1.0).astype(jnp.bfloat16)
    qkv_ref[:, turned:] = joined[:, turned:].astype(jnp.bfloat16)


def project(x, params, weight, bias, table):
    rows, width = x.shape
    block = row_block(rows)
    cols = weight.shape[1]

    def by_row(n):
        return pl.BlockSpec((block, n), lambda i: (i, 0))

    def whole(array):
        return pl.BlockSpec(array.shape, lambda i: (0, 0))

    return pl.pallas_call(
        project_kernel,
        grid=(rows // block,),
        in_specs=[by_row(width), whole(params), whole(weight), whole(bias), by_row(table.shape[1])],
        out_specs=[by_row(width), by_row(cols)],
        out_shape=[jax.ShapeDtypeStruct((rows, width), jnp.bfloat16), jax.ShapeDtypeStruct((rows, cols), jnp.bfloat16)],
        cost_estimate=pl.CostEstimate(
            flops=2 * rows * width * cols, bytes_accessed=4 * rows * width, transcendentals=0
        ),
        compiler_params=pltpu.CompilerParams(vmem_limit_bytes=48 << 20),
    )(x, params, weight, bias, table)


def attend_kernel(
    heads, q_ref, qkv_ref, proj_ref, pq_ref, dq_ref, pk_ref, dk_ref, mixed_ref, low_ref, tot_ref, branch_ref
):
    width = heads * HEAD_DIM
    allowed = (pk_ref[...] <= pq_ref[...]) & (dk_ref[...] == dq_ref[...])
    for head in range(heads):
        cols, key, value = (slice(p * width + head * HEAD_DIM, p * width + (head + 1) * HEAD_DIM) for p in range(3))
        scores = dot_t(q_ref[:, cols], qkv_ref[:, key]) * SCALE
        weights = jnp.where(allowed, jnp.exp(scores), 0.0)
        total = jnp.sum(weights, axis=1, keepdims=True)
        weighted = jnp.dot(weights.astype(jnp.bfloat16), qkv_ref[:, value], preferred_element_type=jnp.float32)
        mixed = weighted / total
        mixed_ref[:, cols] = mixed
        low_ref[:, cols] = mixed.astype(jnp.bfloat16)
        tot_ref[:, head : head + 1] = total
    branch_ref[...] = jnp.dot(low_ref[...], proj_ref[...], preferred_element_type=jnp.float32).astype(jnp.bfloat16)


def attend(qkv, proj, marks, heads):
    pos_col, doc_col, pos_row, doc_row = marks
    rows, cols = qkv.shape
    width = cols // 3
    block = row_block(rows)

    def by_row(n):
        return pl.BlockSpec((block, n), lambda i: (i, 0))

    def whole(array):
        return pl.BlockSpec(array.shape, lambda i: (0, 0))

    return pl.pallas_call(
        functools.partial(attend_kernel, heads),
        grid=(rows // block,),
        in_specs=[by_row(cols), whole(qkv), whole(proj), by_row(1), by_row(1), whole(pos_row), whole(doc_row)],
        out_specs=[by_row(width), by_row(width), by_row(heads), by_row(D)],
        out_shape=[
            jax.ShapeDtypeStruct((rows, width), jnp.float32),
            jax.ShapeDtypeStruct((rows, width), jnp.bfloat16),
            jax.ShapeDtypeStruct((rows, heads), jnp.float32),
            jax.ShapeDtypeStruct((rows, D), jnp.bfloat16),
        ],
        cost_estimate=pl.CostEstimate(
            flops=4 * rows * rows * width, bytes_accessed=8 * rows * D, transcendentals=rows * rows * heads
        ),
        compiler_params=pltpu.CompilerParams(vmem_limit_bytes=48 << 20),
    )(qkv, qkv, proj, pos_col, doc_col, pos_row, doc_row)


def attend_back_kernel(
    heads, q_ref, qkv_ref, branch_ref, proj_ref, mixed_ref, tot_ref, pq_ref, dq_ref, pk_ref, dk_ref, table_ref,
    joined_ref, bias_ref, gq_ref, gk_ref, gv_ref,
):
    width = heads * HEAD_DIM
    rows = qkv_ref.shape[0]
    block = q_ref.shape[0]
    step = pl.program_id(0)

    @pl.when(step == 0)
    def _():
        gk_ref[...] = jnp.zeros_like(gk_ref)
        gv_ref[...] = jnp.zeros_like(gv_ref)

    grad_all = dot_t(branch_ref[...], proj_ref[...])
    allowed = (pk_ref[...] <= pq_ref[...]) & (dk_ref[...] == dq_ref[...])
    here = pl.ds(pl.multiple_of(step * block, block), block)
    for head in range(heads):
        cols, key, value = (slice(p * width + head * HEAD_DIM, p * width + (head + 1) * HEAD_DIM) for p in range(3))
        q, k, v = q_ref[:, cols], qkv_ref[:, key], qkv_ref[:, value]
        inverse = 1.0 / tot_ref[:, head : head + 1]
        grad_mixed = grad_all[:, cols]
        grad_weighted = (grad_mixed * inverse).astype(jnp.bfloat16)
        grad_total = -jnp.sum(grad_mixed * mixed_ref[:, cols], axis=1, keepdims=True) * inverse
        weights = jnp.where(allowed, jnp.exp(dot_t(q, k) * SCALE), 0.0)
        grad_scores = (weights * (dot_t(grad_weighted, v) + grad_total)).astype(jnp.bfloat16)
        gq_ref[here, cols] = jnp.dot(grad_scores, k, preferred_element_type=jnp.float32) * SCALE
        gk_ref[:, cols] += cross_dot(grad_scores, q) * SCALE
        gv_ref[:, cols] += cross_dot(weights.astype(jnp.bfloat16), grad_weighted)

    @pl.when(step == rows // block - 1)
    def _():
        for part, ref in enumerate((gq_ref, gk_ref, gv_ref)):
            for start in range(0, width, LANES):
                cols = slice(start, min(start + LANES, width))
                grad = ref[:, cols]
                if part < 2:
                    lanes = cols.stop - cols.start
                    if lanes < LANES:
                        grad = jnp.concatenate([grad, jnp.zeros((rows, LANES - lanes), jnp.float32)], axis=1)
                    grad = turn(grad, table_ref[...], -1.0)[:, :lanes]
                grad = grad.astype(jnp.bfloat16)
                into = slice(part * width + cols.start, part * width + cols.stop)
                joined_ref[:, into] = grad
                bias_ref[:, into] = jnp.sum(grad.astype(jnp.float32), axis=0, keepdims=True)


def attend_back(qkv, grad_branch, proj, mixed, totals, marks, table, heads):
    pos_col, doc_col, pos_row, doc_row = marks
    rows, cols = qkv.shape
    width = cols // 3
    block = row_block(rows)

    def by_row(n):
        return pl.BlockSpec((block, n), lambda i: (i, 0))

    def whole(array):
        return pl.BlockSpec(array.shape, lambda i: (0, 0))

    return pl.pallas_call(
        functools.partial(attend_back_kernel, heads),
        grid=(rows // block,),
        in_specs=[
            by_row(cols), whole(qkv), by_row(D), whole(proj), by_row(width), by_row(heads), by_row(1), by_row(1),
            whole(pos_row), whole(doc_row), whole(table),
        ],
        out_specs=[pl.BlockSpec((rows, cols), lambda i: (0, 0)), pl.BlockSpec((1, cols), lambda i: (0, 0))],
        out_shape=[jax.ShapeDtypeStruct((rows, cols), jnp.bfloat16), jax.ShapeDtypeStruct((1, cols), jnp.float32)],
        scratch_shapes=[pltpu.VMEM((rows, width), jnp.float32)] * 3,
        cost_estimate=pl.CostEstimate(
            flops=10 * rows * rows * width, bytes_accessed=8 * rows * D, transcendentals=rows * rows * heads
        ),
        compiler_params=pltpu.CompilerParams(vmem_limit_bytes=60 << 20),
    )(qkv, qkv, grad_branch, proj, mixed, totals, pos_col, doc_col, pos_row, doc_row, table)


def adam_ffn_kernel(rate, w, m, v, g, w_new, m_new, v_new):
    group, _, cols = g.shape
    parts = w.shape[1] // cols
    units = cols // parts
    for part in range(parts):
        grad = jnp.concatenate(
            [g[owner, :, part * units : (part + 1) * units].astype(jnp.float32) for owner in range(group)], axis=1
        )
        here = slice(part * cols, (part + 1) * cols)
        w_new[:, here], m_new[:, here], v_new[:, here] = adam_update(
            w[:, here], m[:, here], v[:, here], grad, rate, matrix_decay
        )


def adam_ffn(weight, first, second, cut, rate):
    rows = 16
    by_row = pl.BlockSpec((rows, weight.shape[1]), lambda i: (i, 0))
    return pl.pallas_call(
        functools.partial(adam_ffn_kernel, rate),
        grid=(weight.shape[0] // rows,),
        in_specs=[by_row, by_row, by_row, pl.BlockSpec((cut.shape[0], rows, cut.shape[2]), lambda i: (0, i, 0))],
        out_specs=[by_row] * 3,
        out_shape=[jax.ShapeDtypeStruct(weight.shape, jnp.float32)] * 3,
        compiler_params=pltpu.CompilerParams(vmem_limit_bytes=48 << 20),
    )(weight, first, second, cut)


def adam_qkv_kernel(rate, w, m, v, g, w_new, m_new, v_new):
    n, _, cols = g.shape
    width = cols // 3
    for part in range(3):
        grad = jnp.concatenate(
            [g[owner, :, part * width : (part + 1) * width].astype(jnp.float32) for owner in range(n)], axis=1
        )
        here = slice(part * n * width, (part + 1) * n * width)
        w_new[:, here], m_new[:, here], v_new[:, here] = adam_update(
            w[:, here], m[:, here], v[:, here], grad, rate, matrix_decay
        )


def adam_qkv(weight, first, second, cut, rate):
    rows = 16
    by_row = pl.BlockSpec((rows, weight.shape[1]), lambda i: (i, 0))
    return pl.pallas_call(
        functools.partial(adam_qkv_kernel, rate),
        grid=(weight.shape[0] // rows,),
        in_specs=[by_row, by_row, by_row, pl.BlockSpec((cut.shape[0], rows, cut.shape[2]), lambda i: (0, i, 0))],
        out_specs=[by_row] * 3,
        out_shape=[jax.ShapeDtypeStruct(weight.shape, jnp.float32)] * 3,
        compiler_params=pltpu.CompilerParams(vmem_limit_bytes=48 << 20),
    )(weight, first, second, cut)


MESH = pl.DeviceIdType.MESH
ANY = pl.BlockSpec(memory_space=pl.ANY)
VMEM = pl.BlockSpec(memory_space=pltpu.VMEM)
DMA = pltpu.SemaphoreType.DMA
BF16, F32 = jnp.bfloat16, jnp.float32


class Transfer:
    def __init__(self, src, dst, send, recv, device):
        self.parts = (src, dst, send, recv, device)

    def copy(self):
        src, dst, send, recv, device = self.parts
        return pltpu.make_async_remote_copy(
            src_ref=src, dst_ref=dst, send_sem=send, recv_sem=recv, device_id=device, device_id_type=MESH
        )

    def start(self):
        self.copy().start()

    def wait_recv(self):
        self.copy().wait_recv()

    def wait_send(self):
        self.copy().wait_send()

    def wait(self):
        self.copy().wait()


rcopy = Transfer


def flip(index, mask):
    bit = 1
    while bit <= mask:
        if mask & bit:
            index = index + bit * (1 - 2 * lax.rem(index // bit, 2))
        bit *= 2
    return index


def place():
    return lax.axis_index("cu"), lax.axis_index("cl"), lax.axis_index("fsdp")


def sizes():
    return lax.axis_size("cu"), lax.axis_size("cl"), lax.axis_size("fsdp")


def greet(row, line):
    u, c, z = place()
    cu, cl, zs = sizes()
    n, me = cu * cl, u * cl + c
    barrier = pltpu.get_barrier_semaphore()

    def signal_row(m, carry):
        other = lax.rem(me + m, n)
        pl.semaphore_signal(barrier, inc=1, device_id=(other // cl, lax.rem(other, cl), z), device_id_type=MESH)
        return carry

    def signal_line(m, carry):
        pl.semaphore_signal(barrier, inc=1, device_id=(u, c, lax.rem(z + m, zs)), device_id_type=MESH)
        return carry

    if row:
        lax.fori_loop(1, n, signal_row, 0)
    if line:
        lax.fori_loop(1, zs, signal_line, 0)
    pl.semaphore_wait(barrier, row * (n - 1) + line * (zs - 1))


def head_kernel(
    x, small, qkv, ffn_in, row, par, wq, in_cut, own, x_send, x_recv, s_send, s_recv, p_send, p_recv, q_send, q_recv,
    a_send, a_recv, up_send, up_recv, dn_send, dn_recv,
):
    u, c, z = place()
    cu, cl, zs = sizes()
    n, me = cu * cl, u * cl + c
    sibling = (u, 1 - c, z)
    mine = [
        pltpu.make_async_copy(qkv.at[me], wq.at[me, z], own.at[0]),
        pltpu.make_async_copy(x, row.at[u, c], own.at[1]),
        pltpu.make_async_copy(small, par.at[me, z], own.at[2]),
    ]
    for copy in mine:
        copy.start()
    greet(True, True)

    def exchange(m):
        other, source = lax.rem(me + m, n), lax.rem(me - m + n, n)
        out = rcopy(
            qkv.at[other], wq.at[me, z], a_send.at[m], a_recv.at[m], (other // cl, lax.rem(other, cl), z)
        )
        into = rcopy(qkv.at[other], wq.at[source, z], a_send.at[m], a_recv.at[m], sibling)
        return out, into

    def params_line(m):
        other, source = lax.rem(z + m, zs), lax.rem(z - m + zs, zs)
        return (
            rcopy(small, par.at[me, z], p_send.at[m], p_recv.at[m], (u, c, other)),
            rcopy(small, par.at[me, source], p_send.at[m], p_recv.at[m], sibling),
        )

    def params_row(m):
        other, source = lax.rem(me + m, n), lax.rem(me - m + n, n)
        return (
            rcopy(par.at[me], par.at[me], q_send.at[m], q_recv.at[m], (other // cl, lax.rem(other, cl), z)),
            rcopy(par.at[me], par.at[source], q_send.at[m], q_recv.at[m], sibling),
        )

    def x_far(i):
        out = rcopy(x, row.at[u, c], x_send.at[i], x_recv.at[i], (flip(u, i), c, z))
        into = rcopy(x, row.at[flip(u, i), c], x_send.at[i], x_recv.at[i], sibling)
        return out, into

    def x_near(i):
        part = row.at[flip(u, i), c]
        out = rcopy(part, part, s_send.at[i], s_recv.at[i], sibling)
        into = rcopy(part, row.at[flip(u, i), 1 - c], s_send.at[i], s_recv.at[i], sibling)
        return out, into

    def loop(low, high, step):
        def run(m, carry):
            step(m)
            return carry

        lax.fori_loop(low, high, run, 0)

    loop(1, n, lambda m: exchange(m)[0].start())
    loop(1, zs, lambda m: params_line(m)[0].start())
    for copy in mine:
        copy.wait()
    for i in range(1, cu):
        x_far(i)[0].start()
    x_near(0)[0].start()

    def chain(step, m):
        piece = lax.rem(me - m + n, n)
        above, below = wq.at[piece, lax.rem(z + step, zs)], wq.at[piece, lax.rem(z - step + zs, zs)]
        return (
            rcopy(below, below, up_send.at[step, m], up_recv.at[step, m], (u, c, lax.rem(z + 1, zs))),
            rcopy(above, above, dn_send.at[step, m], dn_recv.at[step, m], (u, c, lax.rem(z - 1 + zs, zs))),
        )

    def arrival(step, m):
        piece = lax.rem(me - m + n, n)
        above, below = wq.at[piece, lax.rem(z + step + 1, zs)], wq.at[piece, lax.rem(z - step - 1 + zs, zs)]
        return (
            rcopy(below, below, up_send.at[step, m], up_recv.at[step, m], sibling),
            rcopy(above, above, dn_send.at[step, m], dn_recv.at[step, m], sibling),
        )

    def first(m):
        @pl.when(m > 0)
        def _():
            exchange(m)[1].wait_recv()

        @pl.when(z + 1 < zs)
        def _():
            chain(0, m)[0].start()

        @pl.when(z > 0)
        def _():
            chain(0, m)[1].start()

    loop(0, n, first)
    group, units = cl * zs, ffn_in.shape[1] // (2 * n * zs)
    for part in range(2 * cu):
        for owner in range(group):
            start = (part * group + owner) * units
            in_cut[owner, :, part * units : (part + 1) * units] = ffn_in[:, start : start + units].astype(BF16)
    for m in range(1, zs):
        params_line(m)[1].wait_recv()
    loop(1, n, lambda m: params_row(m)[0].start())
    for i in range(1, cu):
        x_far(i)[1].wait_recv()
        x_near(i)[0].start()
    for step in range(1, zs):

        def later(m, step=step):
            @pl.when(z >= step)
            def _():
                arrival(step - 1, m)[0].wait_recv()

            @pl.when((z >= step) & (z + 1 < zs))
            def _():
                chain(step, m)[0].start()

            @pl.when(z + step < zs)
            def _():
                arrival(step - 1, m)[1].wait_recv()

            @pl.when((z + step < zs) & (z > 0))
            def _():
                chain(step, m)[1].start()

        loop(0, n, later)
    loop(1, n, lambda m: params_row(m)[1].wait_recv())
    for i in range(cu):
        x_near(i)[1].wait_recv()
    loop(1, n, lambda m: exchange(m)[0].wait_send())
    loop(1, zs, lambda m: params_line(m)[0].wait_send())
    loop(1, n, lambda m: params_row(m)[0].wait_send())
    for i in range(cu):
        x_near(i)[0].wait_send()
        if i:
            x_far(i)[0].wait_send()
    for step in range(zs - 1):

        def sent(m, step=step):
            @pl.when((z >= step) & (z + 1 < zs))
            def _():
                chain(step, m)[0].wait_send()

            @pl.when((z + step < zs) & (z > 0))
            def _():
                chain(step, m)[1].wait_send()

        loop(0, n, sent)


def gather_head(x, small, qkv_cut, ffn_in):
    cu, cl, zs = sizes()
    n = cu * cl
    return pl.pallas_call(
        head_kernel,
        in_specs=[ANY, ANY, ANY, VMEM],
        out_specs=[ANY, ANY, ANY, VMEM],
        out_shape=[
            jax.ShapeDtypeStruct((cu, cl, *x.shape), x.dtype),
            jax.ShapeDtypeStruct((n, zs, *small.shape), small.dtype),
            jax.ShapeDtypeStruct((n, zs, *qkv_cut.shape[1:]), qkv_cut.dtype),
            jax.ShapeDtypeStruct((cl * zs, ffn_in.shape[0], ffn_in.shape[1] // (cl * zs)), BF16),
        ],
        scratch_shapes=[
            DMA((3,)), DMA((cu,)), DMA((cu,)), DMA((cu,)), DMA((cu,)), DMA((zs,)), DMA((zs,)), DMA((n,)), DMA((n,)),
            DMA((n,)), DMA((n,)), DMA((zs, n)), DMA((zs, n)), DMA((zs, n)), DMA((zs, n)),
        ],
        cost_estimate=pl.CostEstimate(flops=0, bytes_accessed=200 << 20, transcendentals=0),
        compiler_params=pltpu.CompilerParams(collective_id=0, has_side_effects=True, vmem_limit_bytes=40 << 20),
    )(x, small, qkv_cut, ffn_in)


ITEMS = 4


def loop(low, high, step):
    def run(m, carry):
        step(m)
        return carry

    lax.fori_loop(low, high, run, 0)


def bits_of(count):
    return [1 << b for b in range(count.bit_length() - 1)]


def combos(bits):
    masks = [0]
    for b in bits:
        masks = masks + [m | b for m in masks]
    return masks


def order_of(item, count):
    return bits_of(count) if item < ITEMS // 2 else bits_of(count)[::-1]


def add_low(left, right):
    return (left.astype(F32) + right.astype(F32)).astype(BF16)


class RowReduce:
    def __init__(self, parts, held, beside, came, load, sib_s, sib_r, out_s, out_r):
        self.parts, self.held, self.beside, self.came = parts, held, beside, came
        self.load, self.sib_s, self.sib_r, self.out_s, self.out_r = load, sib_s, sib_r, out_s, out_r
        self.u, self.c, self.z = place()
        self.count = sizes()[0]
        self.phases = self.count.bit_length() - 1

    def sib(self, mask):
        return Transfer(
            self.parts.at[flip(self.u, mask), 1 - self.c], self.beside.at[mask], self.sib_s.at[mask],
            self.sib_r.at[mask], (self.u, 1 - self.c, self.z),
        )

    def loading(self, mask):
        return pltpu.make_async_copy(
            self.parts.at[flip(self.u, mask), self.c], self.held.at[mask], self.load.at[mask]
        )

    def start(self):
        for mask in reversed(range(self.count)):
            self.sib(mask).start()
            self.loading(mask).start()

    def merge(self):
        for mask in reversed(range(self.count)):
            self.loading(mask).wait()
            self.sib(mask).wait_recv()
            self.held[mask] = add_low(self.held[mask], self.beside[mask])

    def steps(self, item, phase):
        order = order_of(item, self.count)
        slot = self.count - (self.count >> phase)
        for k, rest in enumerate(combos(order[phase + 1 :])):
            yield slot + k, rest, Transfer(
                self.held.at[order[phase] | rest, item], self.came.at[slot + k, item], self.out_s.at[slot + k, item],
                self.out_r.at[slot + k, item], (flip(self.u, order[phase]), self.c, self.z),
            )

    def send(self, item, phase):
        for _, _, transfer in self.steps(item, phase):
            transfer.start()

    def add(self, item, phase):
        for slot, rest, transfer in self.steps(item, phase):
            transfer.wait_recv()
            self.held[rest, item] = add_low(self.held[rest, item], self.came[slot, item])

    def total(self, item):
        ((slot, _, transfer),) = self.steps(item, self.phases - 1)
        transfer.wait_recv()
        return self.held[0, item].astype(F32) + self.came[slot, item].astype(F32)

    def drain(self):
        for mask in range(self.count):
            self.sib(mask).wait_send()
        for item in range(ITEMS):
            for phase in range(self.phases):
                for _, _, transfer in self.steps(item, phase):
                    transfer.wait_send()

    @staticmethod
    def scratch(count, rows, width):
        block = (count, ITEMS, rows // ITEMS, width)
        return [
            pltpu.VMEM(block, BF16), pltpu.VMEM(block, BF16), pltpu.VMEM(block, BF16), DMA((count,)), DMA((count,)),
            DMA((count,)), DMA((count, ITEMS)), DMA((count, ITEMS)),
        ]


class RowGather:
    def __init__(self, own, full, keep, out_s, out_r, sib_s, sib_r):
        self.own, self.full, self.keep = own, full, keep
        self.out_s, self.out_r, self.sib_s, self.sib_r = out_s, out_r, sib_s, sib_r
        self.u, self.c, self.z = place()
        self.count = sizes()[0]
        self.phases = self.count.bit_length() - 1

    def kept(self, item):
        return pltpu.make_async_copy(self.own.at[item], self.full.at[self.u, self.c, item], self.keep.at[item])

    def source(self, mask, item):
        return self.own.at[item] if mask == 0 else self.full.at[flip(self.u, mask), self.c, item]

    def sib(self, mask, item):
        return Transfer(
            self.source(mask, item), self.full.at[flip(self.u, mask), self.c, item], self.sib_s.at[mask, item],
            self.sib_r.at[mask, item], (self.u, 1 - self.c, self.z),
        )

    def steps(self, item, phase):
        order = order_of(item, self.count)
        for k, mask in enumerate(combos(order[:phase])):
            slot = (1 << phase) - 1 + k
            yield mask | order[phase], Transfer(
                self.source(mask, item), self.full.at[flip(self.u, mask), self.c, item], self.out_s.at[slot, item],
                self.out_r.at[slot, item], (flip(self.u, order[phase]), self.c, self.z),
            )

    def start(self, item):
        self.send(item, 0)
        self.sib(0, item).start()
        self.kept(item).start()

    def send(self, item, phase):
        for _, transfer in self.steps(item, phase):
            transfer.start()

    def pass_on(self, item, phase):
        for mask, transfer in self.steps(item, phase):
            transfer.wait_recv()
            self.sib(mask, item).start()

    def drain(self):
        for item in range(ITEMS):
            self.kept(item).wait()
            for mask in range(self.count):
                self.sib(mask, item).wait()
            for phase in range(self.phases):
                for _, transfer in self.steps(item, phase):
                    transfer.wait_send()

    @staticmethod
    def scratch(count):
        return [DMA((ITEMS,)), *[DMA((count, ITEMS))] * 4]


class LineGather:
    def __init__(self, own, full, keep, up_s, up_r, dn_s, dn_r, sib_s, sib_r):
        self.own, self.full, self.keep = own, full, keep
        self.up_s, self.up_r, self.dn_s, self.dn_r, self.sib_s, self.sib_r = up_s, up_r, dn_s, dn_r, sib_s, sib_r
        self.u, self.c, self.z = place()
        self.count = sizes()[2]

    def kept(self, item):
        return pltpu.make_async_copy(self.own.at[item], self.full.at[self.c, self.z, item], self.keep.at[item])

    def up(self, item, step):
        origin = lax.rem(self.z - step + self.count, self.count)
        block = self.full.at[self.c, origin, item]
        source = self.own.at[item] if step == 0 else block
        to = lax.rem(self.z + 1, self.count)
        return Transfer(source, block, self.up_s.at[step, item], self.up_r.at[step, item], (self.u, self.c, to))

    def down(self, item, step):
        block = self.full.at[self.c, lax.rem(self.z + step, self.count), item]
        source = self.own.at[item] if step == 0 else block
        to = lax.rem(self.z - 1 + self.count, self.count)
        return Transfer(source, block, self.dn_s.at[step, item], self.dn_r.at[step, item], (self.u, self.c, to))

    def sib(self, item, origin, own=False):
        block = self.full.at[self.c, origin, item]
        return Transfer(
            self.own.at[item] if own else block, block, self.sib_s.at[origin, item], self.sib_r.at[origin, item],
            (self.u, 1 - self.c, self.z),
        )

    def start(self, item):
        @pl.when(self.z + 1 < self.count)
        def _():
            self.up(item, 0).start()

        @pl.when(self.z > 0)
        def _():
            self.down(item, 0).start()

        self.sib(item, self.z, True).start()
        self.kept(item).start()

    def forward(self, item, step):
        z, count = self.z, self.count

        @pl.when(z >= step)
        def _():
            self.up(item, step - 1).wait_recv()
            if step < count - 1:

                @pl.when(z + 1 < count)
                def _():
                    self.up(item, step).start()

            self.sib(item, z - step).start()

        @pl.when(z + step < count)
        def _():
            self.down(item, step - 1).wait_recv()
            if step < count - 1:

                @pl.when(z > 0)
                def _():
                    self.down(item, step).start()

            self.sib(item, z + step).start()

    def drain(self):
        z, count = self.z, self.count
        for item in range(ITEMS):
            self.kept(item).wait()
            for origin in range(count):
                self.sib(item, origin).wait()
            for step in range(count - 1):

                @pl.when((z >= step) & (z + 1 < count))
                def _(item=item, step=step):
                    self.up(item, step).wait_send()

                @pl.when((z + step < count) & (z > 0))
                def _(item=item, step=step):
                    self.down(item, step).wait_send()

    @staticmethod
    def scratch(count):
        return [DMA((ITEMS,)), *[DMA((count, ITEMS))] * 6]


class LineReduce:
    def __init__(self, held, from_below, from_above, pieces, up_s, up_r, dn_s, dn_r):
        self.held, self.from_below, self.from_above, self.pieces = held, from_below, from_above, pieces
        self.up_s, self.up_r, self.dn_s, self.dn_r = up_s, up_r, dn_s, dn_r
        self.u, self.c, self.z = place()
        self.count = sizes()[2]

    def up(self, to, piece):
        return Transfer(
            self.held.at[to, piece], self.from_below.at[to, piece], self.up_s.at[to, piece], self.up_r.at[to, piece],
            (self.u, self.c, lax.rem(self.z + 1, self.count)),
        )

    def down(self, to, piece):
        return Transfer(
            self.held.at[to, piece], self.from_above.at[to, piece], self.dn_s.at[to, piece], self.dn_r.at[to, piece],
            (self.u, self.c, lax.rem(self.z - 1 + self.count, self.count)),
        )

    def step(self, t):
        z, count = self.z, self.count
        far_up, far_down = count - 1 - t, t

        def upward(piece):
            @pl.when(z > 0)
            def _():
                self.up(far_up, piece).wait_recv()
                self.held[far_up, piece] = add_low(self.held[far_up, piece], self.from_below[far_up, piece])

            self.up(far_up, piece).start()

        def downward(piece):
            @pl.when(z < count - 1)
            def _():
                self.down(far_down, piece).wait_recv()
                self.held[far_down, piece] = add_low(self.held[far_down, piece], self.from_above[far_down, piece])

            self.down(far_down, piece).start()

        lag = min(3, self.pieces // 2)
        late_up = lag * ((2 * z) // count)

        def one(i):
            piece_up, piece_down = i - late_up, i - (lag - late_up)

            @pl.when((z < far_up) & (piece_up >= 0) & (piece_up < self.pieces))
            def _():
                upward(piece_up)

            @pl.when((z > far_down) & (piece_down >= 0) & (piece_down < self.pieces))
            def _():
                downward(piece_down)

        loop(0, self.pieces + lag, one)

    def total(self, piece, into):
        z, count = self.z, self.count
        into[...] = self.held[z, piece].astype(F32)

        @pl.when(z > 0)
        def _():
            self.up(z, piece).wait_recv()
            into[...] += self.from_below[z, piece].astype(F32)

        @pl.when(z < count - 1)
        def _():
            self.down(z, piece).wait_recv()
            into[...] += self.from_above[z, piece].astype(F32)

    def drain(self):
        z, count = self.z, self.count
        for t in range(count - 1):
            far_up, far_down = count - 1 - t, t

            def one(piece, far_up=far_up, far_down=far_down):
                @pl.when(z < far_up)
                def _():
                    self.up(far_up, piece).wait_send()

                @pl.when(z > far_down)
                def _():
                    self.down(far_down, piece).wait_send()

            loop(0, self.pieces, one)

    @staticmethod
    def scratch(count, pieces, block):
        shape = (count, pieces, *block)
        return [*[pltpu.VMEM(shape, BF16)] * 3, *[DMA((count, pieces))] * 4]


def mid_forward_kernel(branch, x, out_grad, params, hidden, mlp, grads, low, *scratch):
    reduce = RowReduce(branch, *scratch[:8])
    gather = LineGather(low, mlp, *scratch[8:15])
    gather_grads = LineGather(out_grad, grads, *scratch[15:])
    greet(True, True)
    reduce.start()
    for item in range(ITEMS):
        gather_grads.start(item)
    reduce.merge()
    for item in range(ITEMS):
        reduce.send(item, 0)
    for item in range(ITEMS):
        gather_grads.forward(item, 1)
    for phase in range(1, reduce.phases):
        for item in range(ITEMS):
            reduce.add(item, phase - 1)
            reduce.send(item, phase)
    for step in range(2, gather.count):
        for item in range(ITEMS):
            gather_grads.forward(item, step)
    for item in range(ITEMS):
        state = x[item].astype(F32) + reduce.total(item)
        hidden[item] = state
        low[item] = norm_rows(state, params[0:1], params[1:2])[0].astype(BF16)
        gather.start(item)
    for step in range(1, gather.count):
        for item in range(ITEMS):
            gather.forward(item, step)
    gather_grads.drain()
    gather.drain()
    reduce.drain()


def mid_forward(branch, x, out_grad, params):
    cu, cl, zs = sizes()
    rows, width = x.shape
    block = (ITEMS, rows // ITEMS, width)
    full = jax.ShapeDtypeStruct((cl, zs, *block), BF16)
    hidden, mlp, grads, _ = pl.pallas_call(
        mid_forward_kernel,
        in_specs=[ANY, VMEM, VMEM, VMEM],
        out_specs=[VMEM, ANY, ANY, VMEM],
        out_shape=[
            jax.ShapeDtypeStruct(block, F32), full, full, jax.ShapeDtypeStruct(block, BF16),
        ],
        scratch_shapes=[*RowReduce.scratch(cu, rows, width), *LineGather.scratch(zs), *LineGather.scratch(zs)],
        cost_estimate=pl.CostEstimate(flops=0, bytes_accessed=200 << 20, transcendentals=0),
        compiler_params=pltpu.CompilerParams(collective_id=1, has_side_effects=True, vmem_limit_bytes=56 << 20),
    )(branch.reshape(cu, cl, *block), x.reshape(block), out_grad.reshape(block), params)
    return hidden.reshape(rows, width), mlp.reshape(cl * zs * rows, width), grads.reshape(cl * zs * rows, width)


def mid_backward_kernel(
    parts, hidden, out_grad, params, inner, weight, grads, grad_hidden, full, sums, layer_out, weight_grad, low,
    held, below, above, up_s, up_r, dn_s, dn_r, beside, total, load, sib_s, sib_r,
    held_out, below_out, above_out, up_so, up_ro, dn_so, dn_ro, beside_out, away, sib_so, sib_ro,
    inner_v, weight_v, grads_v, fetch, *scratch,
):
    u, c, z = place()
    zs = sizes()[2]
    rows = ITEMS * held.shape[2]
    reduce = LineReduce(held, below, above, ITEMS, up_s, up_r, dn_s, dn_r)
    reduce_out = LineReduce(held_out, below_out, above_out, ITEMS, up_so, up_ro, dn_so, dn_ro)
    gather = RowGather(low, full, *scratch)
    fetches = [
        pltpu.make_async_copy(inner, inner_v, fetch.at[0]),
        pltpu.make_async_copy(weight, weight_v, fetch.at[1]),
        pltpu.make_async_copy(grads, grads_v, fetch.at[2]),
    ]

    def sib(to):
        return Transfer(parts.at[1 - c, to], beside.at[to], sib_s.at[to], sib_r.at[to], (u, 1 - c, z))

    def sib_out(to):
        return Transfer(away.at[to], beside_out.at[to], sib_so.at[to], sib_ro.at[to], (u, 1 - c, z))

    def loading(to):
        return pltpu.make_async_copy(parts.at[c, to], held.at[to], load.at[to])

    order = sorted(range(zs), key=lambda to: -abs(2 * to - zs + 1))
    for to in order:
        loading(to).start()
    for copy in fetches:
        copy.start()
    greet(True, True)
    for to in order:
        sib(to).start()
    for to in order:
        loading(to).wait()
        sib(to).wait_recv()
        held[to] = add_low(held[to], beside[to])
    reduce.step(0)
    for copy in fetches:
        copy.wait()

    tile = 512
    width = weight_v.shape[1]

    def multiply(core, into):
        def one(i):
            to, col = i // (width // tile), lax.rem(i, width // tile) * tile
            cols = pl.ds(pl.multiple_of(col, tile), tile)
            left = inner_v[pl.ds(pl.multiple_of((core * zs + to) * rows, rows), rows)]
            part = jnp.dot(left, weight_v[:, cols], preferred_element_type=F32)
            into[to, :, :, cols] = part.astype(BF16).reshape(ITEMS, rows // ITEMS, tile)

        loop(0, zs * (width // tile), one)

    multiply(1 - c, away)
    for to in order:
        sib_out(to).start()
    reduce.step(1)
    multiply(c, held_out)
    for t in range(2, zs - 1):
        reduce.step(t)
    sums[...] = jnp.zeros_like(sums)
    for item in range(ITEMS):
        reduce.total(item, total)
        _, hat, inverse = norm_rows(hidden[item], params[0:1], params[1:2])
        grad = total[...]
        sums[0:1] += jnp.sum(grad * hat, axis=0, keepdims=True)
        sums[1:2] += jnp.sum(grad, axis=0, keepdims=True)
        grad = out_grad[item].astype(F32) + norm_back(grad, hat, inverse, params[0:1])
        grad_hidden[item] = grad
        low[item] = grad.astype(BF16)
        gather.start(item)
    for to in order:
        sib_out(to).wait_recv()
        held_out[to] = add_low(held_out[to], beside_out[to])
    reduce_out.step(0)
    for phase in range(gather.phases):
        for item in range(ITEMS):
            gather.pass_on(item, phase)
            if phase + 1 < gather.phases:
                gather.send(item, phase + 1)

    def outer(i):
        cols = pl.ds(pl.multiple_of(i * tile, tile), tile)
        weight_grad[:, cols] = cross_dot(inner_v[...], grads_v[:, cols]).astype(BF16)

    loop(0, width // tile, outer)
    for t in range(1, zs - 1):
        reduce_out.step(t)
    for item in range(ITEMS):
        reduce_out.total(item, total)
        layer_out[item] = (hidden[item] + total[...]).astype(BF16)
    gather.drain()
    reduce.drain()
    reduce_out.drain()
    for to in range(zs):
        sib(to).wait_send()
        sib_out(to).wait_send()


def mid_backward(parts, hidden, out_grad, params, inner, weight, grads):
    cu, cl, zs = sizes()
    rows, width = out_grad.shape
    block = (ITEMS, rows // ITEMS, width)
    shares = pltpu.VMEM((zs, *block), BF16)
    grad_hidden, full, sums, layer_out, weight_grad, _ = pl.pallas_call(
        mid_backward_kernel,
        in_specs=[ANY, VMEM, VMEM, VMEM, ANY, ANY, ANY],
        out_specs=[VMEM, ANY, VMEM, VMEM, VMEM, VMEM],
        out_shape=[
            jax.ShapeDtypeStruct(block, F32),
            jax.ShapeDtypeStruct((cu, cl, *block), BF16),
            jax.ShapeDtypeStruct((2, width), F32),
            jax.ShapeDtypeStruct(block, BF16),
            jax.ShapeDtypeStruct(weight.shape, BF16),
            jax.ShapeDtypeStruct(block, BF16),
        ],
        scratch_shapes=[
            *LineReduce.scratch(zs, ITEMS, block[1:]), shares, pltpu.VMEM(block[1:], F32),
            DMA((zs,)), DMA((zs,)), DMA((zs,)),
            *LineReduce.scratch(zs, ITEMS, block[1:]), shares, shares, DMA((zs,)), DMA((zs,)),
            pltpu.VMEM(inner.shape, BF16), pltpu.VMEM(weight.shape, BF16), pltpu.VMEM(grads.shape, BF16), DMA((3,)),
            *RowGather.scratch(cu),
        ],
        cost_estimate=pl.CostEstimate(flops=0, bytes_accessed=200 << 20, transcendentals=0),
        compiler_params=pltpu.CompilerParams(collective_id=2, has_side_effects=True, vmem_limit_bytes=60 << 20),
    )(parts.reshape(cl, zs, *block), hidden.reshape(block), out_grad.reshape(block), params, inner, weight, grads)
    return (
        grad_hidden.reshape(rows, width), full.reshape(cu * cl * rows, width), sums, layer_out.reshape(rows, width),
        weight_grad,
    )


def tail_kernel(parts, x, grad_hidden, params, terms, grads, input_grad, small, cut, pile, line_in, row_in, total,
                row_total, line_s, line_r, row_s, row_r, a_send, a_recv, own, held_load, low, *scratch):
    u, c, z = place()
    cu, cl, zs = sizes()
    n, me = cu * cl, u * cl + c
    reduce = RowReduce(parts, *scratch[:8])
    held = scratch[8]
    line = LineReduce(*scratch[8:11], n, *scratch[11:])
    load = pltpu.make_async_copy(grads, held, held_load.at[0])
    load.start()
    greet(True, True)
    reduce.start()
    load.wait()
    line.step(0)
    reduce.merge()
    for item in range(ITEMS):
        reduce.send(item, 0)
    for t in range(1, zs - 1):
        line.step(t)
    for phase in range(1, reduce.phases):
        for item in range(ITEMS):
            reduce.add(item, phase - 1)
            reduce.send(item, phase)
    pile[...] = terms[...]
    for item in range(ITEMS):
        grad = reduce.total(item)
        _, hat, inverse = norm_rows(x[item].astype(F32), params[0:1], params[1:2])
        pile[0:1] += jnp.sum(grad * hat, axis=0, keepdims=True)
        pile[1:2] += jnp.sum(grad, axis=0, keepdims=True)
        grad = grad_hidden[item] + norm_back(grad, hat, inverse, params[0:1])
        input_grad[item] = grad.astype(BF16)

    def along_line(m):
        return Transfer(pile, line_in.at[m], line_s.at[m], line_r.at[m], (u, c, lax.rem(z + m, zs)))

    def along_row(m):
        other = lax.rem(me + m, n)
        return Transfer(
            total, row_in.at[m], row_s.at[m], row_r.at[m], (other // cl, lax.rem(other, cl), z)
        )

    def exchange(m):
        other = lax.rem(me + m, n)
        return Transfer(
            low.at[other], cut.at[me], a_send.at[m], a_recv.at[m], (other // cl, lax.rem(other, cl), z)
        )

    def landed(m):
        source = lax.rem(me - m + n, n)
        return Transfer(
            low.at[source], cut.at[source], a_send.at[m], a_recv.at[m], (u, 1 - c, z)
        )

    loop(1, zs, lambda m: along_line(m).start())

    def finish(m):
        piece = lax.rem(me + m, n)
        line.total(piece, row_total)
        low[piece] = row_total[...].astype(BF16)

        @pl.when(m > 0)
        def _():
            exchange(m).start()

    loop(0, n, finish)
    mine = pltpu.make_async_copy(low.at[me], cut.at[me], own.at[0])
    mine.start()
    total[...] = pile[...]
    for m in range(1, zs):
        along_line(m).wait_recv()
        total[...] += line_in[m]
    loop(1, n, lambda m: along_row(m).start())
    small[...] = total[...]

    def collect(m):
        along_row(m).wait_recv()
        small[...] += row_in[m]

    loop(1, n, collect)
    loop(1, n, lambda m: landed(m).wait_recv())
    mine.wait()
    loop(1, n, lambda m: exchange(m).wait_send())
    loop(1, n, lambda m: along_row(m).wait_send())
    loop(1, zs, lambda m: along_line(m).wait_send())
    reduce.drain()
    line.drain()


def tail(parts, x, grad_hidden, params, terms, grads):
    cu, cl, zs = sizes()
    n = cu * cl
    rows, width = x.shape
    block = (ITEMS, rows // ITEMS, width)
    piece = grads.shape[2:]
    input_grad, small, cut = pl.pallas_call(
        tail_kernel,
        in_specs=[ANY, VMEM, VMEM, VMEM, VMEM, ANY],
        out_specs=[VMEM, VMEM, ANY],
        out_shape=[
            jax.ShapeDtypeStruct(block, BF16),
            jax.ShapeDtypeStruct((8, width), F32),
            jax.ShapeDtypeStruct((n, *piece), BF16),
        ],
        scratch_shapes=[
            pltpu.VMEM((8, width), F32), pltpu.VMEM((zs, 8, width), F32), pltpu.VMEM((n, 8, width), F32),
            pltpu.VMEM((8, width), F32), pltpu.VMEM(piece, F32), DMA((zs,)), DMA((zs,)), DMA((n,)), DMA((n,)),
            DMA((n,)), DMA((n,)), DMA((1,)), DMA((1,)), pltpu.VMEM((n, *piece), BF16),
            *RowReduce.scratch(cu, rows, width), *LineReduce.scratch(zs, n, piece),
        ],
        cost_estimate=pl.CostEstimate(flops=0, bytes_accessed=200 << 20, transcendentals=0),
        compiler_params=pltpu.CompilerParams(collective_id=3, has_side_effects=True, vmem_limit_bytes=60 << 20),
    )(parts.reshape(cu, cl, *block), x.reshape(block), grad_hidden.reshape(block), params, terms, grads)
    return input_grad.reshape(rows, width), small, cut


def body(
    inputs, out_grad, doc_ids, block_pairs, qkv_weight, proj_weight, ffn_in_weight, ffn_out_weight, small_params,
    qkv_first, proj_first, ffn_in_first, ffn_out_first, small_first,
    qkv_second, proj_second, ffn_in_second, ffn_out_second, small_second,
):
    bf16 = jnp.bfloat16
    tok_rows = inputs.shape[1]
    half_rows = tok_rows // 2
    cu, cl, zs = lax.axis_size("cu"), lax.axis_size("cl"), lax.axis_size("fsdp")
    ctx_count = cu * cl
    group = cl * zs
    seq_len = tok_rows * ctx_count
    my_index = lax.axis_index(ROW)
    heads = HEADS // ctx_count
    width = heads * HEAD_DIM
    slab = qkv_weight.shape[0]
    units = ffn_out_weight.shape[0]
    hidden = units * cu
    offsets = jnp.arange(half_rows, dtype=jnp.int32)
    all_pos = (block_pairs[:, :, None] * half_rows + offsets[None, None, :]).reshape(seq_len)
    chosen = block_pairs.reshape(-1, 1) == jnp.arange(2 * ctx_count, dtype=jnp.int32)[None, :]
    key_docs = jnp.sum(jnp.where(chosen[:, :, None], doc_ids.reshape(1, 2 * ctx_count, half_rows), 0), axis=1)
    key_docs = key_docs.reshape(seq_len)
    marks = (all_pos[:, None], key_docs[:, None], all_pos[None, :], key_docs[None, :])
    table = rotary_tables(all_pos)

    qkv_cut = qkv_weight.astype(bf16).reshape(slab, 3, ctx_count, width).transpose(2, 0, 1, 3)
    small_pad = jnp.pad(small_params, ((0, 1), (0, -slab % 128)))
    row_in, params, qkv_low, in_cast = gather_head(
        inputs[0], small_pad, qkv_cut.reshape(ctx_count, slab, 3 * width), ffn_in_weight
    )
    row_in = row_in.reshape(seq_len, D)
    params = params[:, :, :7, :slab].transpose(2, 0, 1, 3).reshape(7, D)
    qkv_low = qkv_low.reshape(D, 3 * width)
    proj_low = lax.all_gather(proj_weight.astype(bf16), "fsdp", axis=0, tiled=True)
    out_low = lax.all_gather(ffn_out_weight.astype(bf16), "cu", axis=0, tiled=True)
    row_in, in_cast, proj_low, out_low = lax.optimization_barrier((row_in, in_cast, proj_low, out_low))
    in_cut = lax.all_to_all(in_cast.reshape(group * slab, 2 * hidden), FFN_GROUP, split_axis=0, concat_axis=0, tiled=True)

    bias = lax.dynamic_slice_in_dim(params[4:7], my_index * width, width, 1).reshape(1, 3 * width)
    attn_in, qkv = project(row_in, params[0:2], qkv_low, bias, table)
    mixed, mixed_low, totals, branch = attend(qkv, proj_low, marks, heads)
    branch, in_cut = lax.optimization_barrier((branch, in_cut))
    in_low = lax.all_gather(in_cut, "cu", axis=0, tiled=True)
    hidden_state, mlp_in, grad_all = mid_forward(branch, inputs[0], out_grad[0], params[2:4])

    gate_up = jnp.dot(mlp_in, in_low, preferred_element_type=jnp.float32)
    gate_part, up_part = gate_up[:, :hidden], gate_up[:, hidden:]
    sigmoid_gate = jax.nn.sigmoid(gate_part)
    silu_gate = gate_part * sigmoid_gate
    inner_low = (silu_gate * up_part).astype(bf16)
    grad_inner = back_dot(grad_all, out_low)
    grad_up = grad_inner * silu_gate
    grad_gate = grad_inner * up_part * (sigmoid_gate * (1.0 + gate_part * (1.0 - sigmoid_gate)))
    grad_gate_up = jnp.concatenate([grad_gate, grad_up], axis=1).astype(bf16)
    grad_mid_part = back_dot(grad_gate_up, in_low).astype(bf16)
    grad_ffn_in = cross_dot(mlp_in, grad_gate_up).astype(bf16)
    grad_mid_part, grad_ffn_in = lax.optimization_barrier((grad_mid_part, grad_ffn_in))
    in_grad_cut = lax.psum_scatter(grad_ffn_in, "cu", scatter_dimension=0, tiled=True)

    grad_hidden, grad_branch, mid_sums, layer_out, grad_ffn_out = mid_backward(
        grad_mid_part, hidden_state, out_grad[0], params[2:4], inner_low, out_low, grad_all
    )
    layer_out = layer_out[None]
    in_grad_cut, grad_branch = lax.optimization_barrier((in_grad_cut, grad_branch))
    in_grad = lax.all_to_all(in_grad_cut, FFN_GROUP, split_axis=0, concat_axis=0, tiled=True)
    grad_proj = cross_dot(mixed_low, grad_branch).astype(bf16)
    proj_grad = lax.psum_scatter(grad_proj, "fsdp", scatter_dimension=0, tiled=True)
    grad_joined, bias_own = attend_back(qkv, grad_branch, proj_low, mixed, totals, marks, table, heads)
    grad_norm_part = back_dot(grad_joined, qkv_low).astype(bf16)
    grad_norm_part, in_grad, proj_grad, grad_ffn_out = lax.optimization_barrier(
        (grad_norm_part, in_grad, proj_grad, grad_ffn_out)
    )
    ffn_out_grad = lax.psum_scatter(grad_ffn_out, "cu", scatter_dimension=0, tiled=True)
    grad_qkv = (
        cross_dot(attn_in, grad_joined).astype(bf16).reshape(ctx_count, zs, slab, 3 * width).transpose(1, 0, 2, 3)
    )
    bias_own = bias_own.reshape(3, width)
    grad_bias = lax.dynamic_update_slice(jnp.zeros((3, D), jnp.float32), bias_own, (0, my_index * width))
    zero_rows = jnp.zeros((2, D), jnp.float32)
    terms = jnp.concatenate([zero_rows, mid_sums, grad_bias, zero_rows[:1]], axis=0)
    input_grad, small_sum, qkv_grad_cut = tail(
        grad_norm_part, inputs[0], grad_hidden, params[0:2], terms, grad_qkv
    )
    input_grad = input_grad[None]
    my_slab = (my_index * zs + lax.axis_index("fsdp")) * slab
    small_grad = lax.dynamic_slice_in_dim(small_sum, my_slab, slab, 1)[:7]

    proj_fan = max(8 * D // seq_len, 1)
    f32 = jnp.float32
    qkv_new = adam_qkv(qkv_weight, qkv_first, qkv_second, qkv_grad_cut, 2.0 / math.sqrt(D))
    proj_new = adam_update(
        proj_weight, proj_first, proj_second, proj_grad.astype(f32), 2.0 / math.sqrt(proj_fan), matrix_decay
    )
    in_new = adam_ffn(
        ffn_in_weight, ffn_in_first, ffn_in_second, in_grad.reshape(group, slab, 2 * hidden), 2.0 / math.sqrt(D)
    )
    out_new = adam_update(
        ffn_out_weight, ffn_out_first, ffn_out_second, ffn_out_grad.astype(f32), 2.0 / math.sqrt(FF), matrix_decay
    )
    small_new = adam_update(small_params, small_first, small_second, small_grad, small_rate, 0.0)
    news = (qkv_new, proj_new, in_new, out_new, small_new)
    return (layer_out, input_grad, *(n[0] for n in news), *(n[1] for n in news), *(n[2] for n in news), small_grad)


def solution(mesh):
    ctx_count, fsdp_count = mesh.devices.shape
    fine = Mesh(mesh.devices.reshape(ctx_count // 2, 2, fsdp_count), ("cu", "cl", "fsdp"))
    tokens = P("fsdp", ROW, None)
    matrix = P(EVERY, None)
    small = P(None, EVERY)
    five = (matrix, matrix, matrix, matrix, small)
    in_specs = (tokens, tokens, P("fsdp", None), P(), *five, *five, *five)
    out_specs = (tokens, tokens, *five, *five, *five, small)
    return jax.shard_map(body, mesh=fine, in_specs=in_specs, out_specs=out_specs, check_vma=False)
```

```python
import functools
import math

import jax
import jax.numpy as jnp
from jax import lax
from jax.experimental import pallas as pl
from jax.experimental.pallas import tpu as pltpu
from jax.sharding import Mesh, PartitionSpec as P

D = 2048
HEADS = 32
HEAD_DIM = 64
FF = 5632
ROT = 16
STEP = 10


norm_eps = 1e-05
beta_first = 0.9
beta_second = 0.95
adam_eps = 1e-08
matrix_decay = 0.1
small_rate = 0.5


def norm_rows(values, gain_row, shift_row):
    center_mean = jnp.mean(values, axis=-1, keepdims=True)
    centered = values - center_mean
    inv_std = lax.rsqrt(jnp.mean(centered * centered, axis=-1, keepdims=True) + norm_eps)
    normed = centered * inv_std
    return (normed * gain_row + shift_row, normed, inv_std)


def norm_back(grad_rows, normed, inv_std, gain_row):
    scaled = grad_rows * gain_row
    return inv_std * (
        scaled
        - jnp.mean(scaled, axis=-1, keepdims=True)
        - normed * jnp.mean(scaled * normed, axis=-1, keepdims=True)
    )


def cross_dot(left_mat, right_mat):
    return lax.dot_general(
        left_mat, right_mat, (((0,), (0,)), ((), ())), preferred_element_type=jnp.float32
    )


def back_dot(left_mat, weight):
    return lax.dot_general(
        left_mat, weight, (((1,), (1,)), ((), ())), preferred_element_type=jnp.float32
    )


def adam_update(weight, first_moment, second_moment, gradient, step_rate, decay_factor):
    new_first = beta_first * first_moment + (1.0 - beta_first) * gradient
    new_second = beta_second * second_moment + (1.0 - beta_second) * gradient * gradient
    correct_first = 1.0 - beta_first**STEP
    correct_second = 1.0 - beta_second**STEP
    update = new_first / correct_first / (jnp.sqrt(new_second / correct_second) + adam_eps)
    return (weight - step_rate * (update + decay_factor * weight), new_first, new_second)


ROW = ("cu", "cl")
FFN_GROUP = ("cl", "fsdp")
EVERY = ("cu", "cl", "fsdp")
SCALE = HEAD_DIM**-0.5


LANES = 128


def fill_table(table, positions, start, rows):
    half_rot = ROT // 2
    here = pl.ds(pl.multiple_of(start, rows), rows)
    lane = lax.rem(lax.broadcasted_iota(jnp.int32, (1, LANES), 1), HEAD_DIM)
    inverse = jnp.zeros((1, LANES), jnp.float32)
    for i in range(half_rot):
        inverse = jnp.where(lax.rem(lane, half_rot) == i, 10000.0 ** (-2.0 * i / ROT), inverse)
    angles = positions[here, :].astype(jnp.float32) * jnp.where(lane < ROT, inverse, 0.0)
    sine = jnp.sin(angles)
    table[here, 0:LANES] = jnp.cos(angles)
    table[here, LANES : 2 * LANES] = jnp.where(lane < half_rot, -sine, 0.0)
    table[here, 2 * LANES : 3 * LANES] = jnp.where(lane < half_rot, 0.0, sine)


def turn(values, table, sign):
    keep, lower, upper = (table[:, i * LANES : (i + 1) * LANES] for i in range(3))
    half_rot = ROT // 2
    shifted = pltpu.roll(values, LANES - half_rot, 1) * lower + pltpu.roll(values, half_rot, 1) * upper
    return values * keep + sign * shifted


def dot_t(left, right):
    return lax.dot_general(left, right, (((1,), (1,)), ((), ())), preferred_element_type=jnp.float32)


def row_block(rows):
    return min(256, rows)


def project_kernel(x_ref, params_ref, w_ref, bias_ref, table_ref, normed_ref, qkv_ref):
    normed = norm_rows(x_ref[...].astype(jnp.float32), params_ref[0:1], params_ref[1:2])[0].astype(jnp.bfloat16)
    normed_ref[...] = normed
    joined = jnp.dot(normed, w_ref[...], preferred_element_type=jnp.float32) + bias_ref[...]
    turned = 2 * (joined.shape[1] // 3)
    for start in range(0, turned, LANES):
        cols = slice(start, start + LANES)
        qkv_ref[:, cols] = turn(joined[:, cols], table_ref[...], 1.0).astype(jnp.bfloat16)
    qkv_ref[:, turned:] = joined[:, turned:].astype(jnp.bfloat16)


def project(x, params, weight, bias, table):
    rows, width = x.shape
    block = row_block(rows)
    cols = weight.shape[1]

    def by_row(n):
        return pl.BlockSpec((block, n), lambda i: (i, 0))

    def whole(array):
        return pl.BlockSpec(array.shape, lambda i: (0, 0))

    return pl.pallas_call(
        project_kernel,
        grid=(rows // block,),
        in_specs=[by_row(width), whole(params), whole(weight), whole(bias), by_row(table.shape[1])],
        out_specs=[by_row(width), by_row(cols)],
        out_shape=[jax.ShapeDtypeStruct((rows, width), jnp.bfloat16), jax.ShapeDtypeStruct((rows, cols), jnp.bfloat16)],
        cost_estimate=pl.CostEstimate(
            flops=2 * rows * width * cols, bytes_accessed=4 * rows * width, transcendentals=0
        ),
        compiler_params=pltpu.CompilerParams(vmem_limit_bytes=48 << 20),
    )(x, params, weight, bias, table)


def attend_kernel(
    heads, q_ref, qkv_ref, proj_ref, pq_ref, dq_ref, pk_ref, dk_ref, mixed_ref, low_ref, tot_ref, branch_ref
):
    width = heads * HEAD_DIM
    allowed = (pk_ref[...] <= pq_ref[...]) & (dk_ref[...] == dq_ref[...])
    for head in range(heads):
        cols, key, value = (slice(p * width + head * HEAD_DIM, p * width + (head + 1) * HEAD_DIM) for p in range(3))
        scores = dot_t(q_ref[:, cols], qkv_ref[:, key]) * SCALE
        weights = jnp.where(allowed, jnp.exp(scores), 0.0)
        total = jnp.sum(weights, axis=1, keepdims=True)
        weighted = jnp.dot(weights.astype(jnp.bfloat16), qkv_ref[:, value], preferred_element_type=jnp.float32)
        mixed = weighted / total
        mixed_ref[:, cols] = mixed
        low_ref[:, cols] = mixed.astype(jnp.bfloat16)
        tot_ref[:, head : head + 1] = total
    branch_ref[...] = jnp.dot(low_ref[...], proj_ref[...], preferred_element_type=jnp.float32).astype(jnp.bfloat16)


def attend(qkv, proj, marks, heads):
    pos_col, doc_col, pos_row, doc_row = marks
    rows, cols = qkv.shape
    width = cols // 3
    block = row_block(rows)

    def by_row(n):
        return pl.BlockSpec((block, n), lambda i: (i, 0))

    def whole(array):
        return pl.BlockSpec(array.shape, lambda i: (0, 0))

    return pl.pallas_call(
        functools.partial(attend_kernel, heads),
        grid=(rows // block,),
        in_specs=[by_row(cols), whole(qkv), whole(proj), by_row(1), by_row(1), whole(pos_row), whole(doc_row)],
        out_specs=[by_row(width), by_row(width), by_row(heads), by_row(D)],
        out_shape=[
            jax.ShapeDtypeStruct((rows, width), jnp.float32),
            jax.ShapeDtypeStruct((rows, width), jnp.bfloat16),
            jax.ShapeDtypeStruct((rows, heads), jnp.float32),
            jax.ShapeDtypeStruct((rows, D), jnp.bfloat16),
        ],
        cost_estimate=pl.CostEstimate(
            flops=4 * rows * rows * width, bytes_accessed=8 * rows * D, transcendentals=rows * rows * heads
        ),
        compiler_params=pltpu.CompilerParams(vmem_limit_bytes=48 << 20),
    )(qkv, qkv, proj, pos_col, doc_col, pos_row, doc_row)


def attend_back_kernel(
    heads, qkv_ref, branch_ref, proj_ref, mixed_ref, tot_ref, pq_ref, dq_ref, pk_ref, dk_ref, table_ref, cut,
    joined_ref, bias_ref, pieces, gq_ref, gk_ref, gv_ref, own, send, recv,
):
    width = heads * HEAD_DIM
    rows = qkv_ref.shape[0]
    block = row_block(rows)
    group = cut.shape[0]

    def exchange(m):
        device, after, _, me = in_group(m)
        return Transfer(cut.at[after], pieces.at[me], send.at[m], recv.at[m], device)

    def landed(m):
        device, _, before, _ = in_group(m)
        return Transfer(cut.at[before], pieces.at[before], send.at[m], recv.at[m], device)

    me = in_group(0)[3]
    kept = pltpu.make_async_copy(cut.at[me], pieces.at[me], own.at[0])
    kept.start()
    greet_group()
    loop(1, group, lambda m: exchange(m).start())
    gk_ref[...] = jnp.zeros_like(gk_ref)
    gv_ref[...] = jnp.zeros_like(gv_ref)

    def one(step):
        here = pl.ds(pl.multiple_of(step * block, block), block)
        grad_all = dot_t(branch_ref[here], proj_ref[...])
        allowed = (pk_ref[...] <= pq_ref[here]) & (dk_ref[...] == dq_ref[here])
        for head in range(heads):
            cols, key, value = (
                slice(p * width + head * HEAD_DIM, p * width + (head + 1) * HEAD_DIM) for p in range(3)
            )
            q, k, v = qkv_ref[here, cols], qkv_ref[:, key], qkv_ref[:, value]
            inverse = 1.0 / tot_ref[here, head : head + 1]
            grad_mixed = grad_all[:, cols]
            grad_weighted = (grad_mixed * inverse).astype(jnp.bfloat16)
            grad_total = -jnp.sum(grad_mixed * mixed_ref[here, cols], axis=1, keepdims=True) * inverse
            weights = jnp.where(allowed, jnp.exp(dot_t(q, k) * SCALE), 0.0)
            grad_scores = (weights * (dot_t(grad_weighted, v) + grad_total)).astype(jnp.bfloat16)
            gq_ref[here, cols] = jnp.dot(grad_scores, k, preferred_element_type=jnp.float32) * SCALE
            gk_ref[:, cols] += cross_dot(grad_scores, q) * SCALE
            gv_ref[:, cols] += cross_dot(weights.astype(jnp.bfloat16), grad_weighted)

    loop(0, rows // block, one)
    for part, ref in enumerate((gq_ref, gk_ref, gv_ref)):
        for start in range(0, width, LANES):
            cols = slice(start, min(start + LANES, width))
            grad = ref[:, cols]
            if part < 2:
                lanes = cols.stop - cols.start
                if lanes < LANES:
                    grad = jnp.concatenate([grad, jnp.zeros((rows, LANES - lanes), jnp.float32)], axis=1)
                grad = turn(grad, table_ref[...], -1.0)[:, :lanes]
            grad = grad.astype(jnp.bfloat16)
            into = slice(part * width + cols.start, part * width + cols.stop)
            joined_ref[:, into] = grad
            bias_ref[:, into] = jnp.sum(grad.astype(jnp.float32), axis=0, keepdims=True)
    loop(1, group, lambda m: landed(m).wait_recv())
    loop(1, group, lambda m: exchange(m).wait_send())
    kept.wait()


def attend_back(qkv, grad_branch, proj, mixed, totals, marks, table, cut, heads):
    rows, cols = qkv.shape
    width = cols // 3
    return pl.pallas_call(
        functools.partial(attend_back_kernel, heads),
        in_specs=[*[VMEM] * 10, ANY],
        out_specs=[VMEM, VMEM, ANY],
        out_shape=[
            jax.ShapeDtypeStruct((rows, cols), jnp.bfloat16), jax.ShapeDtypeStruct((1, cols), jnp.float32),
            jax.ShapeDtypeStruct(cut.shape, BF16),
        ],
        scratch_shapes=[
            *[pltpu.VMEM((rows, width), jnp.float32)] * 3, DMA((1,)), DMA((cut.shape[0],)), DMA((cut.shape[0],)),
        ],
        cost_estimate=pl.CostEstimate(
            flops=10 * rows * rows * width, bytes_accessed=8 * rows * D, transcendentals=rows * rows * heads
        ),
        compiler_params=pltpu.CompilerParams(collective_id=4, has_side_effects=True, vmem_limit_bytes=60 << 20),
    )(qkv, grad_branch, proj, mixed, totals, *marks, table, cut)


def adam_ffn_kernel(rate, w, m, v, g, w_new, m_new, v_new):
    group, _, cols = g.shape
    parts = w.shape[1] // cols
    units = cols // parts
    for part in range(parts):
        grad = jnp.concatenate(
            [g[owner, :, part * units : (part + 1) * units].astype(jnp.float32) for owner in range(group)], axis=1
        )
        here = slice(part * cols, (part + 1) * cols)
        w_new[:, here], m_new[:, here], v_new[:, here] = adam_update(
            w[:, here], m[:, here], v[:, here], grad, rate, matrix_decay
        )


def adam_ffn(weight, first, second, cut, rate):
    rows = 16
    by_row = pl.BlockSpec((rows, weight.shape[1]), lambda i: (i, 0))
    return pl.pallas_call(
        functools.partial(adam_ffn_kernel, rate),
        grid=(weight.shape[0] // rows,),
        in_specs=[by_row, by_row, by_row, pl.BlockSpec((cut.shape[0], rows, cut.shape[2]), lambda i: (0, i, 0))],
        out_specs=[by_row] * 3,
        out_shape=[jax.ShapeDtypeStruct(weight.shape, jnp.float32)] * 3,
        compiler_params=pltpu.CompilerParams(vmem_limit_bytes=48 << 20),
    )(weight, first, second, cut)


def adam_qkv_kernel(rate, w, m, v, g, w_new, m_new, v_new):
    n, _, cols = g.shape
    width = cols // 3
    for part in range(3):
        grad = jnp.concatenate(
            [g[owner, :, part * width : (part + 1) * width].astype(jnp.float32) for owner in range(n)], axis=1
        )
        here = slice(part * n * width, (part + 1) * n * width)
        w_new[:, here], m_new[:, here], v_new[:, here] = adam_update(
            w[:, here], m[:, here], v[:, here], grad, rate, matrix_decay
        )


def adam_qkv(weight, first, second, cut, rate):
    rows = 16
    by_row = pl.BlockSpec((rows, weight.shape[1]), lambda i: (i, 0))
    return pl.pallas_call(
        functools.partial(adam_qkv_kernel, rate),
        grid=(weight.shape[0] // rows,),
        in_specs=[by_row, by_row, by_row, pl.BlockSpec((cut.shape[0], rows, cut.shape[2]), lambda i: (0, i, 0))],
        out_specs=[by_row] * 3,
        out_shape=[jax.ShapeDtypeStruct(weight.shape, jnp.float32)] * 3,
        compiler_params=pltpu.CompilerParams(vmem_limit_bytes=48 << 20),
    )(weight, first, second, cut)


MESH = pl.DeviceIdType.MESH
ANY = pl.BlockSpec(memory_space=pl.ANY)
VMEM = pl.BlockSpec(memory_space=pltpu.VMEM)
DMA = pltpu.SemaphoreType.DMA
BF16, F32 = jnp.bfloat16, jnp.float32


class Transfer:
    def __init__(self, src, dst, send, recv, device):
        self.parts = (src, dst, send, recv, device)

    def copy(self):
        src, dst, send, recv, device = self.parts
        return pltpu.make_async_remote_copy(
            src_ref=src, dst_ref=dst, send_sem=send, recv_sem=recv, device_id=device, device_id_type=MESH
        )

    def start(self):
        self.copy().start()

    def wait_recv(self):
        self.copy().wait_recv()

    def wait_send(self):
        self.copy().wait_send()

    def wait(self):
        self.copy().wait()


rcopy = Transfer


def flip(index, mask):
    bit = 1
    while bit <= mask:
        if mask & bit:
            index = index + bit * (1 - 2 * lax.rem(index // bit, 2))
        bit *= 2
    return index


def place():
    return lax.axis_index("cu"), lax.axis_index("cl"), lax.axis_index("fsdp")


def sizes():
    return lax.axis_size("cu"), lax.axis_size("cl"), lax.axis_size("fsdp")


def in_group(m):
    u, c, z = place()
    _, cl, zs = sizes()
    group, me = cl * zs, c * zs + z
    after, before = lax.rem(me + m, group), lax.rem(me - m + group, group)
    return (u, after // zs, lax.rem(after, zs)), after, before, me


def greet_group():
    _, cl, zs = sizes()
    barrier = pltpu.get_barrier_semaphore()

    def signal(m, carry):
        pl.semaphore_signal(barrier, inc=1, device_id=in_group(m)[0], device_id_type=MESH)
        return carry

    lax.fori_loop(1, cl * zs, signal, 0)
    pl.semaphore_wait(barrier, cl * zs - 1)


def greet(row, line, twins=False):
    u, c, z = place()
    cu, cl, zs = sizes()
    n, me = cu * cl, u * cl + c
    barrier = pltpu.get_barrier_semaphore()

    def signal_row(m, carry):
        other = lax.rem(me + m, n)
        pl.semaphore_signal(barrier, inc=1, device_id=(other // cl, lax.rem(other, cl), z), device_id_type=MESH)
        return carry

    def signal_line(m, carry):
        pl.semaphore_signal(barrier, inc=1, device_id=(u, c, lax.rem(z + m, zs)), device_id_type=MESH)
        return carry

    def signal_twins(m, carry):
        pl.semaphore_signal(barrier, inc=1, device_id=(u, 1 - c, lax.rem(z + m, zs)), device_id_type=MESH)
        return carry

    if row:
        lax.fori_loop(1, n, signal_row, 0)
    if line:
        lax.fori_loop(1, zs, signal_line, 0)
    if twins:
        lax.fori_loop(1, zs, signal_twins, 0)
    pl.semaphore_wait(barrier, row * (n - 1) + (line + twins) * (zs - 1))


def head_kernel(
    x, small_in, qkv_in, ffn_in, pairs, docs, row, par, wq, in_cut, pos_col, doc_col, pos_row, doc_row, table,
    qkv, small, own, x_send, x_recv, s_send, s_recv, p_send, p_recv, q_send, q_recv,
    a_send, a_recv, up_send, up_recv, dn_send, dn_recv,
):
    u, c, z = place()
    cu, cl, zs = sizes()
    n, me = cu * cl, u * cl + c
    sibling = (u, 1 - c, z)
    slab, width = qkv_in.shape[0], qkv_in.shape[1] // (3 * n)
    small[...] = jnp.zeros_like(small)
    small[: small_in.shape[0], : small_in.shape[1]] = small_in[...]
    for owner in range(n):
        for part in range(3):
            start = (part * n + owner) * width
            qkv[owner, :, part * width : (part + 1) * width] = qkv_in[:, start : start + width].astype(BF16)
    mine = [
        pltpu.make_async_copy(qkv.at[me], wq.at[me, z], own.at[0]),
        pltpu.make_async_copy(x, row.at[u, c], own.at[1]),
        pltpu.make_async_copy(small, par.at[me, z], own.at[2]),
    ]
    for copy in mine:
        copy.start()
    greet(True, True)

    def exchange(m):
        other, source = lax.rem(me + m, n), lax.rem(me - m + n, n)
        out = rcopy(
            qkv.at[other], wq.at[me, z], a_send.at[m], a_recv.at[m], (other // cl, lax.rem(other, cl), z)
        )
        into = rcopy(qkv.at[other], wq.at[source, z], a_send.at[m], a_recv.at[m], sibling)
        return out, into

    def params_line(m):
        other, source = lax.rem(z + m, zs), lax.rem(z - m + zs, zs)
        return (
            rcopy(small, par.at[me, z], p_send.at[m], p_recv.at[m], (u, c, other)),
            rcopy(small, par.at[me, source], p_send.at[m], p_recv.at[m], sibling),
        )

    def params_row(m):
        other, source = lax.rem(me + m, n), lax.rem(me - m + n, n)
        return (
            rcopy(par.at[me], par.at[me], q_send.at[m], q_recv.at[m], (other // cl, lax.rem(other, cl), z)),
            rcopy(par.at[me], par.at[source], q_send.at[m], q_recv.at[m], sibling),
        )

    def x_far(i):
        out = rcopy(x, row.at[u, c], x_send.at[i], x_recv.at[i], (flip(u, i), c, z))
        into = rcopy(x, row.at[flip(u, i), c], x_send.at[i], x_recv.at[i], sibling)
        return out, into

    def x_near(i):
        part = row.at[flip(u, i), c]
        out = rcopy(part, part, s_send.at[i], s_recv.at[i], sibling)
        into = rcopy(part, row.at[flip(u, i), 1 - c], s_send.at[i], s_recv.at[i], sibling)
        return out, into

    def loop(low, high, step):
        def run(m, carry):
            step(m)
            return carry

        lax.fori_loop(low, high, run, 0)

    loop(1, n, lambda m: exchange(m)[0].start())
    loop(1, zs, lambda m: params_line(m)[0].start())
    for copy in mine:
        copy.wait()
    for i in range(1, cu):
        x_far(i)[0].start()
    x_near(0)[0].start()

    def chain(step, m):
        piece = lax.rem(me - m + n, n)
        above, below = wq.at[piece, lax.rem(z + step, zs)], wq.at[piece, lax.rem(z - step + zs, zs)]
        return (
            rcopy(below, below, up_send.at[step, m], up_recv.at[step, m], (u, c, lax.rem(z + 1, zs))),
            rcopy(above, above, dn_send.at[step, m], dn_recv.at[step, m], (u, c, lax.rem(z - 1 + zs, zs))),
        )

    def arrival(step, m):
        piece = lax.rem(me - m + n, n)
        above, below = wq.at[piece, lax.rem(z + step + 1, zs)], wq.at[piece, lax.rem(z - step - 1 + zs, zs)]
        return (
            rcopy(below, below, up_send.at[step, m], up_recv.at[step, m], sibling),
            rcopy(above, above, dn_send.at[step, m], dn_recv.at[step, m], sibling),
        )

    def first(m):
        @pl.when(m > 0)
        def _():
            exchange(m)[1].wait_recv()

        @pl.when(z + 1 < zs)
        def _():
            chain(0, m)[0].start()

        @pl.when(z > 0)
        def _():
            chain(0, m)[1].start()

    loop(0, n, first)
    group, units = cl * zs, ffn_in.shape[1] // (2 * n * zs)
    for part in range(2 * cu):
        for owner in range(group):
            start = (part * group + owner) * units
            in_cut[owner, :, part * units : (part + 1) * units] = ffn_in[:, start : start + units].astype(BF16)
    half = docs.shape[1]
    lane, line_of = (lax.broadcasted_iota(jnp.int32, (half, half), d) for d in (1, 0))

    def column(values):
        return jnp.sum(jnp.where(lane == line_of, values, 0), axis=1, keepdims=True)

    for slot in range(n):
        for part in range(2):
            here = slice((2 * slot + part) * half, (2 * slot + part + 1) * half)
            number = pairs[slot, part]
            positions = number * half + lax.broadcasted_iota(jnp.int32, (1, half), 1)
            documents = docs[pl.ds(number, 1), :]
            pos_row[:, here], doc_row[:, here] = positions, documents
            pos_col[here, :], doc_col[here, :] = column(positions), column(documents)
    loop(0, n, lambda i: fill_table(table, pos_col, i * 2 * half, 2 * half))
    for m in range(1, zs):
        params_line(m)[1].wait_recv()
    loop(1, n, lambda m: params_row(m)[0].start())
    for step in range(1, zs):

        def later(m, step=step):
            @pl.when(z >= step)
            def _():
                arrival(step - 1, m)[0].wait_recv()

            @pl.when((z >= step) & (z + 1 < zs))
            def _():
                chain(step, m)[0].start()

            @pl.when(z + step < zs)
            def _():
                arrival(step - 1, m)[1].wait_recv()

            @pl.when((z + step < zs) & (z > 0))
            def _():
                chain(step, m)[1].start()

        loop(0, n, later)
        if step == 1:
            for i in range(1, cu):
                x_far(i)[1].wait_recv()
                x_near(i)[0].start()
    loop(1, n, lambda m: params_row(m)[1].wait_recv())
    for i in range(cu):
        x_near(i)[1].wait_recv()
    loop(1, n, lambda m: exchange(m)[0].wait_send())
    loop(1, zs, lambda m: params_line(m)[0].wait_send())
    loop(1, n, lambda m: params_row(m)[0].wait_send())
    for i in range(cu):
        x_near(i)[0].wait_send()
        if i:
            x_far(i)[0].wait_send()
    for step in range(zs - 1):

        def sent(m, step=step):
            @pl.when((z >= step) & (z + 1 < zs))
            def _():
                chain(step, m)[0].wait_send()

            @pl.when((z + step < zs) & (z > 0))
            def _():
                chain(step, m)[1].wait_send()

        loop(0, n, sent)


def gather_head(x, small, qkv_weight, ffn_in, pairs, docs):
    cu, cl, zs = sizes()
    n = cu * cl
    slab, cols = qkv_weight.shape
    cut = (n, slab, cols // n)
    pad = (8, LANES)
    rows = docs.shape[0] * docs.shape[1]
    column, line = jax.ShapeDtypeStruct((rows, 1), jnp.int32), jax.ShapeDtypeStruct((1, rows), jnp.int32)
    return pl.pallas_call(
        head_kernel,
        in_specs=[ANY, VMEM, VMEM, VMEM, pl.BlockSpec(memory_space=pltpu.SMEM), VMEM],
        out_specs=[ANY, ANY, ANY, *[VMEM] * 6],
        out_shape=[
            jax.ShapeDtypeStruct((cu, cl, *x.shape), x.dtype),
            jax.ShapeDtypeStruct((n, zs, *pad), F32),
            jax.ShapeDtypeStruct((n, zs, *cut[1:]), BF16),
            jax.ShapeDtypeStruct((cl * zs, ffn_in.shape[0], ffn_in.shape[1] // (cl * zs)), BF16),
            column, column, line, line, jax.ShapeDtypeStruct((rows, 3 * LANES), F32),
        ],
        scratch_shapes=[
            pltpu.VMEM(cut, BF16), pltpu.VMEM(pad, F32),
            DMA((3,)), DMA((cu,)), DMA((cu,)), DMA((cu,)), DMA((cu,)), DMA((zs,)), DMA((zs,)), DMA((n,)), DMA((n,)),
            DMA((n,)), DMA((n,)), DMA((zs, n)), DMA((zs, n)), DMA((zs, n)), DMA((zs, n)),
        ],
        cost_estimate=pl.CostEstimate(flops=0, bytes_accessed=200 << 20, transcendentals=0),
        compiler_params=pltpu.CompilerParams(collective_id=0, has_side_effects=True, vmem_limit_bytes=48 << 20),
    )(x, small, qkv_weight, ffn_in, pairs, docs)


ITEMS = 4


def loop(low, high, step):
    def run(m, carry):
        step(m)
        return carry

    lax.fori_loop(low, high, run, 0)


def bits_of(count):
    return [1 << b for b in range(count.bit_length() - 1)]


def combos(bits):
    masks = [0]
    for b in bits:
        masks = masks + [m | b for m in masks]
    return masks


def order_of(item, count):
    return bits_of(count) if item < ITEMS // 2 else bits_of(count)[::-1]


def add_low(left, right):
    return (left.astype(F32) + right.astype(F32)).astype(BF16)


class RowReduce:
    def __init__(self, parts, held, beside, came, load, sib_s, sib_r, out_s, out_r):
        self.parts, self.held, self.beside, self.came = parts, held, beside, came
        self.load, self.sib_s, self.sib_r, self.out_s, self.out_r = load, sib_s, sib_r, out_s, out_r
        self.u, self.c, self.z = place()
        self.count = sizes()[0]
        self.phases = self.count.bit_length() - 1

    def sib(self, mask):
        return Transfer(
            self.parts.at[flip(self.u, mask), 1 - self.c], self.beside.at[mask], self.sib_s.at[mask],
            self.sib_r.at[mask], (self.u, 1 - self.c, self.z),
        )

    def loading(self, mask):
        return pltpu.make_async_copy(
            self.parts.at[flip(self.u, mask), self.c], self.held.at[mask], self.load.at[mask]
        )

    def start(self):
        for mask in reversed(range(self.count)):
            self.sib(mask).start()
            self.loading(mask).start()

    def merge(self):
        for mask in reversed(range(self.count)):
            self.loading(mask).wait()
            self.sib(mask).wait_recv()
            self.held[mask] = add_low(self.held[mask], self.beside[mask])

    def steps(self, item, phase):
        order = order_of(item, self.count)
        slot = self.count - (self.count >> phase)
        for k, rest in enumerate(combos(order[phase + 1 :])):
            yield slot + k, rest, Transfer(
                self.held.at[order[phase] | rest, item], self.came.at[slot + k, item], self.out_s.at[slot + k, item],
                self.out_r.at[slot + k, item], (flip(self.u, order[phase]), self.c, self.z),
            )

    def send(self, item, phase):
        for _, _, transfer in self.steps(item, phase):
            transfer.start()

    def add(self, item, phase):
        for slot, rest, transfer in self.steps(item, phase):
            transfer.wait_recv()
            self.held[rest, item] = add_low(self.held[rest, item], self.came[slot, item])

    def total(self, item):
        ((slot, _, transfer),) = self.steps(item, self.phases - 1)
        transfer.wait_recv()
        return self.held[0, item].astype(F32) + self.came[slot, item].astype(F32)

    def drain(self):
        for mask in range(self.count):
            self.sib(mask).wait_send()
        for item in range(ITEMS):
            for phase in range(self.phases):
                for _, _, transfer in self.steps(item, phase):
                    transfer.wait_send()

    @staticmethod
    def scratch(count, rows, width):
        block = (count, ITEMS, rows // ITEMS, width)
        return [
            pltpu.VMEM(block, BF16), pltpu.VMEM(block, BF16), pltpu.VMEM(block, BF16), DMA((count,)), DMA((count,)),
            DMA((count,)), DMA((count, ITEMS)), DMA((count, ITEMS)),
        ]


class RowGather:
    def __init__(self, own, full, keep, out_s, out_r, sib_s, sib_r):
        self.own, self.full, self.keep = own, full, keep
        self.out_s, self.out_r, self.sib_s, self.sib_r = out_s, out_r, sib_s, sib_r
        self.u, self.c, self.z = place()
        self.count = sizes()[0]
        self.phases = self.count.bit_length() - 1

    def kept(self, item):
        return pltpu.make_async_copy(self.own.at[item], self.full.at[self.u, self.c, item], self.keep.at[item])

    def source(self, mask, item):
        return self.own.at[item] if mask == 0 else self.full.at[flip(self.u, mask), self.c, item]

    def sib(self, mask, item):
        return Transfer(
            self.source(mask, item), self.full.at[flip(self.u, mask), self.c, item], self.sib_s.at[mask, item],
            self.sib_r.at[mask, item], (self.u, 1 - self.c, self.z),
        )

    def steps(self, item, phase):
        order = order_of(item, self.count)
        for k, mask in enumerate(combos(order[:phase])):
            slot = (1 << phase) - 1 + k
            yield mask | order[phase], Transfer(
                self.source(mask, item), self.full.at[flip(self.u, mask), self.c, item], self.out_s.at[slot, item],
                self.out_r.at[slot, item], (flip(self.u, order[phase]), self.c, self.z),
            )

    def start(self, item):
        self.send(item, 0)
        self.sib(0, item).start()
        self.kept(item).start()

    def send(self, item, phase):
        for _, transfer in self.steps(item, phase):
            transfer.start()

    def pass_on(self, item, phase):
        for mask, transfer in self.steps(item, phase):
            transfer.wait_recv()
            self.sib(mask, item).start()

    def drain(self):
        for item in range(ITEMS):
            self.kept(item).wait()
            for mask in range(self.count):
                self.sib(mask, item).wait()
            for phase in range(self.phases):
                for _, transfer in self.steps(item, phase):
                    transfer.wait_send()

    @staticmethod
    def scratch(count):
        return [DMA((ITEMS,)), *[DMA((count, ITEMS))] * 4]


class LineGather:
    def __init__(self, own, full, keep, up_s, up_r, dn_s, dn_r, sib_s, sib_r):
        self.own, self.full, self.keep = own, full, keep
        self.up_s, self.up_r, self.dn_s, self.dn_r, self.sib_s, self.sib_r = up_s, up_r, dn_s, dn_r, sib_s, sib_r
        self.u, self.c, self.z = place()
        self.count = sizes()[2]

    def kept(self, item):
        return pltpu.make_async_copy(self.own.at[item], self.full.at[self.c, self.z, item], self.keep.at[item])

    def up(self, item, step):
        origin = lax.rem(self.z - step + self.count, self.count)
        block = self.full.at[self.c, origin, item]
        source = self.own.at[item] if step == 0 else block
        to = lax.rem(self.z + 1, self.count)
        return Transfer(source, block, self.up_s.at[step, item], self.up_r.at[step, item], (self.u, self.c, to))

    def down(self, item, step):
        block = self.full.at[self.c, lax.rem(self.z + step, self.count), item]
        source = self.own.at[item] if step == 0 else block
        to = lax.rem(self.z - 1 + self.count, self.count)
        return Transfer(source, block, self.dn_s.at[step, item], self.dn_r.at[step, item], (self.u, self.c, to))

    def sib(self, item, origin, own=False):
        block = self.full.at[self.c, origin, item]
        return Transfer(
            self.own.at[item] if own else block, block, self.sib_s.at[origin, item], self.sib_r.at[origin, item],
            (self.u, 1 - self.c, self.z),
        )

    def start(self, item):
        @pl.when(self.z + 1 < self.count)
        def _():
            self.up(item, 0).start()

        @pl.when(self.z > 0)
        def _():
            self.down(item, 0).start()

        self.sib(item, self.z, True).start()
        self.kept(item).start()

    def forward(self, item, step):
        z, count = self.z, self.count

        @pl.when(z >= step)
        def _():
            self.up(item, step - 1).wait_recv()
            if step < count - 1:

                @pl.when(z + 1 < count)
                def _():
                    self.up(item, step).start()

            self.sib(item, z - step).start()

        @pl.when(z + step < count)
        def _():
            self.down(item, step - 1).wait_recv()
            if step < count - 1:

                @pl.when(z > 0)
                def _():
                    self.down(item, step).start()

            self.sib(item, z + step).start()

    def drain(self):
        z, count = self.z, self.count
        for item in range(ITEMS):
            self.kept(item).wait()
            for origin in range(count):
                self.sib(item, origin).wait()
            for step in range(count - 1):

                @pl.when((z >= step) & (z + 1 < count))
                def _(item=item, step=step):
                    self.up(item, step).wait_send()

                @pl.when((z + step < count) & (z > 0))
                def _(item=item, step=step):
                    self.down(item, step).wait_send()

    @staticmethod
    def scratch(count):
        return [DMA((ITEMS,)), *[DMA((count, ITEMS))] * 6]


class LineReduce:
    def __init__(self, held, from_below, from_above, pieces, up_s, up_r, dn_s, dn_r):
        self.held, self.from_below, self.from_above, self.pieces = held, from_below, from_above, pieces
        self.up_s, self.up_r, self.dn_s, self.dn_r = up_s, up_r, dn_s, dn_r
        self.u, self.c, self.z = place()
        self.count = sizes()[2]

    def up(self, to, piece):
        return Transfer(
            self.held.at[to, piece], self.from_below.at[to, piece], self.up_s.at[to, piece], self.up_r.at[to, piece],
            (self.u, self.c, lax.rem(self.z + 1, self.count)),
        )

    def down(self, to, piece):
        return Transfer(
            self.held.at[to, piece], self.from_above.at[to, piece], self.dn_s.at[to, piece], self.dn_r.at[to, piece],
            (self.u, self.c, lax.rem(self.z - 1 + self.count, self.count)),
        )

    def step(self, t):
        z, count = self.z, self.count
        far_up, far_down = count - 1 - t, t

        def upward(piece):
            @pl.when(z > 0)
            def _():
                self.up(far_up, piece).wait_recv()
                self.held[far_up, piece] = add_low(self.held[far_up, piece], self.from_below[far_up, piece])

            self.up(far_up, piece).start()

        def downward(piece):
            @pl.when(z < count - 1)
            def _():
                self.down(far_down, piece).wait_recv()
                self.held[far_down, piece] = add_low(self.held[far_down, piece], self.from_above[far_down, piece])

            self.down(far_down, piece).start()

        lag = min(3, self.pieces // 2)
        late_up = lag * ((2 * z) // count)

        def one(i):
            piece_up, piece_down = i - late_up, i - (lag - late_up)

            @pl.when((z < far_up) & (piece_up >= 0) & (piece_up < self.pieces))
            def _():
                upward(piece_up)

            @pl.when((z > far_down) & (piece_down >= 0) & (piece_down < self.pieces))
            def _():
                downward(piece_down)

        loop(0, self.pieces + lag, one)

    def total(self, piece, into):
        z, count = self.z, self.count
        into[...] = self.held[z, piece].astype(F32)

        @pl.when(z > 0)
        def _():
            self.up(z, piece).wait_recv()
            into[...] += self.from_below[z, piece].astype(F32)

        @pl.when(z < count - 1)
        def _():
            self.down(z, piece).wait_recv()
            into[...] += self.from_above[z, piece].astype(F32)

    def drain(self):
        z, count = self.z, self.count
        for t in range(count - 1):
            far_up, far_down = count - 1 - t, t

            def one(piece, far_up=far_up, far_down=far_down):
                @pl.when(z < far_up)
                def _():
                    self.up(far_up, piece).wait_send()

                @pl.when(z > far_down)
                def _():
                    self.down(far_down, piece).wait_send()

            loop(0, self.pieces, one)

    @staticmethod
    def scratch(count, pieces, block):
        shape = (count, pieces, *block)
        return [*[pltpu.VMEM(shape, BF16)] * 3, *[DMA((count, pieces))] * 4]


def mid_forward_kernel(branch, x, out_grad, params, hidden, mlp, grads, low, *scratch):
    reduce = RowReduce(branch, *scratch[:8])
    gather = LineGather(low, mlp, *scratch[8:15])
    gather_grads = LineGather(out_grad, grads, *scratch[15:])
    greet(True, True)
    reduce.start()
    for item in range(ITEMS):
        gather_grads.start(item)
    reduce.merge()
    for item in range(ITEMS):
        reduce.send(item, 0)
    for item in range(ITEMS):
        gather_grads.forward(item, 1)
    for phase in range(1, reduce.phases):
        for item in range(ITEMS):
            reduce.add(item, phase - 1)
            reduce.send(item, phase)
    for step in range(2, gather.count):
        for item in range(ITEMS):
            gather_grads.forward(item, step)
    for item in range(ITEMS):
        state = x[item].astype(F32) + reduce.total(item)
        hidden[item] = state
        low[item] = norm_rows(state, params[0:1], params[1:2])[0].astype(BF16)
        gather.start(item)
    for step in range(1, gather.count):
        for item in range(ITEMS):
            gather.forward(item, step)
    gather_grads.drain()
    gather.drain()
    reduce.drain()


def mid_forward(branch, x, out_grad, params):
    cu, cl, zs = sizes()
    rows, width = x.shape
    block = (ITEMS, rows // ITEMS, width)
    full = jax.ShapeDtypeStruct((cl, zs, *block), BF16)
    hidden, mlp, grads, _ = pl.pallas_call(
        mid_forward_kernel,
        in_specs=[ANY, VMEM, VMEM, VMEM],
        out_specs=[VMEM, ANY, ANY, VMEM],
        out_shape=[
            jax.ShapeDtypeStruct(block, F32), full, full, jax.ShapeDtypeStruct(block, BF16),
        ],
        scratch_shapes=[*RowReduce.scratch(cu, rows, width), *LineGather.scratch(zs), *LineGather.scratch(zs)],
        cost_estimate=pl.CostEstimate(flops=0, bytes_accessed=200 << 20, transcendentals=0),
        compiler_params=pltpu.CompilerParams(collective_id=1, has_side_effects=True, vmem_limit_bytes=56 << 20),
    )(branch.reshape(cu, cl, *block), x.reshape(block), out_grad.reshape(block), params)
    return hidden.reshape(rows, width), mlp.reshape(cl * zs * rows, width), grads.reshape(cl * zs * rows, width)


def mid_backward_kernel(
    parts, hidden, out_grad, params, inner, weight, grads, grad_hidden, full, sums, layer_out, weight_grad, low,
    held, below, above, up_s, up_r, dn_s, dn_r, beside, total, load, sib_s, sib_r,
    held_out, below_out, above_out, up_so, up_ro, dn_so, dn_ro, beside_out, away, sib_so, sib_ro,
    inner_v, weight_v, grads_v, fetch, *scratch,
):
    u, c, z = place()
    zs = sizes()[2]
    rows = ITEMS * held.shape[2]
    reduce = LineReduce(held, below, above, ITEMS, up_s, up_r, dn_s, dn_r)
    reduce_out = LineReduce(held_out, below_out, above_out, ITEMS, up_so, up_ro, dn_so, dn_ro)
    gather = RowGather(low, full, *scratch)
    fetches = [
        pltpu.make_async_copy(inner, inner_v, fetch.at[0]),
        pltpu.make_async_copy(weight, weight_v, fetch.at[1]),
        pltpu.make_async_copy(grads, grads_v, fetch.at[2]),
    ]

    def sib(to):
        return Transfer(parts.at[1 - c, to], beside.at[to], sib_s.at[to], sib_r.at[to], (u, 1 - c, z))

    def sib_out(to):
        return Transfer(away.at[to], beside_out.at[to], sib_so.at[to], sib_ro.at[to], (u, 1 - c, z))

    def loading(to):
        return pltpu.make_async_copy(parts.at[c, to], held.at[to], load.at[to])

    order = sorted(range(zs), key=lambda to: -abs(2 * to - zs + 1))
    for to in order:
        loading(to).start()
    for copy in fetches:
        copy.start()
    greet(True, True)
    for to in order:
        sib(to).start()
    for to in order:
        loading(to).wait()
        sib(to).wait_recv()
        held[to] = add_low(held[to], beside[to])
    reduce.step(0)
    for copy in fetches:
        copy.wait()

    tile = 512
    width = weight_v.shape[1]

    def multiply(core, into):
        def one(i):
            to, col = i // (width // tile), lax.rem(i, width // tile) * tile
            cols = pl.ds(pl.multiple_of(col, tile), tile)
            left = inner_v[pl.ds(pl.multiple_of((core * zs + to) * rows, rows), rows)]
            part = jnp.dot(left, weight_v[:, cols], preferred_element_type=F32)
            into[to, :, :, cols] = part.astype(BF16).reshape(ITEMS, rows // ITEMS, tile)

        loop(0, zs * (width // tile), one)

    multiply(1 - c, away)
    for to in order:
        sib_out(to).start()
    reduce.step(1)
    multiply(c, held_out)
    for t in range(2, zs - 1):
        reduce.step(t)
    for to in order:
        sib_out(to).wait_recv()
        held_out[to] = add_low(held_out[to], beside_out[to])
    reduce_out.step(0)
    sums[...] = jnp.zeros_like(sums)
    for item in range(ITEMS):
        reduce.total(item, total)
        _, hat, inverse = norm_rows(hidden[item], params[0:1], params[1:2])
        grad = total[...]
        sums[0:1] += jnp.sum(grad * hat, axis=0, keepdims=True)
        sums[1:2] += jnp.sum(grad, axis=0, keepdims=True)
        grad = out_grad[item].astype(F32) + norm_back(grad, hat, inverse, params[0:1])
        grad_hidden[item] = grad
        low[item] = grad.astype(BF16)
        gather.start(item)
    reduce_out.step(1)
    for phase in range(gather.phases):
        for item in range(ITEMS):
            gather.pass_on(item, phase)
            if phase + 1 < gather.phases:
                gather.send(item, phase + 1)
        if phase == 0:
            for t in range(2, zs - 1):
                reduce_out.step(t)

    def outer(i):
        cols = pl.ds(pl.multiple_of(i * tile, tile), tile)
        weight_grad[:, cols] = cross_dot(inner_v[...], grads_v[:, cols]).astype(BF16)

    loop(0, width // tile, outer)
    for item in range(ITEMS):
        reduce_out.total(item, total)
        layer_out[item] = (hidden[item] + total[...]).astype(BF16)
    gather.drain()
    reduce.drain()
    reduce_out.drain()
    for to in range(zs):
        sib(to).wait_send()
        sib_out(to).wait_send()


def mid_backward(parts, hidden, out_grad, params, inner, weight, grads):
    cu, cl, zs = sizes()
    rows, width = out_grad.shape
    block = (ITEMS, rows // ITEMS, width)
    shares = pltpu.VMEM((zs, *block), BF16)
    grad_hidden, full, sums, layer_out, weight_grad, _ = pl.pallas_call(
        mid_backward_kernel,
        in_specs=[ANY, VMEM, VMEM, VMEM, ANY, ANY, ANY],
        out_specs=[VMEM, ANY, VMEM, VMEM, VMEM, VMEM],
        out_shape=[
            jax.ShapeDtypeStruct(block, F32),
            jax.ShapeDtypeStruct((cu, cl, *block), BF16),
            jax.ShapeDtypeStruct((2, width), F32),
            jax.ShapeDtypeStruct(block, BF16),
            jax.ShapeDtypeStruct(weight.shape, BF16),
            jax.ShapeDtypeStruct(block, BF16),
        ],
        scratch_shapes=[
            *LineReduce.scratch(zs, ITEMS, block[1:]), shares, pltpu.VMEM(block[1:], F32),
            DMA((zs,)), DMA((zs,)), DMA((zs,)),
            *LineReduce.scratch(zs, ITEMS, block[1:]), shares, shares, DMA((zs,)), DMA((zs,)),
            pltpu.VMEM(inner.shape, BF16), pltpu.VMEM(weight.shape, BF16), pltpu.VMEM(grads.shape, BF16), DMA((3,)),
            *RowGather.scratch(cu),
        ],
        cost_estimate=pl.CostEstimate(flops=0, bytes_accessed=200 << 20, transcendentals=0),
        compiler_params=pltpu.CompilerParams(collective_id=2, has_side_effects=True, vmem_limit_bytes=60 << 20),
    )(parts.reshape(cl, zs, *block), hidden.reshape(block), out_grad.reshape(block), params, inner, weight, grads)
    return (
        grad_hidden.reshape(rows, width), full.reshape(cu * cl * rows, width), sums, layer_out.reshape(rows, width),
        weight_grad,
    )


def tail_kernel(parts, x, grad_hidden, params, terms, grads, proj, input_grad, small, cut, proj_grad, pile, line_in, row_in, total,
                row_total, line_s, line_r, row_s, row_r, a_send, a_recv, own, held_load, low, *scratch):
    u, c, z = place()
    cu, cl, zs = sizes()
    n, me = cu * cl, u * cl + c
    reduce = RowReduce(parts, *scratch[:8])
    held, held_proj = scratch[8], scratch[15]
    line = LineReduce(*scratch[8:11], n, *scratch[11:15])
    line_proj = LineReduce(*scratch[15:18], 1, *scratch[18:])
    load = pltpu.make_async_copy(grads, held, held_load.at[0])
    load_proj = pltpu.make_async_copy(proj, held_proj, held_load.at[1])
    load.start()
    load_proj.start()
    greet(True, True)
    reduce.start()
    load.wait()
    load_proj.wait()
    line.step(0)
    line_proj.step(0)
    reduce.merge()
    for item in range(ITEMS):
        reduce.send(item, 0)
    for t in range(1, zs - 1):
        line.step(t)
        line_proj.step(t)
    for phase in range(1, reduce.phases):
        for item in range(ITEMS):
            reduce.add(item, phase - 1)
            reduce.send(item, phase)
    pile[...] = terms[...]
    for item in range(ITEMS):
        grad = reduce.total(item)
        _, hat, inverse = norm_rows(x[item].astype(F32), params[0:1], params[1:2])
        pile[0:1] += jnp.sum(grad * hat, axis=0, keepdims=True)
        pile[1:2] += jnp.sum(grad, axis=0, keepdims=True)
        grad = grad_hidden[item] + norm_back(grad, hat, inverse, params[0:1])
        input_grad[item] = grad.astype(BF16)

    def along_line(m):
        return Transfer(pile, line_in.at[m], line_s.at[m], line_r.at[m], (u, c, lax.rem(z + m, zs)))

    def along_row(m):
        other = lax.rem(me + m, n)
        return Transfer(
            total, row_in.at[m], row_s.at[m], row_r.at[m], (other // cl, lax.rem(other, cl), z)
        )

    def exchange(m):
        other = lax.rem(me + m, n)
        return Transfer(
            low.at[other], cut.at[me], a_send.at[m], a_recv.at[m], (other // cl, lax.rem(other, cl), z)
        )

    def landed(m):
        source = lax.rem(me - m + n, n)
        return Transfer(
            low.at[source], cut.at[source], a_send.at[m], a_recv.at[m], (u, 1 - c, z)
        )

    loop(1, zs, lambda m: along_line(m).start())

    def finish(m):
        piece = lax.rem(me + m, n)
        line.total(piece, row_total)
        low[piece] = row_total[...].astype(BF16)

        @pl.when(m > 0)
        def _():
            exchange(m).start()

    loop(0, n, finish)
    line_proj.total(0, proj_grad)
    mine = pltpu.make_async_copy(low.at[me], cut.at[me], own.at[0])
    mine.start()
    total[...] = pile[...]
    for m in range(1, zs):
        along_line(m).wait_recv()
        total[...] += line_in[m]
    loop(1, n, lambda m: along_row(m).start())
    small[...] = total[...]

    def collect(m):
        along_row(m).wait_recv()
        small[...] += row_in[m]

    loop(1, n, collect)
    loop(1, n, lambda m: landed(m).wait_recv())
    mine.wait()
    loop(1, n, lambda m: exchange(m).wait_send())
    loop(1, n, lambda m: along_row(m).wait_send())
    loop(1, zs, lambda m: along_line(m).wait_send())
    reduce.drain()
    line.drain()
    line_proj.drain()


def tail(parts, x, grad_hidden, params, terms, grads, proj):
    cu, cl, zs = sizes()
    n = cu * cl
    rows, width = x.shape
    block = (ITEMS, rows // ITEMS, width)
    piece = grads.shape[2:]
    input_grad, small, cut, proj_grad = pl.pallas_call(
        tail_kernel,
        in_specs=[ANY, VMEM, VMEM, VMEM, VMEM, ANY, ANY],
        out_specs=[VMEM, VMEM, ANY, VMEM],
        out_shape=[
            jax.ShapeDtypeStruct(block, BF16),
            jax.ShapeDtypeStruct((8, width), F32),
            jax.ShapeDtypeStruct((n, *piece), BF16),
            jax.ShapeDtypeStruct(proj.shape[2:], F32),
        ],
        scratch_shapes=[
            pltpu.VMEM((8, width), F32), pltpu.VMEM((zs, 8, width), F32), pltpu.VMEM((n, 8, width), F32),
            pltpu.VMEM((8, width), F32), pltpu.VMEM(piece, F32), DMA((zs,)), DMA((zs,)), DMA((n,)), DMA((n,)),
            DMA((n,)), DMA((n,)), DMA((1,)), DMA((2,)), pltpu.VMEM((n, *piece), BF16),
            *RowReduce.scratch(cu, rows, width), *LineReduce.scratch(zs, n, piece),
            *LineReduce.scratch(zs, 1, proj.shape[2:]),
        ],
        cost_estimate=pl.CostEstimate(flops=0, bytes_accessed=200 << 20, transcendentals=0),
        compiler_params=pltpu.CompilerParams(collective_id=3, has_side_effects=True, vmem_limit_bytes=60 << 20),
    )(parts.reshape(cu, cl, *block), x.reshape(block), grad_hidden.reshape(block), params, terms, grads, proj)
    return input_grad.reshape(rows, width), small, cut, proj_grad


def back_kernel(
    heads, qkv_ref, branch_ref, proj_ref, mixed_ref, low_ref, tot_ref, pq_ref, dq_ref, pk_ref, dk_ref, table_ref,
    x, grad_hidden, params, mid_sums, normed, weight, in_cut,
    input_grad, small, cut, proj_grad, in_pieces,
    gq_ref, gk_ref, gv_ref, joined_ref, normed_v, weight_v, parts, fetch, in_s, in_r,
    pile, line_in, row_in, total, row_total, line_s, line_r, row_s, row_r, a_s, a_r, own, low, *scratch,
):
    u, c, z = place()
    cu, cl, zs = sizes()
    n, me = cu * cl, u * cl + c
    width = heads * HEAD_DIM
    rows = qkv_ref.shape[0]
    block = row_block(rows)
    slab = low.shape[1]
    group = in_cut.shape[0]
    reduce = RowReduce(parts, *scratch[:8])
    held, held_proj = scratch[8], scratch[15]
    line = LineReduce(*scratch[8:11], n, *scratch[11:15])
    line_proj = LineReduce(*scratch[15:18], 1, *scratch[18:])
    my_place = in_group(0)[3]
    kept = pltpu.make_async_copy(in_cut.at[my_place], in_pieces.at[my_place], own.at[1])
    fetches = [
        pltpu.make_async_copy(normed, normed_v, fetch.at[0]), pltpu.make_async_copy(weight, weight_v, fetch.at[1])
    ]

    def in_exchange(m):
        device, after, _, mine = in_group(m)
        return Transfer(in_cut.at[after], in_pieces.at[mine], in_s.at[m], in_r.at[m], device)

    def in_landed(m):
        device, _, before, _ = in_group(m)
        return Transfer(in_cut.at[before], in_pieces.at[before], in_s.at[m], in_r.at[m], device)

    for copy in (kept, *fetches):
        copy.start()
    greet(True, True, True)
    loop(1, group, lambda m: in_exchange(m).start())

    tile = 512

    def proj_tile(i):
        cols = pl.ds(pl.multiple_of(i * tile, tile), tile)
        grad = cross_dot(low_ref[...], branch_ref[:, cols]).astype(BF16)
        held_proj[:, 0, :, cols] = grad.reshape(zs, slab, tile)

    loop(0, D // tile, proj_tile)
    at_end = (z == 0) | (z == zs - 1)

    @pl.when(at_end)
    def _():
        for t in range(zs - 1):
            line_proj.step(t)

    gk_ref[...] = jnp.zeros_like(gk_ref)
    gv_ref[...] = jnp.zeros_like(gv_ref)

    def one(step):
        here = pl.ds(pl.multiple_of(step * block, block), block)
        grad_all = dot_t(branch_ref[here], proj_ref[...])
        allowed = (pk_ref[...] <= pq_ref[here]) & (dk_ref[...] == dq_ref[here])
        for head in range(heads):
            cols, key, value = (
                slice(p * width + head * HEAD_DIM, p * width + (head + 1) * HEAD_DIM) for p in range(3)
            )
            q, k, v = qkv_ref[here, cols], qkv_ref[:, key], qkv_ref[:, value]
            inverse = 1.0 / tot_ref[here, head : head + 1]
            grad_mixed = grad_all[:, cols]
            grad_weighted = (grad_mixed * inverse).astype(BF16)
            grad_total = -jnp.sum(grad_mixed * mixed_ref[here, cols], axis=1, keepdims=True) * inverse
            weights = jnp.where(allowed, jnp.exp(dot_t(q, k) * SCALE), 0.0)
            grad_scores = (weights * (dot_t(grad_weighted, v) + grad_total)).astype(BF16)
            gq_ref[here, cols] = jnp.dot(grad_scores, k, preferred_element_type=F32) * SCALE
            gk_ref[:, cols] += cross_dot(grad_scores, q) * SCALE
            gv_ref[:, cols] += cross_dot(weights.astype(BF16), grad_weighted)

    blocks = rows // block
    loop(0, blocks // 2, one)

    @pl.when(jnp.logical_not(at_end))
    def _():
        line_proj.step(0)

    loop(blocks // 2, blocks, one)

    @pl.when(jnp.logical_not(at_end))
    def _():
        for t in range(1, zs - 1):
            line_proj.step(t)


    pile[...] = jnp.zeros_like(pile)
    for part, ref in enumerate((gq_ref, gk_ref, gv_ref)):
        for start in range(0, width, LANES):
            grad = ref[:, start : start + LANES]
            if part < 2:
                grad = turn(grad, table_ref[...], -1.0)
            grad = grad.astype(BF16)
            joined_ref[:, part * width + start : part * width + start + LANES] = grad
            there = pl.ds(pl.multiple_of(me * width + start, LANES), LANES)
            pile[4 + part : 5 + part, there] = jnp.sum(grad.astype(F32), axis=0, keepdims=True)
    for copy in fetches:
        copy.wait()

    def qkv_tile(i):
        cols = pl.ds(pl.multiple_of(i * zs * slab, zs * slab), zs * slab)
        grad = cross_dot(normed_v[:, cols], joined_ref[...]).astype(BF16)
        for to in range(zs):
            held[to, i] = grad[to * slab : (to + 1) * slab]

    loop(0, n, qkv_tile)
    line.step(0)

    def norm_tile(i):
        to, col = i // (D // tile), lax.rem(i, D // tile) * tile
        cols = pl.ds(pl.multiple_of(col, tile), tile)
        here = pl.ds(pl.multiple_of(to * (rows // cu), rows // cu), rows // cu)
        part = dot_t(joined_ref[here], weight_v[cols]).astype(BF16)
        parts[to, :, :, :, cols] = part.reshape(cl, ITEMS, rows // (n * ITEMS), tile)

    loop(0, cu * (D // tile), norm_tile)
    reduce.start()
    reduce.merge()
    for item in range(ITEMS):
        reduce.send(item, 0)
    line.step(1)
    for phase in range(1, reduce.phases):
        for item in range(ITEMS):
            reduce.add(item, phase - 1)
            reduce.send(item, phase)
    for t in range(2, zs - 1):
        line.step(t)
    pile[2:4] = mid_sums[...]
    for item in range(ITEMS):
        grad = reduce.total(item)
        _, hat, inverse = norm_rows(x[item].astype(F32), params[0:1], params[1:2])
        pile[0:1] += jnp.sum(grad * hat, axis=0, keepdims=True)
        pile[1:2] += jnp.sum(grad, axis=0, keepdims=True)
        grad = grad_hidden[item] + norm_back(grad, hat, inverse, params[0:1])
        input_grad[item] = grad.astype(BF16)

    def along_line(m):
        return Transfer(pile, line_in.at[m], line_s.at[m], line_r.at[m], (u, c, lax.rem(z + m, zs)))

    def along_row(m):
        other = lax.rem(me + m, n)
        return Transfer(total, row_in.at[m], row_s.at[m], row_r.at[m], (other // cl, lax.rem(other, cl), z))

    def exchange(m):
        other = lax.rem(me + m, n)
        return Transfer(low.at[other], cut.at[me], a_s.at[m], a_r.at[m], (other // cl, lax.rem(other, cl), z))

    def landed(m):
        source = lax.rem(me - m + n, n)
        return Transfer(low.at[source], cut.at[source], a_s.at[m], a_r.at[m], (u, 1 - c, z))

    loop(1, zs, lambda m: along_line(m).start())

    def finish(m):
        piece = lax.rem(me + m, n)
        line.total(piece, row_total)
        low[piece] = row_total[...].astype(BF16)

        @pl.when(m > 0)
        def _():
            exchange(m).start()

    loop(1, n, finish)
    finish(0)
    mine = pltpu.make_async_copy(low.at[me], cut.at[me], own.at[0])
    mine.start()
    total[...] = pile[...]
    for m in range(1, zs):
        along_line(m).wait_recv()
        total[...] += line_in[m]
    loop(1, n, lambda m: along_row(m).start())
    line_proj.total(0, proj_grad)
    small[...] = total[...]

    def collect(m):
        along_row(m).wait_recv()
        small[...] += row_in[m]

    loop(1, n, collect)
    loop(1, group, lambda m: in_landed(m).wait_recv())
    loop(1, n, lambda m: landed(m).wait_recv())
    mine.wait()
    kept.wait()
    loop(1, group, lambda m: in_exchange(m).wait_send())
    loop(1, n, lambda m: exchange(m).wait_send())
    loop(1, n, lambda m: along_row(m).wait_send())
    loop(1, zs, lambda m: along_line(m).wait_send())
    reduce.drain()
    line.drain()
    line_proj.drain()


def back(qkv, grad_branch, proj, mixed, mixed_low, totals, marks, table, x, grad_hidden, params, mid_sums, normed,
         weight, in_cut, heads):
    cu, cl, zs = sizes()
    n = cu * cl
    rows, width = x.shape
    total_rows, cols = qkv.shape
    slab = width // (n * zs)
    block = (ITEMS, rows // ITEMS, width)
    piece = (slab, cols)
    group = in_cut.shape[0]
    input_grad, small, cut, proj_grad, in_pieces = pl.pallas_call(
        functools.partial(back_kernel, heads),
        in_specs=[*[VMEM] * 15, ANY, ANY, ANY],
        out_specs=[VMEM, VMEM, ANY, VMEM, ANY],
        out_shape=[
            jax.ShapeDtypeStruct(block, BF16),
            jax.ShapeDtypeStruct((8, width), F32),
            jax.ShapeDtypeStruct((n, *piece), BF16),
            jax.ShapeDtypeStruct((slab, width), F32),
            jax.ShapeDtypeStruct(in_cut.shape, BF16),
        ],
        scratch_shapes=[
            *[pltpu.VMEM((total_rows, cols // 3), F32)] * 3, pltpu.VMEM(qkv.shape, BF16),
            pltpu.VMEM(normed.shape, BF16), pltpu.VMEM(weight.shape, BF16), pltpu.VMEM((cu, cl, *block), BF16),
            DMA((2,)), DMA((group,)), DMA((group,)),
            pltpu.VMEM((8, width), F32), pltpu.VMEM((zs, 8, width), F32), pltpu.VMEM((n, 8, width), F32),
            pltpu.VMEM((8, width), F32), pltpu.VMEM(piece, F32), DMA((zs,)), DMA((zs,)), DMA((n,)), DMA((n,)),
            DMA((n,)), DMA((n,)), DMA((2,)), pltpu.VMEM((n, *piece), BF16),
            *RowReduce.scratch(cu, rows, width), *LineReduce.scratch(zs, n, piece),
            *LineReduce.scratch(zs, 1, (slab, width)),
        ],
        cost_estimate=pl.CostEstimate(flops=0, bytes_accessed=400 << 20, transcendentals=0),
        compiler_params=pltpu.CompilerParams(collective_id=5, has_side_effects=True, vmem_limit_bytes=63 << 20),
    )(
        qkv, grad_branch, proj, mixed, mixed_low, totals, *marks, table, x.reshape(block), grad_hidden.reshape(block),
        params, mid_sums, normed, weight, in_cut,
    )
    return input_grad.reshape(rows, width), small, cut, proj_grad, in_pieces


def body(
    inputs, out_grad, doc_ids, block_pairs, qkv_weight, proj_weight, ffn_in_weight, ffn_out_weight, small_params,
    qkv_first, proj_first, ffn_in_first, ffn_out_first, small_first,
    qkv_second, proj_second, ffn_in_second, ffn_out_second, small_second,
):
    bf16 = jnp.bfloat16
    tok_rows = inputs.shape[1]
    half_rows = tok_rows // 2
    cu, cl, zs = lax.axis_size("cu"), lax.axis_size("cl"), lax.axis_size("fsdp")
    ctx_count = cu * cl
    group = cl * zs
    seq_len = tok_rows * ctx_count
    my_index = lax.axis_index(ROW)
    heads = HEADS // ctx_count
    width = heads * HEAD_DIM
    slab = qkv_weight.shape[0]
    units = ffn_out_weight.shape[0]
    hidden = units * cu
    proj_low = lax.all_gather(proj_weight.astype(bf16), "fsdp", axis=0, tiled=True)
    out_low = lax.all_gather(ffn_out_weight.astype(bf16), "cu", axis=0, tiled=True)
    row_in, params, qkv_low, in_cast, pos_col, doc_col, pos_row, doc_row, table = gather_head(
        inputs[0], small_params, qkv_weight, ffn_in_weight, block_pairs, doc_ids.reshape(2 * ctx_count, half_rows)
    )
    marks = (pos_col, doc_col, pos_row, doc_row)
    row_in, in_cast, proj_low = lax.optimization_barrier((row_in, in_cast, proj_low))
    in_cut = lax.all_to_all(in_cast.reshape(group * slab, 2 * hidden), FFN_GROUP, split_axis=0, concat_axis=0, tiled=True)
    row_in = row_in.reshape(seq_len, D)
    params = params[:, :, :7, :slab].transpose(2, 0, 1, 3).reshape(7, D)
    qkv_low = qkv_low.reshape(D, 3 * width)

    bias = lax.dynamic_slice_in_dim(params[4:7], my_index * width, width, 1).reshape(1, 3 * width)
    attn_in, qkv = project(row_in, params[0:2], qkv_low, bias, table)
    mixed, mixed_low, totals, branch = attend(qkv, proj_low, marks, heads)
    branch, in_cut, out_low = lax.optimization_barrier((branch, in_cut, out_low))
    in_low = lax.all_gather(in_cut, "cu", axis=0, tiled=True)
    hidden_state, mlp_in, grad_all = mid_forward(branch, inputs[0], out_grad[0], params[2:4])

    gate_up = jnp.dot(mlp_in, in_low, preferred_element_type=jnp.float32)
    gate_part, up_part = gate_up[:, :hidden], gate_up[:, hidden:]
    sigmoid_gate = jax.nn.sigmoid(gate_part)
    silu_gate = gate_part * sigmoid_gate
    inner_low = (silu_gate * up_part).astype(bf16)
    grad_inner = back_dot(grad_all, out_low)
    grad_up = grad_inner * silu_gate
    grad_gate = grad_inner * up_part * (sigmoid_gate * (1.0 + gate_part * (1.0 - sigmoid_gate)))
    grad_gate_up = jnp.concatenate([grad_gate, grad_up], axis=1).astype(bf16)
    grad_mid_part = back_dot(grad_gate_up, in_low).astype(bf16)
    grad_ffn_in = cross_dot(mlp_in, grad_gate_up).astype(bf16)
    grad_mid_part, grad_ffn_in = lax.optimization_barrier((grad_mid_part, grad_ffn_in))
    in_grad_cut = lax.psum_scatter(grad_ffn_in, "cu", scatter_dimension=0, tiled=True)

    grad_hidden, grad_branch, mid_sums, layer_out, grad_ffn_out = mid_backward(
        grad_mid_part, hidden_state, out_grad[0], params[2:4], inner_low, out_low, grad_all
    )
    layer_out = layer_out[None]
    in_grad_cut, grad_branch = lax.optimization_barrier((in_grad_cut, grad_branch))
    in_grad_cut = in_grad_cut.reshape(group, slab, 2 * hidden)
    grad_ffn_out, in_grad_cut = lax.optimization_barrier((grad_ffn_out, in_grad_cut))
    ffn_out_grad = lax.psum_scatter(grad_ffn_out, "cu", scatter_dimension=0, tiled=True)
    if seq_len <= 1024 and width % LANES == 0:
        input_grad, small_sum, qkv_grad_cut, proj_grad, in_grad = back(
            qkv, grad_branch, proj_low, mixed, mixed_low, totals, marks, table, inputs[0], grad_hidden, params[0:2],
            mid_sums, attn_in, qkv_low, in_grad_cut, heads,
        )
    else:
        grad_proj = cross_dot(mixed_low, grad_branch).astype(bf16)
        grad_joined, bias_own, in_grad = attend_back(
            qkv, grad_branch, proj_low, mixed, totals, marks, table, in_grad_cut, heads
        )
        grad_norm_part = back_dot(grad_joined, qkv_low).astype(bf16)
        grad_qkv = (
            cross_dot(attn_in, grad_joined).astype(bf16).reshape(ctx_count, zs, slab, 3 * width).transpose(1, 0, 2, 3)
        )
        bias_own = bias_own.reshape(3, width)
        grad_bias = lax.dynamic_update_slice(jnp.zeros((3, D), jnp.float32), bias_own, (0, my_index * width))
        zero_rows = jnp.zeros((2, D), jnp.float32)
        terms = jnp.concatenate([zero_rows, mid_sums, grad_bias, zero_rows[:1]], axis=0)
        input_grad, small_sum, qkv_grad_cut, proj_grad = tail(
            grad_norm_part, inputs[0], grad_hidden, params[0:2], terms, grad_qkv, grad_proj.reshape(zs, 1, slab, D)
        )
    input_grad = input_grad[None]
    my_slab = (my_index * zs + lax.axis_index("fsdp")) * slab
    small_grad = lax.dynamic_slice_in_dim(small_sum, my_slab, slab, 1)[:7]

    proj_fan = max(8 * D // seq_len, 1)
    f32 = jnp.float32
    qkv_new = adam_qkv(qkv_weight, qkv_first, qkv_second, qkv_grad_cut, 2.0 / math.sqrt(D))
    in_new = adam_ffn(ffn_in_weight, ffn_in_first, ffn_in_second, in_grad, 2.0 / math.sqrt(D))
    proj_new = adam_update(
        proj_weight, proj_first, proj_second, proj_grad.astype(f32), 2.0 / math.sqrt(proj_fan), matrix_decay
    )
    out_new = adam_update(
        ffn_out_weight, ffn_out_first, ffn_out_second, ffn_out_grad.astype(f32), 2.0 / math.sqrt(FF), matrix_decay
    )
    small_new = adam_update(small_params, small_first, small_second, small_grad, small_rate, 0.0)
    news = (qkv_new, proj_new, in_new, out_new, small_new)
    return (layer_out, input_grad, *(n[0] for n in news), *(n[1] for n in news), *(n[2] for n in news), small_grad)


def solution(mesh):
    ctx_count, fsdp_count = mesh.devices.shape
    fine = Mesh(mesh.devices.reshape(ctx_count // 2, 2, fsdp_count), ("cu", "cl", "fsdp"))
    tokens = P("fsdp", ROW, None)
    matrix = P(EVERY, None)
    small = P(None, EVERY)
    five = (matrix, matrix, matrix, matrix, small)
    in_specs = (tokens, tokens, P("fsdp", None), P(), *five, *five, *five)
    out_specs = (tokens, tokens, *five, *five, *five, small)
    return jax.shard_map(body, mesh=fine, in_specs=in_specs, out_specs=out_specs, check_vma=False)
```

```python
import functools
import math

import jax
import jax.numpy as jnp
from jax import lax
from jax.experimental import pallas as pl
from jax.experimental.pallas import tpu as pltpu
from jax.sharding import Mesh, PartitionSpec as P

D = 2048
HEADS = 32
HEAD_DIM = 64
FF = 5632
ROT = 16
STEP = 10


norm_eps = 1e-05
beta_first = 0.9
beta_second = 0.95
adam_eps = 1e-08
matrix_decay = 0.1
small_rate = 0.5


def norm_rows(values, gain_row, shift_row):
    center_mean = jnp.mean(values, axis=-1, keepdims=True)
    centered = values - center_mean
    inv_std = lax.rsqrt(jnp.mean(centered * centered, axis=-1, keepdims=True) + norm_eps)
    normed = centered * inv_std
    return (normed * gain_row + shift_row, normed, inv_std)


def norm_back(grad_rows, normed, inv_std, gain_row):
    scaled = grad_rows * gain_row
    return inv_std * (
        scaled
        - jnp.mean(scaled, axis=-1, keepdims=True)
        - normed * jnp.mean(scaled * normed, axis=-1, keepdims=True)
    )


def cross_dot(left_mat, right_mat):
    return lax.dot_general(
        left_mat, right_mat, (((0,), (0,)), ((), ())), preferred_element_type=jnp.float32
    )


def back_dot(left_mat, weight):
    return lax.dot_general(
        left_mat, weight, (((1,), (1,)), ((), ())), preferred_element_type=jnp.float32
    )


def adam_update(weight, first_moment, second_moment, gradient, step_rate, decay_factor):
    new_first = beta_first * first_moment + (1.0 - beta_first) * gradient
    new_second = beta_second * second_moment + (1.0 - beta_second) * gradient * gradient
    correct_first = 1.0 - beta_first**STEP
    correct_second = 1.0 - beta_second**STEP
    update = new_first / correct_first / (jnp.sqrt(new_second / correct_second) + adam_eps)
    return (weight - step_rate * (update + decay_factor * weight), new_first, new_second)


ROW = ("cu", "cl")
FFN_GROUP = ("cl", "fsdp")
EVERY = ("cu", "cl", "fsdp")
SCALE = HEAD_DIM**-0.5


LANES = 128


def fill_table(table, positions, start, rows):
    half_rot = ROT // 2
    here = pl.ds(pl.multiple_of(start, rows), rows)
    lane = lax.rem(lax.broadcasted_iota(jnp.int32, (1, LANES), 1), HEAD_DIM)
    inverse = jnp.zeros((1, LANES), jnp.float32)
    for i in range(half_rot):
        inverse = jnp.where(lax.rem(lane, half_rot) == i, 10000.0 ** (-2.0 * i / ROT), inverse)
    angles = positions[here, :].astype(jnp.float32) * jnp.where(lane < ROT, inverse, 0.0)
    sine = jnp.sin(angles)
    table[here, 0:LANES] = jnp.cos(angles)
    table[here, LANES : 2 * LANES] = jnp.where(lane < half_rot, -sine, 0.0)
    table[here, 2 * LANES : 3 * LANES] = jnp.where(lane < half_rot, 0.0, sine)


def turn(values, table, sign):
    keep, lower, upper = (table[:, i * LANES : (i + 1) * LANES] for i in range(3))
    half_rot = ROT // 2
    shifted = pltpu.roll(values, LANES - half_rot, 1) * lower + pltpu.roll(values, half_rot, 1) * upper
    return values * keep + sign * shifted


def dot_t(left, right):
    return lax.dot_general(left, right, (((1,), (1,)), ((), ())), preferred_element_type=jnp.float32)


def row_block(rows):
    return min(256, rows)


def project_kernel(x_ref, params_ref, w_ref, bias_ref, table_ref, normed_ref, qkv_ref):
    normed = norm_rows(x_ref[...].astype(jnp.float32), params_ref[0:1], params_ref[1:2])[0].astype(jnp.bfloat16)
    normed_ref[...] = normed
    joined = jnp.dot(normed, w_ref[...], preferred_element_type=jnp.float32) + bias_ref[...]
    turned = 2 * (joined.shape[1] // 3)
    for start in range(0, turned, LANES):
        cols = slice(start, start + LANES)
        qkv_ref[:, cols] = turn(joined[:, cols], table_ref[...], 1.0).astype(jnp.bfloat16)
    qkv_ref[:, turned:] = joined[:, turned:].astype(jnp.bfloat16)


def project(x, params, weight, bias, table):
    rows, width = x.shape
    block = row_block(rows)
    cols = weight.shape[1]

    def by_row(n):
        return pl.BlockSpec((block, n), lambda i: (i, 0))

    def whole(array):
        return pl.BlockSpec(array.shape, lambda i: (0, 0))

    return pl.pallas_call(
        project_kernel,
        grid=(rows // block,),
        in_specs=[by_row(width), whole(params), whole(weight), whole(bias), by_row(table.shape[1])],
        out_specs=[by_row(width), by_row(cols)],
        out_shape=[jax.ShapeDtypeStruct((rows, width), jnp.bfloat16), jax.ShapeDtypeStruct((rows, cols), jnp.bfloat16)],
        cost_estimate=pl.CostEstimate(
            flops=2 * rows * width * cols, bytes_accessed=4 * rows * width, transcendentals=0
        ),
        compiler_params=pltpu.CompilerParams(vmem_limit_bytes=48 << 20),
    )(x, params, weight, bias, table)


def attend_kernel(
    heads, q_ref, qkv_ref, proj_ref, pq_ref, dq_ref, pk_ref, dk_ref, mixed_ref, low_ref, tot_ref, branch_ref
):
    width = heads * HEAD_DIM
    allowed = (pk_ref[...] <= pq_ref[...]) & (dk_ref[...] == dq_ref[...])
    for head in range(heads):
        cols, key, value = (slice(p * width + head * HEAD_DIM, p * width + (head + 1) * HEAD_DIM) for p in range(3))
        scores = dot_t(q_ref[:, cols], qkv_ref[:, key]) * SCALE
        weights = jnp.where(allowed, jnp.exp(scores), 0.0)
        total = jnp.sum(weights, axis=1, keepdims=True)
        weighted = jnp.dot(weights.astype(jnp.bfloat16), qkv_ref[:, value], preferred_element_type=jnp.float32)
        mixed = weighted / total
        mixed_ref[:, cols] = mixed
        low_ref[:, cols] = mixed.astype(jnp.bfloat16)
        tot_ref[:, head : head + 1] = total
    branch_ref[...] = jnp.dot(low_ref[...], proj_ref[...], preferred_element_type=jnp.float32).astype(jnp.bfloat16)


def attend(qkv, proj, marks, heads):
    pos_col, doc_col, pos_row, doc_row = marks
    rows, cols = qkv.shape
    width = cols // 3
    block = row_block(rows)

    def by_row(n):
        return pl.BlockSpec((block, n), lambda i: (i, 0))

    def whole(array):
        return pl.BlockSpec(array.shape, lambda i: (0, 0))

    return pl.pallas_call(
        functools.partial(attend_kernel, heads),
        grid=(rows // block,),
        in_specs=[by_row(cols), whole(qkv), whole(proj), by_row(1), by_row(1), whole(pos_row), whole(doc_row)],
        out_specs=[by_row(width), by_row(width), by_row(heads), by_row(D)],
        out_shape=[
            jax.ShapeDtypeStruct((rows, width), jnp.float32),
            jax.ShapeDtypeStruct((rows, width), jnp.bfloat16),
            jax.ShapeDtypeStruct((rows, heads), jnp.float32),
            jax.ShapeDtypeStruct((rows, D), jnp.bfloat16),
        ],
        cost_estimate=pl.CostEstimate(
            flops=4 * rows * rows * width, bytes_accessed=8 * rows * D, transcendentals=rows * rows * heads
        ),
        compiler_params=pltpu.CompilerParams(vmem_limit_bytes=48 << 20),
    )(qkv, qkv, proj, pos_col, doc_col, pos_row, doc_row)


def attend_back_kernel(
    heads, qkv_ref, branch_ref, proj_ref, mixed_ref, tot_ref, pq_ref, dq_ref, pk_ref, dk_ref, table_ref, cut,
    joined_ref, bias_ref, pieces, gq_ref, gk_ref, gv_ref, own, send, recv,
):
    width = heads * HEAD_DIM
    rows = qkv_ref.shape[0]
    block = row_block(rows)
    group = cut.shape[0]

    def exchange(m):
        device, after, _, me = in_group(m)
        return Transfer(cut.at[after], pieces.at[me], send.at[m], recv.at[m], device)

    def landed(m):
        device, _, before, _ = in_group(m)
        return Transfer(cut.at[before], pieces.at[before], send.at[m], recv.at[m], device)

    me = in_group(0)[3]
    kept = pltpu.make_async_copy(cut.at[me], pieces.at[me], own.at[0])
    kept.start()
    greet_group()
    loop(1, group, lambda m: exchange(m).start())
    gk_ref[...] = jnp.zeros_like(gk_ref)
    gv_ref[...] = jnp.zeros_like(gv_ref)

    def one(step):
        here = pl.ds(pl.multiple_of(step * block, block), block)
        grad_all = dot_t(branch_ref[here], proj_ref[...])
        allowed = (pk_ref[...] <= pq_ref[here]) & (dk_ref[...] == dq_ref[here])
        for head in range(heads):
            cols, key, value = (
                slice(p * width + head * HEAD_DIM, p * width + (head + 1) * HEAD_DIM) for p in range(3)
            )
            q, k, v = qkv_ref[here, cols], qkv_ref[:, key], qkv_ref[:, value]
            inverse = 1.0 / tot_ref[here, head : head + 1]
            grad_mixed = grad_all[:, cols]
            grad_weighted = (grad_mixed * inverse).astype(jnp.bfloat16)
            grad_total = -jnp.sum(grad_mixed * mixed_ref[here, cols], axis=1, keepdims=True) * inverse
            weights = jnp.where(allowed, jnp.exp(dot_t(q, k) * SCALE), 0.0)
            grad_scores = (weights * (dot_t(grad_weighted, v) + grad_total)).astype(jnp.bfloat16)
            gq_ref[here, cols] = jnp.dot(grad_scores, k, preferred_element_type=jnp.float32) * SCALE
            gk_ref[:, cols] += cross_dot(grad_scores, q) * SCALE
            gv_ref[:, cols] += cross_dot(weights.astype(jnp.bfloat16), grad_weighted)

    loop(0, rows // block, one)
    for part, ref in enumerate((gq_ref, gk_ref, gv_ref)):
        for start in range(0, width, LANES):
            cols = slice(start, min(start + LANES, width))
            grad = ref[:, cols]
            if part < 2:
                lanes = cols.stop - cols.start
                if lanes < LANES:
                    grad = jnp.concatenate([grad, jnp.zeros((rows, LANES - lanes), jnp.float32)], axis=1)
                grad = turn(grad, table_ref[...], -1.0)[:, :lanes]
            grad = grad.astype(jnp.bfloat16)
            into = slice(part * width + cols.start, part * width + cols.stop)
            joined_ref[:, into] = grad
            bias_ref[:, into] = jnp.sum(grad.astype(jnp.float32), axis=0, keepdims=True)
    loop(1, group, lambda m: landed(m).wait_recv())
    loop(1, group, lambda m: exchange(m).wait_send())
    kept.wait()


def attend_back(qkv, grad_branch, proj, mixed, totals, marks, table, cut, heads):
    rows, cols = qkv.shape
    width = cols // 3
    return pl.pallas_call(
        functools.partial(attend_back_kernel, heads),
        in_specs=[*[VMEM] * 10, ANY],
        out_specs=[VMEM, VMEM, ANY],
        out_shape=[
            jax.ShapeDtypeStruct((rows, cols), jnp.bfloat16), jax.ShapeDtypeStruct((1, cols), jnp.float32),
            jax.ShapeDtypeStruct(cut.shape, BF16),
        ],
        scratch_shapes=[
            *[pltpu.VMEM((rows, width), jnp.float32)] * 3, DMA((1,)), DMA((cut.shape[0],)), DMA((cut.shape[0],)),
        ],
        cost_estimate=pl.CostEstimate(
            flops=10 * rows * rows * width, bytes_accessed=8 * rows * D, transcendentals=rows * rows * heads
        ),
        compiler_params=pltpu.CompilerParams(collective_id=4, has_side_effects=True, vmem_limit_bytes=60 << 20),
    )(qkv, grad_branch, proj, mixed, totals, *marks, table, cut)


def feed_kernel(x_ref, grad_ref, in_ref, out_ref, inner_ref, back_ref):
    hidden = out_ref.shape[0]
    gate_up = jnp.dot(x_ref[...], in_ref[...], preferred_element_type=jnp.float32)
    gate, up = gate_up[:, :hidden], gate_up[:, hidden:]
    grad_inner = dot_t(grad_ref[...], out_ref[...])
    sigmoid = 1.0 / (1.0 + jnp.exp(-gate))
    silu = gate * sigmoid
    inner_ref[...] = (silu * up).astype(jnp.bfloat16)
    grad_gate = grad_inner * up * (sigmoid * (1.0 + gate * (1.0 - sigmoid)))
    back_ref[...] = jnp.concatenate([grad_gate, grad_inner * silu], axis=1).astype(jnp.bfloat16)


def feed(x, grad, in_weight, out_weight):
    rows, width = x.shape
    hidden = out_weight.shape[0]
    block = row_block(rows)

    def by_row(n):
        return pl.BlockSpec((block, n), lambda i: (i, 0))

    def whole(array):
        return pl.BlockSpec(array.shape, lambda i: (0, 0))

    return pl.pallas_call(
        feed_kernel,
        grid=(rows // block,),
        in_specs=[by_row(width), by_row(width), whole(in_weight), whole(out_weight)],
        out_specs=[by_row(hidden), by_row(2 * hidden)],
        out_shape=[
            jax.ShapeDtypeStruct((rows, hidden), jnp.bfloat16), jax.ShapeDtypeStruct((rows, 2 * hidden), jnp.bfloat16)
        ],
        cost_estimate=pl.CostEstimate(
            flops=6 * rows * width * hidden, bytes_accessed=8 * rows * width, transcendentals=rows * hidden
        ),
        compiler_params=pltpu.CompilerParams(vmem_limit_bytes=48 << 20),
    )(x, grad, in_weight, out_weight)


def adam_kernel(rates, counts, *refs):
    step = pl.program_id(0)
    in_count, out_count = counts

    def pieces(g, parts):
        width = g.shape[2] // parts
        for part in range(parts):
            yield part, jnp.concatenate(
                [g[owner, :, part * width : (part + 1) * width].astype(jnp.float32) for owner in range(g.shape[0])],
                axis=1,
            )

    def update(k, grads, rate):
        w, m, v = refs[4 * k : 4 * k + 3]
        outs = refs[16 + 3 * k : 19 + 3 * k]
        for part, grad in grads:
            here = slice(part * grad.shape[1], (part + 1) * grad.shape[1])
            new = adam_update(w[:, here], m[:, here], v[:, here], grad, rate, matrix_decay)
            for out, value in zip(outs, new):
                out[:, here] = value

    @pl.when(step < in_count)
    def _():
        g = refs[3]
        update(0, pieces(g, refs[0].shape[1] // g.shape[2]), rates[0])
        update(3, [(0, refs[15][...].astype(jnp.float32))], rates[3])

    @pl.when((step >= in_count) & (step < 2 * in_count))
    def _():
        update(1, pieces(refs[7], 3), rates[1])

    @pl.when(step < out_count)
    def _():
        update(2, [(0, refs[11][...].astype(jnp.float32))], rates[2])


def adam_all(states, rates):
    slab, units = states[0][0].shape[0], states[2][0].shape[0]
    rows = 16
    in_count = slab // rows
    out_rows = rows if units % rows == 0 else units
    out_count = units // out_rows
    places = (
        lambda i: jnp.minimum(i, in_count - 1),
        lambda i: jnp.clip(i - in_count, 0, in_count - 1),
        lambda i: jnp.minimum(i, out_count - 1),
        lambda i: jnp.minimum(i, in_count - 1),
    )
    in_specs, out_specs, out_shape, operands = [], [], [], []
    for (weight, first, second, grad), place_of, block in zip(states, places, (rows, rows, out_rows, rows)):
        by_row = pl.BlockSpec((block, weight.shape[1]), lambda i, place_of=place_of: (place_of(i), 0))
        by_grad = by_row
        if grad.ndim == 3:
            by_grad = pl.BlockSpec(
                (grad.shape[0], block, grad.shape[2]), lambda i, place_of=place_of: (0, place_of(i), 0)
            )
        in_specs += [by_row, by_row, by_row, by_grad]
        out_specs += [by_row] * 3
        out_shape += [jax.ShapeDtypeStruct(weight.shape, jnp.float32)] * 3
        operands += [weight, first, second, grad]
    out = pl.pallas_call(
        functools.partial(adam_kernel, rates, (in_count, out_count)),
        grid=(max(2 * in_count, out_count),),
        in_specs=in_specs,
        out_specs=out_specs,
        out_shape=out_shape,
        compiler_params=pltpu.CompilerParams(vmem_limit_bytes=60 << 20),
    )(*operands)
    return [tuple(out[3 * k : 3 * k + 3]) for k in range(4)]


MESH = pl.DeviceIdType.MESH
ANY = pl.BlockSpec(memory_space=pl.ANY)
VMEM = pl.BlockSpec(memory_space=pltpu.VMEM)
DMA = pltpu.SemaphoreType.DMA
BF16, F32 = jnp.bfloat16, jnp.float32


class Transfer:
    def __init__(self, src, dst, send, recv, device):
        self.parts = (src, dst, send, recv, device)

    def copy(self):
        src, dst, send, recv, device = self.parts
        return pltpu.make_async_remote_copy(
            src_ref=src, dst_ref=dst, send_sem=send, recv_sem=recv, device_id=device, device_id_type=MESH
        )

    def start(self):
        self.copy().start()

    def wait_recv(self):
        self.copy().wait_recv()

    def wait_send(self):
        self.copy().wait_send()

    def wait(self):
        self.copy().wait()


rcopy = Transfer


def flip(index, mask):
    bit = 1
    while bit <= mask:
        if mask & bit:
            index = index + bit * (1 - 2 * lax.rem(index // bit, 2))
        bit *= 2
    return index


def place():
    return lax.axis_index("cu"), lax.axis_index("cl"), lax.axis_index("fsdp")


def sizes():
    return lax.axis_size("cu"), lax.axis_size("cl"), lax.axis_size("fsdp")


def in_group(m):
    u, c, z = place()
    _, cl, zs = sizes()
    group, me = cl * zs, c * zs + z
    after, before = lax.rem(me + m, group), lax.rem(me - m + group, group)
    return (u, after // zs, lax.rem(after, zs)), after, before, me


def greet_group():
    _, cl, zs = sizes()
    barrier = pltpu.get_barrier_semaphore()

    def signal(m, carry):
        pl.semaphore_signal(barrier, inc=1, device_id=in_group(m)[0], device_id_type=MESH)
        return carry

    lax.fori_loop(1, cl * zs, signal, 0)
    pl.semaphore_wait(barrier, cl * zs - 1)


def greet(row, line, twins=False):
    u, c, z = place()
    cu, cl, zs = sizes()
    n, me = cu * cl, u * cl + c
    barrier = pltpu.get_barrier_semaphore()

    def signal_row(m, carry):
        other = lax.rem(me + m, n)
        pl.semaphore_signal(barrier, inc=1, device_id=(other // cl, lax.rem(other, cl), z), device_id_type=MESH)
        return carry

    def signal_line(m, carry):
        pl.semaphore_signal(barrier, inc=1, device_id=(u, c, lax.rem(z + m, zs)), device_id_type=MESH)
        return carry

    def signal_twins(m, carry):
        pl.semaphore_signal(barrier, inc=1, device_id=(u, 1 - c, lax.rem(z + m, zs)), device_id_type=MESH)
        return carry

    if row:
        lax.fori_loop(1, n, signal_row, 0)
    if line:
        lax.fori_loop(1, zs, signal_line, 0)
    if twins:
        lax.fori_loop(1, zs, signal_twins, 0)
    pl.semaphore_wait(barrier, row * (n - 1) + (line + twins) * (zs - 1))


def head_kernel(
    x, small_in, qkv_far, ffn_far, proj_far, pairs, docs_in, row, par, wq, wp, in_cut, pos_col, doc_col, pos_row, doc_row,
    table, qkv_in, ffn_in, proj_in, docs, fetch, qkv, proj, small, own, x_send, x_recv, s_send, s_recv, p_send, p_recv, q_send, q_recv,
    a_send, a_recv, up_send, up_recv, dn_send, dn_recv,
):
    u, c, z = place()
    cu, cl, zs = sizes()
    n, me = cu * cl, u * cl + c
    sibling = (u, 1 - c, z)
    slab, width = qkv_in.shape[0], qkv_in.shape[1] // (3 * n)
    half = docs.shape[1]
    fetches = [
        pltpu.make_async_copy(source, into, fetch.at[i])
        for i, (source, into) in enumerate(((qkv_far, qkv_in), (proj_far, proj_in), (ffn_far, ffn_in)))
    ]
    for copy in fetches:
        copy.start()
    for i in range(docs.shape[0]):
        docs[i : i + 1] = docs_in[:, i * half : (i + 1) * half]
    small[...] = jnp.zeros_like(small)
    small[: small_in.shape[0], : small_in.shape[1]] = small_in[...]
    fetches[0].wait()
    for owner in range(n):
        for part in range(3):
            start = (part * n + owner) * width
            qkv[owner, :, part * width : (part + 1) * width] = qkv_in[:, start : start + width].astype(BF16)
    mine = [
        pltpu.make_async_copy(qkv.at[me], wq.at[me, z], own.at[0]),
        pltpu.make_async_copy(x, row.at[u, c], own.at[1]),
        pltpu.make_async_copy(small, par.at[me, z], own.at[2]),
        pltpu.make_async_copy(proj, wp.at[z], own.at[3]),
    ]
    fetches[1].wait()
    proj[...] = proj_in[...].astype(BF16)
    for copy in mine:
        copy.start()
    greet(True, True)

    def exchange(m):
        other, source = lax.rem(me + m, n), lax.rem(me - m + n, n)
        out = rcopy(
            qkv.at[other], wq.at[me, z], a_send.at[m], a_recv.at[m], (other // cl, lax.rem(other, cl), z)
        )
        into = rcopy(qkv.at[other], wq.at[source, z], a_send.at[m], a_recv.at[m], sibling)
        return out, into

    def params_line(m):
        other, source = lax.rem(z + m, zs), lax.rem(z - m + zs, zs)
        return (
            rcopy(small, par.at[me, z], p_send.at[m], p_recv.at[m], (u, c, other)),
            rcopy(small, par.at[me, source], p_send.at[m], p_recv.at[m], sibling),
        )

    def params_row(m):
        other, source = lax.rem(me + m, n), lax.rem(me - m + n, n)
        return (
            rcopy(par.at[me], par.at[me], q_send.at[m], q_recv.at[m], (other // cl, lax.rem(other, cl), z)),
            rcopy(par.at[me], par.at[source], q_send.at[m], q_recv.at[m], sibling),
        )

    def x_far(i):
        out = rcopy(x, row.at[u, c], x_send.at[i], x_recv.at[i], (flip(u, i), c, z))
        into = rcopy(x, row.at[flip(u, i), c], x_send.at[i], x_recv.at[i], sibling)
        return out, into

    def x_near(i):
        part = row.at[flip(u, i), c]
        out = rcopy(part, part, s_send.at[i], s_recv.at[i], sibling)
        into = rcopy(part, row.at[flip(u, i), 1 - c], s_send.at[i], s_recv.at[i], sibling)
        return out, into

    def loop(low, high, step):
        def run(m, carry):
            step(m)
            return carry

        lax.fori_loop(low, high, run, 0)

    loop(1, n, lambda m: exchange(m)[0].start())
    loop(1, zs, lambda m: params_line(m)[0].start())
    for copy in mine:
        copy.wait()
    for i in range(1, cu):
        x_far(i)[0].start()
    x_near(0)[0].start()

    def chain(step, m):
        piece = lax.rem(me - m + n, n)
        above, below = wq.at[piece, lax.rem(z + step, zs)], wq.at[piece, lax.rem(z - step + zs, zs)]
        return (
            rcopy(below, below, up_send.at[step, m], up_recv.at[step, m], (u, c, lax.rem(z + 1, zs))),
            rcopy(above, above, dn_send.at[step, m], dn_recv.at[step, m], (u, c, lax.rem(z - 1 + zs, zs))),
        )

    def arrival(step, m):
        piece = lax.rem(me - m + n, n)
        above, below = wq.at[piece, lax.rem(z + step + 1, zs)], wq.at[piece, lax.rem(z - step - 1 + zs, zs)]
        return (
            rcopy(below, below, up_send.at[step, m], up_recv.at[step, m], sibling),
            rcopy(above, above, dn_send.at[step, m], dn_recv.at[step, m], sibling),
        )

    def chain_proj(step):
        above, below = wp.at[lax.rem(z + step, zs)], wp.at[lax.rem(z - step + zs, zs)]
        return (
            rcopy(below, below, up_send.at[step, n], up_recv.at[step, n], (u, c, lax.rem(z + 1, zs))),
            rcopy(above, above, dn_send.at[step, n], dn_recv.at[step, n], (u, c, lax.rem(z - 1 + zs, zs))),
        )

    def forward_proj(step):
        if step:

            @pl.when(z >= step)
            def _():
                chain_proj(step - 1)[0].wait_recv()

            @pl.when(z + step < zs)
            def _():
                chain_proj(step - 1)[1].wait_recv()

        if step < zs - 1:

            @pl.when((z >= step) & (z + 1 < zs))
            def _():
                chain_proj(step)[0].start()

            @pl.when((z + step < zs) & (z > 0))
            def _():
                chain_proj(step)[1].start()

    def sent_proj(step):
        @pl.when((z >= step) & (z + 1 < zs))
        def _():
            chain_proj(step)[0].wait_send()

        @pl.when((z + step < zs) & (z > 0))
        def _():
            chain_proj(step)[1].wait_send()

    def first(m):
        @pl.when(m > 0)
        def _():
            exchange(m)[1].wait_recv()

        @pl.when(z + 1 < zs)
        def _():
            chain(0, m)[0].start()

        @pl.when(z > 0)
        def _():
            chain(0, m)[1].start()

    loop(0, n, first)
    forward_proj(0)
    fetches[2].wait()
    group, units = cl * zs, ffn_in.shape[1] // (2 * n * zs)
    for part in range(2 * cu):
        for owner in range(group):
            start = (part * group + owner) * units
            in_cut[owner, :, part * units : (part + 1) * units] = ffn_in[:, start : start + units].astype(BF16)
    lane, line_of = (lax.broadcasted_iota(jnp.int32, (half, half), d) for d in (1, 0))

    def column(values):
        return jnp.sum(jnp.where(lane == line_of, values, 0), axis=1, keepdims=True)

    for slot in range(n):
        for part in range(2):
            here = slice((2 * slot + part) * half, (2 * slot + part + 1) * half)
            number = pairs[slot, part]
            positions = number * half + lax.broadcasted_iota(jnp.int32, (1, half), 1)
            documents = docs[pl.ds(number, 1), :]
            pos_row[:, here], doc_row[:, here] = positions, documents
            pos_col[here, :], doc_col[here, :] = column(positions), column(documents)
    loop(0, n, lambda i: fill_table(table, pos_col, i * 2 * half, 2 * half))
    for m in range(1, zs):
        params_line(m)[1].wait_recv()
    loop(1, n, lambda m: params_row(m)[0].start())
    for step in range(1, zs):

        def later(m, step=step):
            @pl.when(z >= step)
            def _():
                arrival(step - 1, m)[0].wait_recv()

            @pl.when((z >= step) & (z + 1 < zs))
            def _():
                chain(step, m)[0].start()

            @pl.when(z + step < zs)
            def _():
                arrival(step - 1, m)[1].wait_recv()

            @pl.when((z + step < zs) & (z > 0))
            def _():
                chain(step, m)[1].start()

        loop(0, n, later)
        forward_proj(step)
        if step == 1:
            for i in range(1, cu):
                x_far(i)[1].wait_recv()
                x_near(i)[0].start()
    loop(1, n, lambda m: params_row(m)[1].wait_recv())
    for i in range(cu):
        x_near(i)[1].wait_recv()
    loop(1, n, lambda m: exchange(m)[0].wait_send())
    loop(1, zs, lambda m: params_line(m)[0].wait_send())
    loop(1, n, lambda m: params_row(m)[0].wait_send())
    for i in range(cu):
        x_near(i)[0].wait_send()
        if i:
            x_far(i)[0].wait_send()
    for step in range(zs - 1):

        def sent(m, step=step):
            @pl.when((z >= step) & (z + 1 < zs))
            def _():
                chain(step, m)[0].wait_send()

            @pl.when((z + step < zs) & (z > 0))
            def _():
                chain(step, m)[1].wait_send()

        loop(0, n, sent)
        sent_proj(step)


def gather_head(x, small, qkv_weight, ffn_in, proj, pairs, docs):
    cu, cl, zs = sizes()
    n = cu * cl
    slab, cols = qkv_weight.shape
    cut = (n, slab, cols // n)
    pad = (8, LANES)
    rows = docs.shape[1]
    column, line = jax.ShapeDtypeStruct((rows, 1), jnp.int32), jax.ShapeDtypeStruct((1, rows), jnp.int32)
    return pl.pallas_call(
        head_kernel,
        in_specs=[ANY, VMEM, ANY, ANY, ANY, pl.BlockSpec(memory_space=pltpu.SMEM), VMEM],
        out_specs=[ANY, ANY, ANY, ANY, *[VMEM] * 6],
        out_shape=[
            jax.ShapeDtypeStruct((cu, cl, *x.shape), x.dtype),
            jax.ShapeDtypeStruct((n, zs, *pad), F32),
            jax.ShapeDtypeStruct((n, zs, *cut[1:]), BF16),
            jax.ShapeDtypeStruct((zs, *proj.shape), BF16),
            jax.ShapeDtypeStruct((cl * zs, ffn_in.shape[0], ffn_in.shape[1] // (cl * zs)), BF16),
            column, column, line, line, jax.ShapeDtypeStruct((rows, 3 * LANES), F32),
        ],
        scratch_shapes=[
            pltpu.VMEM(qkv_weight.shape, F32), pltpu.VMEM(ffn_in.shape, F32), pltpu.VMEM(proj.shape, F32),
            pltpu.VMEM((2 * n, rows // (2 * n)), jnp.int32), DMA((3,)),
            pltpu.VMEM(cut, BF16), pltpu.VMEM(proj.shape, BF16), pltpu.VMEM(pad, F32),
            DMA((4,)), DMA((cu,)), DMA((cu,)), DMA((cu,)), DMA((cu,)), DMA((zs,)), DMA((zs,)), DMA((n,)), DMA((n,)),
            DMA((n,)), DMA((n,)), *[DMA((zs, n + 1))] * 4,
        ],
        cost_estimate=pl.CostEstimate(flops=0, bytes_accessed=200 << 20, transcendentals=0),
        compiler_params=pltpu.CompilerParams(collective_id=0, has_side_effects=True, vmem_limit_bytes=48 << 20),
    )(x, small, qkv_weight, ffn_in, proj, pairs, docs)


ITEMS = 4


def loop(low, high, step):
    def run(m, carry):
        step(m)
        return carry

    lax.fori_loop(low, high, run, 0)


def bits_of(count):
    return [1 << b for b in range(count.bit_length() - 1)]


def combos(bits):
    masks = [0]
    for b in bits:
        masks = masks + [m | b for m in masks]
    return masks


def order_of(item, count):
    return bits_of(count) if item < ITEMS // 2 else bits_of(count)[::-1]


def add_low(left, right):
    return (left.astype(F32) + right.astype(F32)).astype(BF16)


class RowReduce:
    def __init__(self, parts, held, beside, came, load, sib_s, sib_r, out_s, out_r):
        self.parts, self.held, self.beside, self.came = parts, held, beside, came
        self.load, self.sib_s, self.sib_r, self.out_s, self.out_r = load, sib_s, sib_r, out_s, out_r
        self.u, self.c, self.z = place()
        self.count = sizes()[0]
        self.phases = self.count.bit_length() - 1

    def sib(self, mask):
        return Transfer(
            self.parts.at[flip(self.u, mask), 1 - self.c], self.beside.at[mask], self.sib_s.at[mask],
            self.sib_r.at[mask], (self.u, 1 - self.c, self.z),
        )

    def loading(self, mask):
        return pltpu.make_async_copy(
            self.parts.at[flip(self.u, mask), self.c], self.held.at[mask], self.load.at[mask]
        )

    def start(self):
        for mask in reversed(range(self.count)):
            self.sib(mask).start()
            self.loading(mask).start()

    def merge(self):
        for mask in reversed(range(self.count)):
            self.loading(mask).wait()
            self.sib(mask).wait_recv()
            self.held[mask] = add_low(self.held[mask], self.beside[mask])

    def steps(self, item, phase):
        order = order_of(item, self.count)
        slot = self.count - (self.count >> phase)
        for k, rest in enumerate(combos(order[phase + 1 :])):
            yield slot + k, rest, Transfer(
                self.held.at[order[phase] | rest, item], self.came.at[slot + k, item], self.out_s.at[slot + k, item],
                self.out_r.at[slot + k, item], (flip(self.u, order[phase]), self.c, self.z),
            )

    def send(self, item, phase):
        for _, _, transfer in self.steps(item, phase):
            transfer.start()

    def add(self, item, phase):
        for slot, rest, transfer in self.steps(item, phase):
            transfer.wait_recv()
            self.held[rest, item] = add_low(self.held[rest, item], self.came[slot, item])

    def total(self, item):
        ((slot, _, transfer),) = self.steps(item, self.phases - 1)
        transfer.wait_recv()
        return self.held[0, item].astype(F32) + self.came[slot, item].astype(F32)

    def drain(self):
        for mask in range(self.count):
            self.sib(mask).wait_send()
        for item in range(ITEMS):
            for phase in range(self.phases):
                for _, _, transfer in self.steps(item, phase):
                    transfer.wait_send()

    @staticmethod
    def scratch(count, rows, width):
        block = (count, ITEMS, rows // ITEMS, width)
        return [
            pltpu.VMEM(block, BF16), pltpu.VMEM(block, BF16), pltpu.VMEM(block, BF16), DMA((count,)), DMA((count,)),
            DMA((count,)), DMA((count, ITEMS)), DMA((count, ITEMS)),
        ]


class RowGather:
    def __init__(self, own, full, keep, out_s, out_r, sib_s, sib_r):
        self.own, self.full, self.keep = own, full, keep
        self.out_s, self.out_r, self.sib_s, self.sib_r = out_s, out_r, sib_s, sib_r
        self.u, self.c, self.z = place()
        self.count = sizes()[0]
        self.phases = self.count.bit_length() - 1

    def kept(self, item):
        return pltpu.make_async_copy(self.own.at[item], self.full.at[self.u, self.c, item], self.keep.at[item])

    def source(self, mask, item):
        return self.own.at[item] if mask == 0 else self.full.at[flip(self.u, mask), self.c, item]

    def sib(self, mask, item):
        return Transfer(
            self.source(mask, item), self.full.at[flip(self.u, mask), self.c, item], self.sib_s.at[mask, item],
            self.sib_r.at[mask, item], (self.u, 1 - self.c, self.z),
        )

    def steps(self, item, phase):
        order = order_of(item, self.count)
        for k, mask in enumerate(combos(order[:phase])):
            slot = (1 << phase) - 1 + k
            yield mask | order[phase], Transfer(
                self.source(mask, item), self.full.at[flip(self.u, mask), self.c, item], self.out_s.at[slot, item],
                self.out_r.at[slot, item], (flip(self.u, order[phase]), self.c, self.z),
            )

    def start(self, item):
        self.send(item, 0)
        self.sib(0, item).start()
        self.kept(item).start()

    def send(self, item, phase):
        for _, transfer in self.steps(item, phase):
            transfer.start()

    def pass_on(self, item, phase):
        for mask, transfer in self.steps(item, phase):
            transfer.wait_recv()
            self.sib(mask, item).start()

    def drain(self):
        for item in range(ITEMS):
            self.kept(item).wait()
            for mask in range(self.count):
                self.sib(mask, item).wait()
            for phase in range(self.phases):
                for _, transfer in self.steps(item, phase):
                    transfer.wait_send()

    @staticmethod
    def scratch(count):
        return [DMA((ITEMS,)), *[DMA((count, ITEMS))] * 4]


class PlaneGather:
    def __init__(self, own, full, keep, out_s, out_r):
        self.own, self.full, self.keep, self.out_s, self.out_r = own, full, keep, out_s, out_r
        self.u, self.c, self.z = place()
        self.count = sizes()[0]
        self.items = own.shape[0]
        self.phases = self.count.bit_length() - 1

    def kept(self, item):
        return pltpu.make_async_copy(self.own.at[item], self.full.at[self.u, item], self.keep.at[item])

    def steps(self, item, phase):
        order = bits_of(self.count) if item % 2 else bits_of(self.count)[::-1]
        for k, mask in enumerate(combos(order[:phase])):
            slot = (1 << phase) - 1 + k
            block = self.full.at[flip(self.u, mask), item]
            yield Transfer(
                self.own.at[item] if mask == 0 else block, block, self.out_s.at[slot, item],
                self.out_r.at[slot, item], (flip(self.u, order[phase]), self.c, self.z),
            )

    def start(self):
        for item in range(self.items):
            self.kept(item).start()
            for transfer in self.steps(item, 0):
                transfer.start()

    def step(self, phase):
        for item in range(self.items):
            for transfer in self.steps(item, phase - 1):
                transfer.wait_recv()
            if phase < self.phases:
                for transfer in self.steps(item, phase):
                    transfer.start()

    def drain(self):
        for item in range(self.items):
            self.kept(item).wait()
            for phase in range(self.phases):
                for transfer in self.steps(item, phase):
                    transfer.wait_send()

    @staticmethod
    def scratch(count, items):
        return [DMA((items,)), DMA((count, items)), DMA((count, items))]


class LineGather:
    def __init__(self, own, full, keep, up_s, up_r, dn_s, dn_r, sib_s, sib_r):
        self.own, self.full, self.keep = own, full, keep
        self.up_s, self.up_r, self.dn_s, self.dn_r, self.sib_s, self.sib_r = up_s, up_r, dn_s, dn_r, sib_s, sib_r
        self.u, self.c, self.z = place()
        self.count = sizes()[2]

    def kept(self, item):
        return pltpu.make_async_copy(self.own.at[item], self.full.at[self.z, self.c, item], self.keep.at[item])

    def up(self, item, step):
        origin = lax.rem(self.z - step + self.count, self.count)
        block = self.full.at[origin, self.c, item]
        source = self.own.at[item] if step == 0 else block
        to = lax.rem(self.z + 1, self.count)
        return Transfer(source, block, self.up_s.at[step, item], self.up_r.at[step, item], (self.u, self.c, to))

    def down(self, item, step):
        block = self.full.at[lax.rem(self.z + step, self.count), self.c, item]
        source = self.own.at[item] if step == 0 else block
        to = lax.rem(self.z - 1 + self.count, self.count)
        return Transfer(source, block, self.dn_s.at[step, item], self.dn_r.at[step, item], (self.u, self.c, to))

    def sib(self, item, origin, own=False):
        block = self.full.at[origin, self.c, item]
        return Transfer(
            self.own.at[item] if own else block, block, self.sib_s.at[origin, item], self.sib_r.at[origin, item],
            (self.u, 1 - self.c, self.z),
        )

    def start(self, item):
        @pl.when(self.z + 1 < self.count)
        def _():
            self.up(item, 0).start()

        @pl.when(self.z > 0)
        def _():
            self.down(item, 0).start()

        self.sib(item, self.z, True).start()
        self.kept(item).start()

    def forward(self, item, step):
        z, count = self.z, self.count

        @pl.when(z >= step)
        def _():
            self.up(item, step - 1).wait_recv()
            if step < count - 1:

                @pl.when(z + 1 < count)
                def _():
                    self.up(item, step).start()

            self.sib(item, z - step).start()

        @pl.when(z + step < count)
        def _():
            self.down(item, step - 1).wait_recv()
            if step < count - 1:

                @pl.when(z > 0)
                def _():
                    self.down(item, step).start()

            self.sib(item, z + step).start()

    def drain(self):
        z, count = self.z, self.count
        for item in range(ITEMS):
            self.kept(item).wait()
            for origin in range(count):
                self.sib(item, origin).wait()
            for step in range(count - 1):

                @pl.when((z >= step) & (z + 1 < count))
                def _(item=item, step=step):
                    self.up(item, step).wait_send()

                @pl.when((z + step < count) & (z > 0))
                def _(item=item, step=step):
                    self.down(item, step).wait_send()

    @staticmethod
    def scratch(count):
        return [DMA((ITEMS,)), *[DMA((count, ITEMS))] * 6]


def far_first(count, z):
    table = []
    for i in range(count):
        ends = sorted(range(count), key=lambda to: (-abs(to - i), 0 if (to > i) == (2 * i < count) else 1))
        lead = [to for to in ends if (to > i) == (2 * i < count) and to != i]
        rest = [to for to in ends if (to > i) != (2 * i < count) and to != i]
        mixed = []
        while lead or rest:
            mixed += lead[:1] + rest[:1]
            lead, rest = lead[1:], rest[1:]
        table.append(mixed + [i])
    power, term = 1, 1
    for k in range(1, count):
        term = (term * (z - k + 1) * (count - 1)) // k
        power = power + term
    packed = [sum(table[i][k] * count**i for i in range(count)) for k in range(count)]
    return [lax.rem(p // power, count) for p in packed]


class LineReduce:
    def __init__(self, held, from_below, from_above, pieces, up_s, up_r, dn_s, dn_r):
        self.held, self.from_below, self.from_above, self.pieces = held, from_below, from_above, pieces
        self.up_s, self.up_r, self.dn_s, self.dn_r = up_s, up_r, dn_s, dn_r
        self.u, self.c, self.z = place()
        self.count = sizes()[2]

    def up(self, to, piece):
        return Transfer(
            self.held.at[to, piece], self.from_below.at[to, piece], self.up_s.at[to, piece], self.up_r.at[to, piece],
            (self.u, self.c, lax.rem(self.z + 1, self.count)),
        )

    def down(self, to, piece):
        return Transfer(
            self.held.at[to, piece], self.from_above.at[to, piece], self.dn_s.at[to, piece], self.dn_r.at[to, piece],
            (self.u, self.c, lax.rem(self.z - 1 + self.count, self.count)),
        )

    def step(self, t):
        z, count = self.z, self.count
        far_up, far_down = count - 1 - t, t

        def upward(piece):
            @pl.when(z > 0)
            def _():
                self.up(far_up, piece).wait_recv()
                self.held[far_up, piece] = add_low(self.held[far_up, piece], self.from_below[far_up, piece])

            self.up(far_up, piece).start()

        def downward(piece):
            @pl.when(z < count - 1)
            def _():
                self.down(far_down, piece).wait_recv()
                self.held[far_down, piece] = add_low(self.held[far_down, piece], self.from_above[far_down, piece])

            self.down(far_down, piece).start()

        lag = min(3, self.pieces // 2)
        late_up = lag * ((2 * z) // count)

        def one(i):
            piece_up, piece_down = i - late_up, i - (lag - late_up)

            @pl.when((z < far_up) & (piece_up >= 0) & (piece_up < self.pieces))
            def _():
                upward(piece_up)

            @pl.when((z > far_down) & (piece_down >= 0) & (piece_down < self.pieces))
            def _():
                downward(piece_down)

        loop(0, self.pieces + lag, one)

    def total(self, piece, into):
        z, count = self.z, self.count
        into[...] = self.held[z, piece].astype(F32)

        @pl.when(z > 0)
        def _():
            self.up(z, piece).wait_recv()
            into[...] += self.from_below[z, piece].astype(F32)

        @pl.when(z < count - 1)
        def _():
            self.down(z, piece).wait_recv()
            into[...] += self.from_above[z, piece].astype(F32)

    def drain(self):
        z, count = self.z, self.count
        for t in range(count - 1):
            far_up, far_down = count - 1 - t, t

            def one(piece, far_up=far_up, far_down=far_down):
                @pl.when(z < far_up)
                def _():
                    self.up(far_up, piece).wait_send()

                @pl.when(z > far_down)
                def _():
                    self.down(far_down, piece).wait_send()

            loop(0, self.pieces, one)

    @staticmethod
    def scratch(count, pieces, block):
        shape = (count, pieces, *block)
        return [*[pltpu.VMEM(shape, BF16)] * 3, *[DMA((count, pieces))] * 4]


def mid_forward_kernel(branch, x, out_grad, params, cut, hidden, mlp, grads, weight, low, *scratch):
    reduce = RowReduce(branch, *scratch[:8])
    gather = LineGather(low, mlp, *scratch[8:15])
    gather_grads = LineGather(out_grad, grads, *scratch[15:22])
    plane = PlaneGather(cut, weight, *scratch[22:])
    greet(True, True)
    reduce.start()
    for item in range(ITEMS):
        gather_grads.start(item)
    reduce.merge()
    for item in range(ITEMS):
        reduce.send(item, 0)
    plane.start()
    for item in range(ITEMS):
        gather_grads.forward(item, 1)
    for phase in range(1, reduce.phases):
        for item in range(ITEMS):
            reduce.add(item, phase - 1)
            reduce.send(item, phase)
    for step in range(2, gather.count - 1):
        for item in range(ITEMS):
            gather_grads.forward(item, step)
    for item in range(ITEMS):
        state = x[item].astype(F32) + reduce.total(item)
        hidden[item] = state
        low[item] = norm_rows(state, params[0:1], params[1:2])[0].astype(BF16)
        gather.start(item)
    plane.step(1)
    for step in range(1, gather.count):
        for item in range(ITEMS):
            gather.forward(item, step)
        if step == 1:
            for item in range(ITEMS):
                gather_grads.forward(item, gather.count - 1)
    for phase in range(2, plane.phases + 1):
        plane.step(phase)
    gather_grads.drain()
    gather.drain()
    plane.drain()
    reduce.drain()


def mid_forward(branch, x, out_grad, params, cut):
    cu, cl, zs = sizes()
    rows, width = x.shape
    block = (ITEMS, rows // ITEMS, width)
    full = jax.ShapeDtypeStruct((zs, cl, *block), BF16)
    hidden, mlp, grads, weight, _ = pl.pallas_call(
        mid_forward_kernel,
        in_specs=[ANY, VMEM, VMEM, VMEM, ANY],
        out_specs=[VMEM, ANY, ANY, ANY, VMEM],
        out_shape=[
            jax.ShapeDtypeStruct(block, F32), full, full, jax.ShapeDtypeStruct((cu, *cut.shape), BF16),
            jax.ShapeDtypeStruct(block, BF16),
        ],
        scratch_shapes=[
            *RowReduce.scratch(cu, rows, width), *LineGather.scratch(zs), *LineGather.scratch(zs),
            *PlaneGather.scratch(cu, cut.shape[0]),
        ],
        cost_estimate=pl.CostEstimate(flops=0, bytes_accessed=200 << 20, transcendentals=0),
        compiler_params=pltpu.CompilerParams(collective_id=1, has_side_effects=True, vmem_limit_bytes=56 << 20),
    )(branch.reshape(cu, cl, *block), x.reshape(block), out_grad.reshape(block), params, cut)
    group_rows = cl * zs * rows
    return (
        hidden.reshape(rows, width), mlp.reshape(group_rows, width), grads.reshape(group_rows, width),
        weight.reshape(width, cut.shape[2]),
    )


def mid_backward_kernel(
    back, in_weight, hidden, out_grad, params, inner, weight, grads,
    grad_hidden, full, sums, layer_out, weight_grad, low,
    held, below, above, up_s, up_r, dn_s, dn_r, both, beside, total, sib_s, sib_r,
    held_out, below_out, above_out, up_so, up_ro, dn_so, dn_ro, both_out, beside_out, sib_so, sib_ro,
    back_v, in_weight_v, inner_v, weight_v, grads_v, fetch, *scratch,
):
    u, c, z = place()
    _, cl, zs = sizes()
    rows = ITEMS * held.shape[2]
    width = weight_v.shape[1]
    reduce = LineReduce(held, below, above, ITEMS, up_s, up_r, dn_s, dn_r)
    reduce_out = LineReduce(held_out, below_out, above_out, ITEMS, up_so, up_ro, dn_so, dn_ro)
    gather = RowGather(low, full, *scratch)
    fetches = [
        pltpu.make_async_copy(source, into, fetch.at[i])
        for i, (source, into) in enumerate(
            ((back, back_v), (in_weight, in_weight_v), (inner, inner_v), (weight, weight_v), (grads, grads_v))
        )
    ]
    for copy in fetches:
        copy.start()

    def sib(to):
        return Transfer(both.at[to, 1 - c], beside.at[to], sib_s.at[to], sib_r.at[to], (u, 1 - c, z))

    def sib_out(to):
        return Transfer(both_out.at[to, 1 - c], beside_out.at[to], sib_so.at[to], sib_ro.at[to], (u, 1 - c, z))

    tile = 512

    def multiply(to, into, left, product):
        def one(i):
            cols = pl.ds(pl.multiple_of(i * tile, tile), tile)
            here = pl.ds(pl.multiple_of(to * (cl * rows), cl * rows), cl * rows)
            part = product(left[here], cols).astype(BF16)
            into[to, :, :, :, cols] = part.reshape(cl, ITEMS, rows // ITEMS, tile)

        loop(0, width // tile, one)

    order = far_first(zs, z)
    fetches[0].wait()
    fetches[1].wait()
    multiply(order[0], both, back_v, lambda left, cols: dot_t(left, in_weight_v[cols]))
    greet(True, True)
    sib(order[0]).start()
    def settle(to):
        sib(to).wait_recv()
        held[to] = add_low(both[to, c], beside[to])

    def settle_out(to):
        sib_out(to).wait_recv()
        held_out[to] = add_low(both_out[to, c], beside_out[to])

    at_end = (z == 0) | (z == zs - 1)
    inside = jnp.logical_not(at_end)
    for k in range(1, zs):
        multiply(order[k], both, back_v, lambda left, cols: dot_t(left, in_weight_v[cols]))
        sib(order[k]).start()
        settle(order[k - 1])

        @pl.when(at_end)
        def _(t=k - 1):
            reduce.step(t)

    settle(order[zs - 1])

    @pl.when(inside)
    def _():
        reduce.step(0)

    fetches[2].wait()
    fetches[3].wait()
    for k in range(zs):
        multiply(
            order[k], both_out, inner_v,
            lambda left, cols: jnp.dot(left, weight_v[:, cols], preferred_element_type=F32),
        )
        sib_out(order[k]).start()

    @pl.when(inside)
    def _():
        for t in range(1, zs - 1):
            reduce.step(t)

    for to in order:
        settle_out(to)

    @pl.when(at_end)
    def _():
        for t in range(zs - 1):
            reduce_out.step(t)

    sums[...] = jnp.zeros_like(sums)
    for item in range(ITEMS):
        reduce.total(item, total)
        _, hat, inverse = norm_rows(hidden[item], params[0:1], params[1:2])
        grad = total[...]
        sums[0:1] += jnp.sum(grad * hat, axis=0, keepdims=True)
        sums[1:2] += jnp.sum(grad, axis=0, keepdims=True)
        grad = out_grad[item].astype(F32) + norm_back(grad, hat, inverse, params[0:1])
        grad_hidden[item] = grad
        low[item] = grad.astype(BF16)
        gather.start(item)
    fetches[4].wait()

    def outer(i):
        cols = pl.ds(pl.multiple_of(i * tile, tile), tile)
        weight_grad[:, cols] = cross_dot(inner_v[...], grads_v[:, cols]).astype(BF16)

    loop(0, width // tile, outer)
    for phase in range(gather.phases):
        for item in range(ITEMS):
            gather.pass_on(item, phase)
            if phase + 1 < gather.phases:
                gather.send(item, phase + 1)
        if phase == 0:

            @pl.when(inside)
            def _():
                reduce_out.step(0)

    @pl.when(inside)
    def _():
        for t in range(1, zs - 1):
            reduce_out.step(t)

    for item in range(ITEMS):
        reduce_out.total(item, total)
        layer_out[item] = (hidden[item] + total[...]).astype(BF16)
    gather.drain()
    reduce.drain()
    reduce_out.drain()
    for to in range(zs):
        sib(to).wait_send()
        sib_out(to).wait_send()


def mid_backward(back_rows, in_weight, hidden, out_grad, params, inner, weight, grads):
    cu, cl, zs = sizes()
    rows, width = out_grad.shape
    block = (ITEMS, rows // ITEMS, width)
    shares = pltpu.VMEM((zs, *block), BF16)
    both = pltpu.VMEM((zs, cl, *block), BF16)
    grad_hidden, full, sums, layer_out, weight_grad, _ = pl.pallas_call(
        mid_backward_kernel,
        in_specs=[ANY, ANY, VMEM, VMEM, VMEM, ANY, ANY, ANY],
        out_specs=[VMEM, ANY, VMEM, VMEM, VMEM, VMEM],
        out_shape=[
            jax.ShapeDtypeStruct(block, F32),
            jax.ShapeDtypeStruct((cu, cl, *block), BF16),
            jax.ShapeDtypeStruct((2, width), F32),
            jax.ShapeDtypeStruct(block, BF16),
            jax.ShapeDtypeStruct(weight.shape, BF16),
            jax.ShapeDtypeStruct(block, BF16),
        ],
        scratch_shapes=[
            *LineReduce.scratch(zs, ITEMS, block[1:]), both, shares, pltpu.VMEM(block[1:], F32), DMA((zs,)), DMA((zs,)),
            *LineReduce.scratch(zs, ITEMS, block[1:]), both, shares, DMA((zs,)), DMA((zs,)),
            pltpu.VMEM(back_rows.shape, BF16), pltpu.VMEM(in_weight.shape, BF16), pltpu.VMEM(inner.shape, BF16),
            pltpu.VMEM(weight.shape, BF16), pltpu.VMEM(grads.shape, BF16), DMA((5,)), *RowGather.scratch(cu),
        ],
        cost_estimate=pl.CostEstimate(flops=0, bytes_accessed=200 << 20, transcendentals=0),
        compiler_params=pltpu.CompilerParams(collective_id=2, has_side_effects=True, vmem_limit_bytes=62 << 20),
    )(back_rows, in_weight, hidden.reshape(block), out_grad.reshape(block), params, inner, weight, grads)
    return (
        grad_hidden.reshape(rows, width), full.reshape(cu * cl * rows, width), sums, layer_out.reshape(rows, width),
        weight_grad,
    )


def tail_kernel(parts, x, grad_hidden, params, terms, grads, proj, input_grad, small, cut, proj_grad, pile, line_in, row_in, total,
                row_total, line_s, line_r, row_s, row_r, a_send, a_recv, own, held_load, low, *scratch):
    u, c, z = place()
    cu, cl, zs = sizes()
    n, me = cu * cl, u * cl + c
    reduce = RowReduce(parts, *scratch[:8])
    held, held_proj = scratch[8], scratch[15]
    line = LineReduce(*scratch[8:11], n, *scratch[11:15])
    line_proj = LineReduce(*scratch[15:18], 1, *scratch[18:])
    load = pltpu.make_async_copy(grads, held, held_load.at[0])
    load_proj = pltpu.make_async_copy(proj, held_proj, held_load.at[1])
    load.start()
    load_proj.start()
    greet(True, True)
    reduce.start()
    load.wait()
    load_proj.wait()
    line.step(0)
    line_proj.step(0)
    reduce.merge()
    for item in range(ITEMS):
        reduce.send(item, 0)
    for t in range(1, zs - 1):
        line.step(t)
        line_proj.step(t)
    for phase in range(1, reduce.phases):
        for item in range(ITEMS):
            reduce.add(item, phase - 1)
            reduce.send(item, phase)
    pile[...] = terms[...]
    for item in range(ITEMS):
        grad = reduce.total(item)
        _, hat, inverse = norm_rows(x[item].astype(F32), params[0:1], params[1:2])
        pile[0:1] += jnp.sum(grad * hat, axis=0, keepdims=True)
        pile[1:2] += jnp.sum(grad, axis=0, keepdims=True)
        grad = grad_hidden[item] + norm_back(grad, hat, inverse, params[0:1])
        input_grad[item] = grad.astype(BF16)

    def along_line(m):
        return Transfer(pile, line_in.at[m], line_s.at[m], line_r.at[m], (u, c, lax.rem(z + m, zs)))

    def along_row(m):
        other = lax.rem(me + m, n)
        return Transfer(
            total, row_in.at[m], row_s.at[m], row_r.at[m], (other // cl, lax.rem(other, cl), z)
        )

    def exchange(m):
        other = lax.rem(me + m, n)
        return Transfer(
            low.at[other], cut.at[me], a_send.at[m], a_recv.at[m], (other // cl, lax.rem(other, cl), z)
        )

    def landed(m):
        source = lax.rem(me - m + n, n)
        return Transfer(
            low.at[source], cut.at[source], a_send.at[m], a_recv.at[m], (u, 1 - c, z)
        )

    loop(1, zs, lambda m: along_line(m).start())

    def finish(m):
        piece = lax.rem(me + m, n)
        line.total(piece, row_total)
        low[piece] = row_total[...].astype(BF16)

        @pl.when(m > 0)
        def _():
            exchange(m).start()

    loop(0, n, finish)
    line_proj.total(0, proj_grad)
    mine = pltpu.make_async_copy(low.at[me], cut.at[me], own.at[0])
    mine.start()
    total[...] = pile[...]
    for m in range(1, zs):
        along_line(m).wait_recv()
        total[...] += line_in[m]
    loop(1, n, lambda m: along_row(m).start())
    small[...] = total[...]

    def collect(m):
        along_row(m).wait_recv()
        small[...] += row_in[m]

    loop(1, n, collect)
    loop(1, n, lambda m: landed(m).wait_recv())
    mine.wait()
    loop(1, n, lambda m: exchange(m).wait_send())
    loop(1, n, lambda m: along_row(m).wait_send())
    loop(1, zs, lambda m: along_line(m).wait_send())
    reduce.drain()
    line.drain()
    line_proj.drain()


def tail(parts, x, grad_hidden, params, terms, grads, proj):
    cu, cl, zs = sizes()
    n = cu * cl
    rows, width = x.shape
    block = (ITEMS, rows // ITEMS, width)
    piece = grads.shape[2:]
    input_grad, small, cut, proj_grad = pl.pallas_call(
        tail_kernel,
        in_specs=[ANY, VMEM, VMEM, VMEM, VMEM, ANY, ANY],
        out_specs=[VMEM, VMEM, ANY, VMEM],
        out_shape=[
            jax.ShapeDtypeStruct(block, BF16),
            jax.ShapeDtypeStruct((8, width), F32),
            jax.ShapeDtypeStruct((n, *piece), BF16),
            jax.ShapeDtypeStruct(proj.shape[2:], F32),
        ],
        scratch_shapes=[
            pltpu.VMEM((8, width), F32), pltpu.VMEM((zs, 8, width), F32), pltpu.VMEM((n, 8, width), F32),
            pltpu.VMEM((8, width), F32), pltpu.VMEM(piece, F32), DMA((zs,)), DMA((zs,)), DMA((n,)), DMA((n,)),
            DMA((n,)), DMA((n,)), DMA((1,)), DMA((2,)), pltpu.VMEM((n, *piece), BF16),
            *RowReduce.scratch(cu, rows, width), *LineReduce.scratch(zs, n, piece),
            *LineReduce.scratch(zs, 1, proj.shape[2:]),
        ],
        cost_estimate=pl.CostEstimate(flops=0, bytes_accessed=200 << 20, transcendentals=0),
        compiler_params=pltpu.CompilerParams(collective_id=3, has_side_effects=True, vmem_limit_bytes=60 << 20),
    )(parts.reshape(cu, cl, *block), x.reshape(block), grad_hidden.reshape(block), params, terms, grads, proj)
    return input_grad.reshape(rows, width), small, cut, proj_grad


def back_kernel(
    heads, qkv_ref, low_ref, tot_ref, pq_ref, dq_ref, pk_ref, dk_ref, table_ref,
    x, grad_hidden, params, mid_sums, branch, proj, mixed, normed, weight, in_cut,
    input_grad, small, cut, proj_grad, in_pieces,
    gq_ref, gk_ref, gv_ref, joined_ref, branch_ref, proj_ref, mixed_ref, normed_v, weight_v, parts, fetch, in_s, in_r,
    pile, line_in, row_in, total, row_total, line_s, line_r, row_s, row_r, a_s, a_r, own, low, *scratch,
):
    u, c, z = place()
    cu, cl, zs = sizes()
    n, me = cu * cl, u * cl + c
    width = heads * HEAD_DIM
    rows = qkv_ref.shape[0]
    block = row_block(rows)
    slab = low.shape[1]
    group = in_cut.shape[0]
    reduce = RowReduce(parts, *scratch[:8])
    held, held_proj = scratch[8], scratch[15]
    line = LineReduce(*scratch[8:11], n, *scratch[11:15])
    line_proj = LineReduce(*scratch[15:18], 1, *scratch[18:])
    my_place = in_group(0)[3]
    kept = pltpu.make_async_copy(in_cut.at[my_place], in_pieces.at[my_place], own.at[1])
    fetches = [
        pltpu.make_async_copy(source, into, fetch.at[i])
        for i, (source, into) in enumerate(
            ((branch, branch_ref), (proj, proj_ref), (mixed, mixed_ref), (normed, normed_v), (weight, weight_v))
        )
    ]

    def in_exchange(m):
        device, after, _, mine = in_group(m)
        return Transfer(in_cut.at[after], in_pieces.at[mine], in_s.at[m], in_r.at[m], device)

    def in_landed(m):
        device, _, before, _ = in_group(m)
        return Transfer(in_cut.at[before], in_pieces.at[before], in_s.at[m], in_r.at[m], device)

    for copy in (kept, *fetches):
        copy.start()
    greet(True, True, True)
    loop(1, group, lambda m: in_exchange(m).start())
    for copy in fetches[:3]:
        copy.wait()
    tile = 512

    def proj_tile(i):
        cols = pl.ds(pl.multiple_of(i * tile, tile), tile)
        grad = cross_dot(low_ref[...], branch_ref[:, cols]).astype(BF16)
        held_proj[:, 0, :, cols] = grad.reshape(zs, slab, tile)

    loop(0, D // tile, proj_tile)
    at_end = (z == 0) | (z == zs - 1)

    @pl.when(at_end)
    def _():
        for t in range(zs - 1):
            line_proj.step(t)

    gk_ref[...] = jnp.zeros_like(gk_ref)
    gv_ref[...] = jnp.zeros_like(gv_ref)

    def one(step):
        here = pl.ds(pl.multiple_of(step * block, block), block)
        grad_all = dot_t(branch_ref[here], proj_ref[...])
        allowed = (pk_ref[...] <= pq_ref[here]) & (dk_ref[...] == dq_ref[here])
        for head in range(heads):
            cols, key, value = (
                slice(p * width + head * HEAD_DIM, p * width + (head + 1) * HEAD_DIM) for p in range(3)
            )
            q, k, v = qkv_ref[here, cols], qkv_ref[:, key], qkv_ref[:, value]
            inverse = 1.0 / tot_ref[here, head : head + 1]
            grad_mixed = grad_all[:, cols]
            grad_weighted = (grad_mixed * inverse).astype(BF16)
            grad_total = -jnp.sum(grad_mixed * mixed_ref[here, cols], axis=1, keepdims=True) * inverse
            weights = jnp.where(allowed, jnp.exp(dot_t(q, k) * SCALE), 0.0)
            grad_scores = (weights * (dot_t(grad_weighted, v) + grad_total)).astype(BF16)
            gq_ref[here, cols] = jnp.dot(grad_scores, k, preferred_element_type=F32) * SCALE
            gk_ref[:, cols] += cross_dot(grad_scores, q) * SCALE
            gv_ref[:, cols] += cross_dot(weights.astype(BF16), grad_weighted)

    blocks = rows // block
    loop(0, blocks // 2, one)

    @pl.when(jnp.logical_not(at_end))
    def _():
        line_proj.step(0)

    loop(blocks // 2, blocks, one)

    @pl.when(jnp.logical_not(at_end))
    def _():
        for t in range(1, zs - 1):
            line_proj.step(t)


    pile[...] = jnp.zeros_like(pile)
    for part, ref in enumerate((gq_ref, gk_ref, gv_ref)):
        for start in range(0, width, LANES):
            grad = ref[:, start : start + LANES]
            if part < 2:
                grad = turn(grad, table_ref[...], -1.0)
            grad = grad.astype(BF16)
            joined_ref[:, part * width + start : part * width + start + LANES] = grad
            there = pl.ds(pl.multiple_of(me * width + start, LANES), LANES)
            pile[4 + part : 5 + part, there] = jnp.sum(grad.astype(F32), axis=0, keepdims=True)
    for copy in fetches[3:]:
        copy.wait()

    def qkv_tile(i):
        cols = pl.ds(pl.multiple_of(i * zs * slab, zs * slab), zs * slab)
        grad = cross_dot(normed_v[:, cols], joined_ref[...]).astype(BF16)
        for to in range(zs):
            held[to, i] = grad[to * slab : (to + 1) * slab]

    loop(0, n, qkv_tile)

    @pl.when(at_end)
    def _():
        for t in range(zs - 1):
            line.step(t)


    def norm_tile(i):
        to, col = i // (D // tile), lax.rem(i, D // tile) * tile
        cols = pl.ds(pl.multiple_of(col, tile), tile)
        here = pl.ds(pl.multiple_of(to * (rows // cu), rows // cu), rows // cu)
        part = dot_t(joined_ref[here], weight_v[cols]).astype(BF16)
        parts[to, :, :, :, cols] = part.reshape(cl, ITEMS, rows // (n * ITEMS), tile)

    loop(0, cu * (D // tile), norm_tile)
    reduce.start()
    reduce.merge()
    for item in range(ITEMS):
        reduce.send(item, 0)

    @pl.when(jnp.logical_not(at_end))
    def _():
        line.step(0)

    for phase in range(1, reduce.phases):
        for item in range(ITEMS):
            reduce.add(item, phase - 1)
            reduce.send(item, phase)
    pile[2:4] = mid_sums[...]
    for item in range(ITEMS):
        grad = reduce.total(item)
        _, hat, inverse = norm_rows(x[item].astype(F32), params[0:1], params[1:2])
        pile[0:1] += jnp.sum(grad * hat, axis=0, keepdims=True)
        pile[1:2] += jnp.sum(grad, axis=0, keepdims=True)
        grad = grad_hidden[item] + norm_back(grad, hat, inverse, params[0:1])
        input_grad[item] = grad.astype(BF16)

    def along_line(m):
        return Transfer(pile, line_in.at[m], line_s.at[m], line_r.at[m], (u, c, lax.rem(z + m, zs)))

    def along_row(m):
        other = lax.rem(me + m, n)
        return Transfer(total, row_in.at[m], row_s.at[m], row_r.at[m], (other // cl, lax.rem(other, cl), z))

    def exchange(m):
        other = lax.rem(me + m, n)
        return Transfer(low.at[other], cut.at[me], a_s.at[m], a_r.at[m], (other // cl, lax.rem(other, cl), z))

    def landed(m):
        source = lax.rem(me - m + n, n)
        return Transfer(low.at[source], cut.at[source], a_s.at[m], a_r.at[m], (u, 1 - c, z))

    loop(1, zs, lambda m: along_line(m).start())

    @pl.when(jnp.logical_not(at_end))
    def _():
        for t in range(1, zs - 1):
            line.step(t)

    total[...] = pile[...]
    for m in range(1, zs):
        along_line(m).wait_recv()
        total[...] += line_in[m]
    loop(1, n, lambda m: along_row(m).start())

    def finish(piece):
        line.total(piece, row_total)
        low[piece] = row_total[...].astype(BF16)
        m = lax.rem(piece - me + n, n)

        @pl.when(m > 0)
        def _():
            exchange(m).start()

    loop(0, n, finish)
    mine = pltpu.make_async_copy(low.at[me], cut.at[me], own.at[0])
    mine.start()
    line_proj.total(0, proj_grad)
    small[...] = total[...]

    def collect(m):
        along_row(m).wait_recv()
        small[...] += row_in[m]

    loop(1, n, collect)
    loop(1, group, lambda m: in_landed(m).wait_recv())
    loop(1, n, lambda m: landed(m).wait_recv())
    mine.wait()
    kept.wait()
    loop(1, group, lambda m: in_exchange(m).wait_send())
    loop(1, n, lambda m: exchange(m).wait_send())
    loop(1, n, lambda m: along_row(m).wait_send())
    loop(1, zs, lambda m: along_line(m).wait_send())
    reduce.drain()
    line.drain()
    line_proj.drain()


def back(qkv, grad_branch, proj, mixed, mixed_low, totals, marks, table, x, grad_hidden, params, mid_sums, normed,
         weight, in_cut, heads):
    cu, cl, zs = sizes()
    n = cu * cl
    rows, width = x.shape
    total_rows, cols = qkv.shape
    slab = width // (n * zs)
    block = (ITEMS, rows // ITEMS, width)
    piece = (slab, cols)
    group = in_cut.shape[0]
    input_grad, small, cut, proj_grad, in_pieces = pl.pallas_call(
        functools.partial(back_kernel, heads),
        in_specs=[*[VMEM] * 12, *[ANY] * 6],
        out_specs=[VMEM, VMEM, ANY, VMEM, ANY],
        out_shape=[
            jax.ShapeDtypeStruct(block, BF16),
            jax.ShapeDtypeStruct((8, width), F32),
            jax.ShapeDtypeStruct((n, *piece), BF16),
            jax.ShapeDtypeStruct((slab, width), F32),
            jax.ShapeDtypeStruct(in_cut.shape, BF16),
        ],
        scratch_shapes=[
            *[pltpu.VMEM((total_rows, cols // 3), F32)] * 3, pltpu.VMEM(qkv.shape, BF16),
            pltpu.VMEM(grad_branch.shape, BF16), pltpu.VMEM(proj.shape, BF16), pltpu.VMEM(mixed.shape, F32),
            pltpu.VMEM(normed.shape, BF16), pltpu.VMEM(weight.shape, BF16), pltpu.VMEM((cu, cl, *block), BF16),
            DMA((5,)), DMA((group,)), DMA((group,)),
            pltpu.VMEM((8, width), F32), pltpu.VMEM((zs, 8, width), F32), pltpu.VMEM((n, 8, width), F32),
            pltpu.VMEM((8, width), F32), pltpu.VMEM(piece, F32), DMA((zs,)), DMA((zs,)), DMA((n,)), DMA((n,)),
            DMA((n,)), DMA((n,)), DMA((2,)), pltpu.VMEM((n, *piece), BF16),
            *RowReduce.scratch(cu, rows, width), *LineReduce.scratch(zs, n, piece),
            *LineReduce.scratch(zs, 1, (slab, width)),
        ],
        cost_estimate=pl.CostEstimate(flops=0, bytes_accessed=400 << 20, transcendentals=0),
        compiler_params=pltpu.CompilerParams(collective_id=5, has_side_effects=True, vmem_limit_bytes=63 << 20),
    )(
        qkv, mixed_low, totals, *marks, table, x.reshape(block), grad_hidden.reshape(block), params, mid_sums,
        grad_branch, proj, mixed, normed, weight, in_cut,
    )
    return input_grad.reshape(rows, width), small, cut, proj_grad, in_pieces


def body(
    inputs, out_grad, doc_ids, block_pairs, qkv_weight, proj_weight, ffn_in_weight, ffn_out_weight, small_params,
    qkv_first, proj_first, ffn_in_first, ffn_out_first, small_first,
    qkv_second, proj_second, ffn_in_second, ffn_out_second, small_second,
):
    bf16 = jnp.bfloat16
    tok_rows = inputs.shape[1]
    half_rows = tok_rows // 2
    cu, cl, zs = lax.axis_size("cu"), lax.axis_size("cl"), lax.axis_size("fsdp")
    ctx_count = cu * cl
    group = cl * zs
    seq_len = tok_rows * ctx_count
    my_index = lax.axis_index(ROW)
    heads = HEADS // ctx_count
    width = heads * HEAD_DIM
    slab = qkv_weight.shape[0]
    units = ffn_out_weight.shape[0]
    hidden = units * cu
    row_in, params, qkv_low, proj_low, in_cast, pos_col, doc_col, pos_row, doc_row, table = gather_head(
        inputs[0], small_params, qkv_weight, ffn_in_weight, proj_weight, block_pairs, doc_ids
    )
    proj_low = proj_low.reshape(width, D)
    marks = (pos_col, doc_col, pos_row, doc_row)
    row_in, in_cast, out_weight_later = lax.optimization_barrier((row_in, in_cast, ffn_out_weight))
    out_low = lax.all_gather(out_weight_later.astype(bf16), "cu", axis=0, tiled=True)
    in_cut = lax.all_to_all(in_cast.reshape(group * slab, 2 * hidden), FFN_GROUP, split_axis=0, concat_axis=0, tiled=True)
    row_in = row_in.reshape(seq_len, D)
    params = params[:, :, :7, :slab].transpose(2, 0, 1, 3).reshape(7, D)
    qkv_low = qkv_low.reshape(D, 3 * width)

    bias = lax.dynamic_slice_in_dim(params[4:7], my_index * width, width, 1).reshape(1, 3 * width)
    attn_in, qkv = project(row_in, params[0:2], qkv_low, bias, table)
    mixed, mixed_low, totals, branch = attend(qkv, proj_low, marks, heads)
    branch, in_cut = lax.optimization_barrier((branch, in_cut))
    hidden_state, mlp_in, grad_all, in_low = mid_forward(
        branch, inputs[0], out_grad[0], params[2:4], in_cut.reshape(group, slab, 2 * hidden)
    )

    inner_low, grad_gate_up = feed(mlp_in, grad_all, in_low, out_low)
    grad_ffn_in = cross_dot(mlp_in, grad_gate_up).astype(bf16)
    grad_gate_up, grad_ffn_in = lax.optimization_barrier((grad_gate_up, grad_ffn_in))
    in_grad_cut = lax.psum_scatter(grad_ffn_in, "cu", scatter_dimension=0, tiled=True)

    grad_hidden, grad_branch, mid_sums, layer_out, grad_ffn_out = mid_backward(
        grad_gate_up, in_low, hidden_state, out_grad[0], params[2:4], inner_low, out_low, grad_all
    )
    layer_out = layer_out[None]
    in_grad_cut, grad_branch = lax.optimization_barrier((in_grad_cut, grad_branch))
    in_grad_cut = in_grad_cut.reshape(group, slab, 2 * hidden)
    grad_ffn_out, in_grad_cut = lax.optimization_barrier((grad_ffn_out, in_grad_cut))
    ffn_out_grad = lax.psum_scatter(grad_ffn_out, "cu", scatter_dimension=0, tiled=True)
    if seq_len <= 1024 and width % LANES == 0:
        input_grad, small_sum, qkv_grad_cut, proj_grad, in_grad = back(
            qkv, grad_branch, proj_low, mixed, mixed_low, totals, marks, table, inputs[0], grad_hidden, params[0:2],
            mid_sums, attn_in, qkv_low, in_grad_cut, heads,
        )
    else:
        grad_proj = cross_dot(mixed_low, grad_branch).astype(bf16)
        grad_joined, bias_own, in_grad = attend_back(
            qkv, grad_branch, proj_low, mixed, totals, marks, table, in_grad_cut, heads
        )
        grad_norm_part = back_dot(grad_joined, qkv_low).astype(bf16)
        grad_qkv = (
            cross_dot(attn_in, grad_joined).astype(bf16).reshape(ctx_count, zs, slab, 3 * width).transpose(1, 0, 2, 3)
        )
        bias_own = bias_own.reshape(3, width)
        grad_bias = lax.dynamic_update_slice(jnp.zeros((3, D), jnp.float32), bias_own, (0, my_index * width))
        zero_rows = jnp.zeros((2, D), jnp.float32)
        terms = jnp.concatenate([zero_rows, mid_sums, grad_bias, zero_rows[:1]], axis=0)
        input_grad, small_sum, qkv_grad_cut, proj_grad = tail(
            grad_norm_part, inputs[0], grad_hidden, params[0:2], terms, grad_qkv, grad_proj.reshape(zs, 1, slab, D)
        )
    input_grad = input_grad[None]
    my_slab = (my_index * zs + lax.axis_index("fsdp")) * slab
    small_grad = lax.dynamic_slice_in_dim(small_sum, my_slab, slab, 1)[:7]

    proj_fan = max(8 * D // seq_len, 1)
    in_new, qkv_new, out_new, proj_new = adam_all(
        (
            (ffn_in_weight, ffn_in_first, ffn_in_second, in_grad),
            (qkv_weight, qkv_first, qkv_second, qkv_grad_cut),
            (ffn_out_weight, ffn_out_first, ffn_out_second, ffn_out_grad),
            (proj_weight, proj_first, proj_second, proj_grad),
        ),
        (2.0 / math.sqrt(D), 2.0 / math.sqrt(D), 2.0 / math.sqrt(FF), 2.0 / math.sqrt(proj_fan)),
    )
    small_new = adam_update(small_params, small_first, small_second, small_grad, small_rate, 0.0)
    news = (qkv_new, proj_new, in_new, out_new, small_new)
    return (layer_out, input_grad, *(n[0] for n in news), *(n[1] for n in news), *(n[2] for n in news), small_grad)


def solution(mesh):
    ctx_count, fsdp_count = mesh.devices.shape
    fine = Mesh(mesh.devices.reshape(ctx_count // 2, 2, fsdp_count), ("cu", "cl", "fsdp"))
    tokens = P("fsdp", ROW, None)
    matrix = P(EVERY, None)
    small = P(None, EVERY)
    five = (matrix, matrix, matrix, matrix, small)
    in_specs = (tokens, tokens, P("fsdp", None), P(), *five, *five, *five)
    out_specs = (tokens, tokens, *five, *five, *five, small)
    return jax.shard_map(body, mesh=fine, in_specs=in_specs, out_specs=out_specs, check_vma=False)
```

```python
import functools
import math

import jax
import jax.numpy as jnp
from jax import lax
from jax.experimental import pallas as pl
from jax.experimental.pallas import tpu as pltpu
from jax.sharding import Mesh, PartitionSpec as P

D = 2048
HEADS = 32
HEAD_DIM = 64
FF = 5632
ROT = 16
STEP = 10


norm_eps = 1e-05
beta_first = 0.9
beta_second = 0.95
adam_eps = 1e-08
matrix_decay = 0.1
small_rate = 0.5


def norm_rows(values, gain_row, shift_row):
    center_mean = jnp.mean(values, axis=-1, keepdims=True)
    centered = values - center_mean
    inv_std = lax.rsqrt(jnp.mean(centered * centered, axis=-1, keepdims=True) + norm_eps)
    normed = centered * inv_std
    return (normed * gain_row + shift_row, normed, inv_std)


def norm_back(grad_rows, normed, inv_std, gain_row):
    scaled = grad_rows * gain_row
    return inv_std * (
        scaled
        - jnp.mean(scaled, axis=-1, keepdims=True)
        - normed * jnp.mean(scaled * normed, axis=-1, keepdims=True)
    )


def cross_dot(left_mat, right_mat):
    return lax.dot_general(
        left_mat, right_mat, (((0,), (0,)), ((), ())), preferred_element_type=jnp.float32
    )


def back_dot(left_mat, weight):
    return lax.dot_general(
        left_mat, weight, (((1,), (1,)), ((), ())), preferred_element_type=jnp.float32
    )


def adam_update(weight, first_moment, second_moment, gradient, step_rate, decay_factor):
    new_first = beta_first * first_moment + (1.0 - beta_first) * gradient
    new_second = beta_second * second_moment + (1.0 - beta_second) * gradient * gradient
    correct_first = 1.0 - beta_first**STEP
    correct_second = 1.0 - beta_second**STEP
    update = new_first / correct_first / (jnp.sqrt(new_second / correct_second) + adam_eps)
    return (weight - step_rate * (update + decay_factor * weight), new_first, new_second)


ROW = ("cu", "cl")
FFN_GROUP = ("cl", "fsdp")
EVERY = ("cu", "cl", "fsdp")
SCALE = HEAD_DIM**-0.5


LANES = 128


def fill_table(table, positions, start, rows):
    half_rot = ROT // 2
    here = pl.ds(pl.multiple_of(start, rows), rows)
    lane = lax.rem(lax.broadcasted_iota(jnp.int32, (1, LANES), 1), HEAD_DIM)
    inverse = jnp.zeros((1, LANES), jnp.float32)
    for i in range(half_rot):
        inverse = jnp.where(lax.rem(lane, half_rot) == i, 10000.0 ** (-2.0 * i / ROT), inverse)
    angles = positions[here, :].astype(jnp.float32) * jnp.where(lane < ROT, inverse, 0.0)
    sine = jnp.sin(angles)
    table[here, 0:LANES] = jnp.cos(angles)
    table[here, LANES : 2 * LANES] = jnp.where(lane < half_rot, -sine, 0.0)
    table[here, 2 * LANES : 3 * LANES] = jnp.where(lane < half_rot, 0.0, sine)


def turn(values, table, sign):
    keep, lower, upper = (table[:, i * LANES : (i + 1) * LANES] for i in range(3))
    half_rot = ROT // 2
    shifted = pltpu.roll(values, LANES - half_rot, 1) * lower + pltpu.roll(values, half_rot, 1) * upper
    return values * keep + sign * shifted


def dot_t(left, right):
    return lax.dot_general(left, right, (((1,), (1,)), ((), ())), preferred_element_type=jnp.float32)


def row_block(rows):
    return min(256, rows)


def project_kernel(x_ref, params_ref, w_ref, bias_ref, table_ref, normed_ref, qkv_ref):
    normed = norm_rows(x_ref[...].astype(jnp.float32), params_ref[0:1], params_ref[1:2])[0].astype(jnp.bfloat16)
    normed_ref[...] = normed
    joined = jnp.dot(normed, w_ref[...], preferred_element_type=jnp.float32) + bias_ref[...]
    turned = 2 * (joined.shape[1] // 3)
    for start in range(0, turned, LANES):
        cols = slice(start, start + LANES)
        qkv_ref[:, cols] = turn(joined[:, cols], table_ref[...], 1.0).astype(jnp.bfloat16)
    qkv_ref[:, turned:] = joined[:, turned:].astype(jnp.bfloat16)


def project(x, params, weight, bias, table):
    rows, width = x.shape
    block = row_block(rows)
    cols = weight.shape[1]

    def by_row(n):
        return pl.BlockSpec((block, n), lambda i: (i, 0))

    def whole(array):
        return pl.BlockSpec(array.shape, lambda i: (0, 0))

    return pl.pallas_call(
        project_kernel,
        grid=(rows // block,),
        in_specs=[by_row(width), whole(params), whole(weight), whole(bias), by_row(table.shape[1])],
        out_specs=[by_row(width), by_row(cols)],
        out_shape=[jax.ShapeDtypeStruct((rows, width), jnp.bfloat16), jax.ShapeDtypeStruct((rows, cols), jnp.bfloat16)],
        cost_estimate=pl.CostEstimate(
            flops=2 * rows * width * cols, bytes_accessed=4 * rows * width, transcendentals=0
        ),
        compiler_params=pltpu.CompilerParams(vmem_limit_bytes=48 << 20),
    )(x, params, weight, bias, table)


def attend_kernel(
    heads, q_ref, qkv_ref, proj_ref, pq_ref, dq_ref, pk_ref, dk_ref, mixed_ref, low_ref, tot_ref, branch_ref
):
    width = heads * HEAD_DIM
    allowed = (pk_ref[...] <= pq_ref[...]) & (dk_ref[...] == dq_ref[...])
    for head in range(heads):
        cols, key, value = (slice(p * width + head * HEAD_DIM, p * width + (head + 1) * HEAD_DIM) for p in range(3))
        scores = dot_t(q_ref[:, cols], qkv_ref[:, key]) * SCALE
        weights = jnp.where(allowed, jnp.exp(scores), 0.0)
        total = jnp.sum(weights, axis=1, keepdims=True)
        weighted = jnp.dot(weights.astype(jnp.bfloat16), qkv_ref[:, value], preferred_element_type=jnp.float32)
        mixed = weighted / total
        mixed_ref[:, cols] = mixed
        low_ref[:, cols] = mixed.astype(jnp.bfloat16)
        tot_ref[:, head : head + 1] = total
    branch_ref[...] = jnp.dot(low_ref[...], proj_ref[...], preferred_element_type=jnp.float32).astype(jnp.bfloat16)


def attend(qkv, proj, marks, heads):
    pos_col, doc_col, pos_row, doc_row = marks
    rows, cols = qkv.shape
    width = cols // 3
    block = row_block(rows)

    def by_row(n):
        return pl.BlockSpec((block, n), lambda i: (i, 0))

    def whole(array):
        return pl.BlockSpec(array.shape, lambda i: (0, 0))

    return pl.pallas_call(
        functools.partial(attend_kernel, heads),
        grid=(rows // block,),
        in_specs=[by_row(cols), whole(qkv), whole(proj), by_row(1), by_row(1), whole(pos_row), whole(doc_row)],
        out_specs=[by_row(width), by_row(width), by_row(heads), by_row(D)],
        out_shape=[
            jax.ShapeDtypeStruct((rows, width), jnp.float32),
            jax.ShapeDtypeStruct((rows, width), jnp.bfloat16),
            jax.ShapeDtypeStruct((rows, heads), jnp.float32),
            jax.ShapeDtypeStruct((rows, D), jnp.bfloat16),
        ],
        cost_estimate=pl.CostEstimate(
            flops=4 * rows * rows * width, bytes_accessed=8 * rows * D, transcendentals=rows * rows * heads
        ),
        compiler_params=pltpu.CompilerParams(vmem_limit_bytes=48 << 20),
    )(qkv, qkv, proj, pos_col, doc_col, pos_row, doc_row)


def attend_back_kernel(
    heads, qkv_ref, branch_ref, proj_ref, mixed_ref, tot_ref, pq_ref, dq_ref, pk_ref, dk_ref, table_ref, cut,
    joined_ref, bias_ref, pieces, gq_ref, gk_ref, gv_ref, own, send, recv,
):
    width = heads * HEAD_DIM
    rows = qkv_ref.shape[0]
    block = row_block(rows)
    group = cut.shape[0]

    def exchange(m):
        device, after, _, me = in_group(m)
        return Transfer(cut.at[after], pieces.at[me], send.at[m], recv.at[m], device)

    def landed(m):
        device, _, before, _ = in_group(m)
        return Transfer(cut.at[before], pieces.at[before], send.at[m], recv.at[m], device)

    me = in_group(0)[3]
    kept = pltpu.make_async_copy(cut.at[me], pieces.at[me], own.at[0])
    kept.start()
    greet_group()
    loop(1, group, lambda m: exchange(m).start())
    gk_ref[...] = jnp.zeros_like(gk_ref)
    gv_ref[...] = jnp.zeros_like(gv_ref)

    def one(step):
        here = pl.ds(pl.multiple_of(step * block, block), block)
        grad_all = dot_t(branch_ref[here], proj_ref[...])
        allowed = (pk_ref[...] <= pq_ref[here]) & (dk_ref[...] == dq_ref[here])
        for head in range(heads):
            cols, key, value = (
                slice(p * width + head * HEAD_DIM, p * width + (head + 1) * HEAD_DIM) for p in range(3)
            )
            q, k, v = qkv_ref[here, cols], qkv_ref[:, key], qkv_ref[:, value]
            inverse = 1.0 / tot_ref[here, head : head + 1]
            grad_mixed = grad_all[:, cols]
            grad_weighted = (grad_mixed * inverse).astype(jnp.bfloat16)
            grad_total = -jnp.sum(grad_mixed * mixed_ref[here, cols], axis=1, keepdims=True) * inverse
            weights = jnp.where(allowed, jnp.exp(dot_t(q, k) * SCALE), 0.0)
            grad_scores = (weights * (dot_t(grad_weighted, v) + grad_total)).astype(jnp.bfloat16)
            gq_ref[here, cols] = jnp.dot(grad_scores, k, preferred_element_type=jnp.float32) * SCALE
            gk_ref[:, cols] += cross_dot(grad_scores, q) * SCALE
            gv_ref[:, cols] += cross_dot(weights.astype(jnp.bfloat16), grad_weighted)

    loop(0, rows // block, one)
    for part, ref in enumerate((gq_ref, gk_ref, gv_ref)):
        for start in range(0, width, LANES):
            cols = slice(start, min(start + LANES, width))
            grad = ref[:, cols]
            if part < 2:
                lanes = cols.stop - cols.start
                if lanes < LANES:
                    grad = jnp.concatenate([grad, jnp.zeros((rows, LANES - lanes), jnp.float32)], axis=1)
                grad = turn(grad, table_ref[...], -1.0)[:, :lanes]
            grad = grad.astype(jnp.bfloat16)
            into = slice(part * width + cols.start, part * width + cols.stop)
            joined_ref[:, into] = grad
            bias_ref[:, into] = jnp.sum(grad.astype(jnp.float32), axis=0, keepdims=True)
    loop(1, group, lambda m: landed(m).wait_recv())
    loop(1, group, lambda m: exchange(m).wait_send())
    kept.wait()


def attend_back(qkv, grad_branch, proj, mixed, totals, marks, table, cut, heads):
    rows, cols = qkv.shape
    width = cols // 3
    return pl.pallas_call(
        functools.partial(attend_back_kernel, heads),
        in_specs=[*[VMEM] * 10, ANY],
        out_specs=[VMEM, VMEM, ANY],
        out_shape=[
            jax.ShapeDtypeStruct((rows, cols), jnp.bfloat16), jax.ShapeDtypeStruct((1, cols), jnp.float32),
            jax.ShapeDtypeStruct(cut.shape, BF16),
        ],
        scratch_shapes=[
            *[pltpu.VMEM((rows, width), jnp.float32)] * 3, DMA((1,)), DMA((cut.shape[0],)), DMA((cut.shape[0],)),
        ],
        cost_estimate=pl.CostEstimate(
            flops=10 * rows * rows * width, bytes_accessed=8 * rows * D, transcendentals=rows * rows * heads
        ),
        compiler_params=pltpu.CompilerParams(collective_id=4, has_side_effects=True, vmem_limit_bytes=60 << 20),
    )(qkv, grad_branch, proj, mixed, totals, *marks, table, cut)


def feed_kernel(x_ref, grad_ref, in_ref, out_ref, inner_ref, back_ref, in_grad_ref, x_all, back_all):
    step = pl.program_id(0)
    block = x_ref.shape[0]
    here = pl.ds(pl.multiple_of(step * block, block), block)
    hidden = out_ref.shape[0]
    gate_up = jnp.dot(x_ref[...], in_ref[...], preferred_element_type=jnp.float32)
    gate, up = gate_up[:, :hidden], gate_up[:, hidden:]
    grad_inner = dot_t(grad_ref[...], out_ref[...])
    sigmoid = 1.0 / (1.0 + jnp.exp(-gate))
    silu = gate * sigmoid
    inner_ref[...] = (silu * up).astype(jnp.bfloat16)
    grad_gate = grad_inner * up * (sigmoid * (1.0 + gate * (1.0 - sigmoid)))
    back = jnp.concatenate([grad_gate, grad_inner * silu], axis=1).astype(jnp.bfloat16)
    back_ref[...] = back
    x_all[here] = x_ref[...]
    back_all[here] = back

    @pl.when(step == x_all.shape[0] // block - 1)
    def _():
        tile = 256

        def one(i, carry):
            rows = pl.ds(pl.multiple_of(i * tile, tile), tile)
            in_grad_ref[rows] = cross_dot(x_all[:, rows], back_all[...]).astype(jnp.bfloat16)
            return carry

        lax.fori_loop(0, x_all.shape[1] // tile, one, 0)


def feed(x, grad, in_weight, out_weight):
    rows, width = x.shape
    hidden = out_weight.shape[0]
    block = row_block(rows)

    def by_row(n):
        return pl.BlockSpec((block, n), lambda i: (i, 0))

    def whole(array):
        return pl.BlockSpec(array.shape, lambda i: (0, 0))

    return pl.pallas_call(
        feed_kernel,
        grid=(rows // block,),
        in_specs=[by_row(width), by_row(width), whole(in_weight), whole(out_weight)],
        out_specs=[by_row(hidden), by_row(2 * hidden), whole(in_weight)],
        out_shape=[
            jax.ShapeDtypeStruct((rows, hidden), jnp.bfloat16), jax.ShapeDtypeStruct((rows, 2 * hidden), jnp.bfloat16),
            jax.ShapeDtypeStruct(in_weight.shape, jnp.bfloat16),
        ],
        scratch_shapes=[pltpu.VMEM((rows, width), jnp.bfloat16), pltpu.VMEM((rows, 2 * hidden), jnp.bfloat16)],
        cost_estimate=pl.CostEstimate(
            flops=10 * rows * width * hidden, bytes_accessed=8 * rows * width, transcendentals=rows * hidden
        ),
        compiler_params=pltpu.CompilerParams(vmem_limit_bytes=60 << 20),
    )(x, grad, in_weight, out_weight)


def adam_kernel(rates, chunks, *refs):
    sources, results, held = refs[:16], refs[16:28], refs[28:44]
    came, left = refs[44:]

    def rows_of(k, i):
        size = held[4 * k].shape[0] // chunks[k]
        return pl.ds(pl.multiple_of(i * size, size), size)

    def load(k, i, part):
        here = rows_of(k, i)
        at = (slice(None), here) if held[4 * k + part].ndim == 3 else (here,)
        return pltpu.make_async_copy(
            sources[4 * k + part].at[at], held[4 * k + part].at[at], came.at[4 * k + part, i]
        )

    def store(k, i, part):
        here = rows_of(k, i)
        return pltpu.make_async_copy(
            held[4 * k + part].at[here], results[3 * k + part].at[here], left.at[3 * k + part, i]
        )

    def run(k, step):
        def one(i, carry):
            step(i)
            return carry

        lax.fori_loop(0, chunks[k], one, 0)

    def start(k):
        def one(i):
            for part in range(4):
                load(k, i, part).start()

        run(k, one)

    def update(k):
        w, m, v, g = held[4 * k : 4 * k + 4]

        def one(i):
            here = rows_of(k, i)
            for part in range(4):
                load(k, i, part).wait()
            cols, parts = w.shape[1], 1
            if g.ndim == 3:
                parts = 3 if k == 1 else cols // g.shape[2]
                cols = cols // parts
            for part in range(parts):
                there = slice(part * cols, (part + 1) * cols)
                if g.ndim == 3:
                    width = g.shape[2] // parts
                    grad = jnp.concatenate(
                        [g[owner, here, part * width : (part + 1) * width] for owner in range(g.shape[0])], axis=1
                    )
                else:
                    grad = g[here, there]
                new = adam_update(
                    w[here, there], m[here, there], v[here, there], grad.astype(jnp.float32), rates[k], matrix_decay
                )
                for ref, value in zip((w, m, v), new):
                    ref[here, there] = value
            for part in range(3):
                store(k, i, part).start()

        run(k, one)

    def finish(k):
        def one(i):
            for part in range(3):
                store(k, i, part).wait()

        run(k, one)

    order = (2, 3, 0, 1)
    for k in order:
        start(k)
    for k in order:
        update(k)
    for k in order:
        finish(k)


def adam_all(states, rates):
    chunks, operands, out_shape = [], [], []
    for state in states:
        rows = state[0].shape[0]
        size = 32 if rows % 32 == 0 else 16
        chunks.append(rows // size if rows % size == 0 else 1)
        operands += state
        out_shape += [jax.ShapeDtypeStruct(state[0].shape, jnp.float32)] * 3
    any_ref = pl.BlockSpec(memory_space=pl.ANY)
    out = pl.pallas_call(
        functools.partial(adam_kernel, rates, chunks),
        in_specs=[any_ref] * 16,
        out_specs=[any_ref] * 12,
        out_shape=out_shape,
        scratch_shapes=[
            *[pltpu.VMEM(array.shape, array.dtype) for array in operands],
            pltpu.SemaphoreType.DMA((16, max(chunks))), pltpu.SemaphoreType.DMA((12, max(chunks))),
        ],
        compiler_params=pltpu.CompilerParams(vmem_limit_bytes=60 << 20),
    )(*operands)
    return [tuple(out[3 * k : 3 * k + 3]) for k in range(4)]


MESH = pl.DeviceIdType.MESH
ANY = pl.BlockSpec(memory_space=pl.ANY)
VMEM = pl.BlockSpec(memory_space=pltpu.VMEM)
DMA = pltpu.SemaphoreType.DMA
BF16, F32 = jnp.bfloat16, jnp.float32


class Transfer:
    def __init__(self, src, dst, send, recv, device):
        self.parts = (src, dst, send, recv, device)

    def copy(self):
        src, dst, send, recv, device = self.parts
        return pltpu.make_async_remote_copy(
            src_ref=src, dst_ref=dst, send_sem=send, recv_sem=recv, device_id=device, device_id_type=MESH
        )

    def start(self):
        self.copy().start()

    def wait_recv(self):
        self.copy().wait_recv()

    def wait_send(self):
        self.copy().wait_send()

    def wait(self):
        self.copy().wait()


rcopy = Transfer


def flip(index, mask):
    bit = 1
    while bit <= mask:
        if mask & bit:
            index = index + bit * (1 - 2 * lax.rem(index // bit, 2))
        bit *= 2
    return index


def place():
    return lax.axis_index("cu"), lax.axis_index("cl"), lax.axis_index("fsdp")


def sizes():
    return lax.axis_size("cu"), lax.axis_size("cl"), lax.axis_size("fsdp")


def in_group(m):
    u, c, z = place()
    _, cl, zs = sizes()
    group, me = cl * zs, c * zs + z
    after, before = lax.rem(me + m, group), lax.rem(me - m + group, group)
    return (u, after // zs, lax.rem(after, zs)), after, before, me


def greet_group():
    _, cl, zs = sizes()
    barrier = pltpu.get_barrier_semaphore()

    def signal(m, carry):
        pl.semaphore_signal(barrier, inc=1, device_id=in_group(m)[0], device_id_type=MESH)
        return carry

    lax.fori_loop(1, cl * zs, signal, 0)
    pl.semaphore_wait(barrier, cl * zs - 1)


def greet(row, line, twins=False):
    u, c, z = place()
    cu, cl, zs = sizes()
    n, me = cu * cl, u * cl + c
    barrier = pltpu.get_barrier_semaphore()

    def signal_row(m, carry):
        other = lax.rem(me + m, n)
        pl.semaphore_signal(barrier, inc=1, device_id=(other // cl, lax.rem(other, cl), z), device_id_type=MESH)
        return carry

    def signal_line(m, carry):
        pl.semaphore_signal(barrier, inc=1, device_id=(u, c, lax.rem(z + m, zs)), device_id_type=MESH)
        return carry

    def signal_twins(m, carry):
        pl.semaphore_signal(barrier, inc=1, device_id=(u, 1 - c, lax.rem(z + m, zs)), device_id_type=MESH)
        return carry

    if row:
        lax.fori_loop(1, n, signal_row, 0)
    if line:
        lax.fori_loop(1, zs, signal_line, 0)
    if twins:
        lax.fori_loop(1, zs, signal_twins, 0)
    pl.semaphore_wait(barrier, row * (n - 1) + (line + twins) * (zs - 1))


def head_kernel(
    x, small_in, qkv_far, ffn_far, proj_far, pairs, docs_in, row, par, wq, wp, in_cut, pos_col, doc_col, pos_row, doc_row,
    table, qkv_in, ffn_in, proj_in, docs, fetch, qkv, proj, small, own, x_send, x_recv, s_send, s_recv, p_send, p_recv, q_send, q_recv,
    a_send, a_recv, up_send, up_recv, dn_send, dn_recv,
):
    u, c, z = place()
    cu, cl, zs = sizes()
    n, me = cu * cl, u * cl + c
    sibling = (u, 1 - c, z)
    slab, width = qkv_in.shape[0], qkv_in.shape[1] // (3 * n)
    half = docs.shape[1]
    fetches = [
        pltpu.make_async_copy(source, into, fetch.at[i])
        for i, (source, into) in enumerate(((qkv_far, qkv_in), (proj_far, proj_in), (ffn_far, ffn_in)))
    ]
    for copy in fetches:
        copy.start()
    for i in range(docs.shape[0]):
        docs[i : i + 1] = docs_in[:, i * half : (i + 1) * half]
    small[...] = jnp.zeros_like(small)
    small[: small_in.shape[0], : small_in.shape[1]] = small_in[...]
    fetches[0].wait()
    for owner in range(n):
        for part in range(3):
            start = (part * n + owner) * width
            qkv[owner, :, part * width : (part + 1) * width] = qkv_in[:, start : start + width].astype(BF16)
    mine = [
        pltpu.make_async_copy(qkv.at[me], wq.at[me, z], own.at[0]),
        pltpu.make_async_copy(x, row.at[u, c], own.at[1]),
        pltpu.make_async_copy(small, par.at[me, z], own.at[2]),
        pltpu.make_async_copy(proj, wp.at[z], own.at[3]),
    ]
    fetches[1].wait()
    proj[...] = proj_in[...].astype(BF16)
    for copy in mine:
        copy.start()
    greet(True, True)

    def exchange(m):
        other, source = lax.rem(me + m, n), lax.rem(me - m + n, n)
        out = rcopy(
            qkv.at[other], wq.at[me, z], a_send.at[m], a_recv.at[m], (other // cl, lax.rem(other, cl), z)
        )
        into = rcopy(qkv.at[other], wq.at[source, z], a_send.at[m], a_recv.at[m], sibling)
        return out, into

    def params_line(m):
        other, source = lax.rem(z + m, zs), lax.rem(z - m + zs, zs)
        return (
            rcopy(small, par.at[me, z], p_send.at[m], p_recv.at[m], (u, c, other)),
            rcopy(small, par.at[me, source], p_send.at[m], p_recv.at[m], sibling),
        )

    def params_row(m):
        other, source = lax.rem(me + m, n), lax.rem(me - m + n, n)
        return (
            rcopy(par.at[me], par.at[me], q_send.at[m], q_recv.at[m], (other // cl, lax.rem(other, cl), z)),
            rcopy(par.at[me], par.at[source], q_send.at[m], q_recv.at[m], sibling),
        )

    def x_far(i):
        out = rcopy(x, row.at[u, c], x_send.at[i], x_recv.at[i], (flip(u, i), c, z))
        into = rcopy(x, row.at[flip(u, i), c], x_send.at[i], x_recv.at[i], sibling)
        return out, into

    def x_near(i):
        part = row.at[flip(u, i), c]
        out = rcopy(part, part, s_send.at[i], s_recv.at[i], sibling)
        into = rcopy(part, row.at[flip(u, i), 1 - c], s_send.at[i], s_recv.at[i], sibling)
        return out, into

    def loop(low, high, step):
        def run(m, carry):
            step(m)
            return carry

        lax.fori_loop(low, high, run, 0)

    loop(1, n, lambda m: exchange(m)[0].start())
    loop(1, zs, lambda m: params_line(m)[0].start())
    for copy in mine:
        copy.wait()
    for i in range(1, cu):
        x_far(i)[0].start()
    x_near(0)[0].start()

    def chain(step, m):
        piece = lax.rem(me - m + n, n)
        above, below = wq.at[piece, lax.rem(z + step, zs)], wq.at[piece, lax.rem(z - step + zs, zs)]
        return (
            rcopy(below, below, up_send.at[step, m], up_recv.at[step, m], (u, c, lax.rem(z + 1, zs))),
            rcopy(above, above, dn_send.at[step, m], dn_recv.at[step, m], (u, c, lax.rem(z - 1 + zs, zs))),
        )

    def arrival(step, m):
        piece = lax.rem(me - m + n, n)
        above, below = wq.at[piece, lax.rem(z + step + 1, zs)], wq.at[piece, lax.rem(z - step - 1 + zs, zs)]
        return (
            rcopy(below, below, up_send.at[step, m], up_recv.at[step, m], sibling),
            rcopy(above, above, dn_send.at[step, m], dn_recv.at[step, m], sibling),
        )

    def chain_proj(step):
        above, below = wp.at[lax.rem(z + step, zs)], wp.at[lax.rem(z - step + zs, zs)]
        return (
            rcopy(below, below, up_send.at[step, n], up_recv.at[step, n], (u, c, lax.rem(z + 1, zs))),
            rcopy(above, above, dn_send.at[step, n], dn_recv.at[step, n], (u, c, lax.rem(z - 1 + zs, zs))),
        )

    def forward_proj(step):
        if step:

            @pl.when(z >= step)
            def _():
                chain_proj(step - 1)[0].wait_recv()

            @pl.when(z + step < zs)
            def _():
                chain_proj(step - 1)[1].wait_recv()

        if step < zs - 1:

            @pl.when((z >= step) & (z + 1 < zs))
            def _():
                chain_proj(step)[0].start()

            @pl.when((z + step < zs) & (z > 0))
            def _():
                chain_proj(step)[1].start()

    def sent_proj(step):
        @pl.when((z >= step) & (z + 1 < zs))
        def _():
            chain_proj(step)[0].wait_send()

        @pl.when((z + step < zs) & (z > 0))
        def _():
            chain_proj(step)[1].wait_send()

    def first(m):
        @pl.when(m > 0)
        def _():
            exchange(m)[1].wait_recv()

        @pl.when(z + 1 < zs)
        def _():
            chain(0, m)[0].start()

        @pl.when(z > 0)
        def _():
            chain(0, m)[1].start()

    loop(0, n, first)
    forward_proj(0)
    fetches[2].wait()
    group, units = cl * zs, ffn_in.shape[1] // (2 * n * zs)
    for part in range(2 * cu):
        for owner in range(group):
            start = (part * group + owner) * units
            in_cut[owner, :, part * units : (part + 1) * units] = ffn_in[:, start : start + units].astype(BF16)
    lane, line_of = (lax.broadcasted_iota(jnp.int32, (half, half), d) for d in (1, 0))

    def column(values):
        return jnp.sum(jnp.where(lane == line_of, values, 0), axis=1, keepdims=True)

    for slot in range(n):
        for part in range(2):
            here = slice((2 * slot + part) * half, (2 * slot + part + 1) * half)
            number = pairs[slot, part]
            positions = number * half + lax.broadcasted_iota(jnp.int32, (1, half), 1)
            documents = docs[pl.ds(number, 1), :]
            pos_row[:, here], doc_row[:, here] = positions, documents
            pos_col[here, :], doc_col[here, :] = column(positions), column(documents)
    loop(0, n, lambda i: fill_table(table, pos_col, i * 2 * half, 2 * half))
    for m in range(1, zs):
        params_line(m)[1].wait_recv()
    loop(1, n, lambda m: params_row(m)[0].start())
    for step in range(1, zs):

        def later(m, step=step):
            @pl.when(z >= step)
            def _():
                arrival(step - 1, m)[0].wait_recv()

            @pl.when((z >= step) & (z + 1 < zs))
            def _():
                chain(step, m)[0].start()

            @pl.when(z + step < zs)
            def _():
                arrival(step - 1, m)[1].wait_recv()

            @pl.when((z + step < zs) & (z > 0))
            def _():
                chain(step, m)[1].start()

        loop(0, n, later)
        forward_proj(step)
        if step == 1:
            for i in range(1, cu):
                x_far(i)[1].wait_recv()
                x_near(i)[0].start()
    loop(1, n, lambda m: params_row(m)[1].wait_recv())
    for i in range(cu):
        x_near(i)[1].wait_recv()
    loop(1, n, lambda m: exchange(m)[0].wait_send())
    loop(1, zs, lambda m: params_line(m)[0].wait_send())
    loop(1, n, lambda m: params_row(m)[0].wait_send())
    for i in range(cu):
        x_near(i)[0].wait_send()
        if i:
            x_far(i)[0].wait_send()
    for step in range(zs - 1):

        def sent(m, step=step):
            @pl.when((z >= step) & (z + 1 < zs))
            def _():
                chain(step, m)[0].wait_send()

            @pl.when((z + step < zs) & (z > 0))
            def _():
                chain(step, m)[1].wait_send()

        loop(0, n, sent)
        sent_proj(step)


def gather_head(x, small, qkv_weight, ffn_in, proj, pairs, docs):
    cu, cl, zs = sizes()
    n = cu * cl
    slab, cols = qkv_weight.shape
    cut = (n, slab, cols // n)
    pad = (8, LANES)
    rows = docs.shape[1]
    column, line = jax.ShapeDtypeStruct((rows, 1), jnp.int32), jax.ShapeDtypeStruct((1, rows), jnp.int32)
    return pl.pallas_call(
        head_kernel,
        in_specs=[ANY, VMEM, ANY, ANY, ANY, pl.BlockSpec(memory_space=pltpu.SMEM), VMEM],
        out_specs=[ANY, ANY, ANY, ANY, *[VMEM] * 6],
        out_shape=[
            jax.ShapeDtypeStruct((cu, cl, *x.shape), x.dtype),
            jax.ShapeDtypeStruct((n, zs, *pad), F32),
            jax.ShapeDtypeStruct((n, zs, *cut[1:]), BF16),
            jax.ShapeDtypeStruct((zs, *proj.shape), BF16),
            jax.ShapeDtypeStruct((cl * zs, ffn_in.shape[0], ffn_in.shape[1] // (cl * zs)), BF16),
            column, column, line, line, jax.ShapeDtypeStruct((rows, 3 * LANES), F32),
        ],
        scratch_shapes=[
            pltpu.VMEM(qkv_weight.shape, F32), pltpu.VMEM(ffn_in.shape, F32), pltpu.VMEM(proj.shape, F32),
            pltpu.VMEM((2 * n, rows // (2 * n)), jnp.int32), DMA((3,)),
            pltpu.VMEM(cut, BF16), pltpu.VMEM(proj.shape, BF16), pltpu.VMEM(pad, F32),
            DMA((4,)), DMA((cu,)), DMA((cu,)), DMA((cu,)), DMA((cu,)), DMA((zs,)), DMA((zs,)), DMA((n,)), DMA((n,)),
            DMA((n,)), DMA((n,)), *[DMA((zs, n + 1))] * 4,
        ],
        cost_estimate=pl.CostEstimate(flops=0, bytes_accessed=200 << 20, transcendentals=0),
        compiler_params=pltpu.CompilerParams(collective_id=0, has_side_effects=True, vmem_limit_bytes=48 << 20),
    )(x, small, qkv_weight, ffn_in, proj, pairs, docs)


ITEMS = 4


def loop(low, high, step):
    def run(m, carry):
        step(m)
        return carry

    lax.fori_loop(low, high, run, 0)


def bits_of(count):
    return [1 << b for b in range(count.bit_length() - 1)]


def combos(bits):
    masks = [0]
    for b in bits:
        masks = masks + [m | b for m in masks]
    return masks


def order_of(item, count):
    return bits_of(count) if item < ITEMS // 2 else bits_of(count)[::-1]


def add_low(left, right):
    return (left.astype(F32) + right.astype(F32)).astype(BF16)


class RowReduce:
    def __init__(self, parts, held, beside, came, load, sib_s, sib_r, out_s, out_r):
        self.parts, self.held, self.beside, self.came = parts, held, beside, came
        self.load, self.sib_s, self.sib_r, self.out_s, self.out_r = load, sib_s, sib_r, out_s, out_r
        self.u, self.c, self.z = place()
        self.count = sizes()[0]
        self.phases = self.count.bit_length() - 1

    def sib(self, mask):
        return Transfer(
            self.parts.at[flip(self.u, mask), 1 - self.c], self.beside.at[mask], self.sib_s.at[mask],
            self.sib_r.at[mask], (self.u, 1 - self.c, self.z),
        )

    def loading(self, mask):
        return pltpu.make_async_copy(
            self.parts.at[flip(self.u, mask), self.c], self.held.at[mask], self.load.at[mask]
        )

    def start(self):
        for mask in reversed(range(self.count)):
            self.sib(mask).start()
            self.loading(mask).start()

    def merge(self):
        for mask in reversed(range(self.count)):
            self.loading(mask).wait()
            self.sib(mask).wait_recv()
            self.held[mask] = add_low(self.held[mask], self.beside[mask])

    def steps(self, item, phase):
        order = order_of(item, self.count)
        slot = self.count - (self.count >> phase)
        for k, rest in enumerate(combos(order[phase + 1 :])):
            yield slot + k, rest, Transfer(
                self.held.at[order[phase] | rest, item], self.came.at[slot + k, item], self.out_s.at[slot + k, item],
                self.out_r.at[slot + k, item], (flip(self.u, order[phase]), self.c, self.z),
            )

    def send(self, item, phase):
        for _, _, transfer in self.steps(item, phase):
            transfer.start()

    def add(self, item, phase):
        for slot, rest, transfer in self.steps(item, phase):
            transfer.wait_recv()
            self.held[rest, item] = add_low(self.held[rest, item], self.came[slot, item])

    def total(self, item):
        ((slot, _, transfer),) = self.steps(item, self.phases - 1)
        transfer.wait_recv()
        return self.held[0, item].astype(F32) + self.came[slot, item].astype(F32)

    def drain(self):
        for mask in range(self.count):
            self.sib(mask).wait_send()
        for item in range(ITEMS):
            for phase in range(self.phases):
                for _, _, transfer in self.steps(item, phase):
                    transfer.wait_send()

    @staticmethod
    def scratch(count, rows, width):
        block = (count, ITEMS, rows // ITEMS, width)
        return [
            pltpu.VMEM(block, BF16), pltpu.VMEM(block, BF16), pltpu.VMEM(block, BF16), DMA((count,)), DMA((count,)),
            DMA((count,)), DMA((count, ITEMS)), DMA((count, ITEMS)),
        ]


class RowGather:
    def __init__(self, own, full, keep, out_s, out_r, sib_s, sib_r):
        self.own, self.full, self.keep = own, full, keep
        self.out_s, self.out_r, self.sib_s, self.sib_r = out_s, out_r, sib_s, sib_r
        self.u, self.c, self.z = place()
        self.count = sizes()[0]
        self.phases = self.count.bit_length() - 1

    def kept(self, item):
        return pltpu.make_async_copy(self.own.at[item], self.full.at[self.u, self.c, item], self.keep.at[item])

    def source(self, mask, item):
        return self.own.at[item] if mask == 0 else self.full.at[flip(self.u, mask), self.c, item]

    def sib(self, mask, item):
        return Transfer(
            self.source(mask, item), self.full.at[flip(self.u, mask), self.c, item], self.sib_s.at[mask, item],
            self.sib_r.at[mask, item], (self.u, 1 - self.c, self.z),
        )

    def steps(self, item, phase):
        order = order_of(item, self.count)
        for k, mask in enumerate(combos(order[:phase])):
            slot = (1 << phase) - 1 + k
            yield mask | order[phase], Transfer(
                self.source(mask, item), self.full.at[flip(self.u, mask), self.c, item], self.out_s.at[slot, item],
                self.out_r.at[slot, item], (flip(self.u, order[phase]), self.c, self.z),
            )

    def start(self, item):
        self.send(item, 0)
        self.sib(0, item).start()
        self.kept(item).start()

    def send(self, item, phase):
        for _, transfer in self.steps(item, phase):
            transfer.start()

    def pass_on(self, item, phase):
        for mask, transfer in self.steps(item, phase):
            transfer.wait_recv()
            self.sib(mask, item).start()

    def drain(self):
        for item in range(ITEMS):
            self.kept(item).wait()
            for mask in range(self.count):
                self.sib(mask, item).wait()
            for phase in range(self.phases):
                for _, transfer in self.steps(item, phase):
                    transfer.wait_send()

    @staticmethod
    def scratch(count):
        return [DMA((ITEMS,)), *[DMA((count, ITEMS))] * 4]


class PlaneGather:
    def __init__(self, own, full, keep, out_s, out_r):
        self.own, self.full, self.keep, self.out_s, self.out_r = own, full, keep, out_s, out_r
        self.u, self.c, self.z = place()
        self.count = sizes()[0]
        self.items = own.shape[0]
        self.phases = self.count.bit_length() - 1

    def kept(self, item):
        return pltpu.make_async_copy(self.own.at[item], self.full.at[self.u, item], self.keep.at[item])

    def steps(self, item, phase):
        order = bits_of(self.count) if item % 2 else bits_of(self.count)[::-1]
        for k, mask in enumerate(combos(order[:phase])):
            slot = (1 << phase) - 1 + k
            block = self.full.at[flip(self.u, mask), item]
            yield Transfer(
                self.own.at[item] if mask == 0 else block, block, self.out_s.at[slot, item],
                self.out_r.at[slot, item], (flip(self.u, order[phase]), self.c, self.z),
            )

    def start(self):
        for item in range(self.items):
            self.kept(item).start()
            for transfer in self.steps(item, 0):
                transfer.start()

    def step(self, phase):
        for item in range(self.items):
            for transfer in self.steps(item, phase - 1):
                transfer.wait_recv()
            if phase < self.phases:
                for transfer in self.steps(item, phase):
                    transfer.start()

    def drain(self):
        for item in range(self.items):
            self.kept(item).wait()
            for phase in range(self.phases):
                for transfer in self.steps(item, phase):
                    transfer.wait_send()

    @staticmethod
    def scratch(count, items):
        return [DMA((items,)), DMA((count, items)), DMA((count, items))]


class LineGather:
    def __init__(self, own, full, keep, up_s, up_r, dn_s, dn_r, sib_s, sib_r):
        self.own, self.full, self.keep = own, full, keep
        self.up_s, self.up_r, self.dn_s, self.dn_r, self.sib_s, self.sib_r = up_s, up_r, dn_s, dn_r, sib_s, sib_r
        self.u, self.c, self.z = place()
        self.count = sizes()[2]

    def kept(self, item):
        return pltpu.make_async_copy(self.own.at[item], self.full.at[self.z, self.c, item], self.keep.at[item])

    def up(self, item, step):
        origin = lax.rem(self.z - step + self.count, self.count)
        block = self.full.at[origin, self.c, item]
        source = self.own.at[item] if step == 0 else block
        to = lax.rem(self.z + 1, self.count)
        return Transfer(source, block, self.up_s.at[step, item], self.up_r.at[step, item], (self.u, self.c, to))

    def down(self, item, step):
        block = self.full.at[lax.rem(self.z + step, self.count), self.c, item]
        source = self.own.at[item] if step == 0 else block
        to = lax.rem(self.z - 1 + self.count, self.count)
        return Transfer(source, block, self.dn_s.at[step, item], self.dn_r.at[step, item], (self.u, self.c, to))

    def sib(self, item, origin, own=False):
        block = self.full.at[origin, self.c, item]
        return Transfer(
            self.own.at[item] if own else block, block, self.sib_s.at[origin, item], self.sib_r.at[origin, item],
            (self.u, 1 - self.c, self.z),
        )

    def start(self, item):
        @pl.when(self.z + 1 < self.count)
        def _():
            self.up(item, 0).start()

        @pl.when(self.z > 0)
        def _():
            self.down(item, 0).start()

        self.sib(item, self.z, True).start()
        self.kept(item).start()

    def forward(self, item, step):
        z, count = self.z, self.count

        @pl.when(z >= step)
        def _():
            self.up(item, step - 1).wait_recv()
            if step < count - 1:

                @pl.when(z + 1 < count)
                def _():
                    self.up(item, step).start()

            self.sib(item, z - step).start()

        @pl.when(z + step < count)
        def _():
            self.down(item, step - 1).wait_recv()
            if step < count - 1:

                @pl.when(z > 0)
                def _():
                    self.down(item, step).start()

            self.sib(item, z + step).start()

    def drain(self):
        z, count = self.z, self.count
        for item in range(ITEMS):
            self.kept(item).wait()
            for origin in range(count):
                self.sib(item, origin).wait()
            for step in range(count - 1):

                @pl.when((z >= step) & (z + 1 < count))
                def _(item=item, step=step):
                    self.up(item, step).wait_send()

                @pl.when((z + step < count) & (z > 0))
                def _(item=item, step=step):
                    self.down(item, step).wait_send()

    @staticmethod
    def scratch(count):
        return [DMA((ITEMS,)), *[DMA((count, ITEMS))] * 6]


def far_first(count, z):
    table = []
    for i in range(count):
        ends = sorted(range(count), key=lambda to: (-abs(to - i), 0 if (to > i) == (2 * i < count) else 1))
        lead = [to for to in ends if (to > i) == (2 * i < count) and to != i]
        rest = [to for to in ends if (to > i) != (2 * i < count) and to != i]
        mixed = []
        while lead or rest:
            mixed += lead[:1] + rest[:1]
            lead, rest = lead[1:], rest[1:]
        table.append(mixed + [i])
    power, term = 1, 1
    for k in range(1, count):
        term = (term * (z - k + 1) * (count - 1)) // k
        power = power + term
    packed = [sum(table[i][k] * count**i for i in range(count)) for k in range(count)]
    return [lax.rem(p // power, count) for p in packed]


class LineReduce:
    def __init__(self, held, from_below, from_above, pieces, up_s, up_r, dn_s, dn_r):
        self.held, self.from_below, self.from_above, self.pieces = held, from_below, from_above, pieces
        self.up_s, self.up_r, self.dn_s, self.dn_r = up_s, up_r, dn_s, dn_r
        self.u, self.c, self.z = place()
        self.count = sizes()[2]

    def up(self, to, piece):
        return Transfer(
            self.held.at[to, piece], self.from_below.at[to, piece], self.up_s.at[to, piece], self.up_r.at[to, piece],
            (self.u, self.c, lax.rem(self.z + 1, self.count)),
        )

    def down(self, to, piece):
        return Transfer(
            self.held.at[to, piece], self.from_above.at[to, piece], self.dn_s.at[to, piece], self.dn_r.at[to, piece],
            (self.u, self.c, lax.rem(self.z - 1 + self.count, self.count)),
        )

    def step(self, t):
        z, count = self.z, self.count
        far_up, far_down = count - 1 - t, t

        def upward(piece):
            @pl.when(z > 0)
            def _():
                self.up(far_up, piece).wait_recv()
                self.held[far_up, piece] = add_low(self.held[far_up, piece], self.from_below[far_up, piece])

            self.up(far_up, piece).start()

        def downward(piece):
            @pl.when(z < count - 1)
            def _():
                self.down(far_down, piece).wait_recv()
                self.held[far_down, piece] = add_low(self.held[far_down, piece], self.from_above[far_down, piece])

            self.down(far_down, piece).start()

        lag = min(3, self.pieces // 2)
        late_up = lag * ((2 * z) // count)

        def one(i):
            piece_up, piece_down = i - late_up, i - (lag - late_up)

            @pl.when((z < far_up) & (piece_up >= 0) & (piece_up < self.pieces))
            def _():
                upward(piece_up)

            @pl.when((z > far_down) & (piece_down >= 0) & (piece_down < self.pieces))
            def _():
                downward(piece_down)

        loop(0, self.pieces + lag, one)

    def total(self, piece, into):
        z, count = self.z, self.count
        into[...] = self.held[z, piece].astype(F32)

        @pl.when(z > 0)
        def _():
            self.up(z, piece).wait_recv()
            into[...] += self.from_below[z, piece].astype(F32)

        @pl.when(z < count - 1)
        def _():
            self.down(z, piece).wait_recv()
            into[...] += self.from_above[z, piece].astype(F32)

    def drain(self):
        z, count = self.z, self.count
        for t in range(count - 1):
            far_up, far_down = count - 1 - t, t

            def one(piece, far_up=far_up, far_down=far_down):
                @pl.when(z < far_up)
                def _():
                    self.up(far_up, piece).wait_send()

                @pl.when(z > far_down)
                def _():
                    self.down(far_down, piece).wait_send()

            loop(0, self.pieces, one)

    @staticmethod
    def scratch(count, pieces, block):
        shape = (count, pieces, *block)
        return [*[pltpu.VMEM(shape, BF16)] * 3, *[DMA((count, pieces))] * 4]


def mid_forward_kernel(branch, x, out_grad, params, cut, hidden, mlp, grads, weight, low, *scratch):
    reduce = RowReduce(branch, *scratch[:8])
    gather = LineGather(low, mlp, *scratch[8:15])
    gather_grads = LineGather(out_grad, grads, *scratch[15:22])
    plane = PlaneGather(cut, weight, *scratch[22:])
    greet(True, True)
    reduce.start()
    for item in range(ITEMS):
        gather_grads.start(item)
    reduce.merge()
    for item in range(ITEMS):
        reduce.send(item, 0)
    plane.start()
    for item in range(ITEMS):
        gather_grads.forward(item, 1)
    for phase in range(1, reduce.phases):
        for item in range(ITEMS):
            reduce.add(item, phase - 1)
            reduce.send(item, phase)
    for step in range(2, gather.count - 1):
        for item in range(ITEMS):
            gather_grads.forward(item, step)
    for item in range(ITEMS):
        state = x[item].astype(F32) + reduce.total(item)
        hidden[item] = state
        low[item] = norm_rows(state, params[0:1], params[1:2])[0].astype(BF16)
        gather.start(item)
    plane.step(1)
    for step in range(1, gather.count):
        for item in range(ITEMS):
            gather.forward(item, step)
        if step == 1:
            for item in range(ITEMS):
                gather_grads.forward(item, gather.count - 1)
    for phase in range(2, plane.phases + 1):
        plane.step(phase)
    gather_grads.drain()
    gather.drain()
    plane.drain()
    reduce.drain()


def mid_forward(branch, x, out_grad, params, cut):
    cu, cl, zs = sizes()
    rows, width = x.shape
    block = (ITEMS, rows // ITEMS, width)
    full = jax.ShapeDtypeStruct((zs, cl, *block), BF16)
    hidden, mlp, grads, weight, _ = pl.pallas_call(
        mid_forward_kernel,
        in_specs=[ANY, VMEM, VMEM, VMEM, ANY],
        out_specs=[VMEM, ANY, ANY, ANY, VMEM],
        out_shape=[
            jax.ShapeDtypeStruct(block, F32), full, full, jax.ShapeDtypeStruct((cu, *cut.shape), BF16),
            jax.ShapeDtypeStruct(block, BF16),
        ],
        scratch_shapes=[
            *RowReduce.scratch(cu, rows, width), *LineGather.scratch(zs), *LineGather.scratch(zs),
            *PlaneGather.scratch(cu, cut.shape[0]),
        ],
        cost_estimate=pl.CostEstimate(flops=0, bytes_accessed=200 << 20, transcendentals=0),
        compiler_params=pltpu.CompilerParams(collective_id=1, has_side_effects=True, vmem_limit_bytes=56 << 20),
    )(branch.reshape(cu, cl, *block), x.reshape(block), out_grad.reshape(block), params, cut)
    group_rows = cl * zs * rows
    return (
        hidden.reshape(rows, width), mlp.reshape(group_rows, width), grads.reshape(group_rows, width),
        weight.reshape(width, cut.shape[2]),
    )


def mid_backward_kernel(
    back, in_weight, hidden, out_grad, params, inner, weight, grads,
    grad_hidden, full, sums, layer_out, weight_grad, low,
    held, below, above, up_s, up_r, dn_s, dn_r, both, beside, total, sib_s, sib_r,
    held_out, below_out, above_out, up_so, up_ro, dn_so, dn_ro, both_out, beside_out, sib_so, sib_ro,
    back_v, in_weight_v, inner_v, weight_v, grads_v, fetch, *scratch,
):
    u, c, z = place()
    _, cl, zs = sizes()
    rows = ITEMS * held.shape[2]
    width = weight_v.shape[1]
    reduce = LineReduce(held, below, above, ITEMS, up_s, up_r, dn_s, dn_r)
    reduce_out = LineReduce(held_out, below_out, above_out, ITEMS, up_so, up_ro, dn_so, dn_ro)
    gather = RowGather(low, full, *scratch)
    fetches = [
        pltpu.make_async_copy(source, into, fetch.at[i])
        for i, (source, into) in enumerate(
            ((back, back_v), (in_weight, in_weight_v), (inner, inner_v), (weight, weight_v), (grads, grads_v))
        )
    ]
    for copy in fetches:
        copy.start()

    def sib(to):
        return Transfer(both.at[to, 1 - c], beside.at[to], sib_s.at[to], sib_r.at[to], (u, 1 - c, z))

    def sib_out(to):
        return Transfer(both_out.at[to, 1 - c], beside_out.at[to], sib_so.at[to], sib_ro.at[to], (u, 1 - c, z))

    tile = 512

    def multiply(to, into, left, product):
        def one(i):
            cols = pl.ds(pl.multiple_of(i * tile, tile), tile)
            here = pl.ds(pl.multiple_of(to * (cl * rows), cl * rows), cl * rows)
            part = product(left[here], cols).astype(BF16)
            into[to, :, :, :, cols] = part.reshape(cl, ITEMS, rows // ITEMS, tile)

        loop(0, width // tile, one)

    order = far_first(zs, z)
    fetches[0].wait()
    fetches[1].wait()
    multiply(order[0], both, back_v, lambda left, cols: dot_t(left, in_weight_v[cols]))
    greet(True, True)
    sib(order[0]).start()
    def settle(to):
        sib(to).wait_recv()
        held[to] = add_low(both[to, c], beside[to])

    def settle_out(to):
        sib_out(to).wait_recv()
        held_out[to] = add_low(both_out[to, c], beside_out[to])

    at_end = (z == 0) | (z == zs - 1)
    inside = jnp.logical_not(at_end)
    for k in range(1, zs):
        multiply(order[k], both, back_v, lambda left, cols: dot_t(left, in_weight_v[cols]))
        sib(order[k]).start()
        settle(order[k - 1])

        @pl.when(at_end)
        def _(t=k - 1):
            reduce.step(t)

    settle(order[zs - 1])

    @pl.when(inside)
    def _():
        reduce.step(0)

    fetches[2].wait()
    fetches[3].wait()
    for k in range(zs):
        multiply(
            order[k], both_out, inner_v,
            lambda left, cols: jnp.dot(left, weight_v[:, cols], preferred_element_type=F32),
        )
        sib_out(order[k]).start()

    @pl.when(inside)
    def _():
        for t in range(1, zs - 1):
            reduce.step(t)

    for to in order:
        settle_out(to)

    @pl.when(at_end)
    def _():
        for t in range(zs - 1):
            reduce_out.step(t)

    sums[...] = jnp.zeros_like(sums)
    for item in range(ITEMS):
        reduce.total(item, total)
        _, hat, inverse = norm_rows(hidden[item], params[0:1], params[1:2])
        grad = total[...]
        sums[0:1] += jnp.sum(grad * hat, axis=0, keepdims=True)
        sums[1:2] += jnp.sum(grad, axis=0, keepdims=True)
        grad = out_grad[item].astype(F32) + norm_back(grad, hat, inverse, params[0:1])
        grad_hidden[item] = grad
        low[item] = grad.astype(BF16)
        gather.start(item)
    fetches[4].wait()

    def outer(i):
        cols = pl.ds(pl.multiple_of(i * tile, tile), tile)
        weight_grad[:, cols] = cross_dot(inner_v[...], grads_v[:, cols]).astype(BF16)

    loop(0, width // tile, outer)
    for phase in range(gather.phases):
        for item in range(ITEMS):
            gather.pass_on(item, phase)
            if phase + 1 < gather.phases:
                gather.send(item, phase + 1)
        if phase == 0:

            @pl.when(inside)
            def _():
                reduce_out.step(0)

    @pl.when(inside)
    def _():
        for t in range(1, zs - 1):
            reduce_out.step(t)

    for item in range(ITEMS):
        reduce_out.total(item, total)
        layer_out[item] = (hidden[item] + total[...]).astype(BF16)
    gather.drain()
    reduce.drain()
    reduce_out.drain()
    for to in range(zs):
        sib(to).wait_send()
        sib_out(to).wait_send()


def mid_backward(back_rows, in_weight, hidden, out_grad, params, inner, weight, grads):
    cu, cl, zs = sizes()
    rows, width = out_grad.shape
    block = (ITEMS, rows // ITEMS, width)
    shares = pltpu.VMEM((zs, *block), BF16)
    both = pltpu.VMEM((zs, cl, *block), BF16)
    grad_hidden, full, sums, layer_out, weight_grad, _ = pl.pallas_call(
        mid_backward_kernel,
        in_specs=[ANY, ANY, VMEM, VMEM, VMEM, ANY, ANY, ANY],
        out_specs=[VMEM, ANY, VMEM, VMEM, VMEM, VMEM],
        out_shape=[
            jax.ShapeDtypeStruct(block, F32),
            jax.ShapeDtypeStruct((cu, cl, *block), BF16),
            jax.ShapeDtypeStruct((2, width), F32),
            jax.ShapeDtypeStruct(block, BF16),
            jax.ShapeDtypeStruct(weight.shape, BF16),
            jax.ShapeDtypeStruct(block, BF16),
        ],
        scratch_shapes=[
            *LineReduce.scratch(zs, ITEMS, block[1:]), both, shares, pltpu.VMEM(block[1:], F32), DMA((zs,)), DMA((zs,)),
            *LineReduce.scratch(zs, ITEMS, block[1:]), both, shares, DMA((zs,)), DMA((zs,)),
            pltpu.VMEM(back_rows.shape, BF16), pltpu.VMEM(in_weight.shape, BF16), pltpu.VMEM(inner.shape, BF16),
            pltpu.VMEM(weight.shape, BF16), pltpu.VMEM(grads.shape, BF16), DMA((5,)), *RowGather.scratch(cu),
        ],
        cost_estimate=pl.CostEstimate(flops=0, bytes_accessed=200 << 20, transcendentals=0),
        compiler_params=pltpu.CompilerParams(collective_id=2, has_side_effects=True, vmem_limit_bytes=62 << 20),
    )(back_rows, in_weight, hidden.reshape(block), out_grad.reshape(block), params, inner, weight, grads)
    return (
        grad_hidden.reshape(rows, width), full.reshape(cu * cl * rows, width), sums, layer_out.reshape(rows, width),
        weight_grad,
    )


def tail_kernel(parts, x, grad_hidden, params, terms, grads, proj, input_grad, small, cut, proj_grad, pile, line_in, row_in, total,
                row_total, line_s, line_r, row_s, row_r, a_send, a_recv, own, held_load, low, *scratch):
    u, c, z = place()
    cu, cl, zs = sizes()
    n, me = cu * cl, u * cl + c
    reduce = RowReduce(parts, *scratch[:8])
    held, held_proj = scratch[8], scratch[15]
    line = LineReduce(*scratch[8:11], n, *scratch[11:15])
    line_proj = LineReduce(*scratch[15:18], 1, *scratch[18:])
    load = pltpu.make_async_copy(grads, held, held_load.at[0])
    load_proj = pltpu.make_async_copy(proj, held_proj, held_load.at[1])
    load.start()
    load_proj.start()
    greet(True, True)
    reduce.start()
    load.wait()
    load_proj.wait()
    line.step(0)
    line_proj.step(0)
    reduce.merge()
    for item in range(ITEMS):
        reduce.send(item, 0)
    for t in range(1, zs - 1):
        line.step(t)
        line_proj.step(t)
    for phase in range(1, reduce.phases):
        for item in range(ITEMS):
            reduce.add(item, phase - 1)
            reduce.send(item, phase)
    pile[...] = terms[...]
    for item in range(ITEMS):
        grad = reduce.total(item)
        _, hat, inverse = norm_rows(x[item].astype(F32), params[0:1], params[1:2])
        pile[0:1] += jnp.sum(grad * hat, axis=0, keepdims=True)
        pile[1:2] += jnp.sum(grad, axis=0, keepdims=True)
        grad = grad_hidden[item] + norm_back(grad, hat, inverse, params[0:1])
        input_grad[item] = grad.astype(BF16)

    def along_line(m):
        return Transfer(pile, line_in.at[m], line_s.at[m], line_r.at[m], (u, c, lax.rem(z + m, zs)))

    def along_row(m):
        other = lax.rem(me + m, n)
        return Transfer(
            total, row_in.at[m], row_s.at[m], row_r.at[m], (other // cl, lax.rem(other, cl), z)
        )

    def exchange(m):
        other = lax.rem(me + m, n)
        return Transfer(
            low.at[other], cut.at[me], a_send.at[m], a_recv.at[m], (other // cl, lax.rem(other, cl), z)
        )

    def landed(m):
        source = lax.rem(me - m + n, n)
        return Transfer(
            low.at[source], cut.at[source], a_send.at[m], a_recv.at[m], (u, 1 - c, z)
        )

    loop(1, zs, lambda m: along_line(m).start())

    def finish(m):
        piece = lax.rem(me + m, n)
        line.total(piece, row_total)
        low[piece] = row_total[...].astype(BF16)

        @pl.when(m > 0)
        def _():
            exchange(m).start()

    loop(0, n, finish)
    line_proj.total(0, proj_grad)
    mine = pltpu.make_async_copy(low.at[me], cut.at[me], own.at[0])
    mine.start()
    total[...] = pile[...]
    for m in range(1, zs):
        along_line(m).wait_recv()
        total[...] += line_in[m]
    loop(1, n, lambda m: along_row(m).start())
    small[...] = total[...]

    def collect(m):
        along_row(m).wait_recv()
        small[...] += row_in[m]

    loop(1, n, collect)
    loop(1, n, lambda m: landed(m).wait_recv())
    mine.wait()
    loop(1, n, lambda m: exchange(m).wait_send())
    loop(1, n, lambda m: along_row(m).wait_send())
    loop(1, zs, lambda m: along_line(m).wait_send())
    reduce.drain()
    line.drain()
    line_proj.drain()


def tail(parts, x, grad_hidden, params, terms, grads, proj):
    cu, cl, zs = sizes()
    n = cu * cl
    rows, width = x.shape
    block = (ITEMS, rows // ITEMS, width)
    piece = grads.shape[2:]
    input_grad, small, cut, proj_grad = pl.pallas_call(
        tail_kernel,
        in_specs=[ANY, VMEM, VMEM, VMEM, VMEM, ANY, ANY],
        out_specs=[VMEM, VMEM, ANY, VMEM],
        out_shape=[
            jax.ShapeDtypeStruct(block, BF16),
            jax.ShapeDtypeStruct((8, width), F32),
            jax.ShapeDtypeStruct((n, *piece), BF16),
            jax.ShapeDtypeStruct(proj.shape[2:], F32),
        ],
        scratch_shapes=[
            pltpu.VMEM((8, width), F32), pltpu.VMEM((zs, 8, width), F32), pltpu.VMEM((n, 8, width), F32),
            pltpu.VMEM((8, width), F32), pltpu.VMEM(piece, F32), DMA((zs,)), DMA((zs,)), DMA((n,)), DMA((n,)),
            DMA((n,)), DMA((n,)), DMA((1,)), DMA((2,)), pltpu.VMEM((n, *piece), BF16),
            *RowReduce.scratch(cu, rows, width), *LineReduce.scratch(zs, n, piece),
            *LineReduce.scratch(zs, 1, proj.shape[2:]),
        ],
        cost_estimate=pl.CostEstimate(flops=0, bytes_accessed=200 << 20, transcendentals=0),
        compiler_params=pltpu.CompilerParams(collective_id=3, has_side_effects=True, vmem_limit_bytes=60 << 20),
    )(parts.reshape(cu, cl, *block), x.reshape(block), grad_hidden.reshape(block), params, terms, grads, proj)
    return input_grad.reshape(rows, width), small, cut, proj_grad


def back_kernel(
    heads, qkv_ref, low_ref, tot_ref, pq_ref, dq_ref, pk_ref, dk_ref, table_ref,
    x, grad_hidden, params, mid_sums, branch, proj, mixed, normed, weight, in_cut,
    input_grad, small, cut, proj_grad, in_pieces,
    gq_ref, gk_ref, gv_ref, joined_ref, branch_ref, proj_ref, mixed_ref, normed_v, weight_v, parts, fetch, in_s, in_r,
    pile, line_in, row_in, total, row_total, line_s, line_r, row_s, row_r, a_s, a_r, own, low, *scratch,
):
    u, c, z = place()
    cu, cl, zs = sizes()
    n, me = cu * cl, u * cl + c
    width = heads * HEAD_DIM
    rows = qkv_ref.shape[0]
    block = row_block(rows)
    slab = low.shape[1]
    group = in_cut.shape[0]
    reduce = RowReduce(parts, *scratch[:8])
    held, held_proj = scratch[8], scratch[15]
    line = LineReduce(*scratch[8:11], n, *scratch[11:15])
    line_proj = LineReduce(*scratch[15:18], 1, *scratch[18:])
    my_place = in_group(0)[3]
    kept = pltpu.make_async_copy(in_cut.at[my_place], in_pieces.at[my_place], own.at[1])
    fetches = [
        pltpu.make_async_copy(source, into, fetch.at[i])
        for i, (source, into) in enumerate(
            ((branch, branch_ref), (proj, proj_ref), (mixed, mixed_ref), (normed, normed_v), (weight, weight_v))
        )
    ]

    def in_exchange(m):
        device, after, _, mine = in_group(m)
        return Transfer(in_cut.at[after], in_pieces.at[mine], in_s.at[m], in_r.at[m], device)

    def in_landed(m):
        device, _, before, _ = in_group(m)
        return Transfer(in_cut.at[before], in_pieces.at[before], in_s.at[m], in_r.at[m], device)

    for copy in (kept, *fetches):
        copy.start()
    greet(True, True, True)
    loop(1, group, lambda m: in_exchange(m).start())
    for copy in fetches[:3]:
        copy.wait()
    tile = 512

    def proj_tile(i):
        cols = pl.ds(pl.multiple_of(i * tile, tile), tile)
        grad = cross_dot(low_ref[...], branch_ref[:, cols]).astype(BF16)
        held_proj[:, 0, :, cols] = grad.reshape(zs, slab, tile)

    loop(0, D // tile, proj_tile)
    at_end = (z == 0) | (z == zs - 1)

    @pl.when(at_end)
    def _():
        for t in range(zs - 1):
            line_proj.step(t)

    gk_ref[...] = jnp.zeros_like(gk_ref)
    gv_ref[...] = jnp.zeros_like(gv_ref)

    def one(step):
        here = pl.ds(pl.multiple_of(step * block, block), block)
        grad_all = dot_t(branch_ref[here], proj_ref[...])
        allowed = (pk_ref[...] <= pq_ref[here]) & (dk_ref[...] == dq_ref[here])
        for head in range(heads):
            cols, key, value = (
                slice(p * width + head * HEAD_DIM, p * width + (head + 1) * HEAD_DIM) for p in range(3)
            )
            q, k, v = qkv_ref[here, cols], qkv_ref[:, key], qkv_ref[:, value]
            inverse = 1.0 / tot_ref[here, head : head + 1]
            grad_mixed = grad_all[:, cols]
            grad_weighted = (grad_mixed * inverse).astype(BF16)
            grad_total = -jnp.sum(grad_mixed * mixed_ref[here, cols], axis=1, keepdims=True) * inverse
            weights = jnp.where(allowed, jnp.exp(dot_t(q, k) * SCALE), 0.0)
            grad_scores = (weights * (dot_t(grad_weighted, v) + grad_total)).astype(BF16)
            gq_ref[here, cols] = jnp.dot(grad_scores, k, preferred_element_type=F32) * SCALE
            gk_ref[:, cols] += cross_dot(grad_scores, q) * SCALE
            gv_ref[:, cols] += cross_dot(weights.astype(BF16), grad_weighted)

    blocks = rows // block
    loop(0, blocks // 2, one)

    @pl.when(jnp.logical_not(at_end))
    def _():
        line_proj.step(0)

    loop(blocks // 2, blocks, one)

    @pl.when(jnp.logical_not(at_end))
    def _():
        for t in range(1, zs - 1):
            line_proj.step(t)


    pile[...] = jnp.zeros_like(pile)
    for part, ref in enumerate((gq_ref, gk_ref, gv_ref)):
        for start in range(0, width, LANES):
            grad = ref[:, start : start + LANES]
            if part < 2:
                grad = turn(grad, table_ref[...], -1.0)
            grad = grad.astype(BF16)
            joined_ref[:, part * width + start : part * width + start + LANES] = grad
            there = pl.ds(pl.multiple_of(me * width + start, LANES), LANES)
            pile[4 + part : 5 + part, there] = jnp.sum(grad.astype(F32), axis=0, keepdims=True)
    for copy in fetches[3:]:
        copy.wait()

    def qkv_tile(i):
        cols = pl.ds(pl.multiple_of(i * zs * slab, zs * slab), zs * slab)
        grad = cross_dot(normed_v[:, cols], joined_ref[...]).astype(BF16)
        for to in range(zs):
            held[to, i] = grad[to * slab : (to + 1) * slab]

    loop(0, n, qkv_tile)

    @pl.when(at_end)
    def _():
        for t in range(zs - 1):
            line.step(t)


    def norm_tile(i):
        to, col = i // (D // tile), lax.rem(i, D // tile) * tile
        cols = pl.ds(pl.multiple_of(col, tile), tile)
        here = pl.ds(pl.multiple_of(to * (rows // cu), rows // cu), rows // cu)
        part = dot_t(joined_ref[here], weight_v[cols]).astype(BF16)
        parts[to, :, :, :, cols] = part.reshape(cl, ITEMS, rows // (n * ITEMS), tile)

    loop(0, cu * (D // tile), norm_tile)
    reduce.start()
    reduce.merge()
    for item in range(ITEMS):
        reduce.send(item, 0)

    @pl.when(jnp.logical_not(at_end))
    def _():
        line.step(0)

    for phase in range(1, reduce.phases):
        for item in range(ITEMS):
            reduce.add(item, phase - 1)
            reduce.send(item, phase)
    pile[2:4] = mid_sums[...]
    for item in range(ITEMS):
        grad = reduce.total(item)
        _, hat, inverse = norm_rows(x[item].astype(F32), params[0:1], params[1:2])
        pile[0:1] += jnp.sum(grad * hat, axis=0, keepdims=True)
        pile[1:2] += jnp.sum(grad, axis=0, keepdims=True)
        grad = grad_hidden[item] + norm_back(grad, hat, inverse, params[0:1])
        input_grad[item] = grad.astype(BF16)

    def along_line(m):
        return Transfer(pile, line_in.at[m], line_s.at[m], line_r.at[m], (u, c, lax.rem(z + m, zs)))

    def along_row(m):
        other = lax.rem(me + m, n)
        return Transfer(total, row_in.at[m], row_s.at[m], row_r.at[m], (other // cl, lax.rem(other, cl), z))

    def exchange(m):
        other = lax.rem(me + m, n)
        return Transfer(low.at[other], cut.at[me], a_s.at[m], a_r.at[m], (other // cl, lax.rem(other, cl), z))

    def landed(m):
        source = lax.rem(me - m + n, n)
        return Transfer(low.at[source], cut.at[source], a_s.at[m], a_r.at[m], (u, 1 - c, z))

    loop(1, zs, lambda m: along_line(m).start())

    @pl.when(jnp.logical_not(at_end))
    def _():
        for t in range(1, zs - 1):
            line.step(t)

    total[...] = pile[...]
    for m in range(1, zs):
        along_line(m).wait_recv()
        total[...] += line_in[m]
    loop(1, n, lambda m: along_row(m).start())

    def finish(piece):
        line.total(piece, row_total)
        low[piece] = row_total[...].astype(BF16)
        m = lax.rem(piece - me + n, n)

        @pl.when(m > 0)
        def _():
            exchange(m).start()

    loop(0, n, finish)
    mine = pltpu.make_async_copy(low.at[me], cut.at[me], own.at[0])
    mine.start()
    line_proj.total(0, proj_grad)
    small[...] = total[...]

    def collect(m):
        along_row(m).wait_recv()
        small[...] += row_in[m]

    loop(1, n, collect)
    loop(1, group, lambda m: in_landed(m).wait_recv())
    loop(1, n, lambda m: landed(m).wait_recv())
    mine.wait()
    kept.wait()
    loop(1, group, lambda m: in_exchange(m).wait_send())
    loop(1, n, lambda m: exchange(m).wait_send())
    loop(1, n, lambda m: along_row(m).wait_send())
    loop(1, zs, lambda m: along_line(m).wait_send())
    reduce.drain()
    line.drain()
    line_proj.drain()


def back(qkv, grad_branch, proj, mixed, mixed_low, totals, marks, table, x, grad_hidden, params, mid_sums, normed,
         weight, in_cut, heads):
    cu, cl, zs = sizes()
    n = cu * cl
    rows, width = x.shape
    total_rows, cols = qkv.shape
    slab = width // (n * zs)
    block = (ITEMS, rows // ITEMS, width)
    piece = (slab, cols)
    group = in_cut.shape[0]
    input_grad, small, cut, proj_grad, in_pieces = pl.pallas_call(
        functools.partial(back_kernel, heads),
        in_specs=[*[VMEM] * 12, *[ANY] * 6],
        out_specs=[VMEM, VMEM, ANY, VMEM, ANY],
        out_shape=[
            jax.ShapeDtypeStruct(block, BF16),
            jax.ShapeDtypeStruct((8, width), F32),
            jax.ShapeDtypeStruct((n, *piece), BF16),
            jax.ShapeDtypeStruct((slab, width), F32),
            jax.ShapeDtypeStruct(in_cut.shape, BF16),
        ],
        scratch_shapes=[
            *[pltpu.VMEM((total_rows, cols // 3), F32)] * 3, pltpu.VMEM(qkv.shape, BF16),
            pltpu.VMEM(grad_branch.shape, BF16), pltpu.VMEM(proj.shape, BF16), pltpu.VMEM(mixed.shape, F32),
            pltpu.VMEM(normed.shape, BF16), pltpu.VMEM(weight.shape, BF16), pltpu.VMEM((cu, cl, *block), BF16),
            DMA((5,)), DMA((group,)), DMA((group,)),
            pltpu.VMEM((8, width), F32), pltpu.VMEM((zs, 8, width), F32), pltpu.VMEM((n, 8, width), F32),
            pltpu.VMEM((8, width), F32), pltpu.VMEM(piece, F32), DMA((zs,)), DMA((zs,)), DMA((n,)), DMA((n,)),
            DMA((n,)), DMA((n,)), DMA((2,)), pltpu.VMEM((n, *piece), BF16),
            *RowReduce.scratch(cu, rows, width), *LineReduce.scratch(zs, n, piece),
            *LineReduce.scratch(zs, 1, (slab, width)),
        ],
        cost_estimate=pl.CostEstimate(flops=0, bytes_accessed=400 << 20, transcendentals=0),
        compiler_params=pltpu.CompilerParams(collective_id=5, has_side_effects=True, vmem_limit_bytes=63 << 20),
    )(
        qkv, mixed_low, totals, *marks, table, x.reshape(block), grad_hidden.reshape(block), params, mid_sums,
        grad_branch, proj, mixed, normed, weight, in_cut,
    )
    return input_grad.reshape(rows, width), small, cut, proj_grad, in_pieces


def body(
    inputs, out_grad, doc_ids, block_pairs, qkv_weight, proj_weight, ffn_in_weight, ffn_out_weight, small_params,
    qkv_first, proj_first, ffn_in_first, ffn_out_first, small_first,
    qkv_second, proj_second, ffn_in_second, ffn_out_second, small_second,
):
    bf16 = jnp.bfloat16
    tok_rows = inputs.shape[1]
    half_rows = tok_rows // 2
    cu, cl, zs = lax.axis_size("cu"), lax.axis_size("cl"), lax.axis_size("fsdp")
    ctx_count = cu * cl
    group = cl * zs
    seq_len = tok_rows * ctx_count
    my_index = lax.axis_index(ROW)
    heads = HEADS // ctx_count
    width = heads * HEAD_DIM
    slab = qkv_weight.shape[0]
    units = ffn_out_weight.shape[0]
    hidden = units * cu
    row_in, params, qkv_low, proj_low, in_cast, pos_col, doc_col, pos_row, doc_row, table = gather_head(
        inputs[0], small_params, qkv_weight, ffn_in_weight, proj_weight, block_pairs, doc_ids
    )
    proj_low = proj_low.reshape(width, D)
    marks = (pos_col, doc_col, pos_row, doc_row)
    row_in, in_cast, out_weight_later = lax.optimization_barrier((row_in, in_cast, ffn_out_weight))
    out_low = lax.all_gather(out_weight_later.astype(bf16), "cu", axis=0, tiled=True)
    in_cut = lax.all_to_all(in_cast.reshape(group * slab, 2 * hidden), FFN_GROUP, split_axis=0, concat_axis=0, tiled=True)
    row_in = row_in.reshape(seq_len, D)
    params = params[:, :, :7, :slab].transpose(2, 0, 1, 3).reshape(7, D)
    qkv_low = qkv_low.reshape(D, 3 * width)

    bias = lax.dynamic_slice_in_dim(params[4:7], my_index * width, width, 1).reshape(1, 3 * width)
    attn_in, qkv = project(row_in, params[0:2], qkv_low, bias, table)
    mixed, mixed_low, totals, branch = attend(qkv, proj_low, marks, heads)
    branch, in_cut = lax.optimization_barrier((branch, in_cut))
    hidden_state, mlp_in, grad_all, in_low = mid_forward(
        branch, inputs[0], out_grad[0], params[2:4], in_cut.reshape(group, slab, 2 * hidden)
    )

    inner_low, grad_gate_up, grad_ffn_in = feed(mlp_in, grad_all, in_low, out_low)
    in_grad_cut = lax.psum_scatter(grad_ffn_in, "cu", scatter_dimension=0, tiled=True)

    grad_hidden, grad_branch, mid_sums, layer_out, grad_ffn_out = mid_backward(
        grad_gate_up, in_low, hidden_state, out_grad[0], params[2:4], inner_low, out_low, grad_all
    )
    layer_out = layer_out[None]
    in_grad_cut, grad_branch = lax.optimization_barrier((in_grad_cut, grad_branch))
    in_grad_cut = in_grad_cut.reshape(group, slab, 2 * hidden)
    grad_ffn_out, in_grad_cut = lax.optimization_barrier((grad_ffn_out, in_grad_cut))
    ffn_out_grad = lax.psum_scatter(grad_ffn_out, "cu", scatter_dimension=0, tiled=True)
    if seq_len <= 1024 and width % LANES == 0:
        input_grad, small_sum, qkv_grad_cut, proj_grad, in_grad = back(
            qkv, grad_branch, proj_low, mixed, mixed_low, totals, marks, table, inputs[0], grad_hidden, params[0:2],
            mid_sums, attn_in, qkv_low, in_grad_cut, heads,
        )
    else:
        grad_proj = cross_dot(mixed_low, grad_branch).astype(bf16)
        grad_joined, bias_own, in_grad = attend_back(
            qkv, grad_branch, proj_low, mixed, totals, marks, table, in_grad_cut, heads
        )
        grad_norm_part = back_dot(grad_joined, qkv_low).astype(bf16)
        grad_qkv = (
            cross_dot(attn_in, grad_joined).astype(bf16).reshape(ctx_count, zs, slab, 3 * width).transpose(1, 0, 2, 3)
        )
        bias_own = bias_own.reshape(3, width)
        grad_bias = lax.dynamic_update_slice(jnp.zeros((3, D), jnp.float32), bias_own, (0, my_index * width))
        zero_rows = jnp.zeros((2, D), jnp.float32)
        terms = jnp.concatenate([zero_rows, mid_sums, grad_bias, zero_rows[:1]], axis=0)
        input_grad, small_sum, qkv_grad_cut, proj_grad = tail(
            grad_norm_part, inputs[0], grad_hidden, params[0:2], terms, grad_qkv, grad_proj.reshape(zs, 1, slab, D)
        )
    input_grad = input_grad[None]
    my_slab = (my_index * zs + lax.axis_index("fsdp")) * slab
    small_grad = lax.dynamic_slice_in_dim(small_sum, my_slab, slab, 1)[:7]

    proj_fan = max(8 * D // seq_len, 1)
    in_new, qkv_new, out_new, proj_new = adam_all(
        (
            (ffn_in_weight, ffn_in_first, ffn_in_second, in_grad),
            (qkv_weight, qkv_first, qkv_second, qkv_grad_cut),
            (ffn_out_weight, ffn_out_first, ffn_out_second, ffn_out_grad),
            (proj_weight, proj_first, proj_second, proj_grad),
        ),
        (2.0 / math.sqrt(D), 2.0 / math.sqrt(D), 2.0 / math.sqrt(FF), 2.0 / math.sqrt(proj_fan)),
    )
    small_new = adam_update(small_params, small_first, small_second, small_grad, small_rate, 0.0)
    news = (qkv_new, proj_new, in_new, out_new, small_new)
    return (layer_out, input_grad, *(n[0] for n in news), *(n[1] for n in news), *(n[2] for n in news), small_grad)


def solution(mesh):
    ctx_count, fsdp_count = mesh.devices.shape
    fine = Mesh(mesh.devices.reshape(ctx_count // 2, 2, fsdp_count), ("cu", "cl", "fsdp"))
    tokens = P("fsdp", ROW, None)
    matrix = P(EVERY, None)
    small = P(None, EVERY)
    five = (matrix, matrix, matrix, matrix, small)
    in_specs = (tokens, tokens, P("fsdp", None), P(), *five, *five, *five)
    out_specs = (tokens, tokens, *five, *five, *five, small)
    return jax.shard_map(body, mesh=fine, in_specs=in_specs, out_specs=out_specs, check_vma=False)
```

```python
import functools
import math

import jax
import jax.numpy as jnp
from jax import lax
from jax.experimental import pallas as pl
from jax.experimental.pallas import tpu as pltpu
from jax.sharding import Mesh, PartitionSpec as P

D = 2048
HEADS = 32
HEAD_DIM = 64
FF = 5632
ROT = 16
STEP = 10


norm_eps = 1e-05
beta_first = 0.9
beta_second = 0.95
adam_eps = 1e-08
matrix_decay = 0.1
small_rate = 0.5


def norm_rows(values, gain_row, shift_row):
    center_mean = jnp.mean(values, axis=-1, keepdims=True)
    centered = values - center_mean
    inv_std = lax.rsqrt(jnp.mean(centered * centered, axis=-1, keepdims=True) + norm_eps)
    normed = centered * inv_std
    return (normed * gain_row + shift_row, normed, inv_std)


def norm_back(grad_rows, normed, inv_std, gain_row):
    scaled = grad_rows * gain_row
    return inv_std * (
        scaled
        - jnp.mean(scaled, axis=-1, keepdims=True)
        - normed * jnp.mean(scaled * normed, axis=-1, keepdims=True)
    )


def cross_dot(left_mat, right_mat):
    return lax.dot_general(
        left_mat, right_mat, (((0,), (0,)), ((), ())), preferred_element_type=jnp.float32
    )


def back_dot(left_mat, weight):
    return lax.dot_general(
        left_mat, weight, (((1,), (1,)), ((), ())), preferred_element_type=jnp.float32
    )


def adam_update(weight, first_moment, second_moment, gradient, step_rate, decay_factor):
    new_first = beta_first * first_moment + (1.0 - beta_first) * gradient
    new_second = beta_second * second_moment + (1.0 - beta_second) * gradient * gradient
    correct_first = 1.0 - beta_first**STEP
    correct_second = 1.0 - beta_second**STEP
    update = new_first / correct_first / (jnp.sqrt(new_second / correct_second) + adam_eps)
    return (weight - step_rate * (update + decay_factor * weight), new_first, new_second)


ROW = ("cu", "cl")
FFN_GROUP = ("cl", "fsdp")
EVERY = ("cu", "cl", "fsdp")
SCALE = HEAD_DIM**-0.5


LANES = 128


def fill_table(table, positions, start, rows):
    half_rot = ROT // 2
    here = pl.ds(pl.multiple_of(start, rows), rows)
    lane = lax.rem(lax.broadcasted_iota(jnp.int32, (1, LANES), 1), HEAD_DIM)
    inverse = jnp.zeros((1, LANES), jnp.float32)
    for i in range(half_rot):
        inverse = jnp.where(lax.rem(lane, half_rot) == i, 10000.0 ** (-2.0 * i / ROT), inverse)
    angles = positions[here, :].astype(jnp.float32) * jnp.where(lane < ROT, inverse, 0.0)
    sine = jnp.sin(angles)
    table[here, 0:LANES] = jnp.cos(angles)
    table[here, LANES : 2 * LANES] = jnp.where(lane < half_rot, -sine, 0.0)
    table[here, 2 * LANES : 3 * LANES] = jnp.where(lane < half_rot, 0.0, sine)


def turn(values, table, sign):
    keep, lower, upper = (table[:, i * LANES : (i + 1) * LANES] for i in range(3))
    half_rot = ROT // 2
    shifted = pltpu.roll(values, LANES - half_rot, 1) * lower + pltpu.roll(values, half_rot, 1) * upper
    return values * keep + sign * shifted


def dot_t(left, right):
    return lax.dot_general(left, right, (((1,), (1,)), ((), ())), preferred_element_type=jnp.float32)


def row_block(rows):
    return min(256, rows)


def project_kernel(x_ref, params_ref, w_ref, bias_ref, table_ref, normed_ref, qkv_ref):
    normed = norm_rows(x_ref[...].astype(jnp.float32), params_ref[0:1], params_ref[1:2])[0].astype(jnp.bfloat16)
    normed_ref[...] = normed
    joined = jnp.dot(normed, w_ref[...], preferred_element_type=jnp.float32) + bias_ref[...]
    turned = 2 * (joined.shape[1] // 3)
    for start in range(0, turned, LANES):
        cols = slice(start, start + LANES)
        qkv_ref[:, cols] = turn(joined[:, cols], table_ref[...], 1.0).astype(jnp.bfloat16)
    qkv_ref[:, turned:] = joined[:, turned:].astype(jnp.bfloat16)


def project(x, params, weight, bias, table):
    rows, width = x.shape
    block = row_block(rows)
    cols = weight.shape[1]

    def by_row(n):
        return pl.BlockSpec((block, n), lambda i: (i, 0))

    def whole(array):
        return pl.BlockSpec(array.shape, lambda i: (0, 0))

    return pl.pallas_call(
        project_kernel,
        grid=(rows // block,),
        in_specs=[by_row(width), whole(params), whole(weight), whole(bias), by_row(table.shape[1])],
        out_specs=[by_row(width), by_row(cols)],
        out_shape=[jax.ShapeDtypeStruct((rows, width), jnp.bfloat16), jax.ShapeDtypeStruct((rows, cols), jnp.bfloat16)],
        cost_estimate=pl.CostEstimate(
            flops=2 * rows * width * cols, bytes_accessed=4 * rows * width, transcendentals=0
        ),
        compiler_params=pltpu.CompilerParams(vmem_limit_bytes=48 << 20),
    )(x, params, weight, bias, table)


def attend_kernel(
    heads, q_ref, qkv_ref, proj_ref, pq_ref, dq_ref, pk_ref, dk_ref, mixed_ref, low_ref, tot_ref, branch_ref
):
    width = heads * HEAD_DIM
    allowed = (pk_ref[...] <= pq_ref[...]) & (dk_ref[...] == dq_ref[...])
    for head in range(heads):
        cols, key, value = (slice(p * width + head * HEAD_DIM, p * width + (head + 1) * HEAD_DIM) for p in range(3))
        scores = dot_t(q_ref[:, cols], qkv_ref[:, key]) * SCALE
        weights = jnp.where(allowed, jnp.exp(scores), 0.0)
        total = jnp.sum(weights, axis=1, keepdims=True)
        weighted = jnp.dot(weights.astype(jnp.bfloat16), qkv_ref[:, value], preferred_element_type=jnp.float32)
        mixed = weighted / total
        mixed_ref[:, cols] = mixed
        low_ref[:, cols] = mixed.astype(jnp.bfloat16)
        tot_ref[:, head : head + 1] = total
    branch_ref[...] = jnp.dot(low_ref[...], proj_ref[...], preferred_element_type=jnp.float32).astype(jnp.bfloat16)


def attend(qkv, proj, marks, heads):
    pos_col, doc_col, pos_row, doc_row = marks
    rows, cols = qkv.shape
    width = cols // 3
    block = row_block(rows)

    def by_row(n):
        return pl.BlockSpec((block, n), lambda i: (i, 0))

    def whole(array):
        return pl.BlockSpec(array.shape, lambda i: (0, 0))

    return pl.pallas_call(
        functools.partial(attend_kernel, heads),
        grid=(rows // block,),
        in_specs=[by_row(cols), whole(qkv), whole(proj), by_row(1), by_row(1), whole(pos_row), whole(doc_row)],
        out_specs=[by_row(width), by_row(width), by_row(heads), by_row(D)],
        out_shape=[
            jax.ShapeDtypeStruct((rows, width), jnp.float32),
            jax.ShapeDtypeStruct((rows, width), jnp.bfloat16),
            jax.ShapeDtypeStruct((rows, heads), jnp.float32),
            jax.ShapeDtypeStruct((rows, D), jnp.bfloat16),
        ],
        cost_estimate=pl.CostEstimate(
            flops=4 * rows * rows * width, bytes_accessed=8 * rows * D, transcendentals=rows * rows * heads
        ),
        compiler_params=pltpu.CompilerParams(vmem_limit_bytes=48 << 20),
    )(qkv, qkv, proj, pos_col, doc_col, pos_row, doc_row)


def attend_back_kernel(
    heads, qkv_ref, branch_ref, proj_ref, mixed_ref, tot_ref, pq_ref, dq_ref, pk_ref, dk_ref, table_ref, cut,
    joined_ref, bias_ref, pieces, gq_ref, gk_ref, gv_ref, own, send, recv,
):
    width = heads * HEAD_DIM
    rows = qkv_ref.shape[0]
    block = row_block(rows)
    group = cut.shape[0]

    def exchange(m):
        device, after, _, me = in_group(m)
        return Transfer(cut.at[after], pieces.at[me], send.at[m], recv.at[m], device)

    def landed(m):
        device, _, before, _ = in_group(m)
        return Transfer(cut.at[before], pieces.at[before], send.at[m], recv.at[m], device)

    me = in_group(0)[3]
    kept = pltpu.make_async_copy(cut.at[me], pieces.at[me], own.at[0])
    kept.start()
    greet_group()
    loop(1, group, lambda m: exchange(m).start())
    gk_ref[...] = jnp.zeros_like(gk_ref)
    gv_ref[...] = jnp.zeros_like(gv_ref)

    def one(step):
        here = pl.ds(pl.multiple_of(step * block, block), block)
        grad_all = dot_t(branch_ref[here], proj_ref[...])
        allowed = (pk_ref[...] <= pq_ref[here]) & (dk_ref[...] == dq_ref[here])
        for head in range(heads):
            cols, key, value = (
                slice(p * width + head * HEAD_DIM, p * width + (head + 1) * HEAD_DIM) for p in range(3)
            )
            q, k, v = qkv_ref[here, cols], qkv_ref[:, key], qkv_ref[:, value]
            inverse = 1.0 / tot_ref[here, head : head + 1]
            grad_mixed = grad_all[:, cols]
            grad_weighted = (grad_mixed * inverse).astype(jnp.bfloat16)
            grad_total = -jnp.sum(grad_mixed * mixed_ref[here, cols], axis=1, keepdims=True) * inverse
            weights = jnp.where(allowed, jnp.exp(dot_t(q, k) * SCALE), 0.0)
            grad_scores = (weights * (dot_t(grad_weighted, v) + grad_total)).astype(jnp.bfloat16)
            gq_ref[here, cols] = jnp.dot(grad_scores, k, preferred_element_type=jnp.float32) * SCALE
            gk_ref[:, cols] += cross_dot(grad_scores, q) * SCALE
            gv_ref[:, cols] += cross_dot(weights.astype(jnp.bfloat16), grad_weighted)

    loop(0, rows // block, one)
    for part, ref in enumerate((gq_ref, gk_ref, gv_ref)):
        for start in range(0, width, LANES):
            cols = slice(start, min(start + LANES, width))
            grad = ref[:, cols]
            if part < 2:
                lanes = cols.stop - cols.start
                if lanes < LANES:
                    grad = jnp.concatenate([grad, jnp.zeros((rows, LANES - lanes), jnp.float32)], axis=1)
                grad = turn(grad, table_ref[...], -1.0)[:, :lanes]
            grad = grad.astype(jnp.bfloat16)
            into = slice(part * width + cols.start, part * width + cols.stop)
            joined_ref[:, into] = grad
            bias_ref[:, into] = jnp.sum(grad.astype(jnp.float32), axis=0, keepdims=True)
    loop(1, group, lambda m: landed(m).wait_recv())
    loop(1, group, lambda m: exchange(m).wait_send())
    kept.wait()


def attend_back(qkv, grad_branch, proj, mixed, totals, marks, table, cut, heads):
    rows, cols = qkv.shape
    width = cols // 3
    return pl.pallas_call(
        functools.partial(attend_back_kernel, heads),
        in_specs=[*[VMEM] * 10, ANY],
        out_specs=[VMEM, VMEM, ANY],
        out_shape=[
            jax.ShapeDtypeStruct((rows, cols), jnp.bfloat16), jax.ShapeDtypeStruct((1, cols), jnp.float32),
            jax.ShapeDtypeStruct(cut.shape, BF16),
        ],
        scratch_shapes=[
            *[pltpu.VMEM((rows, width), jnp.float32)] * 3, DMA((1,)), DMA((cut.shape[0],)), DMA((cut.shape[0],)),
        ],
        cost_estimate=pl.CostEstimate(
            flops=10 * rows * rows * width, bytes_accessed=8 * rows * D, transcendentals=rows * rows * heads
        ),
        compiler_params=pltpu.CompilerParams(collective_id=4, has_side_effects=True, vmem_limit_bytes=60 << 20),
    )(qkv, grad_branch, proj, mixed, totals, *marks, table, cut)


def feed_kernel(x_ref, grad_ref, in_ref, out_ref, inner_ref, back_ref, in_grad_ref, x_all, back_all):
    step = pl.program_id(0)
    block = x_ref.shape[0]
    here = pl.ds(pl.multiple_of(step * block, block), block)
    hidden = out_ref.shape[0]
    gate_up = jnp.dot(x_ref[...], in_ref[...], preferred_element_type=jnp.float32)
    gate, up = gate_up[:, :hidden], gate_up[:, hidden:]
    grad_inner = dot_t(grad_ref[...], out_ref[...])
    sigmoid = 1.0 / (1.0 + jnp.exp(-gate))
    silu = gate * sigmoid
    inner_ref[...] = (silu * up).astype(jnp.bfloat16)
    grad_gate = grad_inner * up * (sigmoid * (1.0 + gate * (1.0 - sigmoid)))
    back = jnp.concatenate([grad_gate, grad_inner * silu], axis=1).astype(jnp.bfloat16)
    back_ref[...] = back
    x_all[here] = x_ref[...]
    back_all[here] = back

    @pl.when(step == x_all.shape[0] // block - 1)
    def _():
        tile = 256

        def one(i, carry):
            rows = pl.ds(pl.multiple_of(i * tile, tile), tile)
            in_grad_ref[rows] = cross_dot(x_all[:, rows], back_all[...]).astype(jnp.bfloat16)
            return carry

        lax.fori_loop(0, x_all.shape[1] // tile, one, 0)


def feed(x, grad, in_weight, out_weight):
    rows, width = x.shape
    hidden = out_weight.shape[0]
    block = row_block(rows)

    def by_row(n):
        return pl.BlockSpec((block, n), lambda i: (i, 0))

    def whole(array):
        return pl.BlockSpec(array.shape, lambda i: (0, 0))

    return pl.pallas_call(
        feed_kernel,
        grid=(rows // block,),
        in_specs=[by_row(width), by_row(width), whole(in_weight), whole(out_weight)],
        out_specs=[by_row(hidden), by_row(2 * hidden), whole(in_weight)],
        out_shape=[
            jax.ShapeDtypeStruct((rows, hidden), jnp.bfloat16), jax.ShapeDtypeStruct((rows, 2 * hidden), jnp.bfloat16),
            jax.ShapeDtypeStruct(in_weight.shape, jnp.bfloat16),
        ],
        scratch_shapes=[pltpu.VMEM((rows, width), jnp.bfloat16), pltpu.VMEM((rows, 2 * hidden), jnp.bfloat16)],
        cost_estimate=pl.CostEstimate(
            flops=10 * rows * width * hidden, bytes_accessed=8 * rows * width, transcendentals=rows * hidden
        ),
        compiler_params=pltpu.CompilerParams(vmem_limit_bytes=60 << 20),
    )(x, grad, in_weight, out_weight)


def adam_kernel(rates, chunks, *refs):
    sources, results, held = refs[:16], refs[16:28], refs[28:44]
    came, left = refs[44:]

    def rows_of(k, i):
        size = held[4 * k].shape[0] // chunks[k]
        return pl.ds(pl.multiple_of(i * size, size), size)

    def load(k, i, part):
        here = rows_of(k, i)
        at = (slice(None), here) if held[4 * k + part].ndim == 3 else (here,)
        return pltpu.make_async_copy(
            sources[4 * k + part].at[at], held[4 * k + part].at[at], came.at[4 * k + part, i]
        )

    def store(k, i, part):
        here = rows_of(k, i)
        return pltpu.make_async_copy(
            held[4 * k + part].at[here], results[3 * k + part].at[here], left.at[3 * k + part, i]
        )

    def run(k, step):
        def one(i, carry):
            step(i)
            return carry

        lax.fori_loop(0, chunks[k], one, 0)

    def start(k):
        def one(i):
            for part in range(4):
                load(k, i, part).start()

        run(k, one)

    def update(k):
        w, m, v, g = held[4 * k : 4 * k + 4]

        def one(i):
            here = rows_of(k, i)
            for part in range(4):
                load(k, i, part).wait()
            cols, parts = w.shape[1], 1
            if g.ndim == 3:
                parts = 3 if k == 1 else cols // g.shape[2]
                cols = cols // parts
            for part in range(parts):
                there = slice(part * cols, (part + 1) * cols)
                if g.ndim == 3:
                    width = g.shape[2] // parts
                    grad = jnp.concatenate(
                        [g[owner, here, part * width : (part + 1) * width] for owner in range(g.shape[0])], axis=1
                    )
                else:
                    grad = g[here, there]
                new = adam_update(
                    w[here, there], m[here, there], v[here, there], grad.astype(jnp.float32), rates[k], matrix_decay
                )
                for ref, value in zip((w, m, v), new):
                    ref[here, there] = value
            for part in range(3):
                store(k, i, part).start()

        run(k, one)

    def finish(k):
        def one(i):
            for part in range(3):
                store(k, i, part).wait()

        run(k, one)

    order = (2, 3, 0, 1)
    for k in order:
        start(k)
    for k in order:
        update(k)
    for k in order:
        finish(k)


def adam_all(states, rates):
    chunks, operands, out_shape = [], [], []
    for state in states:
        rows = state[0].shape[0]
        size = 32 if rows % 32 == 0 else 16
        chunks.append(rows // size if rows % size == 0 else 1)
        operands += state
        out_shape += [jax.ShapeDtypeStruct(state[0].shape, jnp.float32)] * 3
    any_ref = pl.BlockSpec(memory_space=pl.ANY)
    out = pl.pallas_call(
        functools.partial(adam_kernel, rates, chunks),
        in_specs=[any_ref] * 16,
        out_specs=[any_ref] * 12,
        out_shape=out_shape,
        scratch_shapes=[
            *[pltpu.VMEM(array.shape, array.dtype) for array in operands],
            pltpu.SemaphoreType.DMA((16, max(chunks))), pltpu.SemaphoreType.DMA((12, max(chunks))),
        ],
        compiler_params=pltpu.CompilerParams(vmem_limit_bytes=60 << 20),
    )(*operands)
    return [tuple(out[3 * k : 3 * k + 3]) for k in range(4)]


MESH = pl.DeviceIdType.MESH
ANY = pl.BlockSpec(memory_space=pl.ANY)
VMEM = pl.BlockSpec(memory_space=pltpu.VMEM)
DMA = pltpu.SemaphoreType.DMA
BF16, F32 = jnp.bfloat16, jnp.float32


class Transfer:
    def __init__(self, src, dst, send, recv, device):
        self.parts = (src, dst, send, recv, device)

    def copy(self):
        src, dst, send, recv, device = self.parts
        return pltpu.make_async_remote_copy(
            src_ref=src, dst_ref=dst, send_sem=send, recv_sem=recv, device_id=device, device_id_type=MESH
        )

    def start(self):
        self.copy().start()

    def wait_recv(self):
        self.copy().wait_recv()

    def wait_send(self):
        self.copy().wait_send()

    def wait(self):
        self.copy().wait()


rcopy = Transfer


def flip(index, mask):
    bit = 1
    while bit <= mask:
        if mask & bit:
            index = index + bit * (1 - 2 * lax.rem(index // bit, 2))
        bit *= 2
    return index


def place():
    return lax.axis_index("cu"), lax.axis_index("cl"), lax.axis_index("fsdp")


def sizes():
    return lax.axis_size("cu"), lax.axis_size("cl"), lax.axis_size("fsdp")


def in_group(m):
    u, c, z = place()
    _, cl, zs = sizes()
    group, me = cl * zs, c * zs + z
    after, before = lax.rem(me + m, group), lax.rem(me - m + group, group)
    return (u, after // zs, lax.rem(after, zs)), after, before, me


def greet_group():
    _, cl, zs = sizes()
    barrier = pltpu.get_barrier_semaphore()

    def signal(m, carry):
        pl.semaphore_signal(barrier, inc=1, device_id=in_group(m)[0], device_id_type=MESH)
        return carry

    lax.fori_loop(1, cl * zs, signal, 0)
    pl.semaphore_wait(barrier, cl * zs - 1)


def greet(row, line, twins=False):
    u, c, z = place()
    cu, cl, zs = sizes()
    n, me = cu * cl, u * cl + c
    barrier = pltpu.get_barrier_semaphore()

    def signal_row(m, carry):
        other = lax.rem(me + m, n)
        pl.semaphore_signal(barrier, inc=1, device_id=(other // cl, lax.rem(other, cl), z), device_id_type=MESH)
        return carry

    def signal_line(m, carry):
        pl.semaphore_signal(barrier, inc=1, device_id=(u, c, lax.rem(z + m, zs)), device_id_type=MESH)
        return carry

    def signal_twins(m, carry):
        pl.semaphore_signal(barrier, inc=1, device_id=(u, 1 - c, lax.rem(z + m, zs)), device_id_type=MESH)
        return carry

    if row:
        lax.fori_loop(1, n, signal_row, 0)
    if line:
        lax.fori_loop(1, zs, signal_line, 0)
    if twins:
        lax.fori_loop(1, zs, signal_twins, 0)
    pl.semaphore_wait(barrier, row * (n - 1) + (line + twins) * (zs - 1))


def head_kernel(
    x, small_in, qkv_far, ffn_far, proj_far, pairs, docs_in, row, par, wq, wp, in_cut, pos_col, doc_col, pos_row, doc_row,
    table, qkv_in, ffn_in, proj_in, docs, fetch, qkv, proj, small, own, x_send, x_recv, s_send, s_recv, p_send, p_recv, q_send, q_recv,
    a_send, a_recv, up_send, up_recv, dn_send, dn_recv,
):
    u, c, z = place()
    cu, cl, zs = sizes()
    n, me = cu * cl, u * cl + c
    sibling = (u, 1 - c, z)
    slab, width = qkv_in.shape[0], qkv_in.shape[1] // (3 * n)
    half = docs.shape[1]
    fetches = [
        pltpu.make_async_copy(source, into, fetch.at[i])
        for i, (source, into) in enumerate(((qkv_far, qkv_in), (proj_far, proj_in), (ffn_far, ffn_in)))
    ]
    for copy in fetches:
        copy.start()
    for i in range(docs.shape[0]):
        docs[i : i + 1] = docs_in[:, i * half : (i + 1) * half]
    small[...] = jnp.zeros_like(small)
    small[: small_in.shape[0], : small_in.shape[1]] = small_in[...]
    fetches[0].wait()
    for owner in range(n):
        for part in range(3):
            start = (part * n + owner) * width
            qkv[owner, :, part * width : (part + 1) * width] = qkv_in[:, start : start + width].astype(BF16)
    mine = [
        pltpu.make_async_copy(qkv.at[me], wq.at[me, z], own.at[0]),
        pltpu.make_async_copy(x, row.at[u, c], own.at[1]),
        pltpu.make_async_copy(small, par.at[me, z], own.at[2]),
        pltpu.make_async_copy(proj, wp.at[z], own.at[3]),
    ]
    fetches[1].wait()
    proj[...] = proj_in[...].astype(BF16)
    for copy in mine:
        copy.start()
    greet(True, True)

    def exchange(m):
        other, source = lax.rem(me + m, n), lax.rem(me - m + n, n)
        out = rcopy(
            qkv.at[other], wq.at[me, z], a_send.at[m], a_recv.at[m], (other // cl, lax.rem(other, cl), z)
        )
        into = rcopy(qkv.at[other], wq.at[source, z], a_send.at[m], a_recv.at[m], sibling)
        return out, into

    def params_line(m):
        other, source = lax.rem(z + m, zs), lax.rem(z - m + zs, zs)
        return (
            rcopy(small, par.at[me, z], p_send.at[m], p_recv.at[m], (u, c, other)),
            rcopy(small, par.at[me, source], p_send.at[m], p_recv.at[m], sibling),
        )

    def params_row(m):
        other, source = lax.rem(me + m, n), lax.rem(me - m + n, n)
        return (
            rcopy(par.at[me], par.at[me], q_send.at[m], q_recv.at[m], (other // cl, lax.rem(other, cl), z)),
            rcopy(par.at[me], par.at[source], q_send.at[m], q_recv.at[m], sibling),
        )

    def x_far(i):
        out = rcopy(x, row.at[u, c], x_send.at[i], x_recv.at[i], (flip(u, i), c, z))
        into = rcopy(x, row.at[flip(u, i), c], x_send.at[i], x_recv.at[i], sibling)
        return out, into

    def x_near(i):
        part = row.at[flip(u, i), c]
        out = rcopy(part, part, s_send.at[i], s_recv.at[i], sibling)
        into = rcopy(part, row.at[flip(u, i), 1 - c], s_send.at[i], s_recv.at[i], sibling)
        return out, into

    def loop(low, high, step):
        def run(m, carry):
            step(m)
            return carry

        lax.fori_loop(low, high, run, 0)

    loop(1, n, lambda m: exchange(m)[0].start())
    loop(1, zs, lambda m: params_line(m)[0].start())
    for copy in mine:
        copy.wait()
    for i in range(1, cu):
        x_far(i)[0].start()
    x_near(0)[0].start()

    def chain(step, m):
        piece = lax.rem(me - m + n, n)
        above, below = wq.at[piece, lax.rem(z + step, zs)], wq.at[piece, lax.rem(z - step + zs, zs)]
        return (
            rcopy(below, below, up_send.at[step, m], up_recv.at[step, m], (u, c, lax.rem(z + 1, zs))),
            rcopy(above, above, dn_send.at[step, m], dn_recv.at[step, m], (u, c, lax.rem(z - 1 + zs, zs))),
        )

    def arrival(step, m):
        piece = lax.rem(me - m + n, n)
        above, below = wq.at[piece, lax.rem(z + step + 1, zs)], wq.at[piece, lax.rem(z - step - 1 + zs, zs)]
        return (
            rcopy(below, below, up_send.at[step, m], up_recv.at[step, m], sibling),
            rcopy(above, above, dn_send.at[step, m], dn_recv.at[step, m], sibling),
        )

    def chain_proj(step):
        above, below = wp.at[lax.rem(z + step, zs)], wp.at[lax.rem(z - step + zs, zs)]
        return (
            rcopy(below, below, up_send.at[step, n], up_recv.at[step, n], (u, c, lax.rem(z + 1, zs))),
            rcopy(above, above, dn_send.at[step, n], dn_recv.at[step, n], (u, c, lax.rem(z - 1 + zs, zs))),
        )

    def forward_proj(step):
        if step:

            @pl.when(z >= step)
            def _():
                chain_proj(step - 1)[0].wait_recv()

            @pl.when(z + step < zs)
            def _():
                chain_proj(step - 1)[1].wait_recv()

        if step < zs - 1:

            @pl.when((z >= step) & (z + 1 < zs))
            def _():
                chain_proj(step)[0].start()

            @pl.when((z + step < zs) & (z > 0))
            def _():
                chain_proj(step)[1].start()

    def sent_proj(step):
        @pl.when((z >= step) & (z + 1 < zs))
        def _():
            chain_proj(step)[0].wait_send()

        @pl.when((z + step < zs) & (z > 0))
        def _():
            chain_proj(step)[1].wait_send()

    def first(m):
        @pl.when(m > 0)
        def _():
            exchange(m)[1].wait_recv()

        @pl.when(z + 1 < zs)
        def _():
            chain(0, m)[0].start()

        @pl.when(z > 0)
        def _():
            chain(0, m)[1].start()

    loop(0, n, first)
    forward_proj(0)
    fetches[2].wait()
    group, units = cl * zs, ffn_in.shape[1] // (2 * n * zs)
    for part in range(2 * cu):
        for owner in range(group):
            start = (part * group + owner) * units
            in_cut[owner, :, part * units : (part + 1) * units] = ffn_in[:, start : start + units].astype(BF16)
    lane, line_of = (lax.broadcasted_iota(jnp.int32, (half, half), d) for d in (1, 0))

    def column(values):
        return jnp.sum(jnp.where(lane == line_of, values, 0), axis=1, keepdims=True)

    for slot in range(n):
        for part in range(2):
            here = slice((2 * slot + part) * half, (2 * slot + part + 1) * half)
            number = pairs[slot, part]
            positions = number * half + lax.broadcasted_iota(jnp.int32, (1, half), 1)
            documents = docs[pl.ds(number, 1), :]
            pos_row[:, here], doc_row[:, here] = positions, documents
            pos_col[here, :], doc_col[here, :] = column(positions), column(documents)
    loop(0, n, lambda i: fill_table(table, pos_col, i * 2 * half, 2 * half))
    for m in range(1, zs):
        params_line(m)[1].wait_recv()
    loop(1, n, lambda m: params_row(m)[0].start())
    for step in range(1, zs):

        def later(m, step=step):
            @pl.when(z >= step)
            def _():
                arrival(step - 1, m)[0].wait_recv()

            @pl.when((z >= step) & (z + 1 < zs))
            def _():
                chain(step, m)[0].start()

            @pl.when(z + step < zs)
            def _():
                arrival(step - 1, m)[1].wait_recv()

            @pl.when((z + step < zs) & (z > 0))
            def _():
                chain(step, m)[1].start()

        loop(0, n, later)
        forward_proj(step)
        if step == 1:
            for i in range(1, cu):
                x_far(i)[1].wait_recv()
                x_near(i)[0].start()
    loop(1, n, lambda m: params_row(m)[1].wait_recv())
    for i in range(cu):
        x_near(i)[1].wait_recv()
    loop(1, n, lambda m: exchange(m)[0].wait_send())
    loop(1, zs, lambda m: params_line(m)[0].wait_send())
    loop(1, n, lambda m: params_row(m)[0].wait_send())
    for i in range(cu):
        x_near(i)[0].wait_send()
        if i:
            x_far(i)[0].wait_send()
    for step in range(zs - 1):

        def sent(m, step=step):
            @pl.when((z >= step) & (z + 1 < zs))
            def _():
                chain(step, m)[0].wait_send()

            @pl.when((z + step < zs) & (z > 0))
            def _():
                chain(step, m)[1].wait_send()

        loop(0, n, sent)
        sent_proj(step)


def gather_head(x, small, qkv_weight, ffn_in, proj, pairs, docs):
    cu, cl, zs = sizes()
    n = cu * cl
    slab, cols = qkv_weight.shape
    cut = (n, slab, cols // n)
    pad = (8, LANES)
    rows = docs.shape[1]
    column, line = jax.ShapeDtypeStruct((rows, 1), jnp.int32), jax.ShapeDtypeStruct((1, rows), jnp.int32)
    return pl.pallas_call(
        head_kernel,
        in_specs=[ANY, VMEM, ANY, ANY, ANY, pl.BlockSpec(memory_space=pltpu.SMEM), VMEM],
        out_specs=[ANY, ANY, ANY, ANY, *[VMEM] * 6],
        out_shape=[
            jax.ShapeDtypeStruct((cu, cl, *x.shape), x.dtype),
            jax.ShapeDtypeStruct((n, zs, *pad), F32),
            jax.ShapeDtypeStruct((n, zs, *cut[1:]), BF16),
            jax.ShapeDtypeStruct((zs, *proj.shape), BF16),
            jax.ShapeDtypeStruct((cl * zs, ffn_in.shape[0], ffn_in.shape[1] // (cl * zs)), BF16),
            column, column, line, line, jax.ShapeDtypeStruct((rows, 3 * LANES), F32),
        ],
        scratch_shapes=[
            pltpu.VMEM(qkv_weight.shape, F32), pltpu.VMEM(ffn_in.shape, F32), pltpu.VMEM(proj.shape, F32),
            pltpu.VMEM((2 * n, rows // (2 * n)), jnp.int32), DMA((3,)),
            pltpu.VMEM(cut, BF16), pltpu.VMEM(proj.shape, BF16), pltpu.VMEM(pad, F32),
            DMA((4,)), DMA((cu,)), DMA((cu,)), DMA((cu,)), DMA((cu,)), DMA((zs,)), DMA((zs,)), DMA((n,)), DMA((n,)),
            DMA((n,)), DMA((n,)), *[DMA((zs, n + 1))] * 4,
        ],
        cost_estimate=pl.CostEstimate(flops=0, bytes_accessed=200 << 20, transcendentals=0),
        compiler_params=pltpu.CompilerParams(collective_id=0, has_side_effects=True, vmem_limit_bytes=48 << 20),
    )(x, small, qkv_weight, ffn_in, proj, pairs, docs)


ITEMS = 4


def loop(low, high, step):
    def run(m, carry):
        step(m)
        return carry

    lax.fori_loop(low, high, run, 0)


def bits_of(count):
    return [1 << b for b in range(count.bit_length() - 1)]


def combos(bits):
    masks = [0]
    for b in bits:
        masks = masks + [m | b for m in masks]
    return masks


def order_of(item, count):
    return bits_of(count) if item < ITEMS // 2 else bits_of(count)[::-1]


def add_low(left, right):
    return (left.astype(F32) + right.astype(F32)).astype(BF16)


class RowReduce:
    def __init__(self, parts, held, beside, came, load, sib_s, sib_r, out_s, out_r):
        self.parts, self.held, self.beside, self.came = parts, held, beside, came
        self.load, self.sib_s, self.sib_r, self.out_s, self.out_r = load, sib_s, sib_r, out_s, out_r
        self.u, self.c, self.z = place()
        self.count = sizes()[0]
        self.phases = self.count.bit_length() - 1

    def sib(self, mask):
        return Transfer(
            self.parts.at[flip(self.u, mask), 1 - self.c], self.beside.at[mask], self.sib_s.at[mask],
            self.sib_r.at[mask], (self.u, 1 - self.c, self.z),
        )

    def loading(self, mask):
        return pltpu.make_async_copy(
            self.parts.at[flip(self.u, mask), self.c], self.held.at[mask], self.load.at[mask]
        )

    def start(self):
        for mask in reversed(range(self.count)):
            self.sib(mask).start()
            self.loading(mask).start()

    def merge(self):
        for mask in reversed(range(self.count)):
            self.loading(mask).wait()
            self.sib(mask).wait_recv()
            self.held[mask] = add_low(self.held[mask], self.beside[mask])

    def steps(self, item, phase):
        order = order_of(item, self.count)
        slot = self.count - (self.count >> phase)
        for k, rest in enumerate(combos(order[phase + 1 :])):
            yield slot + k, rest, Transfer(
                self.held.at[order[phase] | rest, item], self.came.at[slot + k, item], self.out_s.at[slot + k, item],
                self.out_r.at[slot + k, item], (flip(self.u, order[phase]), self.c, self.z),
            )

    def send(self, item, phase):
        for _, _, transfer in self.steps(item, phase):
            transfer.start()

    def add(self, item, phase):
        for slot, rest, transfer in self.steps(item, phase):
            transfer.wait_recv()
            self.held[rest, item] = add_low(self.held[rest, item], self.came[slot, item])

    def total(self, item):
        ((slot, _, transfer),) = self.steps(item, self.phases - 1)
        transfer.wait_recv()
        return self.held[0, item].astype(F32) + self.came[slot, item].astype(F32)

    def drain(self):
        for mask in range(self.count):
            self.sib(mask).wait_send()
        for item in range(ITEMS):
            for phase in range(self.phases):
                for _, _, transfer in self.steps(item, phase):
                    transfer.wait_send()

    @staticmethod
    def scratch(count, rows, width):
        block = (count, ITEMS, rows // ITEMS, width)
        return [
            pltpu.VMEM(block, BF16), pltpu.VMEM(block, BF16), pltpu.VMEM(block, BF16), DMA((count,)), DMA((count,)),
            DMA((count,)), DMA((count, ITEMS)), DMA((count, ITEMS)),
        ]


class RowGather:
    def __init__(self, own, full, keep, out_s, out_r, sib_s, sib_r):
        self.own, self.full, self.keep = own, full, keep
        self.out_s, self.out_r, self.sib_s, self.sib_r = out_s, out_r, sib_s, sib_r
        self.u, self.c, self.z = place()
        self.count = sizes()[0]
        self.phases = self.count.bit_length() - 1

    def kept(self, item):
        return pltpu.make_async_copy(self.own.at[item], self.full.at[self.u, self.c, item], self.keep.at[item])

    def source(self, mask, item):
        return self.own.at[item] if mask == 0 else self.full.at[flip(self.u, mask), self.c, item]

    def sib(self, mask, item):
        return Transfer(
            self.source(mask, item), self.full.at[flip(self.u, mask), self.c, item], self.sib_s.at[mask, item],
            self.sib_r.at[mask, item], (self.u, 1 - self.c, self.z),
        )

    def steps(self, item, phase):
        order = order_of(item, self.count)
        for k, mask in enumerate(combos(order[:phase])):
            slot = (1 << phase) - 1 + k
            yield mask | order[phase], Transfer(
                self.source(mask, item), self.full.at[flip(self.u, mask), self.c, item], self.out_s.at[slot, item],
                self.out_r.at[slot, item], (flip(self.u, order[phase]), self.c, self.z),
            )

    def start(self, item):
        self.send(item, 0)
        self.sib(0, item).start()
        self.kept(item).start()

    def send(self, item, phase):
        for _, transfer in self.steps(item, phase):
            transfer.start()

    def pass_on(self, item, phase):
        for mask, transfer in self.steps(item, phase):
            transfer.wait_recv()
            self.sib(mask, item).start()

    def drain(self):
        for item in range(ITEMS):
            self.kept(item).wait()
            for mask in range(self.count):
                self.sib(mask, item).wait()
            for phase in range(self.phases):
                for _, transfer in self.steps(item, phase):
                    transfer.wait_send()

    @staticmethod
    def scratch(count):
        return [DMA((ITEMS,)), *[DMA((count, ITEMS))] * 4]


class PlaneGather:
    def __init__(self, own, full, keep, out_s, out_r):
        self.own, self.full, self.keep, self.out_s, self.out_r = own, full, keep, out_s, out_r
        self.u, self.c, self.z = place()
        self.count = sizes()[0]
        self.items = own.shape[0]
        self.phases = self.count.bit_length() - 1

    def kept(self, item):
        return pltpu.make_async_copy(self.own.at[item], self.full.at[self.u, item], self.keep.at[item])

    def steps(self, item, phase):
        order = bits_of(self.count) if item % 2 else bits_of(self.count)[::-1]
        for k, mask in enumerate(combos(order[:phase])):
            slot = (1 << phase) - 1 + k
            block = self.full.at[flip(self.u, mask), item]
            yield Transfer(
                self.own.at[item] if mask == 0 else block, block, self.out_s.at[slot, item],
                self.out_r.at[slot, item], (flip(self.u, order[phase]), self.c, self.z),
            )

    def start(self):
        for item in range(self.items):
            self.kept(item).start()
            for transfer in self.steps(item, 0):
                transfer.start()

    def step(self, phase):
        for item in range(self.items):
            for transfer in self.steps(item, phase - 1):
                transfer.wait_recv()
            if phase < self.phases:
                for transfer in self.steps(item, phase):
                    transfer.start()

    def drain(self):
        for item in range(self.items):
            self.kept(item).wait()
            for phase in range(self.phases):
                for transfer in self.steps(item, phase):
                    transfer.wait_send()

    @staticmethod
    def scratch(count, items):
        return [DMA((items,)), DMA((count, items)), DMA((count, items))]


class LineGather:
    def __init__(self, own, full, keep, up_s, up_r, dn_s, dn_r, sib_s, sib_r):
        self.own, self.full, self.keep = own, full, keep
        self.up_s, self.up_r, self.dn_s, self.dn_r, self.sib_s, self.sib_r = up_s, up_r, dn_s, dn_r, sib_s, sib_r
        self.u, self.c, self.z = place()
        self.count = sizes()[2]

    def kept(self, item):
        return pltpu.make_async_copy(self.own.at[item], self.full.at[self.z, self.c, item], self.keep.at[item])

    def up(self, item, step):
        origin = lax.rem(self.z - step + self.count, self.count)
        block = self.full.at[origin, self.c, item]
        source = self.own.at[item] if step == 0 else block
        to = lax.rem(self.z + 1, self.count)
        return Transfer(source, block, self.up_s.at[step, item], self.up_r.at[step, item], (self.u, self.c, to))

    def down(self, item, step):
        block = self.full.at[lax.rem(self.z + step, self.count), self.c, item]
        source = self.own.at[item] if step == 0 else block
        to = lax.rem(self.z - 1 + self.count, self.count)
        return Transfer(source, block, self.dn_s.at[step, item], self.dn_r.at[step, item], (self.u, self.c, to))

    def sib(self, item, origin, own=False):
        block = self.full.at[origin, self.c, item]
        return Transfer(
            self.own.at[item] if own else block, block, self.sib_s.at[origin, item], self.sib_r.at[origin, item],
            (self.u, 1 - self.c, self.z),
        )

    def start(self, item):
        @pl.when(self.z + 1 < self.count)
        def _():
            self.up(item, 0).start()

        @pl.when(self.z > 0)
        def _():
            self.down(item, 0).start()

        self.sib(item, self.z, True).start()
        self.kept(item).start()

    def forward(self, item, step):
        z, count = self.z, self.count

        @pl.when(z >= step)
        def _():
            self.up(item, step - 1).wait_recv()
            if step < count - 1:

                @pl.when(z + 1 < count)
                def _():
                    self.up(item, step).start()

            self.sib(item, z - step).start()

        @pl.when(z + step < count)
        def _():
            self.down(item, step - 1).wait_recv()
            if step < count - 1:

                @pl.when(z > 0)
                def _():
                    self.down(item, step).start()

            self.sib(item, z + step).start()

    def drain(self):
        z, count = self.z, self.count
        for item in range(ITEMS):
            self.kept(item).wait()
            for origin in range(count):
                self.sib(item, origin).wait()
            for step in range(count - 1):

                @pl.when((z >= step) & (z + 1 < count))
                def _(item=item, step=step):
                    self.up(item, step).wait_send()

                @pl.when((z + step < count) & (z > 0))
                def _(item=item, step=step):
                    self.down(item, step).wait_send()

    @staticmethod
    def scratch(count):
        return [DMA((ITEMS,)), *[DMA((count, ITEMS))] * 6]


def far_first(count, z):
    table = []
    for i in range(count):
        ends = sorted(range(count), key=lambda to: (-abs(to - i), 0 if (to > i) == (2 * i < count) else 1))
        lead = [to for to in ends if (to > i) == (2 * i < count) and to != i]
        rest = [to for to in ends if (to > i) != (2 * i < count) and to != i]
        mixed = []
        while lead or rest:
            mixed += lead[:1] + rest[:1]
            lead, rest = lead[1:], rest[1:]
        table.append(mixed + [i])
    power, term = 1, 1
    for k in range(1, count):
        term = (term * (z - k + 1) * (count - 1)) // k
        power = power + term
    packed = [sum(table[i][k] * count**i for i in range(count)) for k in range(count)]
    return [lax.rem(p // power, count) for p in packed]


class LineReduce:
    def __init__(self, held, from_below, from_above, pieces, up_s, up_r, dn_s, dn_r):
        self.held, self.from_below, self.from_above, self.pieces = held, from_below, from_above, pieces
        self.up_s, self.up_r, self.dn_s, self.dn_r = up_s, up_r, dn_s, dn_r
        self.u, self.c, self.z = place()
        self.count = sizes()[2]

    def up(self, to, piece):
        return Transfer(
            self.held.at[to, piece], self.from_below.at[to, piece], self.up_s.at[to, piece], self.up_r.at[to, piece],
            (self.u, self.c, lax.rem(self.z + 1, self.count)),
        )

    def down(self, to, piece):
        return Transfer(
            self.held.at[to, piece], self.from_above.at[to, piece], self.dn_s.at[to, piece], self.dn_r.at[to, piece],
            (self.u, self.c, lax.rem(self.z - 1 + self.count, self.count)),
        )

    def step(self, t):
        z, count = self.z, self.count
        far_up, far_down = count - 1 - t, t

        def upward(piece):
            @pl.when(z > 0)
            def _():
                self.up(far_up, piece).wait_recv()
                self.held[far_up, piece] = add_low(self.held[far_up, piece], self.from_below[far_up, piece])

            self.up(far_up, piece).start()

        def downward(piece):
            @pl.when(z < count - 1)
            def _():
                self.down(far_down, piece).wait_recv()
                self.held[far_down, piece] = add_low(self.held[far_down, piece], self.from_above[far_down, piece])

            self.down(far_down, piece).start()

        lag = min(3, self.pieces // 2)
        late_up = lag * ((2 * z) // count)

        def one(i):
            piece_up, piece_down = i - late_up, i - (lag - late_up)

            @pl.when((z < far_up) & (piece_up >= 0) & (piece_up < self.pieces))
            def _():
                upward(piece_up)

            @pl.when((z > far_down) & (piece_down >= 0) & (piece_down < self.pieces))
            def _():
                downward(piece_down)

        loop(0, self.pieces + lag, one)

    def total(self, piece, into):
        z, count = self.z, self.count
        into[...] = self.held[z, piece].astype(F32)

        @pl.when(z > 0)
        def _():
            self.up(z, piece).wait_recv()
            into[...] += self.from_below[z, piece].astype(F32)

        @pl.when(z < count - 1)
        def _():
            self.down(z, piece).wait_recv()
            into[...] += self.from_above[z, piece].astype(F32)

    def drain(self):
        z, count = self.z, self.count
        for t in range(count - 1):
            far_up, far_down = count - 1 - t, t

            def one(piece, far_up=far_up, far_down=far_down):
                @pl.when(z < far_up)
                def _():
                    self.up(far_up, piece).wait_send()

                @pl.when(z > far_down)
                def _():
                    self.down(far_down, piece).wait_send()

            loop(0, self.pieces, one)

    @staticmethod
    def scratch(count, pieces, block):
        shape = (count, pieces, *block)
        return [*[pltpu.VMEM(shape, BF16)] * 3, *[DMA((count, pieces))] * 4]


def mid_forward_kernel(branch, x, out_grad, params, cut, hidden, mlp, grads, weight, low, *scratch):
    reduce = RowReduce(branch, *scratch[:8])
    gather = LineGather(low, mlp, *scratch[8:15])
    gather_grads = LineGather(out_grad, grads, *scratch[15:22])
    plane = PlaneGather(cut, weight, *scratch[22:])
    greet(True, True)
    reduce.start()
    for item in range(ITEMS):
        gather_grads.start(item)
    reduce.merge()
    for item in range(ITEMS):
        reduce.send(item, 0)
    for item in range(ITEMS):
        gather_grads.forward(item, 1)
    for phase in range(1, reduce.phases):
        for item in range(ITEMS):
            reduce.add(item, phase - 1)
            reduce.send(item, phase)
    plane.start()
    for step in range(2, gather.count - 1):
        for item in range(ITEMS):
            gather_grads.forward(item, step)
    for item in range(ITEMS):
        state = x[item].astype(F32) + reduce.total(item)
        hidden[item] = state
        low[item] = norm_rows(state, params[0:1], params[1:2])[0].astype(BF16)
        gather.start(item)
    plane.step(1)
    for step in range(1, gather.count):
        for item in range(ITEMS):
            gather.forward(item, step)
        if step == 1:
            for item in range(ITEMS):
                gather_grads.forward(item, gather.count - 1)
    for phase in range(2, plane.phases + 1):
        plane.step(phase)
    gather_grads.drain()
    gather.drain()
    plane.drain()
    reduce.drain()


def mid_forward(branch, x, out_grad, params, cut):
    cu, cl, zs = sizes()
    rows, width = x.shape
    block = (ITEMS, rows // ITEMS, width)
    full = jax.ShapeDtypeStruct((zs, cl, *block), BF16)
    hidden, mlp, grads, weight, _ = pl.pallas_call(
        mid_forward_kernel,
        in_specs=[ANY, VMEM, VMEM, VMEM, ANY],
        out_specs=[VMEM, ANY, ANY, ANY, VMEM],
        out_shape=[
            jax.ShapeDtypeStruct(block, F32), full, full, jax.ShapeDtypeStruct((cu, *cut.shape), BF16),
            jax.ShapeDtypeStruct(block, BF16),
        ],
        scratch_shapes=[
            *RowReduce.scratch(cu, rows, width), *LineGather.scratch(zs), *LineGather.scratch(zs),
            *PlaneGather.scratch(cu, cut.shape[0]),
        ],
        cost_estimate=pl.CostEstimate(flops=0, bytes_accessed=200 << 20, transcendentals=0),
        compiler_params=pltpu.CompilerParams(collective_id=1, has_side_effects=True, vmem_limit_bytes=56 << 20),
    )(branch.reshape(cu, cl, *block), x.reshape(block), out_grad.reshape(block), params, cut)
    group_rows = cl * zs * rows
    return (
        hidden.reshape(rows, width), mlp.reshape(group_rows, width), grads.reshape(group_rows, width),
        weight.reshape(width, cut.shape[2]),
    )


def mid_backward_kernel(
    back, in_weight, hidden, out_grad, params, inner, weight, grads,
    grad_hidden, full, sums, layer_out, weight_grad, low,
    held, below, above, up_s, up_r, dn_s, dn_r, both, beside, total, sib_s, sib_r,
    held_out, below_out, above_out, up_so, up_ro, dn_so, dn_ro, both_out, beside_out, sib_so, sib_ro,
    back_v, in_weight_v, inner_v, weight_v, grads_v, fetch, *scratch,
):
    u, c, z = place()
    _, cl, zs = sizes()
    rows = ITEMS * held.shape[2]
    width = weight_v.shape[1]
    reduce = LineReduce(held, below, above, ITEMS, up_s, up_r, dn_s, dn_r)
    reduce_out = LineReduce(held_out, below_out, above_out, ITEMS, up_so, up_ro, dn_so, dn_ro)
    gather = RowGather(low, full, *scratch)
    fetches = [
        pltpu.make_async_copy(source, into, fetch.at[i])
        for i, (source, into) in enumerate(
            ((back, back_v), (in_weight, in_weight_v), (inner, inner_v), (weight, weight_v), (grads, grads_v))
        )
    ]
    for copy in fetches:
        copy.start()

    def sib(to):
        return Transfer(both.at[to, 1 - c], beside.at[to], sib_s.at[to], sib_r.at[to], (u, 1 - c, z))

    def sib_out(to):
        return Transfer(both_out.at[to, 1 - c], beside_out.at[to], sib_so.at[to], sib_ro.at[to], (u, 1 - c, z))

    tile = 512

    def multiply(to, into, left, product):
        def one(i):
            cols = pl.ds(pl.multiple_of(i * tile, tile), tile)
            here = pl.ds(pl.multiple_of(to * (cl * rows), cl * rows), cl * rows)
            part = product(left[here], cols).astype(BF16)
            into[to, :, :, :, cols] = part.reshape(cl, ITEMS, rows // ITEMS, tile)

        loop(0, width // tile, one)

    order = far_first(zs, z)
    fetches[0].wait()
    fetches[1].wait()
    multiply(order[0], both, back_v, lambda left, cols: dot_t(left, in_weight_v[cols]))
    greet(True, True)
    sib(order[0]).start()
    def settle(to):
        sib(to).wait_recv()
        held[to] = add_low(both[to, c], beside[to])

    def settle_out(to):
        sib_out(to).wait_recv()
        held_out[to] = add_low(both_out[to, c], beside_out[to])

    at_end = (z == 0) | (z == zs - 1)
    inside = jnp.logical_not(at_end)
    for k in range(1, zs):
        multiply(order[k], both, back_v, lambda left, cols: dot_t(left, in_weight_v[cols]))
        sib(order[k]).start()
        settle(order[k - 1])

        @pl.when(at_end)
        def _(t=k - 1):
            reduce.step(t)

    settle(order[zs - 1])

    @pl.when(inside)
    def _():
        reduce.step(0)

    fetches[2].wait()
    fetches[3].wait()
    for k in range(zs):
        multiply(
            order[k], both_out, inner_v,
            lambda left, cols: jnp.dot(left, weight_v[:, cols], preferred_element_type=F32),
        )
        sib_out(order[k]).start()

    @pl.when(inside)
    def _():
        for t in range(1, zs - 1):
            reduce.step(t)

    for to in order:
        settle_out(to)

    @pl.when(at_end)
    def _():
        for t in range(zs - 1):
            reduce_out.step(t)

    sums[...] = jnp.zeros_like(sums)
    for item in range(ITEMS):
        reduce.total(item, total)
        _, hat, inverse = norm_rows(hidden[item], params[0:1], params[1:2])
        grad = total[...]
        sums[0:1] += jnp.sum(grad * hat, axis=0, keepdims=True)
        sums[1:2] += jnp.sum(grad, axis=0, keepdims=True)
        grad = out_grad[item].astype(F32) + norm_back(grad, hat, inverse, params[0:1])
        grad_hidden[item] = grad
        low[item] = grad.astype(BF16)
        gather.start(item)
    fetches[4].wait()

    def outer(i):
        cols = pl.ds(pl.multiple_of(i * tile, tile), tile)
        weight_grad[:, cols] = cross_dot(inner_v[...], grads_v[:, cols]).astype(BF16)

    loop(0, width // tile, outer)
    for phase in range(gather.phases):
        for item in range(ITEMS):
            gather.pass_on(item, phase)
            if phase + 1 < gather.phases:
                gather.send(item, phase + 1)
        if phase == 0:

            @pl.when(inside)
            def _():
                reduce_out.step(0)

    @pl.when(inside)
    def _():
        for t in range(1, zs - 1):
            reduce_out.step(t)

    for item in range(ITEMS):
        reduce_out.total(item, total)
        layer_out[item] = (hidden[item] + total[...]).astype(BF16)
    gather.drain()
    reduce.drain()
    reduce_out.drain()
    for to in range(zs):
        sib(to).wait_send()
        sib_out(to).wait_send()


def mid_backward(back_rows, in_weight, hidden, out_grad, params, inner, weight, grads):
    cu, cl, zs = sizes()
    rows, width = out_grad.shape
    block = (ITEMS, rows // ITEMS, width)
    shares = pltpu.VMEM((zs, *block), BF16)
    both = pltpu.VMEM((zs, cl, *block), BF16)
    grad_hidden, full, sums, layer_out, weight_grad, _ = pl.pallas_call(
        mid_backward_kernel,
        in_specs=[ANY, ANY, VMEM, VMEM, VMEM, ANY, ANY, ANY],
        out_specs=[VMEM, ANY, VMEM, VMEM, VMEM, VMEM],
        out_shape=[
            jax.ShapeDtypeStruct(block, F32),
            jax.ShapeDtypeStruct((cu, cl, *block), BF16),
            jax.ShapeDtypeStruct((2, width), F32),
            jax.ShapeDtypeStruct(block, BF16),
            jax.ShapeDtypeStruct(weight.shape, BF16),
            jax.ShapeDtypeStruct(block, BF16),
        ],
        scratch_shapes=[
            *LineReduce.scratch(zs, ITEMS, block[1:]), both, shares, pltpu.VMEM(block[1:], F32), DMA((zs,)), DMA((zs,)),
            *LineReduce.scratch(zs, ITEMS, block[1:]), both, shares, DMA((zs,)), DMA((zs,)),
            pltpu.VMEM(back_rows.shape, BF16), pltpu.VMEM(in_weight.shape, BF16), pltpu.VMEM(inner.shape, BF16),
            pltpu.VMEM(weight.shape, BF16), pltpu.VMEM(grads.shape, BF16), DMA((5,)), *RowGather.scratch(cu),
        ],
        cost_estimate=pl.CostEstimate(flops=0, bytes_accessed=200 << 20, transcendentals=0),
        compiler_params=pltpu.CompilerParams(collective_id=2, has_side_effects=True, vmem_limit_bytes=62 << 20),
    )(back_rows, in_weight, hidden.reshape(block), out_grad.reshape(block), params, inner, weight, grads)
    return (
        grad_hidden.reshape(rows, width), full.reshape(cu * cl * rows, width), sums, layer_out.reshape(rows, width),
        weight_grad,
    )


def tail_kernel(parts, x, grad_hidden, params, terms, grads, proj, input_grad, small, cut, proj_grad, pile, line_in, row_in, total,
                row_total, line_s, line_r, row_s, row_r, a_send, a_recv, own, held_load, low, *scratch):
    u, c, z = place()
    cu, cl, zs = sizes()
    n, me = cu * cl, u * cl + c
    reduce = RowReduce(parts, *scratch[:8])
    held, held_proj = scratch[8], scratch[15]
    line = LineReduce(*scratch[8:11], n, *scratch[11:15])
    line_proj = LineReduce(*scratch[15:18], 1, *scratch[18:])
    load = pltpu.make_async_copy(grads, held, held_load.at[0])
    load_proj = pltpu.make_async_copy(proj, held_proj, held_load.at[1])
    load.start()
    load_proj.start()
    greet(True, True)
    reduce.start()
    load.wait()
    load_proj.wait()
    line.step(0)
    line_proj.step(0)
    reduce.merge()
    for item in range(ITEMS):
        reduce.send(item, 0)
    for t in range(1, zs - 1):
        line.step(t)
        line_proj.step(t)
    for phase in range(1, reduce.phases):
        for item in range(ITEMS):
            reduce.add(item, phase - 1)
            reduce.send(item, phase)
    pile[...] = terms[...]
    for item in range(ITEMS):
        grad = reduce.total(item)
        _, hat, inverse = norm_rows(x[item].astype(F32), params[0:1], params[1:2])
        pile[0:1] += jnp.sum(grad * hat, axis=0, keepdims=True)
        pile[1:2] += jnp.sum(grad, axis=0, keepdims=True)
        grad = grad_hidden[item] + norm_back(grad, hat, inverse, params[0:1])
        input_grad[item] = grad.astype(BF16)

    def along_line(m):
        return Transfer(pile, line_in.at[m], line_s.at[m], line_r.at[m], (u, c, lax.rem(z + m, zs)))

    def along_row(m):
        other = lax.rem(me + m, n)
        return Transfer(
            total, row_in.at[m], row_s.at[m], row_r.at[m], (other // cl, lax.rem(other, cl), z)
        )

    def exchange(m):
        other = lax.rem(me + m, n)
        return Transfer(
            low.at[other], cut.at[me], a_send.at[m], a_recv.at[m], (other // cl, lax.rem(other, cl), z)
        )

    def landed(m):
        source = lax.rem(me - m + n, n)
        return Transfer(
            low.at[source], cut.at[source], a_send.at[m], a_recv.at[m], (u, 1 - c, z)
        )

    loop(1, zs, lambda m: along_line(m).start())

    def finish(m):
        piece = lax.rem(me + m, n)
        line.total(piece, row_total)
        low[piece] = row_total[...].astype(BF16)

        @pl.when(m > 0)
        def _():
            exchange(m).start()

    loop(0, n, finish)
    line_proj.total(0, proj_grad)
    mine = pltpu.make_async_copy(low.at[me], cut.at[me], own.at[0])
    mine.start()
    total[...] = pile[...]
    for m in range(1, zs):
        along_line(m).wait_recv()
        total[...] += line_in[m]
    loop(1, n, lambda m: along_row(m).start())
    small[...] = total[...]

    def collect(m):
        along_row(m).wait_recv()
        small[...] += row_in[m]

    loop(1, n, collect)
    loop(1, n, lambda m: landed(m).wait_recv())
    mine.wait()
    loop(1, n, lambda m: exchange(m).wait_send())
    loop(1, n, lambda m: along_row(m).wait_send())
    loop(1, zs, lambda m: along_line(m).wait_send())
    reduce.drain()
    line.drain()
    line_proj.drain()


def tail(parts, x, grad_hidden, params, terms, grads, proj):
    cu, cl, zs = sizes()
    n = cu * cl
    rows, width = x.shape
    block = (ITEMS, rows // ITEMS, width)
    piece = grads.shape[2:]
    input_grad, small, cut, proj_grad = pl.pallas_call(
        tail_kernel,
        in_specs=[ANY, VMEM, VMEM, VMEM, VMEM, ANY, ANY],
        out_specs=[VMEM, VMEM, ANY, VMEM],
        out_shape=[
            jax.ShapeDtypeStruct(block, BF16),
            jax.ShapeDtypeStruct((8, width), F32),
            jax.ShapeDtypeStruct((n, *piece), BF16),
            jax.ShapeDtypeStruct(proj.shape[2:], F32),
        ],
        scratch_shapes=[
            pltpu.VMEM((8, width), F32), pltpu.VMEM((zs, 8, width), F32), pltpu.VMEM((n, 8, width), F32),
            pltpu.VMEM((8, width), F32), pltpu.VMEM(piece, F32), DMA((zs,)), DMA((zs,)), DMA((n,)), DMA((n,)),
            DMA((n,)), DMA((n,)), DMA((1,)), DMA((2,)), pltpu.VMEM((n, *piece), BF16),
            *RowReduce.scratch(cu, rows, width), *LineReduce.scratch(zs, n, piece),
            *LineReduce.scratch(zs, 1, proj.shape[2:]),
        ],
        cost_estimate=pl.CostEstimate(flops=0, bytes_accessed=200 << 20, transcendentals=0),
        compiler_params=pltpu.CompilerParams(collective_id=3, has_side_effects=True, vmem_limit_bytes=60 << 20),
    )(parts.reshape(cu, cl, *block), x.reshape(block), grad_hidden.reshape(block), params, terms, grads, proj)
    return input_grad.reshape(rows, width), small, cut, proj_grad


def back_kernel(
    heads, qkv_ref, low_ref, tot_ref, pq_ref, dq_ref, pk_ref, dk_ref, table_ref,
    x, grad_hidden, params, mid_sums, branch, proj, mixed, normed, weight, in_cut,
    input_grad, small, cut, proj_grad, in_pieces,
    gq_ref, gk_ref, gv_ref, joined_ref, branch_ref, proj_ref, mixed_ref, normed_v, weight_v, parts, fetch, in_s, in_r,
    pile, line_in, row_in, total, row_total, line_s, line_r, row_s, row_r, a_s, a_r, own, low, *scratch,
):
    u, c, z = place()
    cu, cl, zs = sizes()
    n, me = cu * cl, u * cl + c
    width = heads * HEAD_DIM
    rows = qkv_ref.shape[0]
    block = row_block(rows)
    slab = low.shape[1]
    group = in_cut.shape[0]
    reduce = RowReduce(parts, *scratch[:8])
    held, held_proj = scratch[8], scratch[15]
    line = LineReduce(*scratch[8:11], n, *scratch[11:15])
    line_proj = LineReduce(*scratch[15:18], 1, *scratch[18:])
    my_place = in_group(0)[3]
    kept = pltpu.make_async_copy(in_cut.at[my_place], in_pieces.at[my_place], own.at[1])
    fetches = [
        pltpu.make_async_copy(source, into, fetch.at[i])
        for i, (source, into) in enumerate(
            ((branch, branch_ref), (proj, proj_ref), (mixed, mixed_ref), (normed, normed_v), (weight, weight_v))
        )
    ]

    def in_exchange(m):
        device, after, _, mine = in_group(m)
        return Transfer(in_cut.at[after], in_pieces.at[mine], in_s.at[m], in_r.at[m], device)

    def in_landed(m):
        device, _, before, _ = in_group(m)
        return Transfer(in_cut.at[before], in_pieces.at[before], in_s.at[m], in_r.at[m], device)

    for copy in (kept, *fetches):
        copy.start()
    greet(True, True, True)
    loop(1, group, lambda m: in_exchange(m).start())
    for copy in fetches[:3]:
        copy.wait()
    tile = 512

    def proj_tile(i):
        cols = pl.ds(pl.multiple_of(i * tile, tile), tile)
        grad = cross_dot(low_ref[...], branch_ref[:, cols]).astype(BF16)
        held_proj[:, 0, :, cols] = grad.reshape(zs, slab, tile)

    loop(0, D // tile, proj_tile)
    at_end = (z == 0) | (z == zs - 1)

    @pl.when(at_end)
    def _():
        for t in range(zs - 1):
            line_proj.step(t)

    gk_ref[...] = jnp.zeros_like(gk_ref)
    gv_ref[...] = jnp.zeros_like(gv_ref)

    def one(step):
        here = pl.ds(pl.multiple_of(step * block, block), block)
        grad_all = dot_t(branch_ref[here], proj_ref[...])
        allowed = (pk_ref[...] <= pq_ref[here]) & (dk_ref[...] == dq_ref[here])
        for head in range(heads):
            cols, key, value = (
                slice(p * width + head * HEAD_DIM, p * width + (head + 1) * HEAD_DIM) for p in range(3)
            )
            q, k, v = qkv_ref[here, cols], qkv_ref[:, key], qkv_ref[:, value]
            inverse = 1.0 / tot_ref[here, head : head + 1]
            grad_mixed = grad_all[:, cols]
            grad_weighted = (grad_mixed * inverse).astype(BF16)
            grad_total = -jnp.sum(grad_mixed * mixed_ref[here, cols], axis=1, keepdims=True) * inverse
            weights = jnp.where(allowed, jnp.exp(dot_t(q, k) * SCALE), 0.0)
            grad_scores = (weights * (dot_t(grad_weighted, v) + grad_total)).astype(BF16)
            gq_ref[here, cols] = jnp.dot(grad_scores, k, preferred_element_type=F32) * SCALE
            gk_ref[:, cols] += cross_dot(grad_scores, q) * SCALE
            gv_ref[:, cols] += cross_dot(weights.astype(BF16), grad_weighted)

    blocks = rows // block
    loop(0, blocks // 2, one)

    @pl.when(jnp.logical_not(at_end))
    def _():
        line_proj.step(0)

    loop(blocks // 2, blocks, one)

    @pl.when(jnp.logical_not(at_end))
    def _():
        for t in range(1, zs - 1):
            line_proj.step(t)


    pile[...] = jnp.zeros_like(pile)
    for part, ref in enumerate((gq_ref, gk_ref, gv_ref)):
        for start in range(0, width, LANES):
            grad = ref[:, start : start + LANES]
            if part < 2:
                grad = turn(grad, table_ref[...], -1.0)
            grad = grad.astype(BF16)
            joined_ref[:, part * width + start : part * width + start + LANES] = grad
            there = pl.ds(pl.multiple_of(me * width + start, LANES), LANES)
            pile[4 + part : 5 + part, there] = jnp.sum(grad.astype(F32), axis=0, keepdims=True)
    for copy in fetches[3:]:
        copy.wait()

    def qkv_tile(i):
        cols = pl.ds(pl.multiple_of(i * zs * slab, zs * slab), zs * slab)
        grad = cross_dot(normed_v[:, cols], joined_ref[...]).astype(BF16)
        for to in range(zs):
            held[to, i] = grad[to * slab : (to + 1) * slab]

    loop(0, n, qkv_tile)

    @pl.when(at_end)
    def _():
        for t in range(zs - 1):
            line.step(t)


    def norm_tile(i):
        to, col = i // (D // tile), lax.rem(i, D // tile) * tile
        cols = pl.ds(pl.multiple_of(col, tile), tile)
        here = pl.ds(pl.multiple_of(to * (rows // cu), rows // cu), rows // cu)
        part = dot_t(joined_ref[here], weight_v[cols]).astype(BF16)
        parts[to, :, :, :, cols] = part.reshape(cl, ITEMS, rows // (n * ITEMS), tile)

    loop(0, cu * (D // tile), norm_tile)
    reduce.start()
    reduce.merge()
    for item in range(ITEMS):
        reduce.send(item, 0)

    @pl.when(jnp.logical_not(at_end))
    def _():
        line.step(0)

    for phase in range(1, reduce.phases):
        for item in range(ITEMS):
            reduce.add(item, phase - 1)
            reduce.send(item, phase)
    pile[2:4] = mid_sums[...]
    for item in range(ITEMS):
        grad = reduce.total(item)
        _, hat, inverse = norm_rows(x[item].astype(F32), params[0:1], params[1:2])
        pile[0:1] += jnp.sum(grad * hat, axis=0, keepdims=True)
        pile[1:2] += jnp.sum(grad, axis=0, keepdims=True)
        grad = grad_hidden[item] + norm_back(grad, hat, inverse, params[0:1])
        input_grad[item] = grad.astype(BF16)

    def along_line(m):
        return Transfer(pile, line_in.at[m], line_s.at[m], line_r.at[m], (u, c, lax.rem(z + m, zs)))

    def along_row(m):
        other = lax.rem(me + m, n)
        return Transfer(total, row_in.at[m], row_s.at[m], row_r.at[m], (other // cl, lax.rem(other, cl), z))

    def exchange(m):
        other = lax.rem(me + m, n)
        return Transfer(low.at[other], cut.at[me], a_s.at[m], a_r.at[m], (other // cl, lax.rem(other, cl), z))

    def landed(m):
        source = lax.rem(me - m + n, n)
        return Transfer(low.at[source], cut.at[source], a_s.at[m], a_r.at[m], (u, 1 - c, z))

    loop(1, zs, lambda m: along_line(m).start())

    @pl.when(jnp.logical_not(at_end))
    def _():
        for t in range(1, zs - 1):
            line.step(t)

    total[...] = pile[...]
    for m in range(1, zs):
        along_line(m).wait_recv()
        total[...] += line_in[m]
    loop(1, n, lambda m: along_row(m).start())

    def finish(piece):
        line.total(piece, row_total)
        low[piece] = row_total[...].astype(BF16)
        m = lax.rem(piece - me + n, n)

        @pl.when(m > 0)
        def _():
            exchange(m).start()

    loop(0, n, finish)
    mine = pltpu.make_async_copy(low.at[me], cut.at[me], own.at[0])
    mine.start()
    line_proj.total(0, proj_grad)
    small[...] = total[...]

    def collect(m):
        along_row(m).wait_recv()
        small[...] += row_in[m]

    loop(1, n, collect)
    loop(1, group, lambda m: in_landed(m).wait_recv())
    loop(1, n, lambda m: landed(m).wait_recv())
    mine.wait()
    kept.wait()
    loop(1, group, lambda m: in_exchange(m).wait_send())
    loop(1, n, lambda m: exchange(m).wait_send())
    loop(1, n, lambda m: along_row(m).wait_send())
    loop(1, zs, lambda m: along_line(m).wait_send())
    reduce.drain()
    line.drain()
    line_proj.drain()


def back(qkv, grad_branch, proj, mixed, mixed_low, totals, marks, table, x, grad_hidden, params, mid_sums, normed,
         weight, in_cut, heads):
    cu, cl, zs = sizes()
    n = cu * cl
    rows, width = x.shape
    total_rows, cols = qkv.shape
    slab = width // (n * zs)
    block = (ITEMS, rows // ITEMS, width)
    piece = (slab, cols)
    group = in_cut.shape[0]
    input_grad, small, cut, proj_grad, in_pieces = pl.pallas_call(
        functools.partial(back_kernel, heads),
        in_specs=[*[VMEM] * 12, *[ANY] * 6],
        out_specs=[VMEM, VMEM, ANY, VMEM, ANY],
        out_shape=[
            jax.ShapeDtypeStruct(block, BF16),
            jax.ShapeDtypeStruct((8, width), F32),
            jax.ShapeDtypeStruct((n, *piece), BF16),
            jax.ShapeDtypeStruct((slab, width), F32),
            jax.ShapeDtypeStruct(in_cut.shape, BF16),
        ],
        scratch_shapes=[
            *[pltpu.VMEM((total_rows, cols // 3), F32)] * 3, pltpu.VMEM(qkv.shape, BF16),
            pltpu.VMEM(grad_branch.shape, BF16), pltpu.VMEM(proj.shape, BF16), pltpu.VMEM(mixed.shape, F32),
            pltpu.VMEM(normed.shape, BF16), pltpu.VMEM(weight.shape, BF16), pltpu.VMEM((cu, cl, *block), BF16),
            DMA((5,)), DMA((group,)), DMA((group,)),
            pltpu.VMEM((8, width), F32), pltpu.VMEM((zs, 8, width), F32), pltpu.VMEM((n, 8, width), F32),
            pltpu.VMEM((8, width), F32), pltpu.VMEM(piece, F32), DMA((zs,)), DMA((zs,)), DMA((n,)), DMA((n,)),
            DMA((n,)), DMA((n,)), DMA((2,)), pltpu.VMEM((n, *piece), BF16),
            *RowReduce.scratch(cu, rows, width), *LineReduce.scratch(zs, n, piece),
            *LineReduce.scratch(zs, 1, (slab, width)),
        ],
        cost_estimate=pl.CostEstimate(flops=0, bytes_accessed=400 << 20, transcendentals=0),
        compiler_params=pltpu.CompilerParams(collective_id=5, has_side_effects=True, vmem_limit_bytes=63 << 20),
    )(
        qkv, mixed_low, totals, *marks, table, x.reshape(block), grad_hidden.reshape(block), params, mid_sums,
        grad_branch, proj, mixed, normed, weight, in_cut,
    )
    return input_grad.reshape(rows, width), small, cut, proj_grad, in_pieces


def body(
    inputs, out_grad, doc_ids, block_pairs, qkv_weight, proj_weight, ffn_in_weight, ffn_out_weight, small_params,
    qkv_first, proj_first, ffn_in_first, ffn_out_first, small_first,
    qkv_second, proj_second, ffn_in_second, ffn_out_second, small_second,
):
    bf16 = jnp.bfloat16
    tok_rows = inputs.shape[1]
    half_rows = tok_rows // 2
    cu, cl, zs = lax.axis_size("cu"), lax.axis_size("cl"), lax.axis_size("fsdp")
    ctx_count = cu * cl
    group = cl * zs
    seq_len = tok_rows * ctx_count
    my_index = lax.axis_index(ROW)
    heads = HEADS // ctx_count
    width = heads * HEAD_DIM
    slab = qkv_weight.shape[0]
    units = ffn_out_weight.shape[0]
    hidden = units * cu
    row_in, params, qkv_low, proj_low, in_cast, pos_col, doc_col, pos_row, doc_row, table = gather_head(
        inputs[0], small_params, qkv_weight, ffn_in_weight, proj_weight, block_pairs, doc_ids
    )
    proj_low = proj_low.reshape(width, D)
    marks = (pos_col, doc_col, pos_row, doc_row)
    row_in, in_cast, out_weight_later = lax.optimization_barrier((row_in, in_cast, ffn_out_weight))
    out_low = lax.all_gather(out_weight_later.astype(bf16), "cu", axis=0, tiled=True)
    in_cut = lax.all_to_all(in_cast.reshape(group * slab, 2 * hidden), FFN_GROUP, split_axis=0, concat_axis=0, tiled=True)
    row_in = row_in.reshape(seq_len, D)
    params = params[:, :, :7, :slab].transpose(2, 0, 1, 3).reshape(7, D)
    qkv_low = qkv_low.reshape(D, 3 * width)

    bias = lax.dynamic_slice_in_dim(params[4:7], my_index * width, width, 1).reshape(1, 3 * width)
    attn_in, qkv = project(row_in, params[0:2], qkv_low, bias, table)
    mixed, mixed_low, totals, branch = attend(qkv, proj_low, marks, heads)
    branch, in_cut = lax.optimization_barrier((branch, in_cut))
    hidden_state, mlp_in, grad_all, in_low = mid_forward(
        branch, inputs[0], out_grad[0], params[2:4], in_cut.reshape(group, slab, 2 * hidden)
    )

    inner_low, grad_gate_up, grad_ffn_in = feed(mlp_in, grad_all, in_low, out_low)
    in_grad_cut = lax.psum_scatter(grad_ffn_in, "cu", scatter_dimension=0, tiled=True)

    grad_hidden, grad_branch, mid_sums, layer_out, grad_ffn_out = mid_backward(
        grad_gate_up, in_low, hidden_state, out_grad[0], params[2:4], inner_low, out_low, grad_all
    )
    layer_out = layer_out[None]
    in_grad_cut, grad_branch = lax.optimization_barrier((in_grad_cut, grad_branch))
    in_grad_cut = in_grad_cut.reshape(group, slab, 2 * hidden)
    grad_ffn_out, in_grad_cut = lax.optimization_barrier((grad_ffn_out, in_grad_cut))
    ffn_out_grad = lax.psum_scatter(grad_ffn_out, "cu", scatter_dimension=0, tiled=True)
    if seq_len <= 1024 and width % LANES == 0:
        input_grad, small_sum, qkv_grad_cut, proj_grad, in_grad = back(
            qkv, grad_branch, proj_low, mixed, mixed_low, totals, marks, table, inputs[0], grad_hidden, params[0:2],
            mid_sums, attn_in, qkv_low, in_grad_cut, heads,
        )
    else:
        grad_proj = cross_dot(mixed_low, grad_branch).astype(bf16)
        grad_joined, bias_own, in_grad = attend_back(
            qkv, grad_branch, proj_low, mixed, totals, marks, table, in_grad_cut, heads
        )
        grad_norm_part = back_dot(grad_joined, qkv_low).astype(bf16)
        grad_qkv = (
            cross_dot(attn_in, grad_joined).astype(bf16).reshape(ctx_count, zs, slab, 3 * width).transpose(1, 0, 2, 3)
        )
        bias_own = bias_own.reshape(3, width)
        grad_bias = lax.dynamic_update_slice(jnp.zeros((3, D), jnp.float32), bias_own, (0, my_index * width))
        zero_rows = jnp.zeros((2, D), jnp.float32)
        terms = jnp.concatenate([zero_rows, mid_sums, grad_bias, zero_rows[:1]], axis=0)
        input_grad, small_sum, qkv_grad_cut, proj_grad = tail(
            grad_norm_part, inputs[0], grad_hidden, params[0:2], terms, grad_qkv, grad_proj.reshape(zs, 1, slab, D)
        )
    input_grad = input_grad[None]
    my_slab = (my_index * zs + lax.axis_index("fsdp")) * slab
    small_grad = lax.dynamic_slice_in_dim(small_sum, my_slab, slab, 1)[:7]

    proj_fan = max(8 * D // seq_len, 1)
    in_new, qkv_new, out_new, proj_new = adam_all(
        (
            (ffn_in_weight, ffn_in_first, ffn_in_second, in_grad),
            (qkv_weight, qkv_first, qkv_second, qkv_grad_cut),
            (ffn_out_weight, ffn_out_first, ffn_out_second, ffn_out_grad),
            (proj_weight, proj_first, proj_second, proj_grad),
        ),
        (2.0 / math.sqrt(D), 2.0 / math.sqrt(D), 2.0 / math.sqrt(FF), 2.0 / math.sqrt(proj_fan)),
    )
    small_new = adam_update(small_params, small_first, small_second, small_grad, small_rate, 0.0)
    news = (qkv_new, proj_new, in_new, out_new, small_new)
    return (layer_out, input_grad, *(n[0] for n in news), *(n[1] for n in news), *(n[2] for n in news), small_grad)


def solution(mesh):
    ctx_count, fsdp_count = mesh.devices.shape
    fine = Mesh(mesh.devices.reshape(ctx_count // 2, 2, fsdp_count), ("cu", "cl", "fsdp"))
    tokens = P("fsdp", ROW, None)
    matrix = P(EVERY, None)
    small = P(None, EVERY)
    five = (matrix, matrix, matrix, matrix, small)
    in_specs = (tokens, tokens, P("fsdp", None), P(), *five, *five, *five)
    out_specs = (tokens, tokens, *five, *five, *five, small)
    return jax.shard_map(body, mesh=fine, in_specs=in_specs, out_specs=out_specs, check_vma=False)
```
